32 devices in a mesh: row: 8 (over y, x, core), col: 4 (over z).
Axes of the slice: x: 2, y: 2, z: 4, core: 2. Of those that a mesh axis runs over, the one named last changes fastest.
Arguments:
- inputs: bfloat16 [12288, 768], P(('row', 'col')), may hold values from -6 to 6
- attn_gain: bfloat16 [768], replicated, may hold values from 0.5 to 1.5
- qkv_weight: bfloat16 [768, 2304], P('row', 'col'), may hold values from -0.21875 to 0.21875
- out_weight: bfloat16 [768, 768], P('col', 'row'), may hold values from -1.5 to 1.5
- ffn_gain: bfloat16 [768], replicated, may hold values from 0.5 to 1.5
- router_weight: bfloat16 [768, 12], replicated, may hold values from -0.15625 to 0.15625
- carry_weight: bfloat16 [12, 12], replicated, may hold values from -1.75 to 1.75
- const_weight: bfloat16 [2, 768, 2], replicated, may hold values from -0.21875 to 0.21875
- const_vector: bfloat16 [2, 768], replicated, may hold values from -6 to 6
- gate_weight: bfloat16 [8, 768, 2048], P(None, 'row', 'col'), may hold values from -0.21875 to 0.21875
- up_weight: bfloat16 [8, 768, 2048], P(None, 'row', 'col'), may hold values from -0.21875 to 0.21875
- down_weight: bfloat16 [8, 2048, 768], P(None, 'col', 'row'), may hold values from -0.125 to 0.125
- prev_logits: bfloat16 [12, 12288], P(None, ('row', 'col')), may hold values from -4 to 4
- seq_lengths: int32 [8, 4], P('row'), may hold values from 1 to 1533, as said below
- expert_routes: int32 [12288, 2], P('row'), may hold values from 0 to 11, all different within a row; in each aligned block of 1536 rows (0 to 1535, 1536 to 3071, ...) at most 384 rows name the same one
- cotangent: bfloat16 [12288, 768], P(('row', 'col')), may hold values from -6 to 6
Outputs:
- layer_out: bfloat16 [12288, 768], P(('row', 'col'))
- input_grad: float32 [12288, 768], P(('row', 'col'))
- attn_gain_grad: float32 [768], replicated
- qkv_grad: float32 [768, 2304], P('row', 'col')
- out_grad: float32 [768, 768], P('col', 'row')
- ffn_gain_grad: float32 [768], replicated
- router_grad: float32 [768, 12], replicated
- carry_grad: float32 [12, 12], replicated
- const_grad: float32 [2, 768, 2], replicated
- vector_grad: float32 [2, 768], replicated
- gate_grad: float32 [8, 768, 2048], P(None, 'row', 'col')
- up_grad: float32 [8, 768, 2048], P(None, 'row', 'col')
- down_grad: float32 [8, 2048, 768], P(None, 'col', 'row')
- prev_grad: float32 [12, 12288], P(None, ('row', 'col'))
The draws below stay inside these ranges and needn't reach their ends.
Inputs may be any that keep to these rules, and one draw needn't show every extreme that they name: `seq_lengths`: in each row group the lengths sum to at most 1536; the remaining tokens at the end of the group are padding. One sequence of each group starts within the group's first 384 tokens and ends within its last 384. `expert_routes`: each token names two different routes: 0 to 7 are feed-forward experts, 8 is the zero expert, 9 the copy expert, 10 and 11 the constant experts. Among the tokens of one row group no route is named more than 384 times.
All inputs are finite; a program needn't handle non-finite values.
Results may differ from the reference program's by a relative error of at most 0.02.
Values may be sent and summed in bfloat16 or wider, within the bound.
A program may use at most 256 MiB of HBM per device.

```python
import math
from functools import partial
import jax
import jax.numpy as jnp
import numpy as np
from jax import lax

D = 768
HEADS = 12
HEAD_DIM = 64
FF = 2048
EXPERTS = 8
ROUTES = 12
TOK_DEV = 384
SEQS = 4
GROUPS = 8
TOK_ROW = 1536
TOKENS = 12288
CAPACITY = 384


def draw_seq_lengths(key, part):
    key = jax.random.fold_in(key, 7)
    key_short, key_pad, key_full, key_long = jax.random.split(key, 4)
    short_room = (TOK_DEV - 1) // SEQS
    shorts = jax.random.randint(key_short, (GROUPS, SEQS), 1, short_room + 1)
    padding = jax.random.randint(key_pad, (GROUPS,), 0, short_room + 1)
    full_group = jax.random.randint(key_full, (), 0, GROUPS)
    group_index = jnp.arange(GROUPS)
    shorts = jnp.where(group_index[:, None] == full_group, 1, shorts)
    padding = jnp.where(group_index == full_group, 0, padding)
    long_index = jax.random.randint(key_long, (GROUPS,), 0, SEQS)
    is_long = jnp.arange(SEQS)[None, :] == long_index[:, None]
    others = jnp.sum(jnp.where(is_long, 0, shorts), axis=1)
    longest = TOK_ROW - padding - others
    return jnp.where(is_long, longest[:, None], shorts).astype(jnp.int32)


def block_scale(stream_key, dims, pieces, smallest, top_value):
    factor_of, own = 1.0, jax.random.fold_in(stream_key, 6)
    for dim, shards_of in pieces:
        steps = jnp.exp(jax.random.uniform(jax.random.fold_in(own, dim), (shards_of,), jnp.float32, smallest / len(pieces), top_value / len(pieces)))
        factor_of = factor_of * jnp.repeat(steps, dims[dim] // shards_of).reshape([-1 if axis == dim else 1 for axis in range(len(dims))])
    return factor_of


def shared_out(own_key, own, number, rows, count, top, bound, slope):
    sequence = jax.random.permutation(own_key, count)
    heavy_load, ordinary = load_shares(count, rows * top, bound, slope, True), load_shares(count, rows * top, bound, slope, False)
    places = jnp.arange(count)

    def named(lengths, turn):
        used = int((lengths > 0).sum())
        fixed = max(1, used // 4)
        passed = fixed + (places - fixed + turn * (used - fixed)) % max(1, count - fixed)
        return jnp.zeros((count,), jnp.int32).at[sequence[jnp.where(places < fixed, places, passed)]].set(jnp.asarray(lengths, jnp.int32))

    lengths = jnp.where(number % 4 == 0, named(heavy_load, number // 4), named(ordinary, number - number // 4 - 1))
    mixed = jax.random.permutation(jax.random.fold_in(own, 3), count)
    donor, sink = mixed[0:count // 2 * 2:2], mixed[1:count // 2 * 2:2]
    margin = jnp.minimum(lengths[donor] - 1, bound - lengths[sink]) // 2
    margin = jnp.where((donor == sequence[0]) | (sink == sequence[0]) | (lengths[sink] == 0), 0, jnp.maximum(margin, 0))
    passed = jax.random.randint(jax.random.fold_in(own, 4), (count // 2,), 0, 1 << 20) % (margin + 1)
    lengths = lengths.at[donor].add(-passed).at[sink].add(passed)
    items = jnp.searchsorted(jnp.cumsum(lengths), jnp.arange(rows * top), side="right").astype(jnp.int32)
    grid = items.reshape(top, rows).T
    grid = grid[jax.random.permutation(jax.random.fold_in(own, 1), rows)]
    turn = jax.random.randint(jax.random.fold_in(own, 2), (rows, 1), 0, top)
    return jnp.take_along_axis(grid, (jnp.arange(top)[None, :] + turn) % top, axis=1)


def load_shares(count, total, reach, slope, full):
    portions = [(1 << 20) // math.isqrt(grade ** slope) + 1 for grade in range(1, count + 1)]
    largest = reach if full else min(reach, max(-(-total // count), total * portions[0] // sum(portions)))
    least = 1 if total - largest >= count - 1 else 0
    holding, surplus = [largest] + [least] * (count - 1), total - largest - least * (count - 1)
    while surplus > 0:
        movable = [i for i in range(1, count) if holding[i] < largest] or [i for i in range(1, count) if holding[i] < reach]
        pool, left = sum([portions[i] for i in movable]), surplus
        for i in movable:
            more = min(reach - holding[i], max(1, left * portions[i] // pool), surplus)
            holding[i] = holding[i] + more
            surplus = surplus - more
    return np.array(holding)


def gaussian(own_key, extent, width, reach, shards=(), kind=jnp.bfloat16):
    values = width * jax.random.normal(own_key, extent, jnp.float32)
    if shards:
        values = values * block_scale(own_key, extent, shards, -0.22, 0.18)
    return jnp.clip(values, -reach, reach).astype(kind)


def setup_inputs(seed: int = 0) -> dict:
    arg_keys = jax.random.split(jax.random.key(seed), 17)
    inputs = gaussian(arg_keys[0], (TOKENS, D), 1.0, 6.0, ((0, 32),))
    attn_gain = jnp.clip(1.0 + 0.1 * jax.random.normal(arg_keys[1], (D,), jnp.float32), 0.5, 1.5).astype(jnp.bfloat16)
    qkv_weight = gaussian(arg_keys[2], (D, 3 * D), D ** -0.5, 0.21875, ((0, 8), (1, 4)))
    out_weight = gaussian(arg_keys[3], (D, D), (D // 48) ** -0.5, 1.5, ((0, 4), (1, 8)))
    ffn_gain = jnp.clip(1.0 + 0.1 * jax.random.normal(arg_keys[4], (D,), jnp.float32), 0.5, 1.5).astype(jnp.bfloat16)
    router_weight = gaussian(arg_keys[5], (D, ROUTES), (2 * D) ** -0.5, 0.15625)
    carry_weight = gaussian(arg_keys[6], (ROUTES, ROUTES), ROUTES ** -0.5, 1.75)
    const_weight = gaussian(arg_keys[7], (2, D, 2), D ** -0.5, 0.21875)
    const_vector = gaussian(arg_keys[8], (2, D), 1.0, 6.0)
    gate_weight = gaussian(arg_keys[9], (EXPERTS, D, FF), D ** -0.5, 0.21875, ((1, 8), (2, 4)))
    up_weight = gaussian(arg_keys[10], (EXPERTS, D, FF), D ** -0.5, 0.21875, ((1, 8), (2, 4)))
    down_weight = gaussian(arg_keys[11], (EXPERTS, FF, D), FF ** -0.5, 0.125, ((1, 4), (2, 8)))
    prev_logits = gaussian(arg_keys[12], (ROUTES, TOKENS), 0.5, 4.0, ((1, 32),))
    seq_lengths = draw_seq_lengths(jax.random.fold_in(arg_keys[16], 71), 0)
    expert_routes_keys = jax.random.split(jax.random.fold_in(arg_keys[14], 1), TOKENS // TOK_ROW)
    expert_routes_turns = jax.random.permutation(jax.random.fold_in(arg_keys[14], 3), TOKENS // TOK_ROW)
    expert_routes = jax.vmap(lambda own, number: shared_out(jax.random.fold_in(arg_keys[14], 2), own, number, TOK_ROW, ROUTES, 2, CAPACITY, 1))(expert_routes_keys, expert_routes_turns).reshape((TOKENS, 2))
    cotangent = gaussian(arg_keys[15], (TOKENS, D), 1.0, 6.0, ((0, 32),))
    return dict(inputs=inputs, attn_gain=attn_gain, qkv_weight=qkv_weight, out_weight=out_weight, ffn_gain=ffn_gain, router_weight=router_weight, carry_weight=carry_weight, const_weight=const_weight, const_vector=const_vector, gate_weight=gate_weight, up_weight=up_weight, down_weight=down_weight, prev_logits=prev_logits, seq_lengths=seq_lengths, expert_routes=expert_routes, cotangent=cotangent)


EPS = 1e-06
BASE = 10000.0
NEG = -1e+30
HIGH = lax.Precision.HIGHEST

@jax.custom_vjp
def low(v):
    return lax.optimization_barrier(v.astype(jnp.bfloat16)).astype(jnp.float32)

@jax.custom_vjp
def low_back(v):
    return v

def low_keep(v):
    return (low(v), None)

def low_pass(kept, grad):
    return (grad,)

def back_keep(v):
    return (v, None)

def back_low(kept, grad):
    return (low(grad),)
low.defvjp(low_keep, low_pass)
low_back.defvjp(back_keep, back_low)

def rotate(block_value, positions, first_col, direction):
    row_count, col_count = block_value.shape
    column = first_col + jnp.arange(0, col_count, 2, dtype=jnp.int32)
    inner_col = column % D
    section = column // D
    head_pair = inner_col % HEAD_DIM // 2
    exponent = (2 * head_pair).astype(jnp.float32) / HEAD_DIM
    frequency = jnp.exp(-exponent * math.log(BASE))
    turned_on = (section < 2).astype(jnp.float32)
    angles = positions.astype(jnp.float32)[:, None] * (frequency * turned_on)[None, :]
    cosine = jnp.cos(angles)
    sines = direction * jnp.sin(angles)
    paired = block_value.reshape(row_count, col_count // 2, 2)
    first_part = paired[:, :, 0]
    second_part = paired[:, :, 1]
    rotated = jnp.stack([first_part * cosine - second_part * sines, second_part * cosine + first_part * sines], axis=2)
    return rotated.reshape(row_count, col_count)

def sequence_info(lengths_row, row_total):
    seq_count = lengths_row.shape[0]
    ends = jnp.cumsum(lengths_row).astype(jnp.int32)
    starts = ends - lengths_row
    token_place = jnp.arange(row_total, dtype=jnp.int32)
    seq_index = lax.optimization_barrier(jnp.sum((token_place[:, None] >= ends[None, :]).astype(jnp.int32), axis=1))
    member = seq_index[:, None] == jnp.arange(seq_count, dtype=jnp.int32)[None, :]
    begin = lax.optimization_barrier(jnp.sum(jnp.where(member, starts[None, :], 0), axis=1))
    return (seq_index, token_place - begin, seq_index < seq_count)

def attend(queries, keys, values, seq_index, token_place):
    row_total = queries.shape[0]
    block_rows = min(row_total, 512)
    score_scale = 1.0 / math.sqrt(HEAD_DIM)
    query_heads = queries.reshape(row_total // block_rows, block_rows, HEADS, HEAD_DIM)
    key_heads = keys.reshape(row_total, HEADS, HEAD_DIM)
    value_heads = values.reshape(row_total, HEADS, HEAD_DIM)

    def one_block(block_items):
        query_block, query_seq, query_place = block_items
        raw_scores = jnp.einsum('qhd,khd->hqk', query_block, key_heads, precision=HIGH) * score_scale
        allowed = (query_seq[:, None] == seq_index[None, :]) & (token_place[None, :] <= query_place[:, None])
        scores = low_back(jnp.where(allowed[None], raw_scores, NEG))
        log_total = jax.nn.logsumexp(scores, axis=2, keepdims=True)
        probs = low(jnp.exp(scores - log_total))
        return jnp.einsum('hqk,khd->qhd', probs, value_heads, precision=HIGH)
    blocks_out = lax.map(jax.checkpoint(one_block), (query_heads, seq_index.reshape(-1, block_rows), token_place.reshape(-1, block_rows)))
    return blocks_out.reshape(row_total, D)

def group_forward(weights, inputs_group, prev_group, lengths_row, routes_group):
    attn_gain, qkv_weight, out_weight, ffn_gain, router_weight, carry_weight, const_weight, const_vector, gate_weight, up_weight, down_weight = weights
    row_total = inputs_group.shape[0]
    capacity = row_total // 4
    seq_index, positions, valid_mask = sequence_info(lengths_row, row_total)
    token_place = jnp.arange(row_total, dtype=jnp.int32)
    scale_attn = lax.rsqrt(lax.optimization_barrier(jnp.mean(inputs_group * inputs_group, axis=1, keepdims=True)) + EPS)
    normed1 = low(inputs_group * scale_attn * attn_gain)
    projected = low_back(jnp.dot(normed1, qkv_weight, precision=HIGH))
    turned = low(rotate(projected, positions, 0, 1.0))
    attended = attend(turned[:, :D], turned[:, D:2 * D], turned[:, 2 * D:], seq_index, token_place)
    mixed_in = low(low_back(attended * valid_mask.astype(jnp.float32)[:, None]))
    branch = low_back(jnp.dot(mixed_in, out_weight, precision=HIGH))
    middle = inputs_group + branch
    scale_ffn = lax.rsqrt(lax.optimization_barrier(jnp.mean(middle * middle, axis=1, keepdims=True)) + EPS)
    normed2 = low(middle * scale_ffn * ffn_gain)
    logits = jnp.dot(normed2, router_weight, precision=HIGH) + jnp.dot(prev_group, carry_weight, precision=HIGH)
    picked = jnp.take_along_axis(logits, routes_group, axis=1)
    gate_values = jax.nn.softmax(picked, axis=1)
    flat_route = routes_group.reshape(-1)
    route_hits = (flat_route[:, None] == jnp.arange(EXPERTS, dtype=jnp.int32)[None, :]).astype(jnp.int32)
    slot_index = lax.optimization_barrier(jnp.sum((jnp.cumsum(route_hits, axis=0) - 1) * route_hits, axis=1))
    dump_slot = EXPERTS * capacity
    target = jnp.where(flat_route < EXPERTS, flat_route * capacity + slot_index, dump_slot).astype(jnp.int32)
    slot_owner = jnp.full((dump_slot + 1,), row_total, jnp.int32).at[target].set(jnp.arange(2 * row_total, dtype=jnp.int32) // 2)
    padded = jnp.concatenate([normed2, jnp.zeros((1, D), jnp.float32)], axis=0)
    expert_in = padded[slot_owner[:dump_slot]].reshape(EXPERTS, capacity, D)
    gate_pre = low_back(jnp.einsum('ecd,edf->ecf', expert_in, gate_weight, precision=HIGH))
    up_pre = low_back(jnp.einsum('ecd,edf->ecf', expert_in, up_weight, precision=HIGH))
    hidden = low(jax.nn.silu(gate_pre) * up_pre)
    expert_out = low_back(jnp.einsum('ecf,efd->ecd', hidden, down_weight, precision=HIGH))
    out_rows = jnp.concatenate([expert_out.reshape(dump_slot, D), jnp.zeros((1, D), jnp.float32)], axis=0)
    chosen_out = out_rows[target].reshape(row_total, 2, D)
    copy_hit = (routes_group == EXPERTS + 1).astype(jnp.float32)
    const_alpha = jax.nn.softmax(jnp.einsum('td,jdk->tjk', normed2, const_weight, precision=HIGH), axis=2)
    const_out = const_alpha[:, :, 0:1] * normed2[:, None, :] + const_alpha[:, :, 1:2] * const_vector[None, :, :]
    const_hit = (routes_group[:, :, None] == (EXPERTS + 2 + jnp.arange(2, dtype=jnp.int32))[None, None, :]).astype(jnp.float32)
    slot_out = chosen_out + copy_hit[:, :, None] * normed2[:, None, :] + jnp.einsum('tsj,tjd->tsd', const_hit, const_out, precision=HIGH)
    return middle + lax.optimization_barrier(jnp.sum(gate_values[:, :, None] * slot_out, axis=1))

def reference(inputs, attn_gain, qkv_weight, out_weight, ffn_gain, router_weight, carry_weight, const_weight, const_vector, gate_weight, up_weight, down_weight, prev_logits, seq_lengths, expert_routes, cotangent):
    params = tuple((value.astype(jnp.float32) for value in (attn_gain, qkv_weight, out_weight, ffn_gain, router_weight, carry_weight, const_weight, const_vector, gate_weight, up_weight, down_weight)))
    group_count = seq_lengths.shape[0]
    routes_grouped = expert_routes.reshape(group_count, -1, 2)
    inputs_grouped = inputs.astype(jnp.float32).reshape(group_count, -1, D)
    prev_grouped = prev_logits.astype(jnp.float32).T.reshape(group_count, -1, ROUTES)

    def whole(inputs_all, prev_all, weights):
        one_group = jax.checkpoint(partial(group_forward, weights))

        def step(carry_value, group_items):
            return (carry_value, one_group(*group_items))
        unused, results = lax.scan(step, jnp.zeros((), jnp.float32), (inputs_all, prev_all, seq_lengths, routes_grouped))
        return results
    result, pullback = jax.vjp(whole, inputs_grouped, prev_grouped, params)
    grad_inputs, grad_prev, grad_params = pullback(cotangent.astype(jnp.float32).reshape(group_count, -1, D))
    return (result.reshape(-1, D).astype(jnp.bfloat16), grad_inputs.reshape(-1, D), grad_params[0], grad_params[1], grad_params[2], grad_params[3], grad_params[4], grad_params[5], grad_params[6], grad_params[7], grad_params[8], grad_params[9], grad_params[10], grad_prev.reshape(-1, ROUTES).T)
```

```python
import functools
import math

import jax
import jax.numpy as jnp
from jax import lax
from jax.experimental import pallas as pl
from jax.experimental.pallas import tpu as pltpu
from jax.sharding import PartitionSpec as P

D = 768
HEADS = 12
HEAD_DIM = 64
EXPERTS = 8
ROUTES = 12


EPS = 1e-06
BASE = 10000.0
NEG = -1e30
HIGH = lax.Precision.HIGHEST
CONTRACT_FIRST = (((0,), (0,)), ((), ()))
CONTRACT_LAST = (((1,), (1,)), ((), ()))


def rotate(block_value, positions, first_col, direction):
    row_count, col_count = block_value.shape
    column = first_col + jnp.arange(0, col_count, 2, dtype=jnp.int32)
    inner_col = column % D
    section = column // D
    head_pair = inner_col % HEAD_DIM // 2
    exponent = (2 * head_pair).astype(jnp.float32) / HEAD_DIM
    frequency = jnp.exp(-exponent * math.log(BASE))
    turned_on = (section < 2).astype(jnp.float32)
    angles = positions.astype(jnp.float32)[:, None] * (frequency * turned_on)[None, :]
    cosine = jnp.cos(angles)
    sines = direction * jnp.sin(angles)
    paired = block_value.reshape(row_count, col_count // 2, 2)
    first_part = paired[:, :, 0]
    second_part = paired[:, :, 1]
    rotated = jnp.stack(
        [first_part * cosine - second_part * sines, second_part * cosine + first_part * sines],
        axis=2,
    )
    return rotated.reshape(row_count, col_count)


def sequence_info(lengths_row, row_total):
    seq_count = lengths_row.shape[0]
    ends = jnp.cumsum(lengths_row)
    starts = ends - lengths_row
    token_place = jnp.arange(row_total, dtype=jnp.int32)
    seq_index = jnp.sum((token_place[:, None] >= ends[None, :]).astype(jnp.int32), axis=1)
    member = seq_index[:, None] == jnp.arange(seq_count, dtype=jnp.int32)[None, :]
    begin = jnp.sum(jnp.where(member, starts[None, :], 0), axis=1)
    return (seq_index, token_place - begin, seq_index < seq_count)


def partial_sums(term_value):
    return lax.psum_scatter(
        term_value.astype(jnp.bfloat16), "col", scatter_dimension=0, tiled=True
    ).astype(jnp.float32)


def whole_columns(part_value):
    return lax.all_gather(part_value, "col", axis=0, tiled=True)


def to_heads(block_value):
    return lax.all_to_all(block_value, "col", split_axis=0, concat_axis=1, tiled=True)


def to_features(block_value):
    return lax.all_to_all(block_value, "col", split_axis=1, concat_axis=0, tiled=True)


def key_scores(query_heads, key_block, query_seq, query_place, key_seq, key_place, score_scale):
    raw_scores = (
        jnp.einsum("qhd,khd->hqk", query_heads, key_block, preferred_element_type=jnp.float32)
        * score_scale
    )
    allowed = (query_seq[:, None] == key_seq[None, :]) & (
        key_place[None, :] <= query_place[:, None]
    )
    return (jnp.where(allowed[None], raw_scores, NEG), allowed)


def split_keys(key_values, seq_index, token_place, block_rows):
    count_blocks = key_values.shape[0] // block_rows
    blocks_kv = key_values.reshape(count_blocks, block_rows, 2, HEADS, HEAD_DIM)
    return (
        blocks_kv,
        seq_index.reshape(count_blocks, block_rows),
        token_place.reshape(count_blocks, block_rows),
    )


def attend_forward(
    queries, key_values, query_seq, query_place, seq_index, token_place, block_rows, score_scale
):
    local_rows = queries.shape[0]
    query_heads = queries.reshape(local_rows, HEADS, HEAD_DIM)
    key_items = split_keys(key_values, seq_index, token_place, block_rows)

    def max_step(running, block_items):
        running_max, running_sum = running
        kv_block, key_seq, key_place = block_items
        scores, allowed = key_scores(
            query_heads, kv_block[:, 0], query_seq, query_place, key_seq, key_place, score_scale
        )
        new_max = jnp.maximum(running_max, jnp.max(scores, axis=2))
        shifted = jnp.where(allowed[None], jnp.exp(scores - new_max[:, :, None]), 0.0)
        new_sum = running_sum * jnp.exp(running_max - new_max) + jnp.sum(shifted, axis=2)
        return ((new_max, new_sum), None)

    start_state = (
        jnp.full((HEADS, local_rows), NEG, jnp.float32),
        jnp.zeros((HEADS, local_rows), jnp.float32),
    )
    (final_max, final_sum), unused = lax.scan(max_step, start_state, key_items)
    log_total = final_max + jnp.log(final_sum)

    def out_step(running, block_items):
        kv_block, key_seq, key_place = block_items
        scores, allowed = key_scores(
            query_heads, kv_block[:, 0], query_seq, query_place, key_seq, key_place, score_scale
        )
        probs_low = jnp.exp(scores - log_total[:, :, None]).astype(jnp.bfloat16)
        return (
            running
            + jnp.einsum(
                "hqk,khd->qhd", probs_low, kv_block[:, 1], preferred_element_type=jnp.float32
            ),
            None,
        )

    attended, unused = lax.scan(
        out_step, jnp.zeros((local_rows, HEADS, HEAD_DIM), jnp.float32), key_items
    )
    return (attended.reshape(local_rows, D), log_total)


def attend_backward(
    queries,
    key_values,
    log_total,
    row_delta,
    grad_heads_in,
    query_seq,
    query_place,
    seq_index,
    token_place,
    block_rows,
    score_scale,
):
    local_rows = queries.shape[0]
    query_heads = queries.reshape(local_rows, HEADS, HEAD_DIM)
    grad_heads = grad_heads_in.reshape(local_rows, HEADS, HEAD_DIM)
    key_items = split_keys(key_values, seq_index, token_place, block_rows)

    def grad_step(running, block_items):
        kv_block, key_seq, key_place = block_items
        scores, allowed = key_scores(
            query_heads, kv_block[:, 0], query_seq, query_place, key_seq, key_place, score_scale
        )
        probs_full = jnp.exp(scores - log_total[:, :, None])
        probs_low = probs_full.astype(jnp.bfloat16)
        grad_probs = jnp.einsum(
            "qhd,khd->hqk", grad_heads, kv_block[:, 1], preferred_element_type=jnp.float32
        )
        grad_scores = (probs_full * (grad_probs - row_delta[:, :, None])).astype(jnp.bfloat16)
        new_running = (
            running
            + jnp.einsum(
                "hqk,khd->qhd", grad_scores, kv_block[:, 0], preferred_element_type=jnp.float32
            )
            * score_scale
        )
        grad_keys = (
            jnp.einsum("hqk,qhd->khd", grad_scores, query_heads, preferred_element_type=jnp.float32)
            * score_scale
        )
        grad_values = jnp.einsum(
            "hqk,qhd->khd", probs_low, grad_heads, preferred_element_type=jnp.float32
        )
        return (new_running, jnp.stack([grad_keys, grad_values], axis=1))

    grad_queries, grad_kv = lax.scan(
        grad_step, jnp.zeros((local_rows, HEADS, HEAD_DIM), jnp.float32), key_items
    )
    return (grad_queries.reshape(local_rows, D), grad_kv.reshape(key_values.shape[0], 2 * D))


def on_device(
    inputs,
    attn_gain,
    qkv_weight,
    out_weight,
    ffn_gain,
    router_weight,
    carry_weight,
    const_weight,
    const_vector,
    gate_weight,
    up_weight,
    down_weight,
    prev_logits,
    seq_lengths,
    expert_routes,
    cotangent,
):
    col_index = lax.axis_index("col")
    row_total = expert_routes.shape[0]
    local_rows = inputs.shape[0]
    capacity = row_total // 4
    block_rows = min(row_total, 512)
    score_scale = 1.0 / math.sqrt(HEAD_DIM)
    full_weights = (
        lax.all_gather(qkv_weight, "row", axis=0, tiled=True),
        lax.all_gather(out_weight, "row", axis=1, tiled=True),
        lax.all_gather(gate_weight, "row", axis=1, tiled=True),
        lax.all_gather(up_weight, "row", axis=1, tiled=True),
        lax.all_gather(down_weight, "row", axis=2, tiled=True),
    )
    qkv_full, out_full, gate_full, up_full, down_full = full_weights
    whole_in, whole_cot, whole_prev = (
        lax.all_gather(inputs, "col", axis=0, tiled=True),
        lax.all_gather(cotangent, "col", axis=0, tiled=True),
        lax.all_gather(prev_logits, "col", axis=1, tiled=True),
    )
    seq_index, positions, valid_all = sequence_info(seq_lengths[0], row_total)
    token_place = jnp.arange(row_total, dtype=jnp.int32)
    first_row = col_index * local_rows

    def own_rows(whole_value):
        return lax.dynamic_slice_in_dim(whole_value, first_row, local_rows, 0)

    query_seq = own_rows(seq_index)
    query_place = own_rows(token_place)
    query_pos = own_rows(positions)
    query_valid = own_rows(valid_all).astype(jnp.float32)[:, None]
    input_rows = whole_in.astype(jnp.float32)
    attn_gain_full = attn_gain.astype(jnp.float32)
    scale_attn = lax.rsqrt(jnp.mean(input_rows * input_rows, axis=1, keepdims=True) + EPS)
    normed1 = (input_rows * scale_attn * attn_gain_full).astype(jnp.bfloat16)
    projected = jnp.dot(normed1, qkv_full, preferred_element_type=jnp.float32)
    turned = rotate(projected, positions, col_index * projected.shape[1], 1.0).astype(jnp.bfloat16)
    token_qkv = to_heads(turned)
    queries = token_qkv[:, :D]
    key_values = lax.all_gather(token_qkv[:, D:], "col", axis=0, tiled=True)
    attended, log_total = attend_forward(
        queries, key_values, query_seq, query_place, seq_index, token_place, block_rows, score_scale
    )
    attn_tok = (attended * query_valid).astype(jnp.bfloat16)
    attn_feat = to_features(attn_tok)
    attn_out = partial_sums(jnp.dot(attn_feat, out_full, preferred_element_type=jnp.float32))
    input_local = inputs.astype(jnp.float32)
    middle = input_local + attn_out
    scale_ffn = lax.rsqrt(jnp.mean(middle * middle, axis=1, keepdims=True) + EPS)
    ffn_gain_full = ffn_gain.astype(jnp.float32)
    normed2_local = (middle * scale_ffn * ffn_gain_full).astype(jnp.bfloat16)
    normed2 = whole_columns(normed2_local)
    carry_full = carry_weight.astype(jnp.float32)
    prev_rows = whole_prev.astype(jnp.float32).T
    route_hot = (
        expert_routes[:, :, None] == jnp.arange(ROUTES, dtype=jnp.int32)[None, None, :]
    ).astype(jnp.float32)
    logits = jnp.dot(normed2, router_weight, preferred_element_type=jnp.float32) + jnp.dot(
        prev_rows, carry_full, precision=HIGH
    )
    picked = jnp.sum(route_hot * logits[:, None, :], axis=2)
    gate_values = jax.nn.softmax(picked, axis=1)
    flat_route = expert_routes.reshape(-1)
    route_hits = (flat_route[:, None] == jnp.arange(EXPERTS, dtype=jnp.int32)[None, :]).astype(
        jnp.int32
    )
    slot_index = jnp.sum((jnp.cumsum(route_hits, axis=0) - 1) * route_hits, axis=1)
    dump_slot = EXPERTS * capacity
    target = jnp.where(flat_route < EXPERTS, flat_route * capacity + slot_index, dump_slot)
    slot_owner = (
        jnp.full((dump_slot + 1,), row_total, jnp.int32)
        .at[target]
        .set(jnp.arange(2 * row_total, dtype=jnp.int32) // 2)[:dump_slot]
    )
    slot_gate = (
        jnp.zeros((dump_slot + 1,), jnp.float32)
        .at[target]
        .set(gate_values.reshape(-1))[:dump_slot]
        .reshape(EXPERTS, capacity, 1)
    )
    zero_row = jnp.zeros((1, D), jnp.bfloat16)
    expert_in = jnp.concatenate([normed2, zero_row], axis=0)[slot_owner].reshape(
        EXPERTS, capacity, D
    )
    gate_pre = jnp.einsum("ecd,edf->ecf", expert_in, gate_full, preferred_element_type=jnp.float32)
    up_pre = jnp.einsum("ecd,edf->ecf", expert_in, up_full, preferred_element_type=jnp.float32)
    sigmoid_gate = jax.nn.sigmoid(gate_pre)
    activated = gate_pre * sigmoid_gate
    hidden = (activated * up_pre).astype(jnp.bfloat16)
    expert_out = jnp.einsum("ecf,efd->ecd", hidden, down_full, preferred_element_type=jnp.float32)
    out_rows = jnp.concatenate(
        [expert_out.reshape(dump_slot, D), jnp.zeros((1, D), jnp.float32)], axis=0
    )
    chosen_out = out_rows[target].reshape(row_total, 2, D)
    cot_rows = whole_cot.astype(jnp.float32)
    ffn_mix = jnp.sum(gate_values[:, :, None] * chosen_out, axis=1)
    ffn_dots = jnp.sum(cot_rows[:, None, :] * chosen_out, axis=2)
    mix_local = partial_sums(ffn_mix)
    normed_local = normed2_local.astype(jnp.float32)
    vector_full = const_vector.astype(jnp.float32)
    routes_local = own_rows(expert_routes)
    gates_local = own_rows(gate_values)
    hot_local = own_rows(route_hot)
    copy_hit = (routes_local == EXPERTS + 1).astype(jnp.float32)
    const_hit = (
        routes_local[:, :, None] == (EXPERTS + 2 + jnp.arange(2, dtype=jnp.int32))[None, None, :]
    ).astype(jnp.float32)
    copy_share = jnp.sum(gates_local * copy_hit, axis=1)
    const_share = jnp.sum(gates_local[:, :, None] * const_hit, axis=1)
    const_alpha = jax.nn.softmax(
        jnp.einsum("td,jdk->tjk", normed2_local, const_weight, preferred_element_type=jnp.float32),
        axis=2,
    )
    keep_share = copy_share + jnp.sum(const_share * const_alpha[:, :, 0], axis=1)
    local_mix = keep_share[:, None] * normed_local + jnp.dot(
        const_share * const_alpha[:, :, 1], vector_full, precision=HIGH
    )
    layer_out = (middle + mix_local + local_mix).astype(jnp.bfloat16)
    qkv_full, out_full, gate_full, up_full, down_full = full_weights
    ffn_total = lax.psum(ffn_dots, "col")
    ffn_local = own_rows(ffn_total)
    cot_local = cotangent.astype(jnp.float32)
    dot_keep = jnp.sum(cot_local * normed_local, axis=1)
    dot_vector = jnp.dot(cot_local, vector_full.T, precision=HIGH)
    const_dots = const_alpha[:, :, 0] * dot_keep[:, None] + const_alpha[:, :, 1] * dot_vector
    grad_gates = (
        ffn_local
        + copy_hit * dot_keep[:, None]
        + jnp.sum(const_hit * const_dots[:, None, :], axis=2)
    )
    grad_picked = gates_local * (
        grad_gates - jnp.sum(gates_local * grad_gates, axis=1, keepdims=True)
    )
    grad_logits = jnp.sum(hot_local * grad_picked[:, :, None], axis=1)
    prev_local = prev_logits.astype(jnp.float32).T
    router_grad = lax.dot_general(normed_local, grad_logits, CONTRACT_FIRST, precision=HIGH)
    carry_grad = lax.dot_general(prev_local, grad_logits, CONTRACT_FIRST, precision=HIGH)
    prev_grad = lax.dot_general(carry_full, grad_logits, CONTRACT_LAST, precision=HIGH)
    grad_alpha_keep = const_share * dot_keep[:, None]
    grad_alpha_vector = const_share * dot_vector
    alpha_mean = const_alpha[:, :, 0] * grad_alpha_keep + const_alpha[:, :, 1] * grad_alpha_vector
    grad_alpha_logits = jnp.stack(
        [
            const_alpha[:, :, 0] * (grad_alpha_keep - alpha_mean),
            const_alpha[:, :, 1] * (grad_alpha_vector - alpha_mean),
        ],
        axis=2,
    )
    const_grad = jnp.einsum("td,tjk->jdk", normed_local, grad_alpha_logits, precision=HIGH)
    vector_grad = lax.dot_general(
        const_share * const_alpha[:, :, 1], cot_local, CONTRACT_FIRST, precision=HIGH
    )
    router_full = router_weight.astype(jnp.float32)
    const_full = const_weight.astype(jnp.float32)
    grad_normed_local = (
        keep_share[:, None] * cot_local
        + lax.dot_general(grad_logits, router_full, CONTRACT_LAST, precision=HIGH)
        + jnp.einsum("tjk,jdk->td", grad_alpha_logits, const_full, precision=HIGH)
    )
    cot_in = jnp.concatenate([whole_cot, zero_row], axis=0)[slot_owner].reshape(
        EXPERTS, capacity, D
    )
    grad_expert = (slot_gate * cot_in.astype(jnp.float32)).astype(jnp.bfloat16)
    down_grad = jnp.einsum("ecf,ecd->efd", hidden, grad_expert, preferred_element_type=jnp.float32)
    grad_hidden = jnp.einsum(
        "ecd,efd->ecf", grad_expert, down_full, preferred_element_type=jnp.float32
    )
    grad_gate_pre = (
        grad_hidden * up_pre * sigmoid_gate * (1.0 + gate_pre * (1.0 - sigmoid_gate))
    ).astype(jnp.bfloat16)
    grad_up_pre = (grad_hidden * activated).astype(jnp.bfloat16)
    gate_grad = jnp.einsum(
        "ecd,ecf->edf", expert_in, grad_gate_pre, preferred_element_type=jnp.float32
    )
    up_grad = jnp.einsum("ecd,ecf->edf", expert_in, grad_up_pre, preferred_element_type=jnp.float32)
    grad_expert_in = jnp.einsum(
        "ecf,edf->ecd", grad_gate_pre, gate_full, preferred_element_type=jnp.float32
    ) + jnp.einsum("ecf,edf->ecd", grad_up_pre, up_full, preferred_element_type=jnp.float32)
    grad_slots = jnp.concatenate(
        [grad_expert_in.reshape(dump_slot, D), jnp.zeros((1, D), jnp.float32)], axis=0
    )
    grad_tokens = jnp.sum(grad_slots[target].reshape(row_total, 2, D), axis=1)
    grad_normed = partial_sums(grad_tokens) + grad_normed_local
    gained_ffn = grad_normed * ffn_gain_full
    ffn_dots_rows = jnp.sum(gained_ffn * middle, axis=1, keepdims=True)
    grad_middle = scale_ffn * gained_ffn - middle * scale_ffn**3 * (ffn_dots_rows / D)
    ffn_gain_grad = jnp.sum(grad_normed * middle * scale_ffn, axis=0)
    grad_resid = cot_local + grad_middle
    branch_cot = whole_columns(grad_resid.astype(jnp.bfloat16))
    out_grad = lax.dot_general(
        attn_feat, branch_cot, CONTRACT_FIRST, preferred_element_type=jnp.float32
    )
    grad_mixed = lax.dot_general(
        branch_cot, out_full, CONTRACT_LAST, preferred_element_type=jnp.float32
    )
    grad_tok = to_heads(grad_mixed.astype(jnp.bfloat16))
    grad_heads_in = (grad_tok.astype(jnp.float32) * query_valid).astype(jnp.bfloat16)
    row_delta = jnp.sum(
        grad_heads_in.astype(jnp.float32).reshape(local_rows, HEADS, HEAD_DIM)
        * attended.reshape(local_rows, HEADS, HEAD_DIM),
        axis=2,
    ).T
    grad_queries, grad_kv = attend_backward(
        queries,
        key_values,
        log_total,
        row_delta,
        grad_heads_in,
        query_seq,
        query_place,
        seq_index,
        token_place,
        block_rows,
        score_scale,
    )
    grad_kv_local = lax.psum_scatter(
        grad_kv.astype(jnp.bfloat16), "col", scatter_dimension=0, tiled=True
    ).astype(jnp.float32)
    grad_turned = jnp.concatenate([grad_queries, grad_kv_local], axis=1)
    grad_proj_tok = rotate(grad_turned, query_pos, 0, -1.0).astype(jnp.bfloat16)
    grad_projected = to_features(grad_proj_tok)
    qkv_grad = lax.dot_general(
        normed1, grad_projected, CONTRACT_FIRST, preferred_element_type=jnp.float32
    )
    grad_normed1 = partial_sums(
        lax.dot_general(grad_projected, qkv_full, CONTRACT_LAST, preferred_element_type=jnp.float32)
    )
    scale_attn_local = own_rows(scale_attn)
    gained_attn = grad_normed1 * attn_gain_full
    attn_dots_rows = jnp.sum(gained_attn * input_local, axis=1, keepdims=True)
    input_grad = (
        grad_resid
        + scale_attn_local * gained_attn
        - input_local * scale_attn_local**3 * (attn_dots_rows / D)
    )
    attn_gain_grad = jnp.sum(grad_normed1 * input_local * scale_attn_local, axis=0)
    qkv_grad, out_grad, gate_grad, up_grad, down_grad = (
        lax.psum_scatter(
            qkv_grad.astype(jnp.bfloat16), "row", scatter_dimension=0, tiled=True
        ).astype(jnp.float32),
        lax.psum_scatter(
            out_grad.astype(jnp.bfloat16), "row", scatter_dimension=1, tiled=True
        ).astype(jnp.float32),
        lax.psum_scatter(
            gate_grad.astype(jnp.bfloat16), "row", scatter_dimension=1, tiled=True
        ).astype(jnp.float32),
        lax.psum_scatter(
            up_grad.astype(jnp.bfloat16), "row", scatter_dimension=1, tiled=True
        ).astype(jnp.float32),
        lax.psum_scatter(
            down_grad.astype(jnp.bfloat16), "row", scatter_dimension=2, tiled=True
        ).astype(jnp.float32),
    )
    attn_gain_grad, ffn_gain_grad, router_grad, carry_grad, const_grad, vector_grad = lax.psum(
        (attn_gain_grad, ffn_gain_grad, router_grad, carry_grad, const_grad, vector_grad),
        ("row", "col"),
    )
    return (
        layer_out,
        input_grad,
        attn_gain_grad,
        qkv_grad,
        out_grad,
        ffn_gain_grad,
        router_grad,
        carry_grad,
        const_grad,
        vector_grad,
        gate_grad,
        up_grad,
        down_grad,
        prev_grad,
    )


BF = jnp.bfloat16
F32 = jnp.float32
LANES = 128
NN = (((1,), (0,)), ((), ()))
NT = (((1,), (1,)), ((), ()))
TN = (((0,), (0,)), ((), ()))
ROW_CONST = 12
ROW_VEC = 16
ROW_GAIN = 18
SMALL_ROWS = 24
Q_ROWS = 256
MIB = 1 << 20


def mm(a, b, dims=NN):
    return lax.dot_general(a, b, dims, preferred_element_type=F32)


def lane_iota(shape):
    return lax.broadcasted_iota(jnp.int32, shape, len(shape) - 1)


def whole(shape):
    return pl.BlockSpec(shape, lambda *_: (0,) * len(shape), pipeline_mode=pl.Buffered(1))


def swap_pairs(v):
    even = lane_iota(v.shape) % 2 == 0
    return jnp.where(even, pltpu.roll(v, LANES - 1, 1), pltpu.roll(v, 1, 1))


def norm_rows(x):
    return lax.rsqrt(jnp.mean(x * x, axis=1, keepdims=True) + EPS)


def qkv_kernel(heads, x_ref, gain_ref, w_ref, cos_ref, sin_ref, out_ref):
    x = x_ref[...].astype(F32)
    normed = (x * norm_rows(x) * gain_ref[...]).astype(BF)
    proj = mm(normed, w_ref[...])
    cosine, sines = cos_ref[...], sin_ref[...]
    width = heads * HEAD_DIM
    for part in range(2 * width // LANES):
        v = proj[:, part * LANES : (part + 1) * LANES]
        t = v * cosine + swap_pairs(v) * sines
        for half in range(2):
            head = 2 * part + half
            piece = t[:, half * HEAD_DIM : (half + 1) * HEAD_DIM].astype(BF)
            if head < heads:
                piece = piece * jnp.asarray(1.0 / math.sqrt(HEAD_DIM), BF)
            out_ref[head] = piece
    for head in range(2 * heads, 3 * heads):
        out_ref[head] = proj[:, head * HEAD_DIM : (head + 1) * HEAD_DIM].astype(BF)


def project_heads(heads, whole_in, gain, weight, cosine, sines):
    rows = whole_in.shape[0]
    blk = 256
    return pl.pallas_call(
        functools.partial(qkv_kernel, heads),
        grid=(rows // blk,),
        out_shape=jax.ShapeDtypeStruct((3 * heads, rows, HEAD_DIM), BF),
        in_specs=[
            pl.BlockSpec((blk, D), lambda i: (i, 0)),
            whole((1, D)),
            whole((D, 3 * heads * HEAD_DIM)),
            pl.BlockSpec((blk, LANES), lambda i: (i, 0)),
            pl.BlockSpec((blk, LANES), lambda i: (i, 0)),
        ],
        out_specs=pl.BlockSpec((3 * heads, blk, HEAD_DIM), lambda i: (0, i, 0)),
        compiler_params=pltpu.CompilerParams(vmem_limit_bytes=32 * MIB),
        cost_estimate=pl.CostEstimate(
            flops=2 * rows * D * 3 * heads * HEAD_DIM, bytes_accessed=8 * MIB, transcendentals=0
        ),
        name="project_heads",
    )(whole_in, gain, weight, cosine, sines)


def seen(begin, first, rows, length):
    u = lax.broadcasted_iota(jnp.int32, (rows, length), 1)
    t = lax.broadcasted_iota(jnp.int32, (rows, length), 0) + first
    return (u >= begin) & (u <= t)


def attend_kernel(q_ref, k_ref, v_ref, begin_ref, valid_ref, o_ref, lse_ref):
    rows = q_ref.shape[1]
    for i in range(rows // Q_ROWS):
        at = slice(i * Q_ROWS, (i + 1) * Q_ROWS)
        length = (i + 1) * Q_ROWS
        s = mm(q_ref[0, at], k_ref[0, :length], NT)
        s = jnp.where(seen(begin_ref[at], i * Q_ROWS, Q_ROWS, length), s, NEG)
        top = jnp.max(s, axis=1, keepdims=True)
        p = jnp.exp(s - top)
        total = jnp.sum(p, axis=1, keepdims=True)
        o = mm(p.astype(BF), v_ref[0, :length]) * (valid_ref[at] / total)
        o_ref[0, at] = o.astype(BF)
        lse_ref[0, at] = top + jnp.log(total)


def attend(heads, qkv, begin, valid):
    rows = qkv.shape[1]
    head_block = (1, rows, HEAD_DIM)
    return pl.pallas_call(
        attend_kernel,
        grid=(heads,),
        out_shape=(
            jax.ShapeDtypeStruct((heads, rows, HEAD_DIM), BF),
            jax.ShapeDtypeStruct((heads, rows, 1), F32),
        ),
        in_specs=[
            pl.BlockSpec(head_block, lambda h: (h, 0, 0)),
            pl.BlockSpec(head_block, lambda h: (h + heads, 0, 0)),
            pl.BlockSpec(head_block, lambda h: (h + 2 * heads, 0, 0)),
            whole((rows, 1)),
            whole((rows, 1)),
        ],
        out_specs=(
            pl.BlockSpec(head_block, lambda h: (h, 0, 0)),
            pl.BlockSpec((1, rows, 1), lambda h: (h, 0, 0)),
        ),
        compiler_params=pltpu.CompilerParams(vmem_limit_bytes=48 * MIB),
        cost_estimate=pl.CostEstimate(
            flops=8 * heads * rows * rows * HEAD_DIM, bytes_accessed=8 * MIB, transcendentals=heads * rows * rows
        ),
        name="attend",
    )(qkv, qkv, qkv, begin, valid)


def attend_back_kernel(
    q_ref, k_ref, v_ref, begin_ref, o_ref, lse_ref, do_ref, dq_ref, dk_ref, dv_ref
):
    rows = q_ref.shape[1]
    score_scale = 1.0 / math.sqrt(HEAD_DIM)
    count = rows // Q_ROWS
    for i in reversed(range(count)):
        at = slice(i * Q_ROWS, (i + 1) * Q_ROWS)
        length = (i + 1) * Q_ROWS
        q, do = q_ref[0, at], do_ref[0, at]
        k, v = k_ref[0, :length], v_ref[0, :length]
        delta = jnp.sum(do.astype(F32) * o_ref[0, at].astype(F32), axis=1, keepdims=True)
        s = mm(q, k, NT)
        ok = seen(begin_ref[at], i * Q_ROWS, Q_ROWS, length)
        p = jnp.where(ok, jnp.exp(s - lse_ref[0, at]), 0.0)
        dp = mm(do, v, NT)
        ds = (p * (dp - delta)).astype(BF)
        dq_ref[0, at] = mm(ds, k) * score_scale
        dk, dv = mm(ds, q, TN), mm(p.astype(BF), do, TN)
        if i == count - 1:
            dk_ref[0], dv_ref[0] = dk, dv
        else:
            dk_ref[0, :length] += dk
            dv_ref[0, :length] += dv


def attend_back(heads, qkv, begin, mixed, lse, grad_mixed):
    rows = qkv.shape[1]
    head_block = (1, rows, HEAD_DIM)
    per_head = pl.BlockSpec(head_block, lambda h: (h, 0, 0))
    grad = jax.ShapeDtypeStruct((heads, rows, HEAD_DIM), F32)
    return pl.pallas_call(
        attend_back_kernel,
        grid=(heads,),
        out_shape=(grad, grad, grad),
        in_specs=[
            per_head,
            pl.BlockSpec(head_block, lambda h: (h + heads, 0, 0)),
            pl.BlockSpec(head_block, lambda h: (h + 2 * heads, 0, 0)),
            whole((rows, 1)),
            per_head,
            pl.BlockSpec((1, rows, 1), lambda h: (h, 0, 0)),
            per_head,
        ],
        out_specs=(per_head, per_head, per_head),
        compiler_params=pltpu.CompilerParams(vmem_limit_bytes=56 * MIB),
        cost_estimate=pl.CostEstimate(
            flops=20 * heads * rows * rows * HEAD_DIM, bytes_accessed=12 * MIB, transcendentals=heads * rows * rows
        ),
        name="attend_back",
    )(qkv, qkv, qkv, begin, mixed, lse, grad_mixed)


def branch_kernel(a_ref, w_ref, x_ref, gain_ref, mixed_ref, middle_ref, normed_ref):
    mixed = jnp.concatenate([a_ref[i] for i in range(a_ref.shape[0])], axis=1)
    mixed_ref[...] = mixed
    middle = x_ref[...].astype(F32) + mm(mixed, w_ref[...], NT)
    middle_ref[...] = middle
    normed_ref[...] = (middle * norm_rows(middle) * gain_ref[...]).astype(BF)


def branch(attn_parts, out_t, inputs, gain):
    rows = inputs.shape[0]
    return pl.pallas_call(
        branch_kernel,
        out_shape=(
            jax.ShapeDtypeStruct((rows, D), BF),
            jax.ShapeDtypeStruct((rows, D), F32),
            jax.ShapeDtypeStruct((rows, D), BF),
        ),
        compiler_params=pltpu.CompilerParams(vmem_limit_bytes=32 * MIB),
        cost_estimate=pl.CostEstimate(flops=2 * rows * D * D, bytes_accessed=6 * MIB, transcendentals=0),
        name="branch",
    )(attn_parts, out_t, inputs, gain)


def gate_lanes(logits, routes):
    lane = lane_iota(logits.shape)
    hit = (lane == routes[:, 0:1]) | (lane == routes[:, 1:2])
    held = jnp.where(hit, logits, NEG)
    e = jnp.where(hit, jnp.exp(held - jnp.max(held, axis=1, keepdims=True)), 0.0)
    return e / jnp.sum(e, axis=1, keepdims=True)


def moe_kernel(ranks, capacity, *refs):
    (n2_ref, cotx_ref, rw_ref, carry_ref, routes_ref, tsr_ref, tsc_ref), refs = refs[:7], refs[7:]
    w_parts, refs = refs[:ranks], refs[ranks:]
    (mix_ref, gtx_ref), refs = refs[:2], refs[2:]
    g_parts, refs = refs[:ranks], refs[ranks:]
    wbuf, wsem, gbuf, gsem, gates, mix_acc, gt_acc = refs
    e = pl.program_id(0)
    me = lax.axis_index("row")
    experts = pl.num_programs(0)
    rows = n2_ref.shape[0]
    depth = w_parts[0].shape[2]
    slot = lax.rem(e, 2)

    def at(m):
        return pl.ds(pl.multiple_of((me ^ m) * depth, 16), depth)

    def w_copies(expert, place):
        return [
            pltpu.make_async_copy(
                w_parts[m].at[t, expert], wbuf.at[place, t, at(m)], wsem.at[place, t * ranks + m]
            )
            for t in range(3)
            for m in range(ranks)
        ]

    def g_copies(expert, place):
        return [
            pltpu.make_async_copy(
                gbuf.at[place, t, at(m)], g_parts[m].at[t, expert], gsem.at[place, t * ranks + m]
            )
            for t in range(3)
            for m in range(ranks)
        ]

    @pl.when(e == 0)
    def _():
        for c in w_copies(0, 0):
            c.start()
        logits = mm(n2_ref[...], rw_ref[...], NT) + mm(cotx_ref[:, D:], carry_ref[...])
        g = gate_lanes(logits, routes_ref[...])
        high = g.astype(BF)
        gates[:, :LANES] = high
        gates[:, LANES:] = (g - high.astype(F32)).astype(BF)
        mix_acc[...] = jnp.zeros_like(mix_acc)
        gt_acc[...] = jnp.zeros_like(gt_acc)

    @pl.when(e + 1 < experts)
    def _():
        for c in w_copies(e + 1, 1 - slot):
            c.start()

    one = jnp.where(lax.broadcasted_iota(jnp.int32, (capacity, rows), 0) == tsr_ref[0], 1.0, 0.0).astype(BF)
    x = mm(one, n2_ref[...]).astype(BF)
    c = mm(one, cotx_ref[:, :D]).astype(BF)
    sg = mm(one, gates[...])
    sg = jnp.sum(jnp.where(lane_iota(sg.shape) % LANES == e, sg, 0.0), axis=1, keepdims=True)

    for cp in w_copies(e, slot):
        cp.wait()
    wg, wu, wd = wbuf.at[slot, 0], wbuf.at[slot, 1], wbuf.at[slot, 2]
    g = mm(x, wg[...])
    u = mm(x, wu[...])
    v = mm(c, wd[...])
    sig = jax.nn.sigmoid(g)
    act = g * sig
    h = act * u
    dot = jnp.sum(h * v, axis=1, keepdims=True)
    gh = (h * sg).astype(BF)
    gv = v * sg
    dg = (gv * u * (sig * (1.0 + g * (1.0 - sig)))).astype(BF)
    du = (gv * act).astype(BF)
    y = mm(gh, wd[...], NT).astype(BF)
    dx = (mm(dg, wg[...], NT) + mm(du, wu[...], NT)).astype(BF)
    dot_high = dot.astype(BF).astype(F32)
    lane = lane_iota((capacity, LANES))
    dots = jnp.where(lane == e, dot_high, 0.0) + jnp.where(lane == e + EXPERTS, dot - dot_high, 0.0)
    dxx = jnp.concatenate([dx, dots.astype(BF)], axis=1)

    tsc = jnp.sum(jnp.where(lane_iota(tsc_ref.shape) == e, tsc_ref[...], 0), axis=1, keepdims=True)
    step = 256
    for b in range(rows // step):
        rs = slice(b * step, (b + 1) * step)
        one_t = jnp.where(lane_iota((step, capacity)) == tsc[rs], 1.0, 0.0).astype(BF)
        mix_acc[rs] += mm(one_t, y)
        gt_acc[rs] += mm(one_t, dxx)

    @pl.when(e >= 2)
    def _():
        for cp in g_copies(e - 2, slot):
            cp.wait()

    gbuf[slot, 0] = mm(x, dg, TN).astype(BF)
    gbuf[slot, 1] = mm(x, du, TN).astype(BF)
    gbuf[slot, 2] = mm(c, gh, TN).astype(BF)
    for cp in g_copies(e, slot):
        cp.start()

    @pl.when(e == experts - 1)
    def _():
        mix_ref[...] = mix_acc[...].astype(BF)
        gtx_ref[...] = gt_acc[...].astype(BF)
        for cp in g_copies(e - 1, 1 - slot) + g_copies(e, slot):
            cp.wait()


def experts_both_ways(n2, cotx, rw, carry, routes, slots, w_parts):
    rows = n2.shape[0]
    capacity = rows // 4
    ranks = len(w_parts)
    three, experts, depth, ff = w_parts[0].shape
    anyspec = pl.BlockSpec(memory_space=pl.ANY)
    outs = pl.pallas_call(
        functools.partial(moe_kernel, ranks, capacity),
        grid=(experts,),
        out_shape=[
            jax.ShapeDtypeStruct((rows, D), BF),
            jax.ShapeDtypeStruct((rows, D + LANES), BF),
        ]
        + [jax.ShapeDtypeStruct((three, experts, depth, ff), BF)] * ranks,
        in_specs=[
            whole((rows, D)),
            whole((rows, D + LANES)),
            whole((LANES, D)),
            whole((LANES, LANES)),
            whole((rows, 2)),
            pl.BlockSpec((1, 1, rows), lambda e: (e, 0, 0)),
            whole((rows, experts)),
        ]
        + [anyspec] * ranks,
        out_specs=[whole((rows, D)), whole((rows, D + LANES))] + [anyspec] * ranks,
        scratch_shapes=[
            pltpu.VMEM((2, 3, depth * ranks, ff), BF),
            pltpu.SemaphoreType.DMA((2, 3 * ranks)),
            pltpu.VMEM((2, 3, depth * ranks, ff), BF),
            pltpu.SemaphoreType.DMA((2, 3 * ranks)),
            pltpu.VMEM((rows, 2 * LANES), BF),
            pltpu.VMEM((rows, D), F32),
            pltpu.VMEM((rows, D + LANES), F32),
        ],
        compiler_params=pltpu.CompilerParams(vmem_limit_bytes=60 * MIB),
        cost_estimate=pl.CostEstimate(
            flops=experts * capacity * 2 * D * (9 * ff + 5 * rows),
            bytes_accessed=48 * MIB,
            transcendentals=experts * capacity * ff,
        ),
        name="experts_both_ways",
    )(n2, cotx, rw, carry, routes, slots.T[:, None, :], slots, *w_parts)
    return outs[0], outs[1], outs[2:]


def resid_kernel(
    gtx_ref,
    n2_ref,
    middle_ref,
    cot_ref,
    routes_ref,
    prev_ref,
    rw_ref,
    carry_ref,
    gain_ref,
    out_t_ref,
    mixed_ref,
    valid_ref,
    midmix_ref,
    resid_ref,
    gm_ref,
    og_ref,
    small_ref,
    pg_ref,
):
    n2, cot = n2_ref[...], cot_ref[...]
    n2f, cotf = n2.astype(F32), cot.astype(F32)
    middle = middle_ref[...]
    rw = rw_ref[...]
    lin = mm(n2, rw, NT)
    prev = prev_ref[...]
    gates = gate_lanes(lin + mm(prev, carry_ref[...]), routes_ref[...])
    rows = n2.shape[0]
    lane = lane_iota((rows, LANES))
    cot_lin = mm(cot, rw, NT)
    dot_keep = jnp.sum(cotf * n2f, axis=1, keepdims=True)
    copy_share = gates[:, EXPERTS + 1 : EXPERTS + 2]
    d = gtx_ref[:, D:].astype(F32)
    g_gates = jnp.where(lane < EXPERTS, d + pltpu.roll(d, LANES - EXPERTS, 1), 0.0)
    g_gates = jnp.where(lane == EXPERTS + 1, dot_keep, g_gates)
    keep = copy_share
    mixes, packs = [], jnp.zeros((rows, LANES), F32)
    for j in range(2):
        l0 = lin[:, ROW_CONST + 2 * j : ROW_CONST + 2 * j + 1]
        l1 = lin[:, ROW_CONST + 2 * j + 1 : ROW_CONST + 2 * j + 2]
        top = jnp.maximum(l0, l1)
        e0, e1 = jnp.exp(l0 - top), jnp.exp(l1 - top)
        a0, a1 = e0 / (e0 + e1), e1 / (e0 + e1)
        share = gates[:, EXPERTS + 2 + j : EXPERTS + 3 + j]
        dot_vec = cot_lin[:, ROW_VEC + j : ROW_VEC + j + 1]
        keep = keep + share * a0
        mixes.append(share * a1)
        g_gates = jnp.where(lane == EXPERTS + 2 + j, a0 * dot_keep + a1 * dot_vec, g_gates)
        gk, gv = share * dot_keep, share * dot_vec
        mean = a0 * gk + a1 * gv
        packs = packs + jnp.where(lane == ROW_CONST + 2 * j, a0 * (gk - mean), 0.0)
        packs = packs + jnp.where(lane == ROW_CONST + 2 * j + 1, a1 * (gv - mean), 0.0)
        packs = packs + jnp.where(lane == ROW_VEC + j, share * a1, 0.0)
    packs = packs + gates * (g_gates - jnp.sum(gates * g_gates, axis=1, keepdims=True))
    vec = rw[ROW_VEC : ROW_VEC + 2].astype(F32)
    midmix_ref[...] = middle + keep * n2f + mixes[0] * vec[0:1] + mixes[1] * vec[1:2]

    high = packs.astype(BF)
    low = (packs - high.astype(F32)).astype(BF)
    back = lane < ROW_VEC
    high_b, low_b = jnp.where(back, high, 0), jnp.where(back, low, 0)
    grad_normed = (
        gtx_ref[:, :D].astype(F32) + keep * cotf + mm(high_b, rw) + mm(low_b, rw)
    )
    by_n2 = mm(high, n2, TN) + mm(low, n2, TN)
    by_cot = mm(high, cot, TN) + mm(low, cot, TN)
    by_prev = mm(high, prev, TN) + mm(low, prev, TN)
    pg = mm(carry_ref[...], high_b, NT) + mm(carry_ref[...], low_b, NT)
    pg_ref[...] = pg[:ROUTES]

    scale = norm_rows(middle)
    gained = grad_normed * gain_ref[...]
    mid_dot = jnp.sum(gained * middle, axis=1, keepdims=True)
    resid = cotf + scale * gained - middle * (scale * scale * scale * (mid_dot * (1.0 / D)))
    resid_ref[...] = resid
    gain_grad = jnp.sum(grad_normed * middle * scale, axis=0, keepdims=True)
    sub = lax.broadcasted_iota(jnp.int32, (SMALL_ROWS, D), 0)
    small = jnp.where(sub < ROW_VEC, by_n2[:SMALL_ROWS], by_cot[:SMALL_ROWS])
    small = jnp.where(sub >= ROW_GAIN, jnp.where(sub == ROW_GAIN, gain_grad, 0.0), small)
    small_ref[:, :D] = small
    small_ref[:, D:] = by_prev[:SMALL_ROWS]

    cut = resid.astype(BF)
    gm = (mm(cut, out_t_ref[...]) * valid_ref[...]).astype(BF)
    parts, _, width = gm_ref.shape
    for i in range(parts):
        gm_ref[i] = gm[:, i * width : (i + 1) * width]
    og_ref[...] = mm(cut, mixed_ref[...], TN).astype(BF)


def resid_step(parts, gtx, n2, middle, cot, routes, prev, rw, carry, gain, out_t, mixed, valid):
    rows = n2.shape[0]
    return pl.pallas_call(
        resid_kernel,
        out_shape=(
            jax.ShapeDtypeStruct((rows, D), F32),
            jax.ShapeDtypeStruct((rows, D), F32),
            jax.ShapeDtypeStruct((parts, rows, D // parts), BF),
            jax.ShapeDtypeStruct((D, D), BF),
            jax.ShapeDtypeStruct((SMALL_ROWS, D + LANES), F32),
            jax.ShapeDtypeStruct((ROUTES, rows), F32),
        ),
        compiler_params=pltpu.CompilerParams(vmem_limit_bytes=48 * MIB),
        cost_estimate=pl.CostEstimate(flops=6 * rows * D * D, bytes_accessed=12 * MIB, transcendentals=0),
        name="resid_step",
    )(gtx, n2, middle, cot, routes, prev, rw, carry, gain, out_t, mixed, valid)


def project_back_kernel(
    heads, dq_ref, dk_ref, dv_ref, x_ref, gain_ref, w_ref, cos_ref, sin_ref, gn_ref, wg_ref, gg_ref, acc
):
    step = pl.program_id(0)
    cosine, sines = cos_ref[...], sin_ref[...]
    turned = [dq_ref[h] for h in range(heads)] + [dk_ref[h] for h in range(heads)]
    cols = []
    for part in range(heads):
        v = jnp.concatenate(turned[2 * part : 2 * part + 2], axis=1)
        cols.append((v * cosine - swap_pairs(v) * sines).astype(BF))
    cols += [dv_ref[h].astype(BF) for h in range(heads)]
    gp = jnp.concatenate(cols, axis=1)
    x = x_ref[...].astype(F32)
    xs = x * norm_rows(x)
    normed = (xs * gain_ref[...]).astype(BF)
    gn = mm(gp, w_ref[...], NT)
    gn_ref[...] = gn.astype(BF)
    part_grad = mm(normed, gp, TN)
    gain_part = jnp.sum(gn * xs, axis=0, keepdims=True)

    @pl.when(step == 0)
    def _():
        acc[...] = part_grad
        gg_ref[...] = gain_part

    @pl.when(step > 0)
    def _():
        acc[...] += part_grad
        gg_ref[...] += gain_part

    @pl.when(step == pl.num_programs(0) - 1)
    def _():
        wg_ref[...] = acc[...].astype(BF)


def project_back(heads, dq, dk, dv, whole_in, gain, weight, cosine, sines):
    rows = whole_in.shape[0]
    blk = 256
    width = 3 * heads * HEAD_DIM
    head_spec = pl.BlockSpec((heads, blk, HEAD_DIM), lambda i: (0, i, 0))
    return pl.pallas_call(
        functools.partial(project_back_kernel, heads),
        grid=(rows // blk,),
        out_shape=(
            jax.ShapeDtypeStruct((rows, D), BF),
            jax.ShapeDtypeStruct((D, width), BF),
            jax.ShapeDtypeStruct((1, D), F32),
        ),
        in_specs=[
            head_spec,
            head_spec,
            head_spec,
            pl.BlockSpec((blk, D), lambda i: (i, 0)),
            whole((1, D)),
            whole((D, width)),
            pl.BlockSpec((blk, LANES), lambda i: (i, 0)),
            pl.BlockSpec((blk, LANES), lambda i: (i, 0)),
        ],
        out_specs=(pl.BlockSpec((blk, D), lambda i: (i, 0)), whole((D, width)), whole((1, D))),
        scratch_shapes=[pltpu.VMEM((D, width), F32)],
        compiler_params=pltpu.CompilerParams(vmem_limit_bytes=48 * MIB),
        cost_estimate=pl.CostEstimate(flops=4 * rows * D * width, bytes_accessed=16 * MIB, transcendentals=0),
        name="project_back",
    )(dq, dk, dv, whole_in, gain, weight, cosine, sines)


def swap_rows(value, ranks, mask):
    return lax.ppermute(value, "row", [(i, i ^ mask) for i in range(ranks)])


def gather_rows(value, ranks):
    parts = {0: value}
    for m in range(2, ranks, 2):
        parts[m] = swap_rows(value, ranks, m)
    for m in range(0, ranks, 2):
        parts[m + 1] = swap_rows(parts[m], ranks, 1)
    return [parts[m] for m in range(ranks)]


def scatter_rows(parts, ranks):
    held = {}
    for m in range(0, ranks, 2):
        arrived = swap_rows(parts[m + 1], ranks, 1)
        held[m] = parts[m].astype(F32) + arrived.astype(F32)
    total = held[0]
    for m in range(2, ranks, 2):
        total = total + swap_rows(held[m].astype(BF), ranks, m).astype(F32)
    return total


def on_device_heads(
    sizes,
    inputs,
    attn_gain,
    qkv_weight,
    out_weight,
    ffn_gain,
    router_weight,
    carry_weight,
    const_weight,
    const_vector,
    gate_weight,
    up_weight,
    down_weight,
    prev_logits,
    seq_lengths,
    expert_routes,
    cotangent,
):
    ranks, cols = sizes
    heads = HEADS // cols
    width = heads * HEAD_DIM
    col_index = lax.axis_index("col")
    row_total = expert_routes.shape[0]
    local_rows = inputs.shape[0]
    first_row = col_index * local_rows

    def own_rows(value):
        return lax.dynamic_slice_in_dim(value, first_row, local_rows, 0)

    w_stack = jnp.stack([gate_weight, up_weight, down_weight.transpose(0, 2, 1)])
    w_parts = gather_rows(w_stack, ranks)

    w_cat = jnp.concatenate([out_weight.T, qkv_weight], axis=1)
    w_all = lax.all_gather(w_cat, "col", axis=0, tiled=False)
    depth = qkv_weight.shape[0]
    blocks = w_all[:, :, width:].reshape(cols, depth, 3, width).transpose(0, 2, 1, 3)
    blocks = blocks.reshape(3, cols, depth, width)
    own = lax.dynamic_index_in_dim(blocks, col_index, 1, keepdims=False)
    w_own = jnp.concatenate([own[0], own[1], own[2]], axis=1)
    out_rows = w_all[:, :, :width].transpose(1, 0, 2).reshape(depth, D)
    w_full = lax.all_gather(jnp.concatenate([out_rows, w_own], axis=1), "row", axis=0, tiled=True)
    out_t, qkv_own = w_full[:, :D], w_full[:, D:]

    whole_in = lax.all_gather(inputs, "col", axis=0, tiled=True)
    prev_t = jnp.pad(prev_logits.T, ((0, 0), (0, LANES - ROUTES)))
    cotx = lax.all_gather(jnp.concatenate([cotangent, prev_t], axis=1), "col", axis=0, tiled=True)

    lengths = seq_lengths[0]
    ends = jnp.cumsum(lengths)
    starts = ends - lengths
    place = jnp.arange(row_total, dtype=jnp.int32)
    seq_index = jnp.sum((place[:, None] >= ends[None, :]).astype(jnp.int32), axis=1)
    member = seq_index[:, None] == jnp.arange(lengths.shape[0], dtype=jnp.int32)[None, :]
    begin = jnp.sum(jnp.where(member, starts[None, :], 0), axis=1)
    is_valid = seq_index < lengths.shape[0]
    positions = place - begin
    valid = is_valid.astype(F32)[:, None]
    seq_begin = jnp.where(is_valid, begin, ends[-1])[:, None]
    pair = jnp.arange(HEAD_DIM // 2, dtype=jnp.int32)
    frequency = jnp.exp(-((2 * pair).astype(F32) / HEAD_DIM) * math.log(BASE))
    angles = positions.astype(F32)[:, None] * frequency[None, :]
    cosine, sines = jnp.cos(angles), jnp.sin(angles)
    cosine = jnp.tile(jnp.repeat(cosine, 2, axis=1), (1, LANES // HEAD_DIM))
    sines = jnp.tile(
        jnp.stack([-sines, sines], axis=2).reshape(row_total, HEAD_DIM), (1, LANES // HEAD_DIM)
    )

    hit = jnp.any(
        expert_routes[:, :, None] == jnp.arange(EXPERTS, dtype=jnp.int32)[None, None, :], axis=1
    ).astype(jnp.int32)
    slots = jnp.where(hit > 0, jnp.cumsum(hit, axis=0) - 1, -1)

    rw = jnp.concatenate(
        [
            router_weight.T,
            const_weight.transpose(0, 2, 1).reshape(4, D),
            const_vector,
            jnp.zeros((LANES - ROW_GAIN, D), BF),
        ],
        axis=0,
    )
    carry = jnp.pad(carry_weight, ((0, LANES - ROUTES), (0, LANES - ROUTES)))
    attn_gain_row = attn_gain.astype(F32)[None, :]
    ffn_gain_row = ffn_gain.astype(F32)[None, :]

    qkv = project_heads(heads, whole_in, attn_gain_row, qkv_own, cosine, sines)
    mixed_heads, lse = attend(heads, qkv, seq_begin, valid)
    to_send = mixed_heads.transpose(1, 0, 2).reshape(cols, local_rows, width)
    attn_parts = lax.all_to_all(to_send, "col", split_axis=0, concat_axis=0, tiled=True)
    mixed, middle, n2 = branch(attn_parts, out_t, inputs, ffn_gain_row)
    n2_whole = lax.all_gather(n2, "col", axis=0, tiled=True)
    mix, gtx, g_parts = experts_both_ways(n2_whole, cotx, rw, carry, expert_routes, slots, w_parts)
    gtx_own = lax.psum_scatter(gtx, "col", scatter_dimension=0, tiled=True)
    mix_own = lax.psum_scatter(mix, "col", scatter_dimension=0, tiled=True)
    midmix, resid, gm, og, small, prev_grad = resid_step(
        cols,
        gtx_own,
        n2,
        middle,
        cotangent,
        own_rows(expert_routes),
        prev_t,
        rw,
        carry,
        ffn_gain_row,
        out_t,
        mixed,
        own_rows(valid),
    )
    layer_out = (midmix + mix_own.astype(F32)).astype(BF)
    gm_heads = lax.all_to_all(gm, "col", split_axis=0, concat_axis=0, tiled=True)
    gm_heads = gm_heads.reshape(row_total, heads, HEAD_DIM).transpose(1, 0, 2)
    dq, dk, dv = attend_back(heads, qkv, seq_begin, mixed_heads, lse, gm_heads)
    gn, qg, gain_part = project_back(
        heads, dq, dk, dv, whole_in, attn_gain_row, qkv_own, cosine, sines
    )
    gn_own = lax.psum_scatter(gn, "col", scatter_dimension=0, tiled=True).astype(F32)

    grads = scatter_rows(g_parts, ranks)
    og_rows = lax.psum_scatter(og, "row", scatter_dimension=0, tiled=True)
    og_own = lax.psum_scatter(og_rows, "col", scatter_dimension=1, tiled=True)
    qg_rows = lax.psum_scatter(qg, "row", scatter_dimension=0, tiled=True)
    qg_all = lax.all_gather(qg_rows.reshape(depth, 3, width).transpose(1, 0, 2), "col", axis=1)
    qg_all = qg_all.reshape(3 * cols, depth, width)
    qg_own = lax.dynamic_slice_in_dim(qg_all, 3 * col_index, 3, 0)
    qkv_grad = qg_own.transpose(1, 0, 2).reshape(depth, 3 * width).astype(F32)
    small_all, gain_all = lax.psum((small, gain_part), ("row", "col"))

    x = inputs.astype(F32)
    scale = lax.rsqrt(jnp.mean(x * x, axis=1, keepdims=True) + EPS)
    gained = gn_own * attn_gain_row
    dots = jnp.sum(gained * x, axis=1, keepdims=True)
    input_grad = resid + scale * gained - x * scale**3 * (dots / D)
    return (
        layer_out,
        input_grad,
        gain_all[0],
        qkv_grad,
        og_own.T.astype(F32),
        small_all[ROW_GAIN, :D],
        small_all[:ROUTES, :D].T,
        small_all[:ROUTES, D : D + ROUTES].T,
        small_all[ROW_CONST:ROW_VEC, :D].reshape(2, 2, D).transpose(0, 2, 1),
        small_all[ROW_VEC:ROW_GAIN, :D],
        grads[0],
        grads[1],
        grads[2].transpose(0, 2, 1),
        prev_grad,
    )


def solution(mesh):
    sizes = (mesh.shape["row"], mesh.shape["col"])
    ranks, cols = sizes
    per_heads = HEADS % cols == 0 and ranks == 8 and (HEADS // cols) * HEAD_DIM * 2 % LANES == 0
    body = functools.partial(on_device_heads, sizes) if per_heads else on_device
    placed = (
        P(("row", "col"), None),
        P(),
        P("row", "col"),
        P("col", "row"),
        P(),
        P(),
        P(),
        P(),
        P(),
        P(None, "row", "col"),
        P(None, "row", "col"),
        P(None, "col", "row"),
        P(None, ("row", "col")),
        P("row", None),
        P("row", None),
        P(("row", "col"), None),
    )
    return jax.shard_map(
        body,
        mesh=mesh,
        in_specs=placed,
        out_specs=(
            P(("row", "col"), None),
            P(("row", "col"), None),
            P(),
            P("row", "col"),
            P("col", "row"),
            P(),
            P(),
            P(),
            P(),
            P(),
            P(None, "row", "col"),
            P(None, "row", "col"),
            P(None, "col", "row"),
            P(None, ("row", "col")),
        ),
        check_vma=False,
    )
```

```python
import functools
import math

import jax
import jax.numpy as jnp
from jax import lax
from jax.experimental import pallas as pl
from jax.experimental.pallas import tpu as pltpu
from jax.sharding import PartitionSpec as P

D = 768
HEADS = 12
HEAD_DIM = 64
EXPERTS = 8
ROUTES = 12


EPS = 1e-06
BASE = 10000.0
NEG = -1e30
HIGH = lax.Precision.HIGHEST
CONTRACT_FIRST = (((0,), (0,)), ((), ()))
CONTRACT_LAST = (((1,), (1,)), ((), ()))


def rotate(block_value, positions, first_col, direction):
    row_count, col_count = block_value.shape
    column = first_col + jnp.arange(0, col_count, 2, dtype=jnp.int32)
    inner_col = column % D
    section = column // D
    head_pair = inner_col % HEAD_DIM // 2
    exponent = (2 * head_pair).astype(jnp.float32) / HEAD_DIM
    frequency = jnp.exp(-exponent * math.log(BASE))
    turned_on = (section < 2).astype(jnp.float32)
    angles = positions.astype(jnp.float32)[:, None] * (frequency * turned_on)[None, :]
    cosine = jnp.cos(angles)
    sines = direction * jnp.sin(angles)
    paired = block_value.reshape(row_count, col_count // 2, 2)
    first_part = paired[:, :, 0]
    second_part = paired[:, :, 1]
    rotated = jnp.stack(
        [first_part * cosine - second_part * sines, second_part * cosine + first_part * sines],
        axis=2,
    )
    return rotated.reshape(row_count, col_count)


def sequence_info(lengths_row, row_total):
    seq_count = lengths_row.shape[0]
    ends = jnp.cumsum(lengths_row)
    starts = ends - lengths_row
    token_place = jnp.arange(row_total, dtype=jnp.int32)
    seq_index = jnp.sum((token_place[:, None] >= ends[None, :]).astype(jnp.int32), axis=1)
    member = seq_index[:, None] == jnp.arange(seq_count, dtype=jnp.int32)[None, :]
    begin = jnp.sum(jnp.where(member, starts[None, :], 0), axis=1)
    return (seq_index, token_place - begin, seq_index < seq_count)


def partial_sums(term_value):
    return lax.psum_scatter(
        term_value.astype(jnp.bfloat16), "col", scatter_dimension=0, tiled=True
    ).astype(jnp.float32)


def whole_columns(part_value):
    return lax.all_gather(part_value, "col", axis=0, tiled=True)


def to_heads(block_value):
    return lax.all_to_all(block_value, "col", split_axis=0, concat_axis=1, tiled=True)


def to_features(block_value):
    return lax.all_to_all(block_value, "col", split_axis=1, concat_axis=0, tiled=True)


def key_scores(query_heads, key_block, query_seq, query_place, key_seq, key_place, score_scale):
    raw_scores = (
        jnp.einsum("qhd,khd->hqk", query_heads, key_block, preferred_element_type=jnp.float32)
        * score_scale
    )
    allowed = (query_seq[:, None] == key_seq[None, :]) & (
        key_place[None, :] <= query_place[:, None]
    )
    return (jnp.where(allowed[None], raw_scores, NEG), allowed)


def split_keys(key_values, seq_index, token_place, block_rows):
    count_blocks = key_values.shape[0] // block_rows
    blocks_kv = key_values.reshape(count_blocks, block_rows, 2, HEADS, HEAD_DIM)
    return (
        blocks_kv,
        seq_index.reshape(count_blocks, block_rows),
        token_place.reshape(count_blocks, block_rows),
    )


def attend_forward(
    queries, key_values, query_seq, query_place, seq_index, token_place, block_rows, score_scale
):
    local_rows = queries.shape[0]
    query_heads = queries.reshape(local_rows, HEADS, HEAD_DIM)
    key_items = split_keys(key_values, seq_index, token_place, block_rows)

    def max_step(running, block_items):
        running_max, running_sum = running
        kv_block, key_seq, key_place = block_items
        scores, allowed = key_scores(
            query_heads, kv_block[:, 0], query_seq, query_place, key_seq, key_place, score_scale
        )
        new_max = jnp.maximum(running_max, jnp.max(scores, axis=2))
        shifted = jnp.where(allowed[None], jnp.exp(scores - new_max[:, :, None]), 0.0)
        new_sum = running_sum * jnp.exp(running_max - new_max) + jnp.sum(shifted, axis=2)
        return ((new_max, new_sum), None)

    start_state = (
        jnp.full((HEADS, local_rows), NEG, jnp.float32),
        jnp.zeros((HEADS, local_rows), jnp.float32),
    )
    (final_max, final_sum), unused = lax.scan(max_step, start_state, key_items)
    log_total = final_max + jnp.log(final_sum)

    def out_step(running, block_items):
        kv_block, key_seq, key_place = block_items
        scores, allowed = key_scores(
            query_heads, kv_block[:, 0], query_seq, query_place, key_seq, key_place, score_scale
        )
        probs_low = jnp.exp(scores - log_total[:, :, None]).astype(jnp.bfloat16)
        return (
            running
            + jnp.einsum(
                "hqk,khd->qhd", probs_low, kv_block[:, 1], preferred_element_type=jnp.float32
            ),
            None,
        )

    attended, unused = lax.scan(
        out_step, jnp.zeros((local_rows, HEADS, HEAD_DIM), jnp.float32), key_items
    )
    return (attended.reshape(local_rows, D), log_total)


def attend_backward(
    queries,
    key_values,
    log_total,
    row_delta,
    grad_heads_in,
    query_seq,
    query_place,
    seq_index,
    token_place,
    block_rows,
    score_scale,
):
    local_rows = queries.shape[0]
    query_heads = queries.reshape(local_rows, HEADS, HEAD_DIM)
    grad_heads = grad_heads_in.reshape(local_rows, HEADS, HEAD_DIM)
    key_items = split_keys(key_values, seq_index, token_place, block_rows)

    def grad_step(running, block_items):
        kv_block, key_seq, key_place = block_items
        scores, allowed = key_scores(
            query_heads, kv_block[:, 0], query_seq, query_place, key_seq, key_place, score_scale
        )
        probs_full = jnp.exp(scores - log_total[:, :, None])
        probs_low = probs_full.astype(jnp.bfloat16)
        grad_probs = jnp.einsum(
            "qhd,khd->hqk", grad_heads, kv_block[:, 1], preferred_element_type=jnp.float32
        )
        grad_scores = (probs_full * (grad_probs - row_delta[:, :, None])).astype(jnp.bfloat16)
        new_running = (
            running
            + jnp.einsum(
                "hqk,khd->qhd", grad_scores, kv_block[:, 0], preferred_element_type=jnp.float32
            )
            * score_scale
        )
        grad_keys = (
            jnp.einsum("hqk,qhd->khd", grad_scores, query_heads, preferred_element_type=jnp.float32)
            * score_scale
        )
        grad_values = jnp.einsum(
            "hqk,qhd->khd", probs_low, grad_heads, preferred_element_type=jnp.float32
        )
        return (new_running, jnp.stack([grad_keys, grad_values], axis=1))

    grad_queries, grad_kv = lax.scan(
        grad_step, jnp.zeros((local_rows, HEADS, HEAD_DIM), jnp.float32), key_items
    )
    return (grad_queries.reshape(local_rows, D), grad_kv.reshape(key_values.shape[0], 2 * D))


def on_device(
    inputs,
    attn_gain,
    qkv_weight,
    out_weight,
    ffn_gain,
    router_weight,
    carry_weight,
    const_weight,
    const_vector,
    gate_weight,
    up_weight,
    down_weight,
    prev_logits,
    seq_lengths,
    expert_routes,
    cotangent,
):
    col_index = lax.axis_index("col")
    row_total = expert_routes.shape[0]
    local_rows = inputs.shape[0]
    capacity = row_total // 4
    block_rows = min(row_total, 512)
    score_scale = 1.0 / math.sqrt(HEAD_DIM)
    full_weights = (
        lax.all_gather(qkv_weight, "row", axis=0, tiled=True),
        lax.all_gather(out_weight, "row", axis=1, tiled=True),
        lax.all_gather(gate_weight, "row", axis=1, tiled=True),
        lax.all_gather(up_weight, "row", axis=1, tiled=True),
        lax.all_gather(down_weight, "row", axis=2, tiled=True),
    )
    qkv_full, out_full, gate_full, up_full, down_full = full_weights
    whole_in, whole_cot, whole_prev = (
        lax.all_gather(inputs, "col", axis=0, tiled=True),
        lax.all_gather(cotangent, "col", axis=0, tiled=True),
        lax.all_gather(prev_logits, "col", axis=1, tiled=True),
    )
    seq_index, positions, valid_all = sequence_info(seq_lengths[0], row_total)
    token_place = jnp.arange(row_total, dtype=jnp.int32)
    first_row = col_index * local_rows

    def own_rows(whole_value):
        return lax.dynamic_slice_in_dim(whole_value, first_row, local_rows, 0)

    query_seq = own_rows(seq_index)
    query_place = own_rows(token_place)
    query_pos = own_rows(positions)
    query_valid = own_rows(valid_all).astype(jnp.float32)[:, None]
    input_rows = whole_in.astype(jnp.float32)
    attn_gain_full = attn_gain.astype(jnp.float32)
    scale_attn = lax.rsqrt(jnp.mean(input_rows * input_rows, axis=1, keepdims=True) + EPS)
    normed1 = (input_rows * scale_attn * attn_gain_full).astype(jnp.bfloat16)
    projected = jnp.dot(normed1, qkv_full, preferred_element_type=jnp.float32)
    turned = rotate(projected, positions, col_index * projected.shape[1], 1.0).astype(jnp.bfloat16)
    token_qkv = to_heads(turned)
    queries = token_qkv[:, :D]
    key_values = lax.all_gather(token_qkv[:, D:], "col", axis=0, tiled=True)
    attended, log_total = attend_forward(
        queries, key_values, query_seq, query_place, seq_index, token_place, block_rows, score_scale
    )
    attn_tok = (attended * query_valid).astype(jnp.bfloat16)
    attn_feat = to_features(attn_tok)
    attn_out = partial_sums(jnp.dot(attn_feat, out_full, preferred_element_type=jnp.float32))
    input_local = inputs.astype(jnp.float32)
    middle = input_local + attn_out
    scale_ffn = lax.rsqrt(jnp.mean(middle * middle, axis=1, keepdims=True) + EPS)
    ffn_gain_full = ffn_gain.astype(jnp.float32)
    normed2_local = (middle * scale_ffn * ffn_gain_full).astype(jnp.bfloat16)
    normed2 = whole_columns(normed2_local)
    carry_full = carry_weight.astype(jnp.float32)
    prev_rows = whole_prev.astype(jnp.float32).T
    route_hot = (
        expert_routes[:, :, None] == jnp.arange(ROUTES, dtype=jnp.int32)[None, None, :]
    ).astype(jnp.float32)
    logits = jnp.dot(normed2, router_weight, preferred_element_type=jnp.float32) + jnp.dot(
        prev_rows, carry_full, precision=HIGH
    )
    picked = jnp.sum(route_hot * logits[:, None, :], axis=2)
    gate_values = jax.nn.softmax(picked, axis=1)
    flat_route = expert_routes.reshape(-1)
    route_hits = (flat_route[:, None] == jnp.arange(EXPERTS, dtype=jnp.int32)[None, :]).astype(
        jnp.int32
    )
    slot_index = jnp.sum((jnp.cumsum(route_hits, axis=0) - 1) * route_hits, axis=1)
    dump_slot = EXPERTS * capacity
    target = jnp.where(flat_route < EXPERTS, flat_route * capacity + slot_index, dump_slot)
    slot_owner = (
        jnp.full((dump_slot + 1,), row_total, jnp.int32)
        .at[target]
        .set(jnp.arange(2 * row_total, dtype=jnp.int32) // 2)[:dump_slot]
    )
    slot_gate = (
        jnp.zeros((dump_slot + 1,), jnp.float32)
        .at[target]
        .set(gate_values.reshape(-1))[:dump_slot]
        .reshape(EXPERTS, capacity, 1)
    )
    zero_row = jnp.zeros((1, D), jnp.bfloat16)
    expert_in = jnp.concatenate([normed2, zero_row], axis=0)[slot_owner].reshape(
        EXPERTS, capacity, D
    )
    gate_pre = jnp.einsum("ecd,edf->ecf", expert_in, gate_full, preferred_element_type=jnp.float32)
    up_pre = jnp.einsum("ecd,edf->ecf", expert_in, up_full, preferred_element_type=jnp.float32)
    sigmoid_gate = jax.nn.sigmoid(gate_pre)
    activated = gate_pre * sigmoid_gate
    hidden = (activated * up_pre).astype(jnp.bfloat16)
    expert_out = jnp.einsum("ecf,efd->ecd", hidden, down_full, preferred_element_type=jnp.float32)
    out_rows = jnp.concatenate(
        [expert_out.reshape(dump_slot, D), jnp.zeros((1, D), jnp.float32)], axis=0
    )
    chosen_out = out_rows[target].reshape(row_total, 2, D)
    cot_rows = whole_cot.astype(jnp.float32)
    ffn_mix = jnp.sum(gate_values[:, :, None] * chosen_out, axis=1)
    ffn_dots = jnp.sum(cot_rows[:, None, :] * chosen_out, axis=2)
    mix_local = partial_sums(ffn_mix)
    normed_local = normed2_local.astype(jnp.float32)
    vector_full = const_vector.astype(jnp.float32)
    routes_local = own_rows(expert_routes)
    gates_local = own_rows(gate_values)
    hot_local = own_rows(route_hot)
    copy_hit = (routes_local == EXPERTS + 1).astype(jnp.float32)
    const_hit = (
        routes_local[:, :, None] == (EXPERTS + 2 + jnp.arange(2, dtype=jnp.int32))[None, None, :]
    ).astype(jnp.float32)
    copy_share = jnp.sum(gates_local * copy_hit, axis=1)
    const_share = jnp.sum(gates_local[:, :, None] * const_hit, axis=1)
    const_alpha = jax.nn.softmax(
        jnp.einsum("td,jdk->tjk", normed2_local, const_weight, preferred_element_type=jnp.float32),
        axis=2,
    )
    keep_share = copy_share + jnp.sum(const_share * const_alpha[:, :, 0], axis=1)
    local_mix = keep_share[:, None] * normed_local + jnp.dot(
        const_share * const_alpha[:, :, 1], vector_full, precision=HIGH
    )
    layer_out = (middle + mix_local + local_mix).astype(jnp.bfloat16)
    qkv_full, out_full, gate_full, up_full, down_full = full_weights
    ffn_total = lax.psum(ffn_dots, "col")
    ffn_local = own_rows(ffn_total)
    cot_local = cotangent.astype(jnp.float32)
    dot_keep = jnp.sum(cot_local * normed_local, axis=1)
    dot_vector = jnp.dot(cot_local, vector_full.T, precision=HIGH)
    const_dots = const_alpha[:, :, 0] * dot_keep[:, None] + const_alpha[:, :, 1] * dot_vector
    grad_gates = (
        ffn_local
        + copy_hit * dot_keep[:, None]
        + jnp.sum(const_hit * const_dots[:, None, :], axis=2)
    )
    grad_picked = gates_local * (
        grad_gates - jnp.sum(gates_local * grad_gates, axis=1, keepdims=True)
    )
    grad_logits = jnp.sum(hot_local * grad_picked[:, :, None], axis=1)
    prev_local = prev_logits.astype(jnp.float32).T
    router_grad = lax.dot_general(normed_local, grad_logits, CONTRACT_FIRST, precision=HIGH)
    carry_grad = lax.dot_general(prev_local, grad_logits, CONTRACT_FIRST, precision=HIGH)
    prev_grad = lax.dot_general(carry_full, grad_logits, CONTRACT_LAST, precision=HIGH)
    grad_alpha_keep = const_share * dot_keep[:, None]
    grad_alpha_vector = const_share * dot_vector
    alpha_mean = const_alpha[:, :, 0] * grad_alpha_keep + const_alpha[:, :, 1] * grad_alpha_vector
    grad_alpha_logits = jnp.stack(
        [
            const_alpha[:, :, 0] * (grad_alpha_keep - alpha_mean),
            const_alpha[:, :, 1] * (grad_alpha_vector - alpha_mean),
        ],
        axis=2,
    )
    const_grad = jnp.einsum("td,tjk->jdk", normed_local, grad_alpha_logits, precision=HIGH)
    vector_grad = lax.dot_general(
        const_share * const_alpha[:, :, 1], cot_local, CONTRACT_FIRST, precision=HIGH
    )
    router_full = router_weight.astype(jnp.float32)
    const_full = const_weight.astype(jnp.float32)
    grad_normed_local = (
        keep_share[:, None] * cot_local
        + lax.dot_general(grad_logits, router_full, CONTRACT_LAST, precision=HIGH)
        + jnp.einsum("tjk,jdk->td", grad_alpha_logits, const_full, precision=HIGH)
    )
    cot_in = jnp.concatenate([whole_cot, zero_row], axis=0)[slot_owner].reshape(
        EXPERTS, capacity, D
    )
    grad_expert = (slot_gate * cot_in.astype(jnp.float32)).astype(jnp.bfloat16)
    down_grad = jnp.einsum("ecf,ecd->efd", hidden, grad_expert, preferred_element_type=jnp.float32)
    grad_hidden = jnp.einsum(
        "ecd,efd->ecf", grad_expert, down_full, preferred_element_type=jnp.float32
    )
    grad_gate_pre = (
        grad_hidden * up_pre * sigmoid_gate * (1.0 + gate_pre * (1.0 - sigmoid_gate))
    ).astype(jnp.bfloat16)
    grad_up_pre = (grad_hidden * activated).astype(jnp.bfloat16)
    gate_grad = jnp.einsum(
        "ecd,ecf->edf", expert_in, grad_gate_pre, preferred_element_type=jnp.float32
    )
    up_grad = jnp.einsum("ecd,ecf->edf", expert_in, grad_up_pre, preferred_element_type=jnp.float32)
    grad_expert_in = jnp.einsum(
        "ecf,edf->ecd", grad_gate_pre, gate_full, preferred_element_type=jnp.float32
    ) + jnp.einsum("ecf,edf->ecd", grad_up_pre, up_full, preferred_element_type=jnp.float32)
    grad_slots = jnp.concatenate(
        [grad_expert_in.reshape(dump_slot, D), jnp.zeros((1, D), jnp.float32)], axis=0
    )
    grad_tokens = jnp.sum(grad_slots[target].reshape(row_total, 2, D), axis=1)
    grad_normed = partial_sums(grad_tokens) + grad_normed_local
    gained_ffn = grad_normed * ffn_gain_full
    ffn_dots_rows = jnp.sum(gained_ffn * middle, axis=1, keepdims=True)
    grad_middle = scale_ffn * gained_ffn - middle * scale_ffn**3 * (ffn_dots_rows / D)
    ffn_gain_grad = jnp.sum(grad_normed * middle * scale_ffn, axis=0)
    grad_resid = cot_local + grad_middle
    branch_cot = whole_columns(grad_resid.astype(jnp.bfloat16))
    out_grad = lax.dot_general(
        attn_feat, branch_cot, CONTRACT_FIRST, preferred_element_type=jnp.float32
    )
    grad_mixed = lax.dot_general(
        branch_cot, out_full, CONTRACT_LAST, preferred_element_type=jnp.float32
    )
    grad_tok = to_heads(grad_mixed.astype(jnp.bfloat16))
    grad_heads_in = (grad_tok.astype(jnp.float32) * query_valid).astype(jnp.bfloat16)
    row_delta = jnp.sum(
        grad_heads_in.astype(jnp.float32).reshape(local_rows, HEADS, HEAD_DIM)
        * attended.reshape(local_rows, HEADS, HEAD_DIM),
        axis=2,
    ).T
    grad_queries, grad_kv = attend_backward(
        queries,
        key_values,
        log_total,
        row_delta,
        grad_heads_in,
        query_seq,
        query_place,
        seq_index,
        token_place,
        block_rows,
        score_scale,
    )
    grad_kv_local = lax.psum_scatter(
        grad_kv.astype(jnp.bfloat16), "col", scatter_dimension=0, tiled=True
    ).astype(jnp.float32)
    grad_turned = jnp.concatenate([grad_queries, grad_kv_local], axis=1)
    grad_proj_tok = rotate(grad_turned, query_pos, 0, -1.0).astype(jnp.bfloat16)
    grad_projected = to_features(grad_proj_tok)
    qkv_grad = lax.dot_general(
        normed1, grad_projected, CONTRACT_FIRST, preferred_element_type=jnp.float32
    )
    grad_normed1 = partial_sums(
        lax.dot_general(grad_projected, qkv_full, CONTRACT_LAST, preferred_element_type=jnp.float32)
    )
    scale_attn_local = own_rows(scale_attn)
    gained_attn = grad_normed1 * attn_gain_full
    attn_dots_rows = jnp.sum(gained_attn * input_local, axis=1, keepdims=True)
    input_grad = (
        grad_resid
        + scale_attn_local * gained_attn
        - input_local * scale_attn_local**3 * (attn_dots_rows / D)
    )
    attn_gain_grad = jnp.sum(grad_normed1 * input_local * scale_attn_local, axis=0)
    qkv_grad, out_grad, gate_grad, up_grad, down_grad = (
        lax.psum_scatter(
            qkv_grad.astype(jnp.bfloat16), "row", scatter_dimension=0, tiled=True
        ).astype(jnp.float32),
        lax.psum_scatter(
            out_grad.astype(jnp.bfloat16), "row", scatter_dimension=1, tiled=True
        ).astype(jnp.float32),
        lax.psum_scatter(
            gate_grad.astype(jnp.bfloat16), "row", scatter_dimension=1, tiled=True
        ).astype(jnp.float32),
        lax.psum_scatter(
            up_grad.astype(jnp.bfloat16), "row", scatter_dimension=1, tiled=True
        ).astype(jnp.float32),
        lax.psum_scatter(
            down_grad.astype(jnp.bfloat16), "row", scatter_dimension=2, tiled=True
        ).astype(jnp.float32),
    )
    attn_gain_grad, ffn_gain_grad, router_grad, carry_grad, const_grad, vector_grad = lax.psum(
        (attn_gain_grad, ffn_gain_grad, router_grad, carry_grad, const_grad, vector_grad),
        ("row", "col"),
    )
    return (
        layer_out,
        input_grad,
        attn_gain_grad,
        qkv_grad,
        out_grad,
        ffn_gain_grad,
        router_grad,
        carry_grad,
        const_grad,
        vector_grad,
        gate_grad,
        up_grad,
        down_grad,
        prev_grad,
    )


BF = jnp.bfloat16
F32 = jnp.float32
LANES = 128
NN = (((1,), (0,)), ((), ()))
NT = (((1,), (1,)), ((), ()))
TN = (((0,), (0,)), ((), ()))
ROW_CONST = 12
ROW_VEC = 16
ROW_GAIN = 18
SMALL_ROWS = 24
Q_ROWS = 256
MIB = 1 << 20


def mm(a, b, dims=NN):
    return lax.dot_general(a, b, dims, preferred_element_type=F32)


def lane_iota(shape):
    return lax.broadcasted_iota(jnp.int32, shape, len(shape) - 1)


def whole(shape):
    return pl.BlockSpec(shape, lambda *_: (0,) * len(shape), pipeline_mode=pl.Buffered(1))


def swap_pairs(v):
    even = lane_iota(v.shape) % 2 == 0
    return jnp.where(even, pltpu.roll(v, LANES - 1, 1), pltpu.roll(v, 1, 1))


def norm_rows(x):
    return lax.rsqrt(jnp.mean(x * x, axis=1, keepdims=True) + EPS)


def qkv_kernel(heads, x_ref, gain_ref, w_ref, cos_ref, sin_ref, out_ref):
    x = x_ref[...].astype(F32)
    normed = (x * norm_rows(x) * gain_ref[...]).astype(BF)
    proj = mm(normed, w_ref[...])
    cosine, sines = cos_ref[...], sin_ref[...]
    width = heads * HEAD_DIM
    for part in range(2 * width // LANES):
        v = proj[:, part * LANES : (part + 1) * LANES]
        t = v * cosine + swap_pairs(v) * sines
        for half in range(2):
            head = 2 * part + half
            piece = t[:, half * HEAD_DIM : (half + 1) * HEAD_DIM].astype(BF)
            if head < heads:
                piece = piece * jnp.asarray(1.0 / math.sqrt(HEAD_DIM), BF)
            out_ref[head] = piece
    for head in range(2 * heads, 3 * heads):
        out_ref[head] = proj[:, head * HEAD_DIM : (head + 1) * HEAD_DIM].astype(BF)


def project_heads(heads, whole_in, gain, weight, cosine, sines):
    rows = whole_in.shape[0]
    blk = 256
    return pl.pallas_call(
        functools.partial(qkv_kernel, heads),
        grid=(rows // blk,),
        out_shape=jax.ShapeDtypeStruct((3 * heads, rows, HEAD_DIM), BF),
        in_specs=[
            pl.BlockSpec((blk, D), lambda i: (i, 0)),
            whole((1, D)),
            whole((D, 3 * heads * HEAD_DIM)),
            pl.BlockSpec((blk, LANES), lambda i: (i, 0)),
            pl.BlockSpec((blk, LANES), lambda i: (i, 0)),
        ],
        out_specs=pl.BlockSpec((3 * heads, blk, HEAD_DIM), lambda i: (0, i, 0)),
        compiler_params=pltpu.CompilerParams(vmem_limit_bytes=32 * MIB),
        cost_estimate=pl.CostEstimate(
            flops=2 * rows * D * 3 * heads * HEAD_DIM, bytes_accessed=8 * MIB, transcendentals=0
        ),
        name="project_heads",
    )(whole_in, gain, weight, cosine, sines)


def seen(begin, first, rows, length):
    u = lax.broadcasted_iota(jnp.int32, (rows, length), 1)
    t = lax.broadcasted_iota(jnp.int32, (rows, length), 0) + first
    return (u >= begin) & (u <= t)


def attend_kernel(q_ref, k_ref, v_ref, begin_ref, valid_ref, o_ref, lse_ref):
    rows = q_ref.shape[1]
    for i in range(rows // Q_ROWS):
        at = slice(i * Q_ROWS, (i + 1) * Q_ROWS)
        length = (i + 1) * Q_ROWS
        s = mm(q_ref[0, at], k_ref[0, :length], NT)
        s = jnp.where(seen(begin_ref[at], i * Q_ROWS, Q_ROWS, length), s, NEG)
        top = jnp.max(s, axis=1, keepdims=True)
        p = jnp.exp(s - top)
        total = jnp.sum(p, axis=1, keepdims=True)
        o = mm(p.astype(BF), v_ref[0, :length]) * (valid_ref[at] / total)
        o_ref[0, at] = o.astype(BF)
        lse_ref[0, at] = top + jnp.log(total)


def attend(heads, qkv, begin, valid):
    rows = qkv.shape[1]
    head_block = (1, rows, HEAD_DIM)
    return pl.pallas_call(
        attend_kernel,
        grid=(heads,),
        out_shape=(
            jax.ShapeDtypeStruct((heads, rows, HEAD_DIM), BF),
            jax.ShapeDtypeStruct((heads, rows, 1), F32),
        ),
        in_specs=[
            pl.BlockSpec(head_block, lambda h: (h, 0, 0)),
            pl.BlockSpec(head_block, lambda h: (h + heads, 0, 0)),
            pl.BlockSpec(head_block, lambda h: (h + 2 * heads, 0, 0)),
            whole((rows, 1)),
            whole((rows, 1)),
        ],
        out_specs=(
            pl.BlockSpec(head_block, lambda h: (h, 0, 0)),
            pl.BlockSpec((1, rows, 1), lambda h: (h, 0, 0)),
        ),
        compiler_params=pltpu.CompilerParams(vmem_limit_bytes=48 * MIB),
        cost_estimate=pl.CostEstimate(
            flops=8 * heads * rows * rows * HEAD_DIM, bytes_accessed=8 * MIB, transcendentals=heads * rows * rows
        ),
        name="attend",
    )(qkv, qkv, qkv, begin, valid)


def branch_kernel(a_ref, w_ref, x_ref, gain_ref, mixed_ref, middle_ref, normed_ref):
    mixed = jnp.concatenate([a_ref[i] for i in range(a_ref.shape[0])], axis=1)
    mixed_ref[...] = mixed
    middle = x_ref[...].astype(F32) + mm(mixed, w_ref[...], NT)
    middle_ref[...] = middle
    normed_ref[...] = (middle * norm_rows(middle) * gain_ref[...]).astype(BF)


def branch(attn_parts, out_t, inputs, gain):
    rows = inputs.shape[0]
    return pl.pallas_call(
        branch_kernel,
        out_shape=(
            jax.ShapeDtypeStruct((rows, D), BF),
            jax.ShapeDtypeStruct((rows, D), F32),
            jax.ShapeDtypeStruct((rows, D), BF),
        ),
        compiler_params=pltpu.CompilerParams(vmem_limit_bytes=32 * MIB),
        cost_estimate=pl.CostEstimate(flops=2 * rows * D * D, bytes_accessed=6 * MIB, transcendentals=0),
        name="branch",
    )(attn_parts, out_t, inputs, gain)


def gate_lanes(logits, routes):
    lane = lane_iota(logits.shape)
    hit = (lane == routes[:, 0:1]) | (lane == routes[:, 1:2])
    held = jnp.where(hit, logits, NEG)
    e = jnp.where(hit, jnp.exp(held - jnp.max(held, axis=1, keepdims=True)), 0.0)
    return e / jnp.sum(e, axis=1, keepdims=True)


MESH = pl.DeviceIdType.MESH
ANY = pl.BlockSpec(memory_space=pl.ANY)
PACK = 3 * HEAD_DIM // 2


def place():
    return lax.axis_index("row"), lax.axis_index("col")


def flip(index, mask):
    for bit in (1, 2, 4):
        if mask & bit:
            index = index + bit - 2 * bit * (index // bit % 2)
    return index


def greet(devices):
    barrier = pltpu.get_barrier_semaphore()
    for device in devices:
        pl.semaphore_signal(barrier, inc=1, device_id=device, device_id_type=MESH)
    pl.semaphore_wait(barrier, len(devices))


def send_to(src, dst, send, recv, device):
    return pltpu.make_async_remote_copy(
        src_ref=src, dst_ref=dst, send_sem=send, recv_sem=recv, device_id=device, device_id_type=MESH
    )


def col_peers(n):
    r, c = place()
    return [(r, (c + k) % n) for k in range(1, n)]


def gather_chain(own, dst, send, recv, n):
    r, c = place()

    def right(k):
        i = jnp.maximum(c - k, 0)
        src = own if k == 0 else dst.at[i]
        return send_to(src, dst.at[i], send.at[0, k], recv.at[0, k], (r, jnp.minimum(c + 1, n - 1)))

    def left(k):
        i = jnp.minimum(c + k, n - 1)
        src = own if k == 0 else dst.at[i]
        return send_to(src, dst.at[i], send.at[1, k], recv.at[1, k], (r, jnp.maximum(c - 1, 0)))

    def step(k):
        if k > 0:

            @pl.when(c >= k)
            def _():
                right(k - 1).wait_recv()

            @pl.when(c + k < n)
            def _():
                left(k - 1).wait_recv()

        if k < n - 1:

            @pl.when((c >= k) & (c + 1 < n))
            def _():
                right(k).start()

            @pl.when((c + k < n) & (c >= 1))
            def _():
                left(k).start()

    def drain():
        for k in range(n - 1):

            @pl.when((c >= k) & (c + 1 < n))
            def _():
                right(k).wait_send()

            @pl.when((c + k < n) & (c >= 1))
            def _():
                left(k).wait_send()

    return step, drain


def reduce_chain(own, out, arrived, send, recv, n):
    r, c = place()

    def right(k):
        return send_to(out.at[0, k], arrived.at[0, k], send.at[0, k], recv.at[0, k], (r, jnp.minimum(c + 1, n - 1)))

    def left(k):
        return send_to(out.at[1, k], arrived.at[1, k], send.at[1, k], recv.at[1, k], (r, jnp.maximum(c - 1, 0)))

    def slot(s):
        if s == n - 1:

            @pl.when(c >= 1)
            def _():
                right(n - 1 - c).wait_recv()

            @pl.when(c <= n - 2)
            def _():
                left(c).wait_recv()

            return

        @pl.when(c <= s)
        def _():
            k = jnp.maximum(s - c, 0)

            @pl.when(c >= 1)
            def _():
                right(k).wait_recv()
                out[0, k] = (own(n - 1 - k).astype(F32) + arrived[0, k].astype(F32)).astype(BF)

            @pl.when(c == 0)
            def _():
                out[0, k] = own(n - 1 - k).astype(BF)

            right(k).start()

        @pl.when(n - 1 - c <= s)
        def _():
            k = jnp.maximum(s - (n - 1 - c), 0)

            @pl.when(c <= n - 2)
            def _():
                left(k).wait_recv()
                out[1, k] = (own(k).astype(F32) + arrived[1, k].astype(F32)).astype(BF)

            @pl.when(c == n - 1)
            def _():
                out[1, k] = own(k).astype(BF)

            left(k).start()

    def total(dst):
        dst[...] = own(c).astype(F32)

        @pl.when(c >= 1)
        def _():
            dst[...] += arrived[0, n - 1 - c].astype(F32)

        @pl.when(c <= n - 2)
        def _():
            dst[...] += arrived[1, c].astype(F32)

    def drain():
        for k in range(n - 1):

            @pl.when(c < n - 1 - k)
            def _():
                right(k).wait_send()

            @pl.when(c > k)
            def _():
                left(k).wait_send()

    return slot, total, drain


def chain_scratch(n, rows):
    return [
        pltpu.VMEM((2, n - 1, rows, D), BF),
        pltpu.VMEM((2, n - 1, rows, D), BF),
        pltpu.SemaphoreType.DMA((2, n - 1)),
        pltpu.SemaphoreType.DMA((2, n - 1)),
    ]


def slot_rows(tsr_ref, capacity):
    rows = tsr_ref.shape[2]
    return jnp.where(lax.broadcasted_iota(jnp.int32, (capacity, rows), 0) == tsr_ref[0], 1.0, 0.0).astype(BF)


def slot_column(tsc_ref, e):
    return jnp.sum(jnp.where(lane_iota(tsc_ref.shape) == e, tsc_ref[...], 0), axis=1, keepdims=True)


def full_weight(w_ref, t):
    ranks, _, _, depth, ff = w_ref.shape
    return w_ref[:, t, 0].reshape(ranks * depth, ff)


COMBINE = 256


def experts_forward_kernel(
    cols,
    capacity,
    n2_ref,
    prev_ref,
    cot_ref,
    rw_ref,
    carry_ref,
    routes_ref,
    tsr_ref,
    tsc_ref,
    w_ref,
    x_ref,
    gu_ref,
    mix_ref,
    gates_ref,
    cotw_ref,
    mix_acc,
    send,
    recv,
    local_sem,
):
    e = pl.program_id(0)
    experts = pl.num_programs(0)
    r, c = place()
    rows = n2_ref.shape[0]
    local = rows // cols
    step, drain = gather_chain(cot_ref, cotw_ref, send, recv, cols)
    own_copy = pltpu.make_async_copy(cot_ref, cotw_ref.at[c], local_sem.at[0])

    @pl.when(e == 0)
    def _():
        greet(col_peers(cols))
        own_copy.start()
        step(0)
        prev = jnp.concatenate([mm(prev_ref[i], carry_ref[...], TN) for i in range(cols)], axis=0)
        g = gate_lanes(mm(n2_ref[...], rw_ref[...], NT) + prev, routes_ref[...])
        high = g.astype(BF)
        gates_ref[:, :LANES] = high
        gates_ref[:, LANES:] = (g - high.astype(F32)).astype(BF)
        mix_acc[...] = jnp.zeros_like(mix_acc)

    @pl.when(e == 3)
    def _():
        step(1)

    one = slot_rows(tsr_ref, capacity)
    x = mm(one, n2_ref[...]).astype(BF)
    x_ref[0] = x
    sg = mm(one, gates_ref[...])
    sg = jnp.sum(jnp.where(lane_iota(sg.shape) % LANES == e, sg, 0.0), axis=1, keepdims=True)
    g = mm(x, full_weight(w_ref, 0))
    u = mm(x, full_weight(w_ref, 1))
    gu_ref[0, 0] = g.astype(BF)
    gu_ref[0, 1] = u.astype(BF)
    gh = (g * jax.nn.sigmoid(g) * u * sg).astype(BF)
    y = mm(gh, full_weight(w_ref, 2), NT).astype(BF)
    tsc = slot_column(tsc_ref, e)
    for b in range(rows // COMBINE):
        rs = slice(b * COMBINE, (b + 1) * COMBINE)
        one_t = jnp.where(lane_iota((COMBINE, capacity)) == tsc[rs], 1.0, 0.0).astype(BF)
        mix_acc[rs] += mm(one_t, y)

    @pl.when(e == experts - 1)
    def _():
        for k in range(2, cols):
            step(k)
        for d in range(cols):
            mix_ref[d] = mix_acc[d * local : (d + 1) * local].astype(BF)
        drain()
        own_copy.wait()


def experts_forward(cols, n2, prev, cot, rw, carry, routes, slots, slots_t, w_all):
    rows = n2.shape[0]
    capacity = rows // 4
    ranks, three, experts, depth, ff = w_all.shape
    local = rows // cols
    return pl.pallas_call(
        functools.partial(experts_forward_kernel, cols, capacity),
        grid=(experts,),
        out_shape=(
            jax.ShapeDtypeStruct((experts, capacity, D), BF),
            jax.ShapeDtypeStruct((experts, 2, capacity, ff), BF),
            jax.ShapeDtypeStruct((cols, local, D), BF),
            jax.ShapeDtypeStruct((rows, 2 * LANES), BF),
            jax.ShapeDtypeStruct((cols, local, D), BF),
        ),
        in_specs=[
            whole((rows, D)),
            whole((cols, 16, local)),
            whole((local, D)),
            whole((LANES, D)),
            whole((16, LANES)),
            whole((rows, 2)),
            pl.BlockSpec((1, 1, rows), lambda e: (e, 0, 0)),
            whole((rows, experts)),
            pl.BlockSpec((ranks, three, 1, depth, ff), lambda e: (0, 0, e, 0, 0)),
        ],
        out_specs=(
            pl.BlockSpec((1, capacity, D), lambda e: (e, 0, 0)),
            pl.BlockSpec((1, 2, capacity, ff), lambda e: (e, 0, 0, 0)),
            whole((cols, local, D)),
            whole((rows, 2 * LANES)),
            ANY,
        ),
        scratch_shapes=[
            pltpu.VMEM((rows, D), F32),
            pltpu.SemaphoreType.DMA((2, cols - 1)),
            pltpu.SemaphoreType.DMA((2, cols - 1)),
            pltpu.SemaphoreType.DMA((1,)),
        ],
        compiler_params=pltpu.CompilerParams(
            vmem_limit_bytes=60 * MIB, collective_id=1, has_side_effects=True
        ),
        cost_estimate=pl.CostEstimate(
            flops=experts * capacity * 4 * D * (2 * ff + rows),
            bytes_accessed=40 * MIB,
            transcendentals=experts * capacity * ff,
        ),
        name="experts_forward",
    )(n2, prev, cot, rw, carry, routes, slots_t, slots, w_all)


def experts_backward_kernel(
    cols,
    capacity,
    cot_ref,
    mix_ref,
    gates_ref,
    tsr_ref,
    tsc_ref,
    w_ref,
    x_ref,
    gu_ref,
    gt_ref,
    dots_ref,
    mixsum_ref,
    gown_ref,
    sib_ref,
    gt_acc,
    gbuf,
    out,
    arrived,
    send,
    recv,
    own_sem,
    sib_send,
    sib_recv,
):
    e = pl.program_id(0)
    experts = pl.num_programs(0)
    r, c = place()
    core = r % 2
    rows = cot_ref.shape[0]
    local = rows // cols
    place_now = lax.rem(e, 2)
    slot, total, drain = reduce_chain(lambda d: mix_ref[d], out, arrived, send, recv, cols)

    def own_copy(expert, at):
        return pltpu.make_async_copy(gbuf.at[at, :, :, core], gown_ref.at[expert], own_sem.at[at])

    def sib_copy(expert, at):
        return send_to(
            gbuf.at[at, :, :, 1 - core],
            sib_ref.at[expert],
            sib_send.at[at],
            sib_recv.at[expert],
            (flip(r, 1), c),
        )

    @pl.when(e == 0)
    def _():
        greet(col_peers(cols) + [(flip(r, 1), c)])
        slot(0)
        gt_acc[...] = jnp.zeros_like(gt_acc)

    @pl.when(e == 2)
    def _():
        slot(1)

    @pl.when(e == 5)
    def _():
        slot(2)

    one = slot_rows(tsr_ref, capacity)
    ct = mm(one, cot_ref[...]).astype(BF)
    sg = mm(one, gates_ref[...])
    sg = jnp.sum(jnp.where(lane_iota(sg.shape) % LANES == e, sg, 0.0), axis=1, keepdims=True)
    x = x_ref[0]
    g, u = gu_ref[0, 0].astype(F32), gu_ref[0, 1].astype(F32)
    wg, wu = full_weight(w_ref, 0), full_weight(w_ref, 1)
    v = mm(ct, full_weight(w_ref, 2))
    sig = jax.nn.sigmoid(g)
    act = g * sig
    h = act * u
    dot = jnp.sum(h * v, axis=1, keepdims=True)
    dots_ref[pl.ds(e, 1)] = jnp.sum(one.astype(F32) * dot, axis=0, keepdims=True)
    gh = (h * sg).astype(BF)
    gv = v * sg
    dg = (gv * u * (sig * (1.0 + g * (1.0 - sig)))).astype(BF)
    du = (gv * act).astype(BF)
    dx = (mm(dg, wg, NT) + mm(du, wu, NT)).astype(BF)
    tsc = slot_column(tsc_ref, e)
    for b in range(rows // COMBINE):
        rs = slice(b * COMBINE, (b + 1) * COMBINE)
        one_t = jnp.where(lane_iota((COMBINE, capacity)) == tsc[rs], 1.0, 0.0).astype(BF)
        gt_acc[rs] += mm(one_t, dx)

    @pl.when(e >= 2)
    def _():
        own_copy(e - 2, place_now).wait()
        sib_copy(e - 2, place_now).wait_send()

    shape = gbuf.shape[2:]
    gbuf[place_now, 0] = mm(x, dg, TN).astype(BF).reshape(shape)
    gbuf[place_now, 1] = mm(x, du, TN).astype(BF).reshape(shape)
    gbuf[place_now, 2] = mm(ct, gh, TN).astype(BF).reshape(shape)
    own_copy(e, place_now).start()
    sib_copy(e, place_now).start()

    @pl.when(e == experts - 1)
    def _():
        for d in range(cols):
            gt_ref[d] = gt_acc[d * local : (d + 1) * local].astype(BF)
        for s in range(3, cols):
            slot(s)
        total(mixsum_ref)
        drain()
        for back in (1, 0):
            own_copy(e - back, lax.rem(e - back, 2)).wait()
            sib_copy(e - back, lax.rem(e - back, 2)).wait_send()
        for i in range(8):
            sib_copy(i, i % 2).wait_recv()


def experts_backward(cols, cot, mix, gates, slots, slots_t, w_all, x, gu):
    rows = cot.shape[0]
    capacity = rows // 4
    ranks, three, experts, depth, ff = w_all.shape
    local = rows // cols
    chips = ranks // 2
    half = jax.ShapeDtypeStruct((experts, three, chips, depth, ff), BF)
    return pl.pallas_call(
        functools.partial(experts_backward_kernel, cols, capacity),
        grid=(experts,),
        out_shape=(
            jax.ShapeDtypeStruct((cols, local, D), BF),
            jax.ShapeDtypeStruct((experts, rows), F32),
            jax.ShapeDtypeStruct((local, D), F32),
            half,
            half,
        ),
        in_specs=[
            whole((rows, D)),
            whole((cols, local, D)),
            whole((rows, 2 * LANES)),
            pl.BlockSpec((1, 1, rows), lambda e: (e, 0, 0)),
            whole((rows, experts)),
            pl.BlockSpec((ranks, three, 1, depth, ff), lambda e: (0, 0, e, 0, 0)),
            pl.BlockSpec((1, capacity, D), lambda e: (e, 0, 0)),
            pl.BlockSpec((1, 2, capacity, ff), lambda e: (e, 0, 0, 0)),
        ],
        out_specs=(
            whole((cols, local, D)),
            whole((experts, rows)),
            whole((local, D)),
            ANY,
            ANY,
        ),
        scratch_shapes=[
            pltpu.VMEM((rows, D), F32),
            pltpu.VMEM((2, three, chips, 2, depth, ff), BF),
            *chain_scratch(cols, local),
            pltpu.SemaphoreType.DMA((2,)),
            pltpu.SemaphoreType.DMA((2,)),
            pltpu.SemaphoreType.DMA((experts,)),
        ],
        compiler_params=pltpu.CompilerParams(
            vmem_limit_bytes=60 * MIB, collective_id=2, has_side_effects=True
        ),
        cost_estimate=pl.CostEstimate(
            flops=experts * capacity * 4 * D * (3 * ff + rows),
            bytes_accessed=60 * MIB,
            transcendentals=experts * capacity * ff,
        ),
        name="experts_backward",
    )(cot, mix, gates, slots_t, slots, w_all, x, gu)


def pack_heads(dst, value):
    rows = value.shape[0]
    half = rows // 2
    dst[:rows] = value[:, :LANES]
    dst[rows:] = jnp.concatenate([value[:half, LANES:], value[half:, LANES:]], axis=1)


def unpack_heads(packed, rows):
    top, rest = packed[:rows], packed[rows:]
    return (
        top[:, :HEAD_DIM],
        top[:, HEAD_DIM:],
        jnp.concatenate([rest[:, :HEAD_DIM], rest[:, HEAD_DIM:]], axis=0),
    )


def to_rows(src_of, dst, send, recv, ranks):
    r, c = place()
    copies = []
    for m in range(1, ranks):
        there = flip(r, m)
        copies.append(send_to(src_of(there), dst.at[r], send.at[m - 1], recv.at[m - 1], (there, c)))
    return copies


def to_cols(src_of, dst, send, recv, n):
    r, c = place()
    copies = []
    for k in range(1, n):
        there = (c + k) % n
        copies.append(send_to(src_of(there), dst.at[c], send.at[k - 1], recv.at[k - 1], (r, there)))
    return copies


def all_sum(ref, count):
    total = ref[0].astype(F32)
    for i in range(1, count):
        total = total + ref[i].astype(F32)
    return total


def send_weight_grads(first, count, gown, sib, hin, lbuf, hbuf, load_sem, send, recv):
    r, c = place()
    chip = r // 2

    def loads(i):
        at = lax.rem(i, 2)
        return [
            pltpu.make_async_copy(ref.at[first + i], lbuf.at[at, j], load_sem.at[at, j])
            for j, ref in enumerate((gown, sib))
        ]

    def sends(i):
        return [
            send_to(
                hbuf.at[i, :, flip(chip, k)],
                hin.at[i, k - 1],
                send.at[i, k - 1],
                recv.at[i, k - 1],
                (flip(r, 2 * k), c),
            )
            for k in range(1, 4)
        ]

    for copy in loads(0):
        copy.start()

    def body(i, carry):
        @pl.when(i + 1 < count)
        def _():
            for copy in loads(i + 1):
                copy.start()

        for copy in loads(i):
            copy.wait()
        at = lax.rem(i, 2)
        hbuf[i] = (lbuf[at, 0].astype(F32) + lbuf[at, 1].astype(F32)).astype(BF)
        for copy in sends(i):
            copy.start()
        return carry

    lax.fori_loop(0, count, body, 0)

    def finish():
        def wait(i, carry):
            for copy in sends(i):
                copy.wait()
            return carry

        lax.fori_loop(0, count, wait, 0)

    return finish


def weight_scratch(count, block):
    three, chips, depth, ff = block
    return [
        pltpu.VMEM((2, 2, three, chips, depth, ff), BF),
        pltpu.VMEM((count, three, chips, depth, ff), BF),
        pltpu.SemaphoreType.DMA((2, 2)),
        pltpu.SemaphoreType.DMA((count, 3)),
        pltpu.SemaphoreType.DMA((count, 3)),
    ]


def resid_kernel(
    cols,
    count,
    gt_ref,
    dots_ref,
    mixsum_ref,
    n2_ref,
    middle_ref,
    cot_ref,
    routes_ref,
    prev_ref,
    rw_ref,
    carry_ref,
    gain_ref,
    out_t_ref,
    mixed_ref,
    valid_ref,
    gown_ref,
    sib_ref,
    layer_ref,
    resid_ref,
    gm_ref,
    og_ref,
    small_ref,
    pg_ref,
    hin_ref,
    out,
    arrived,
    send,
    recv,
    dots_in,
    dsend,
    drecv,
    grad,
    gm_out,
    gsend,
    grecv,
    gm_sem,
    *weight_refs,
):
    r, c = place()
    local = n2_ref.shape[0]
    greet(col_peers(cols) + [(flip(r, 2 * k), c) for k in range(1, 4)])
    slot, total, drain = reduce_chain(lambda d: gt_ref[d], out, arrived, send, recv, cols)

    def dots_of(d):
        return dots_ref.at[:, pl.ds(pl.multiple_of(d * local, LANES), local)]

    dot_copies = to_cols(dots_of, dots_in, dsend, drecv, cols)
    for copy in dot_copies:
        copy.start()
    dots_in[c] = dots_of(c)[...]
    slot(0)
    finish = send_weight_grads(0, count, gown_ref, sib_ref, hin_ref, *weight_refs)
    slot(1)

    n2, cot = n2_ref[...], cot_ref[...]
    n2f, cotf = n2.astype(F32), cot.astype(F32)
    middle = middle_ref[...]
    rw = rw_ref[...]
    lin = mm(n2, rw, NT)
    prev = prev_ref[...]
    gates = gate_lanes(lin + mm(prev, carry_ref[...], TN), routes_ref[...])
    lane = lane_iota((local, LANES))
    cot_lin = mm(cot, rw, NT)
    dot_keep = jnp.sum(cotf * n2f, axis=1, keepdims=True)
    for copy in dot_copies:
        copy.wait()
    d = jnp.concatenate([all_sum(dots_in, cols), jnp.zeros((LANES - EXPERTS, local), F32)], axis=0).T
    g_gates = jnp.where(lane == EXPERTS + 1, dot_keep, d)
    keep = gates[:, EXPERTS + 1 : EXPERTS + 2]
    mixes, packs = [], jnp.zeros((local, LANES), F32)
    for j in range(2):
        l0 = lin[:, ROW_CONST + 2 * j : ROW_CONST + 2 * j + 1]
        l1 = lin[:, ROW_CONST + 2 * j + 1 : ROW_CONST + 2 * j + 2]
        top = jnp.maximum(l0, l1)
        e0, e1 = jnp.exp(l0 - top), jnp.exp(l1 - top)
        a0, a1 = e0 / (e0 + e1), e1 / (e0 + e1)
        share = gates[:, EXPERTS + 2 + j : EXPERTS + 3 + j]
        dot_vec = cot_lin[:, ROW_VEC + j : ROW_VEC + j + 1]
        keep = keep + share * a0
        mixes.append(share * a1)
        g_gates = jnp.where(lane == EXPERTS + 2 + j, a0 * dot_keep + a1 * dot_vec, g_gates)
        gk, gv = share * dot_keep, share * dot_vec
        mean = a0 * gk + a1 * gv
        packs = packs + jnp.where(lane == ROW_CONST + 2 * j, a0 * (gk - mean), 0.0)
        packs = packs + jnp.where(lane == ROW_CONST + 2 * j + 1, a1 * (gv - mean), 0.0)
        packs = packs + jnp.where(lane == ROW_VEC + j, share * a1, 0.0)
    packs = packs + gates * (g_gates - jnp.sum(gates * g_gates, axis=1, keepdims=True))
    vec = rw[ROW_VEC : ROW_VEC + 2].astype(F32)
    layer = middle + mixsum_ref[...] + keep * n2f + mixes[0] * vec[0:1] + mixes[1] * vec[1:2]
    layer_ref[...] = layer.astype(BF)

    high = packs.astype(BF)
    low = (packs - high.astype(F32)).astype(BF)
    back = lane < ROW_VEC
    high_b = jnp.where(back, packs, 0.0).astype(BF)
    low_b = jnp.where(back, packs - high.astype(F32), 0.0).astype(BF)
    grad_local = keep * cotf + mm(high_b, rw) + mm(low_b, rw)
    by_n2 = mm(high, n2, TN) + mm(low, n2, TN)
    by_cot = mm(high, cot, TN) + mm(low, cot, TN)
    by_prev = mm(prev, high) + mm(prev, low)
    pg = mm(carry_ref[...], high_b, NT) + mm(carry_ref[...], low_b, NT)
    pg_ref[...] = pg[:ROUTES]
    sub = lax.broadcasted_iota(jnp.int32, (SMALL_ROWS, D), 0)
    small_ref[:, :D] = jnp.where(sub < ROW_VEC, by_n2[:SMALL_ROWS], by_cot[:SMALL_ROWS])
    small_ref[:16, D:] = by_prev
    small_ref[16:, D:] = jnp.zeros((SMALL_ROWS - 16, LANES), F32)

    for s in range(2, cols):
        slot(s)
    total(grad)
    grad_normed = grad[...] + grad_local
    scale = norm_rows(middle)
    gained = grad_normed * gain_ref[...]
    mid_dot = jnp.sum(gained * middle, axis=1, keepdims=True)
    resid = cotf + scale * gained - middle * (scale * scale * scale * (mid_dot * (1.0 / D)))
    resid_ref[...] = resid
    cut = resid.astype(BF)
    gm = (mm(cut, out_t_ref[...]) * valid_ref[...]).astype(BF)
    width = D // cols
    for i in range(cols):
        pack_heads(gm_out.at[i], gm[:, i * width : (i + 1) * width])
    gm_copies = to_cols(lambda i: gm_out.at[i], gm_ref, gsend, grecv, cols)
    for copy in gm_copies:
        copy.start()
    keep_own = pltpu.make_async_copy(gm_out.at[c], gm_ref.at[c], gm_sem.at[0])
    keep_own.start()
    small_ref[ROW_GAIN : ROW_GAIN + 1, :D] = jnp.sum(grad_normed * middle * scale, axis=0, keepdims=True)
    og_ref[...] = mm(cut, mixed_ref[...], TN).astype(BF)
    keep_own.wait()
    for copy in gm_copies:
        copy.wait()
    drain()
    finish()


def resid_step(cols, count, gt, dots, mixsum, n2, middle, cot, routes, prev, rw, carry, gain, out_t, mixed, valid, gown, sib):
    local = n2.shape[0]
    experts, three, chips, depth, ff = gown.shape
    vm = pl.BlockSpec(memory_space=pltpu.VMEM)
    return pl.pallas_call(
        functools.partial(resid_kernel, cols, count),
        out_shape=(
            jax.ShapeDtypeStruct((local, D), BF),
            jax.ShapeDtypeStruct((local, D), F32),
            jax.ShapeDtypeStruct((cols, local * 3 // 2, LANES), BF),
            jax.ShapeDtypeStruct((D, D), BF),
            jax.ShapeDtypeStruct((SMALL_ROWS, D + LANES), F32),
            jax.ShapeDtypeStruct((ROUTES, local), F32),
            jax.ShapeDtypeStruct((count, 3, three, depth, ff), BF),
        ),
        in_specs=[vm] * 14 + [ANY, ANY],
        out_specs=(vm, vm, ANY, vm, vm, vm, ANY),
        scratch_shapes=[
            *chain_scratch(cols, local),
            pltpu.VMEM((cols, EXPERTS, local), F32),
            pltpu.SemaphoreType.DMA((cols - 1,)),
            pltpu.SemaphoreType.DMA((cols - 1,)),
            pltpu.VMEM((local, D), F32),
            pltpu.VMEM((cols, local * 3 // 2, LANES), BF),
            pltpu.SemaphoreType.DMA((cols - 1,)),
            pltpu.SemaphoreType.DMA((cols - 1,)),
            pltpu.SemaphoreType.DMA((1,)),
            *weight_scratch(count, (three, chips, depth, ff)),
        ],
        compiler_params=pltpu.CompilerParams(
            vmem_limit_bytes=60 * MIB, collective_id=3, has_side_effects=True
        ),
        cost_estimate=pl.CostEstimate(flops=6 * local * D * D, bytes_accessed=40 * MIB, transcendentals=0),
        name="resid_step",
    )(gt, dots, mixsum, n2, middle, cot, routes, prev, rw, carry, gain, out_t, mixed, valid, gown, sib)


def finish_kernel(
    cols,
    ranks,
    first,
    count,
    gm_ref,
    qkv_ref,
    begin_ref,
    o_ref,
    lse_ref,
    x_ref,
    gain_ref,
    w_ref,
    cos_ref,
    sin_ref,
    small_ref,
    og_ref,
    resid_ref,
    xown_ref,
    gown_ref,
    sib_ref,
    ig_ref,
    small_out,
    gain_out,
    qg_out,
    og_out,
    hin_ref,
    do_s,
    dq_s,
    dk_s,
    dv_s,
    gn_s,
    qg_acc,
    qg_cut,
    out,
    arrived,
    send,
    recv,
    small_rows,
    small_cols,
    og_rows,
    og_parts,
    og_cols,
    gain_rows,
    gain_cols,
    qg_rows,
    q_parts,
    q_land,
    total_s,
    row_send,
    row_recv,
    col_send,
    col_recv,
    *weight_refs,
):
    r, c = place()
    heads = 3
    rows = x_ref.shape[0]
    local = rows // cols
    depth = D // ranks
    width = heads * HEAD_DIM
    score_scale = 1.0 / math.sqrt(HEAD_DIM)
    greet(col_peers(cols) + [(flip(r, m), c) for m in range(1, ranks)])

    def rows_of(ref, d):
        return ref.at[pl.ds(pl.multiple_of(d * depth, 16), depth)]

    small_to_rows = to_rows(lambda d: small_ref, small_rows, row_send.at[0], row_recv.at[0], ranks)
    og_to_rows = to_rows(lambda d: rows_of(og_ref, d), og_rows, row_send.at[1], row_recv.at[1], ranks)
    for copy in small_to_rows + og_to_rows:
        copy.start()
    small_rows[r] = small_ref[...]
    og_rows[r] = rows_of(og_ref, r)[...]
    finish = send_weight_grads(first, count, gown_ref, sib_ref, hin_ref, *weight_refs)

    for d in range(cols):
        at = slice(d * local, (d + 1) * local)
        for h, value in enumerate(unpack_heads(gm_ref[d], local)):
            do_s[h, at] = value

    blocks = rows // Q_ROWS

    def one_head(h, carry):
        for i in reversed(range(blocks)):
            at = slice(i * Q_ROWS, (i + 1) * Q_ROWS)
            length = (i + 1) * Q_ROWS
            q, do = qkv_ref[h, at], do_s[h, at]
            k, v = qkv_ref[heads + h, :length], qkv_ref[2 * heads + h, :length]
            delta = jnp.sum(do.astype(F32) * o_ref[h, at].astype(F32), axis=1, keepdims=True)
            s = mm(q, k, NT)
            ok = seen(begin_ref[at], i * Q_ROWS, Q_ROWS, length)
            p = jnp.where(ok, jnp.exp(s - lse_ref[h, at]), 0.0)
            ds = (p * (mm(do, v, NT) - delta)).astype(BF)
            dq_s[h, at] = mm(ds, k) * score_scale
            dk, dv = mm(ds, q, TN), mm(p.astype(BF), do, TN)
            if i == blocks - 1:
                dk_s[h], dv_s[h] = dk, dv
            else:
                dk_s[h, :length] += dk
                dv_s[h, :length] += dv
        return carry

    lax.fori_loop(0, 2, one_head, 0)
    for copy in small_to_rows + og_to_rows:
        copy.wait()
    small_cols[c] = all_sum(small_rows, ranks)
    og_sum = all_sum(og_rows, ranks)
    for i in range(cols):
        og_parts[i] = og_sum[:, i * width : (i + 1) * width]
    small_to_cols = to_cols(lambda d: small_cols.at[c], small_cols, col_send.at[0], col_recv.at[0], cols)
    og_to_cols = to_cols(lambda d: og_parts.at[d], og_cols, col_send.at[1], col_recv.at[1], cols)
    for copy in small_to_cols + og_to_cols:
        copy.start()
    og_cols[c] = og_parts[c]
    lax.fori_loop(2, 3, one_head, 0)

    slot, total, drain = reduce_chain(lambda d: gn_s[d], out, arrived, send, recv, cols)
    gain_total = jnp.zeros((1, D), F32)
    weight = w_ref[...]
    for n, d in enumerate((3, 0, 2, 1)):
        at = slice(d * local, (d + 1) * local)
        cosine, sines = cos_ref[at], sin_ref[at]
        turned = [dq_s[h, at] for h in range(heads)] + [dk_s[h, at] for h in range(heads)]
        parts = []
        for part in range(heads):
            v = jnp.concatenate(turned[2 * part : 2 * part + 2], axis=1)
            parts.append((v * cosine - swap_pairs(v) * sines).astype(BF))
        parts += [dv_s[h, at].astype(BF) for h in range(heads)]
        gp = jnp.concatenate(parts, axis=1)
        x = x_ref[at].astype(F32)
        xs = x * norm_rows(x)
        gn = mm(gp, weight, NT)
        gn_s[d] = gn.astype(BF)
        gain_total = gain_total + jnp.sum(gn * xs, axis=0, keepdims=True)
        grad = mm((xs * gain_ref[...]).astype(BF), gp, TN)
        if n == 0:
            qg_acc[...] = grad
        else:
            qg_acc[...] += grad
        if n == 1:
            slot(0)
        if n == 3:
            slot(1)
    qg_cut[...] = qg_acc[...].astype(BF)
    gain_rows[r] = jnp.broadcast_to(gain_total, (8, D))
    qg_to_rows = to_rows(lambda d: rows_of(qg_cut, d), qg_rows, row_send.at[2], row_recv.at[2], ranks)
    gain_to_rows = to_rows(lambda d: gain_rows.at[r], gain_rows, row_send.at[3], row_recv.at[3], ranks)
    for copy in gain_to_rows + qg_to_rows:
        copy.start()
    qg_rows[r] = rows_of(qg_cut, r)[...]
    for s in range(2, cols - 1):
        slot(s)
    for copy in gain_to_rows + qg_to_rows:
        copy.wait()
    gain_cols[c] = all_sum(gain_rows, ranks)
    q_sum = all_sum(qg_rows, ranks)
    for i in range(3):
        q_parts[i] = q_sum[:, i * width : (i + 1) * width]
    gain_to_cols = to_cols(lambda d: gain_cols.at[c], gain_cols, col_send.at[2], col_recv.at[2], cols)
    odd, high = c % 2, c // 2
    q_copies = [
        send_to(
            q_parts.at[1 - odd + high],
            q_land.at[1],
            col_send.at[3, 0],
            col_recv.at[3, 0],
            (r, flip(c, 1)),
        ),
        send_to(
            q_parts.at[2 - 2 * high],
            q_land.at[2 - 2 * odd],
            col_send.at[3, 1],
            col_recv.at[3, 1],
            (r, flip(c, 2)),
        ),
    ]
    for copy in gain_to_cols + q_copies:
        copy.start()
    q_land[2 * odd] = q_parts[(c + 1) // 2]
    slot(cols - 1)
    total(total_s)
    gn = total_s[...]
    x = xown_ref[...].astype(F32)
    scale = norm_rows(x)
    gained = gn * gain_ref[...]
    x_dot = jnp.sum(gained * x, axis=1, keepdims=True)
    ig_ref[...] = resid_ref[...] + scale * gained - x * (scale * scale * scale * (x_dot * (1.0 / D)))
    for copy in small_to_cols + og_to_cols + gain_to_cols + q_copies:
        copy.wait()
    small_out[...] = all_sum(small_cols, cols)
    og_out[...] = all_sum(og_cols, cols)
    gain_out[...] = all_sum(gain_cols, cols)
    qg_out[...] = q_land[...]
    drain()
    finish()


def finish_step(cols, ranks, first, gm, qkv, begin, o, lse, x, gain, w, cosine, sines, small, og, resid, xown, gown, sib):
    rows = x.shape[0]
    local = rows // cols
    experts, three, chips, depth, ff = gown.shape
    count = experts - first
    heads, width = 3, 3 * HEAD_DIM
    vm = pl.BlockSpec(memory_space=pltpu.VMEM)
    wide = D + LANES
    return pl.pallas_call(
        functools.partial(finish_kernel, cols, ranks, first, count),
        out_shape=(
            jax.ShapeDtypeStruct((local, D), F32),
            jax.ShapeDtypeStruct((SMALL_ROWS, wide), F32),
            jax.ShapeDtypeStruct((8, D), F32),
            jax.ShapeDtypeStruct((3, depth, width), F32),
            jax.ShapeDtypeStruct((depth, width), F32),
            jax.ShapeDtypeStruct((count, 3, three, depth, ff), BF),
        ),
        in_specs=[vm] * 14 + [ANY, ANY],
        out_specs=(vm, vm, vm, vm, vm, ANY),
        scratch_shapes=[
            pltpu.VMEM((heads, rows, HEAD_DIM), BF),
            pltpu.VMEM((heads, rows, HEAD_DIM), F32),
            pltpu.VMEM((heads, rows, HEAD_DIM), F32),
            pltpu.VMEM((heads, rows, HEAD_DIM), F32),
            pltpu.VMEM((cols, local, D), BF),
            pltpu.VMEM((D, 3 * width), F32),
            pltpu.VMEM((D, 3 * width), BF),
            *chain_scratch(cols, local),
            pltpu.VMEM((ranks, SMALL_ROWS, wide), F32),
            pltpu.VMEM((cols, SMALL_ROWS, wide), F32),
            pltpu.VMEM((ranks, depth, D), BF),
            pltpu.VMEM((cols, depth, width), F32),
            pltpu.VMEM((cols, depth, width), F32),
            pltpu.VMEM((ranks, 8, D), F32),
            pltpu.VMEM((cols, 8, D), F32),
            pltpu.VMEM((ranks, depth, 3 * width), BF),
            pltpu.VMEM((3, depth, width), F32),
            pltpu.VMEM((3, depth, width), F32),
            pltpu.VMEM((local, D), F32),
            pltpu.SemaphoreType.DMA((4, ranks - 1)),
            pltpu.SemaphoreType.DMA((4, ranks - 1)),
            pltpu.SemaphoreType.DMA((4, cols - 1)),
            pltpu.SemaphoreType.DMA((4, cols - 1)),
            *weight_scratch(count, (three, chips, depth, ff)),
        ],
        compiler_params=pltpu.CompilerParams(
            vmem_limit_bytes=62 * MIB, collective_id=4, has_side_effects=True
        ),
        cost_estimate=pl.CostEstimate(
            flops=20 * heads * rows * rows * HEAD_DIM, bytes_accessed=40 * MIB, transcendentals=heads * rows * rows
        ),
        name="finish_step",
    )(gm, qkv, begin, o, lse, x, gain, w, cosine, sines, small, og, resid, xown, gown, sib)


SENT_FIRST = 5


def on_device_heads(
    sizes,
    inputs,
    attn_gain,
    qkv_weight,
    out_weight,
    ffn_gain,
    router_weight,
    carry_weight,
    const_weight,
    const_vector,
    gate_weight,
    up_weight,
    down_weight,
    prev_logits,
    seq_lengths,
    expert_routes,
    cotangent,
):
    ranks, cols = sizes
    heads = HEADS // cols
    width = heads * HEAD_DIM
    row_index, col_index = lax.axis_index("row"), lax.axis_index("col")
    row_total = expert_routes.shape[0]
    local_rows = inputs.shape[0]
    first_row = col_index * local_rows

    def own_rows(value):
        return lax.dynamic_slice_in_dim(value, first_row, local_rows, 0)

    w_stack = jnp.stack([gate_weight, up_weight, down_weight.transpose(0, 2, 1)])
    w_all = lax.all_gather(w_stack, "row", axis=0)

    lengths = seq_lengths[0]
    ends = jnp.cumsum(lengths)
    starts = ends - lengths
    spot = jnp.arange(row_total, dtype=jnp.int32)
    seq_index = jnp.sum((spot[:, None] >= ends[None, :]).astype(jnp.int32), axis=1)
    member = seq_index[:, None] == jnp.arange(lengths.shape[0], dtype=jnp.int32)[None, :]
    begin = jnp.sum(jnp.where(member, starts[None, :], 0), axis=1)
    is_valid = seq_index < lengths.shape[0]
    positions = spot - begin
    valid = is_valid.astype(F32)[:, None]
    seq_begin = jnp.where(is_valid, begin, ends[-1])[:, None]
    pair = jnp.arange(HEAD_DIM // 2, dtype=jnp.int32)
    frequency = jnp.exp(-((2 * pair).astype(F32) / HEAD_DIM) * math.log(BASE))
    angles = positions.astype(F32)[:, None] * frequency[None, :]
    cosine, sines = jnp.cos(angles), jnp.sin(angles)
    cosine = jnp.tile(jnp.repeat(cosine, 2, axis=1), (1, LANES // HEAD_DIM))
    sines = jnp.tile(
        jnp.stack([-sines, sines], axis=2).reshape(row_total, HEAD_DIM), (1, LANES // HEAD_DIM)
    )

    hit = jnp.any(
        expert_routes[:, :, None] == jnp.arange(EXPERTS, dtype=jnp.int32)[None, None, :], axis=1
    ).astype(jnp.int32)
    slots = jnp.where(hit > 0, jnp.cumsum(hit, axis=0) - 1, -1)
    slots_t = slots.T[:, None, :]

    rw = jnp.concatenate(
        [
            router_weight.T,
            const_weight.transpose(0, 2, 1).reshape(4, D),
            const_vector,
            jnp.zeros((LANES - ROW_GAIN, D), BF),
        ],
        axis=0,
    )
    carry = jnp.pad(carry_weight, ((0, 16 - ROUTES), (0, LANES - ROUTES)))
    prev = jnp.pad(prev_logits, ((0, 16 - ROUTES), (0, 0)))
    attn_gain_row = attn_gain.astype(F32)[None, :]
    ffn_gain_row = ffn_gain.astype(F32)[None, :]

    w_cat = jnp.concatenate([out_weight.T, qkv_weight], axis=1)
    w_cols = lax.all_gather(w_cat, "col", axis=0, tiled=False)
    depth = qkv_weight.shape[0]
    blocks = w_cols[:, :, width:].reshape(cols, depth, 3, width).transpose(0, 2, 1, 3)
    blocks = blocks.reshape(3, cols, depth, width)
    own = lax.dynamic_index_in_dim(blocks, col_index, 1, keepdims=False)
    w_own = jnp.concatenate([own[0], own[1], own[2]], axis=1)
    out_rows = w_cols[:, :, :width].transpose(1, 0, 2).reshape(depth, D)
    w_full = lax.all_gather(jnp.concatenate([out_rows, w_own], axis=1), "row", axis=0, tiled=True)
    out_t, qkv_own = w_full[:, :D], w_full[:, D:]
    whole_in = lax.all_gather(inputs, "col", axis=0, tiled=True)
    prev_whole = lax.all_gather(prev, "col", axis=0)
    qkv = project_heads(heads, whole_in, attn_gain_row, qkv_own, cosine, sines)
    mixed_heads, lse = attend(heads, qkv, seq_begin, valid)
    to_send = mixed_heads.transpose(1, 0, 2).reshape(cols, local_rows, width)
    attn_parts = lax.all_to_all(to_send, "col", split_axis=0, concat_axis=0, tiled=True)
    mixed, middle, n2 = branch(attn_parts, out_t, inputs, ffn_gain_row)
    n2_whole = lax.all_gather(n2, "col", axis=0, tiled=True)
    x, gu, mix, gates, cot_whole = experts_forward(
        cols, n2_whole, prev_whole, cotangent, rw, carry, expert_routes, slots, slots_t, w_all
    )
    gt, dots, mixsum, gown, sib = experts_backward(
        cols, cot_whole.reshape(row_total, D), mix, gates, slots, slots_t, w_all, x, gu
    )
    layer_out, resid, gm, og, small, prev_grad, hin0 = resid_step(
        cols,
        SENT_FIRST,
        gt,
        dots,
        mixsum,
        n2,
        middle,
        cotangent,
        own_rows(expert_routes),
        prev,
        rw,
        carry,
        ffn_gain_row,
        out_t,
        mixed,
        own_rows(valid),
        gown,
        sib,
    )
    input_grad, small_all, gain_all, qg, og_own, hin1 = finish_step(
        cols,
        ranks,
        SENT_FIRST,
        gm,
        qkv,
        seq_begin,
        mixed_heads,
        lse,
        whole_in,
        attn_gain_row,
        qkv_own,
        cosine,
        sines,
        small,
        og,
        resid,
        inputs,
        gown,
        sib,
    )
    chip = row_index // 2
    grads = lax.dynamic_index_in_dim(gown, chip, 2, keepdims=False).astype(F32)
    grads = grads + lax.dynamic_index_in_dim(sib, chip, 2, keepdims=False).astype(F32)
    hin = jnp.concatenate([hin0, hin1], axis=0)
    grads = grads + jnp.sum(hin.astype(F32), axis=1)
    depth = qkv_weight.shape[0]
    return (
        layer_out,
        input_grad,
        gain_all[0],
        qg.transpose(1, 0, 2).reshape(depth, 3 * width),
        og_own.T,
        small_all[ROW_GAIN, :D],
        small_all[:ROUTES, :D].T,
        small_all[:ROUTES, D : D + ROUTES],
        small_all[ROW_CONST:ROW_VEC, :D].reshape(2, 2, D).transpose(0, 2, 1),
        small_all[ROW_VEC:ROW_GAIN, :D],
        grads[:, 0],
        grads[:, 1],
        grads[:, 2].transpose(0, 2, 1),
        prev_grad,
    )


def solution(mesh):
    sizes = (mesh.shape["row"], mesh.shape["col"])
    body = functools.partial(on_device_heads, sizes) if sizes == (8, 4) else on_device
    placed = (
        P(("row", "col"), None),
        P(),
        P("row", "col"),
        P("col", "row"),
        P(),
        P(),
        P(),
        P(),
        P(),
        P(None, "row", "col"),
        P(None, "row", "col"),
        P(None, "col", "row"),
        P(None, ("row", "col")),
        P("row", None),
        P("row", None),
        P(("row", "col"), None),
    )
    return jax.shard_map(
        body,
        mesh=mesh,
        in_specs=placed,
        out_specs=(
            P(("row", "col"), None),
            P(("row", "col"), None),
            P(),
            P("row", "col"),
            P("col", "row"),
            P(),
            P(),
            P(),
            P(),
            P(),
            P(None, "row", "col"),
            P(None, "row", "col"),
            P(None, "col", "row"),
            P(None, ("row", "col")),
        ),
        check_vma=False,
    )
```

```python
import functools
import math

import jax
import jax.numpy as jnp
import numpy as np
from jax import lax
from jax.experimental import pallas as pl
from jax.experimental.pallas import tpu as pltpu
from jax.sharding import PartitionSpec as P

D = 768
HEADS = 12
HEAD_DIM = 64
EXPERTS = 8
ROUTES = 12


EPS = 1e-06
BASE = 10000.0
NEG = -1e30
HIGH = lax.Precision.HIGHEST
CONTRACT_FIRST = (((0,), (0,)), ((), ()))
CONTRACT_LAST = (((1,), (1,)), ((), ()))


def rotate(block_value, positions, first_col, direction):
    row_count, col_count = block_value.shape
    column = first_col + jnp.arange(0, col_count, 2, dtype=jnp.int32)
    inner_col = column % D
    section = column // D
    head_pair = inner_col % HEAD_DIM // 2
    exponent = (2 * head_pair).astype(jnp.float32) / HEAD_DIM
    frequency = jnp.exp(-exponent * math.log(BASE))
    turned_on = (section < 2).astype(jnp.float32)
    angles = positions.astype(jnp.float32)[:, None] * (frequency * turned_on)[None, :]
    cosine = jnp.cos(angles)
    sines = direction * jnp.sin(angles)
    paired = block_value.reshape(row_count, col_count // 2, 2)
    first_part = paired[:, :, 0]
    second_part = paired[:, :, 1]
    rotated = jnp.stack(
        [first_part * cosine - second_part * sines, second_part * cosine + first_part * sines],
        axis=2,
    )
    return rotated.reshape(row_count, col_count)


def sequence_info(lengths_row, row_total):
    seq_count = lengths_row.shape[0]
    ends = jnp.cumsum(lengths_row)
    starts = ends - lengths_row
    token_place = jnp.arange(row_total, dtype=jnp.int32)
    seq_index = jnp.sum((token_place[:, None] >= ends[None, :]).astype(jnp.int32), axis=1)
    member = seq_index[:, None] == jnp.arange(seq_count, dtype=jnp.int32)[None, :]
    begin = jnp.sum(jnp.where(member, starts[None, :], 0), axis=1)
    return (seq_index, token_place - begin, seq_index < seq_count)


def partial_sums(term_value):
    return lax.psum_scatter(
        term_value.astype(jnp.bfloat16), "col", scatter_dimension=0, tiled=True
    ).astype(jnp.float32)


def whole_columns(part_value):
    return lax.all_gather(part_value, "col", axis=0, tiled=True)


def to_heads(block_value):
    return lax.all_to_all(block_value, "col", split_axis=0, concat_axis=1, tiled=True)


def to_features(block_value):
    return lax.all_to_all(block_value, "col", split_axis=1, concat_axis=0, tiled=True)


def key_scores(query_heads, key_block, query_seq, query_place, key_seq, key_place, score_scale):
    raw_scores = (
        jnp.einsum("qhd,khd->hqk", query_heads, key_block, preferred_element_type=jnp.float32)
        * score_scale
    )
    allowed = (query_seq[:, None] == key_seq[None, :]) & (
        key_place[None, :] <= query_place[:, None]
    )
    return (jnp.where(allowed[None], raw_scores, NEG), allowed)


def split_keys(key_values, seq_index, token_place, block_rows):
    count_blocks = key_values.shape[0] // block_rows
    blocks_kv = key_values.reshape(count_blocks, block_rows, 2, HEADS, HEAD_DIM)
    return (
        blocks_kv,
        seq_index.reshape(count_blocks, block_rows),
        token_place.reshape(count_blocks, block_rows),
    )


def attend_forward(
    queries, key_values, query_seq, query_place, seq_index, token_place, block_rows, score_scale
):
    local_rows = queries.shape[0]
    query_heads = queries.reshape(local_rows, HEADS, HEAD_DIM)
    key_items = split_keys(key_values, seq_index, token_place, block_rows)

    def max_step(running, block_items):
        running_max, running_sum = running
        kv_block, key_seq, key_place = block_items
        scores, allowed = key_scores(
            query_heads, kv_block[:, 0], query_seq, query_place, key_seq, key_place, score_scale
        )
        new_max = jnp.maximum(running_max, jnp.max(scores, axis=2))
        shifted = jnp.where(allowed[None], jnp.exp(scores - new_max[:, :, None]), 0.0)
        new_sum = running_sum * jnp.exp(running_max - new_max) + jnp.sum(shifted, axis=2)
        return ((new_max, new_sum), None)

    start_state = (
        jnp.full((HEADS, local_rows), NEG, jnp.float32),
        jnp.zeros((HEADS, local_rows), jnp.float32),
    )
    (final_max, final_sum), unused = lax.scan(max_step, start_state, key_items)
    log_total = final_max + jnp.log(final_sum)

    def out_step(running, block_items):
        kv_block, key_seq, key_place = block_items
        scores, allowed = key_scores(
            query_heads, kv_block[:, 0], query_seq, query_place, key_seq, key_place, score_scale
        )
        probs_low = jnp.exp(scores - log_total[:, :, None]).astype(jnp.bfloat16)
        return (
            running
            + jnp.einsum(
                "hqk,khd->qhd", probs_low, kv_block[:, 1], preferred_element_type=jnp.float32
            ),
            None,
        )

    attended, unused = lax.scan(
        out_step, jnp.zeros((local_rows, HEADS, HEAD_DIM), jnp.float32), key_items
    )
    return (attended.reshape(local_rows, D), log_total)


def attend_backward(
    queries,
    key_values,
    log_total,
    row_delta,
    grad_heads_in,
    query_seq,
    query_place,
    seq_index,
    token_place,
    block_rows,
    score_scale,
):
    local_rows = queries.shape[0]
    query_heads = queries.reshape(local_rows, HEADS, HEAD_DIM)
    grad_heads = grad_heads_in.reshape(local_rows, HEADS, HEAD_DIM)
    key_items = split_keys(key_values, seq_index, token_place, block_rows)

    def grad_step(running, block_items):
        kv_block, key_seq, key_place = block_items
        scores, allowed = key_scores(
            query_heads, kv_block[:, 0], query_seq, query_place, key_seq, key_place, score_scale
        )
        probs_full = jnp.exp(scores - log_total[:, :, None])
        probs_low = probs_full.astype(jnp.bfloat16)
        grad_probs = jnp.einsum(
            "qhd,khd->hqk", grad_heads, kv_block[:, 1], preferred_element_type=jnp.float32
        )
        grad_scores = (probs_full * (grad_probs - row_delta[:, :, None])).astype(jnp.bfloat16)
        new_running = (
            running
            + jnp.einsum(
                "hqk,khd->qhd", grad_scores, kv_block[:, 0], preferred_element_type=jnp.float32
            )
            * score_scale
        )
        grad_keys = (
            jnp.einsum("hqk,qhd->khd", grad_scores, query_heads, preferred_element_type=jnp.float32)
            * score_scale
        )
        grad_values = jnp.einsum(
            "hqk,qhd->khd", probs_low, grad_heads, preferred_element_type=jnp.float32
        )
        return (new_running, jnp.stack([grad_keys, grad_values], axis=1))

    grad_queries, grad_kv = lax.scan(
        grad_step, jnp.zeros((local_rows, HEADS, HEAD_DIM), jnp.float32), key_items
    )
    return (grad_queries.reshape(local_rows, D), grad_kv.reshape(key_values.shape[0], 2 * D))


def on_device(
    inputs,
    attn_gain,
    qkv_weight,
    out_weight,
    ffn_gain,
    router_weight,
    carry_weight,
    const_weight,
    const_vector,
    gate_weight,
    up_weight,
    down_weight,
    prev_logits,
    seq_lengths,
    expert_routes,
    cotangent,
):
    col_index = lax.axis_index("col")
    row_total = expert_routes.shape[0]
    local_rows = inputs.shape[0]
    capacity = row_total // 4
    block_rows = min(row_total, 512)
    score_scale = 1.0 / math.sqrt(HEAD_DIM)
    full_weights = (
        lax.all_gather(qkv_weight, "row", axis=0, tiled=True),
        lax.all_gather(out_weight, "row", axis=1, tiled=True),
        lax.all_gather(gate_weight, "row", axis=1, tiled=True),
        lax.all_gather(up_weight, "row", axis=1, tiled=True),
        lax.all_gather(down_weight, "row", axis=2, tiled=True),
    )
    qkv_full, out_full, gate_full, up_full, down_full = full_weights
    whole_in, whole_cot, whole_prev = (
        lax.all_gather(inputs, "col", axis=0, tiled=True),
        lax.all_gather(cotangent, "col", axis=0, tiled=True),
        lax.all_gather(prev_logits, "col", axis=1, tiled=True),
    )
    seq_index, positions, valid_all = sequence_info(seq_lengths[0], row_total)
    token_place = jnp.arange(row_total, dtype=jnp.int32)
    first_row = col_index * local_rows

    def own_rows(whole_value):
        return lax.dynamic_slice_in_dim(whole_value, first_row, local_rows, 0)

    query_seq = own_rows(seq_index)
    query_place = own_rows(token_place)
    query_pos = own_rows(positions)
    query_valid = own_rows(valid_all).astype(jnp.float32)[:, None]
    input_rows = whole_in.astype(jnp.float32)
    attn_gain_full = attn_gain.astype(jnp.float32)
    scale_attn = lax.rsqrt(jnp.mean(input_rows * input_rows, axis=1, keepdims=True) + EPS)
    normed1 = (input_rows * scale_attn * attn_gain_full).astype(jnp.bfloat16)
    projected = jnp.dot(normed1, qkv_full, preferred_element_type=jnp.float32)
    turned = rotate(projected, positions, col_index * projected.shape[1], 1.0).astype(jnp.bfloat16)
    token_qkv = to_heads(turned)
    queries = token_qkv[:, :D]
    key_values = lax.all_gather(token_qkv[:, D:], "col", axis=0, tiled=True)
    attended, log_total = attend_forward(
        queries, key_values, query_seq, query_place, seq_index, token_place, block_rows, score_scale
    )
    attn_tok = (attended * query_valid).astype(jnp.bfloat16)
    attn_feat = to_features(attn_tok)
    attn_out = partial_sums(jnp.dot(attn_feat, out_full, preferred_element_type=jnp.float32))
    input_local = inputs.astype(jnp.float32)
    middle = input_local + attn_out
    scale_ffn = lax.rsqrt(jnp.mean(middle * middle, axis=1, keepdims=True) + EPS)
    ffn_gain_full = ffn_gain.astype(jnp.float32)
    normed2_local = (middle * scale_ffn * ffn_gain_full).astype(jnp.bfloat16)
    normed2 = whole_columns(normed2_local)
    carry_full = carry_weight.astype(jnp.float32)
    prev_rows = whole_prev.astype(jnp.float32).T
    route_hot = (
        expert_routes[:, :, None] == jnp.arange(ROUTES, dtype=jnp.int32)[None, None, :]
    ).astype(jnp.float32)
    logits = jnp.dot(normed2, router_weight, preferred_element_type=jnp.float32) + jnp.dot(
        prev_rows, carry_full, precision=HIGH
    )
    picked = jnp.sum(route_hot * logits[:, None, :], axis=2)
    gate_values = jax.nn.softmax(picked, axis=1)
    flat_route = expert_routes.reshape(-1)
    route_hits = (flat_route[:, None] == jnp.arange(EXPERTS, dtype=jnp.int32)[None, :]).astype(
        jnp.int32
    )
    slot_index = jnp.sum((jnp.cumsum(route_hits, axis=0) - 1) * route_hits, axis=1)
    dump_slot = EXPERTS * capacity
    target = jnp.where(flat_route < EXPERTS, flat_route * capacity + slot_index, dump_slot)
    slot_owner = (
        jnp.full((dump_slot + 1,), row_total, jnp.int32)
        .at[target]
        .set(jnp.arange(2 * row_total, dtype=jnp.int32) // 2)[:dump_slot]
    )
    slot_gate = (
        jnp.zeros((dump_slot + 1,), jnp.float32)
        .at[target]
        .set(gate_values.reshape(-1))[:dump_slot]
        .reshape(EXPERTS, capacity, 1)
    )
    zero_row = jnp.zeros((1, D), jnp.bfloat16)
    expert_in = jnp.concatenate([normed2, zero_row], axis=0)[slot_owner].reshape(
        EXPERTS, capacity, D
    )
    gate_pre = jnp.einsum("ecd,edf->ecf", expert_in, gate_full, preferred_element_type=jnp.float32)
    up_pre = jnp.einsum("ecd,edf->ecf", expert_in, up_full, preferred_element_type=jnp.float32)
    sigmoid_gate = jax.nn.sigmoid(gate_pre)
    activated = gate_pre * sigmoid_gate
    hidden = (activated * up_pre).astype(jnp.bfloat16)
    expert_out = jnp.einsum("ecf,efd->ecd", hidden, down_full, preferred_element_type=jnp.float32)
    out_rows = jnp.concatenate(
        [expert_out.reshape(dump_slot, D), jnp.zeros((1, D), jnp.float32)], axis=0
    )
    chosen_out = out_rows[target].reshape(row_total, 2, D)
    cot_rows = whole_cot.astype(jnp.float32)
    ffn_mix = jnp.sum(gate_values[:, :, None] * chosen_out, axis=1)
    ffn_dots = jnp.sum(cot_rows[:, None, :] * chosen_out, axis=2)
    mix_local = partial_sums(ffn_mix)
    normed_local = normed2_local.astype(jnp.float32)
    vector_full = const_vector.astype(jnp.float32)
    routes_local = own_rows(expert_routes)
    gates_local = own_rows(gate_values)
    hot_local = own_rows(route_hot)
    copy_hit = (routes_local == EXPERTS + 1).astype(jnp.float32)
    const_hit = (
        routes_local[:, :, None] == (EXPERTS + 2 + jnp.arange(2, dtype=jnp.int32))[None, None, :]
    ).astype(jnp.float32)
    copy_share = jnp.sum(gates_local * copy_hit, axis=1)
    const_share = jnp.sum(gates_local[:, :, None] * const_hit, axis=1)
    const_alpha = jax.nn.softmax(
        jnp.einsum("td,jdk->tjk", normed2_local, const_weight, preferred_element_type=jnp.float32),
        axis=2,
    )
    keep_share = copy_share + jnp.sum(const_share * const_alpha[:, :, 0], axis=1)
    local_mix = keep_share[:, None] * normed_local + jnp.dot(
        const_share * const_alpha[:, :, 1], vector_full, precision=HIGH
    )
    layer_out = (middle + mix_local + local_mix).astype(jnp.bfloat16)
    qkv_full, out_full, gate_full, up_full, down_full = full_weights
    ffn_total = lax.psum(ffn_dots, "col")
    ffn_local = own_rows(ffn_total)
    cot_local = cotangent.astype(jnp.float32)
    dot_keep = jnp.sum(cot_local * normed_local, axis=1)
    dot_vector = jnp.dot(cot_local, vector_full.T, precision=HIGH)
    const_dots = const_alpha[:, :, 0] * dot_keep[:, None] + const_alpha[:, :, 1] * dot_vector
    grad_gates = (
        ffn_local
        + copy_hit * dot_keep[:, None]
        + jnp.sum(const_hit * const_dots[:, None, :], axis=2)
    )
    grad_picked = gates_local * (
        grad_gates - jnp.sum(gates_local * grad_gates, axis=1, keepdims=True)
    )
    grad_logits = jnp.sum(hot_local * grad_picked[:, :, None], axis=1)
    prev_local = prev_logits.astype(jnp.float32).T
    router_grad = lax.dot_general(normed_local, grad_logits, CONTRACT_FIRST, precision=HIGH)
    carry_grad = lax.dot_general(prev_local, grad_logits, CONTRACT_FIRST, precision=HIGH)
    prev_grad = lax.dot_general(carry_full, grad_logits, CONTRACT_LAST, precision=HIGH)
    grad_alpha_keep = const_share * dot_keep[:, None]
    grad_alpha_vector = const_share * dot_vector
    alpha_mean = const_alpha[:, :, 0] * grad_alpha_keep + const_alpha[:, :, 1] * grad_alpha_vector
    grad_alpha_logits = jnp.stack(
        [
            const_alpha[:, :, 0] * (grad_alpha_keep - alpha_mean),
            const_alpha[:, :, 1] * (grad_alpha_vector - alpha_mean),
        ],
        axis=2,
    )
    const_grad = jnp.einsum("td,tjk->jdk", normed_local, grad_alpha_logits, precision=HIGH)
    vector_grad = lax.dot_general(
        const_share * const_alpha[:, :, 1], cot_local, CONTRACT_FIRST, precision=HIGH
    )
    router_full = router_weight.astype(jnp.float32)
    const_full = const_weight.astype(jnp.float32)
    grad_normed_local = (
        keep_share[:, None] * cot_local
        + lax.dot_general(grad_logits, router_full, CONTRACT_LAST, precision=HIGH)
        + jnp.einsum("tjk,jdk->td", grad_alpha_logits, const_full, precision=HIGH)
    )
    cot_in = jnp.concatenate([whole_cot, zero_row], axis=0)[slot_owner].reshape(
        EXPERTS, capacity, D
    )
    grad_expert = (slot_gate * cot_in.astype(jnp.float32)).astype(jnp.bfloat16)
    down_grad = jnp.einsum("ecf,ecd->efd", hidden, grad_expert, preferred_element_type=jnp.float32)
    grad_hidden = jnp.einsum(
        "ecd,efd->ecf", grad_expert, down_full, preferred_element_type=jnp.float32
    )
    grad_gate_pre = (
        grad_hidden * up_pre * sigmoid_gate * (1.0 + gate_pre * (1.0 - sigmoid_gate))
    ).astype(jnp.bfloat16)
    grad_up_pre = (grad_hidden * activated).astype(jnp.bfloat16)
    gate_grad = jnp.einsum(
        "ecd,ecf->edf", expert_in, grad_gate_pre, preferred_element_type=jnp.float32
    )
    up_grad = jnp.einsum("ecd,ecf->edf", expert_in, grad_up_pre, preferred_element_type=jnp.float32)
    grad_expert_in = jnp.einsum(
        "ecf,edf->ecd", grad_gate_pre, gate_full, preferred_element_type=jnp.float32
    ) + jnp.einsum("ecf,edf->ecd", grad_up_pre, up_full, preferred_element_type=jnp.float32)
    grad_slots = jnp.concatenate(
        [grad_expert_in.reshape(dump_slot, D), jnp.zeros((1, D), jnp.float32)], axis=0
    )
    grad_tokens = jnp.sum(grad_slots[target].reshape(row_total, 2, D), axis=1)
    grad_normed = partial_sums(grad_tokens) + grad_normed_local
    gained_ffn = grad_normed * ffn_gain_full
    ffn_dots_rows = jnp.sum(gained_ffn * middle, axis=1, keepdims=True)
    grad_middle = scale_ffn * gained_ffn - middle * scale_ffn**3 * (ffn_dots_rows / D)
    ffn_gain_grad = jnp.sum(grad_normed * middle * scale_ffn, axis=0)
    grad_resid = cot_local + grad_middle
    branch_cot = whole_columns(grad_resid.astype(jnp.bfloat16))
    out_grad = lax.dot_general(
        attn_feat, branch_cot, CONTRACT_FIRST, preferred_element_type=jnp.float32
    )
    grad_mixed = lax.dot_general(
        branch_cot, out_full, CONTRACT_LAST, preferred_element_type=jnp.float32
    )
    grad_tok = to_heads(grad_mixed.astype(jnp.bfloat16))
    grad_heads_in = (grad_tok.astype(jnp.float32) * query_valid).astype(jnp.bfloat16)
    row_delta = jnp.sum(
        grad_heads_in.astype(jnp.float32).reshape(local_rows, HEADS, HEAD_DIM)
        * attended.reshape(local_rows, HEADS, HEAD_DIM),
        axis=2,
    ).T
    grad_queries, grad_kv = attend_backward(
        queries,
        key_values,
        log_total,
        row_delta,
        grad_heads_in,
        query_seq,
        query_place,
        seq_index,
        token_place,
        block_rows,
        score_scale,
    )
    grad_kv_local = lax.psum_scatter(
        grad_kv.astype(jnp.bfloat16), "col", scatter_dimension=0, tiled=True
    ).astype(jnp.float32)
    grad_turned = jnp.concatenate([grad_queries, grad_kv_local], axis=1)
    grad_proj_tok = rotate(grad_turned, query_pos, 0, -1.0).astype(jnp.bfloat16)
    grad_projected = to_features(grad_proj_tok)
    qkv_grad = lax.dot_general(
        normed1, grad_projected, CONTRACT_FIRST, preferred_element_type=jnp.float32
    )
    grad_normed1 = partial_sums(
        lax.dot_general(grad_projected, qkv_full, CONTRACT_LAST, preferred_element_type=jnp.float32)
    )
    scale_attn_local = own_rows(scale_attn)
    gained_attn = grad_normed1 * attn_gain_full
    attn_dots_rows = jnp.sum(gained_attn * input_local, axis=1, keepdims=True)
    input_grad = (
        grad_resid
        + scale_attn_local * gained_attn
        - input_local * scale_attn_local**3 * (attn_dots_rows / D)
    )
    attn_gain_grad = jnp.sum(grad_normed1 * input_local * scale_attn_local, axis=0)
    qkv_grad, out_grad, gate_grad, up_grad, down_grad = (
        lax.psum_scatter(
            qkv_grad.astype(jnp.bfloat16), "row", scatter_dimension=0, tiled=True
        ).astype(jnp.float32),
        lax.psum_scatter(
            out_grad.astype(jnp.bfloat16), "row", scatter_dimension=1, tiled=True
        ).astype(jnp.float32),
        lax.psum_scatter(
            gate_grad.astype(jnp.bfloat16), "row", scatter_dimension=1, tiled=True
        ).astype(jnp.float32),
        lax.psum_scatter(
            up_grad.astype(jnp.bfloat16), "row", scatter_dimension=1, tiled=True
        ).astype(jnp.float32),
        lax.psum_scatter(
            down_grad.astype(jnp.bfloat16), "row", scatter_dimension=2, tiled=True
        ).astype(jnp.float32),
    )
    attn_gain_grad, ffn_gain_grad, router_grad, carry_grad, const_grad, vector_grad = lax.psum(
        (attn_gain_grad, ffn_gain_grad, router_grad, carry_grad, const_grad, vector_grad),
        ("row", "col"),
    )
    return (
        layer_out,
        input_grad,
        attn_gain_grad,
        qkv_grad,
        out_grad,
        ffn_gain_grad,
        router_grad,
        carry_grad,
        const_grad,
        vector_grad,
        gate_grad,
        up_grad,
        down_grad,
        prev_grad,
    )


BF = jnp.bfloat16
F32 = jnp.float32
LANES = 128
NN = (((1,), (0,)), ((), ()))
NT = (((1,), (1,)), ((), ()))
TN = (((0,), (0,)), ((), ()))
ROW_CONST = 12
ROW_VEC = 16
ROW_GAIN = 18
SMALL_ROWS = 24
Q_ROWS = 256
MIB = 1 << 20


def mm(a, b, dims=NN):
    return lax.dot_general(a, b, dims, preferred_element_type=F32)


def lane_iota(shape):
    return lax.broadcasted_iota(jnp.int32, shape, len(shape) - 1)


def whole(shape):
    return pl.BlockSpec(shape, lambda *_: (0,) * len(shape), pipeline_mode=pl.Buffered(1))


def swap_pairs(v):
    even = lane_iota(v.shape) % 2 == 0
    return jnp.where(even, pltpu.roll(v, LANES - 1, 1), pltpu.roll(v, 1, 1))


def norm_rows(x):
    return lax.rsqrt(jnp.mean(x * x, axis=1, keepdims=True) + EPS)


def seen(begin, first, rows, length):
    u = lax.broadcasted_iota(jnp.int32, (rows, length), 1)
    t = lax.broadcasted_iota(jnp.int32, (rows, length), 0) + first
    return (u >= begin) & (u <= t)


def gate_lanes(logits, meta):
    lane = lane_iota(logits.shape)
    hit = (pltpu.roll(meta, LANES - META_HIT, 1) > 0.0) & (lane < ROUTES)
    held = jnp.where(hit, logits, NEG)
    e = jnp.where(hit, jnp.exp(held - jnp.max(held, axis=1, keepdims=True)), 0.0)
    return e / jnp.sum(e, axis=1, keepdims=True)


MESH = pl.DeviceIdType.MESH
ANY = pl.BlockSpec(memory_space=pl.ANY)
PACK = 3 * HEAD_DIM // 2


def place():
    return lax.axis_index("row"), lax.axis_index("col")


def flip(index, mask):
    for bit in (1, 2, 4):
        if mask & bit:
            index = index + bit - 2 * bit * (index // bit % 2)
    return index


def greet(devices):
    barrier = pltpu.get_barrier_semaphore()
    for device in devices:
        pl.semaphore_signal(barrier, inc=1, device_id=device, device_id_type=MESH)
    pl.semaphore_wait(barrier, len(devices))


def send_to(src, dst, send, recv, device):
    return pltpu.make_async_remote_copy(
        src_ref=src, dst_ref=dst, send_sem=send, recv_sem=recv, device_id=device, device_id_type=MESH
    )


def col_peers(n):
    r, c = place()
    return [(r, (c + k) % n) for k in range(1, n)]


def gather_chain(own, dst, send, recv, n):
    r, c = place()

    def right(k):
        i = jnp.maximum(c - k, 0)
        src = own if k == 0 else dst.at[i]
        return send_to(src, dst.at[i], send.at[0, k], recv.at[0, k], (r, jnp.minimum(c + 1, n - 1)))

    def left(k):
        i = jnp.minimum(c + k, n - 1)
        src = own if k == 0 else dst.at[i]
        return send_to(src, dst.at[i], send.at[1, k], recv.at[1, k], (r, jnp.maximum(c - 1, 0)))

    def step(k):
        if k > 0:

            @pl.when(c >= k)
            def _():
                right(k - 1).wait_recv()

            @pl.when(c + k < n)
            def _():
                left(k - 1).wait_recv()

        if k < n - 1:

            @pl.when((c >= k) & (c + 1 < n))
            def _():
                right(k).start()

            @pl.when((c + k < n) & (c >= 1))
            def _():
                left(k).start()

    def drain():
        for k in range(n - 1):

            @pl.when((c >= k) & (c + 1 < n))
            def _():
                right(k).wait_send()

            @pl.when((c + k < n) & (c >= 1))
            def _():
                left(k).wait_send()

    return step, drain


def reduce_chain(own, out, arrived, send, recv, n):
    r, c = place()

    def right(k):
        return send_to(out.at[0, k], arrived.at[0, k], send.at[0, k], recv.at[0, k], (r, jnp.minimum(c + 1, n - 1)))

    def left(k):
        return send_to(out.at[1, k], arrived.at[1, k], send.at[1, k], recv.at[1, k], (r, jnp.maximum(c - 1, 0)))

    def slot(s):
        if s == n - 1:

            @pl.when(c >= 1)
            def _():
                right(n - 1 - c).wait_recv()

            @pl.when(c <= n - 2)
            def _():
                left(c).wait_recv()

            return

        @pl.when(c <= s)
        def _():
            k = jnp.maximum(s - c, 0)

            @pl.when(c >= 1)
            def _():
                right(k).wait_recv()
                out[0, k] = (own(n - 1 - k).astype(F32) + arrived[0, k].astype(F32)).astype(BF)

            @pl.when(c == 0)
            def _():
                out[0, k] = own(n - 1 - k).astype(BF)

            right(k).start()

        @pl.when(n - 1 - c <= s)
        def _():
            k = jnp.maximum(s - (n - 1 - c), 0)

            @pl.when(c <= n - 2)
            def _():
                left(k).wait_recv()
                out[1, k] = (own(k).astype(F32) + arrived[1, k].astype(F32)).astype(BF)

            @pl.when(c == n - 1)
            def _():
                out[1, k] = own(k).astype(BF)

            left(k).start()

    def total(dst):
        dst[...] = own(c).astype(F32)

        @pl.when(c >= 1)
        def _():
            dst[...] += arrived[0, n - 1 - c].astype(F32)

        @pl.when(c <= n - 2)
        def _():
            dst[...] += arrived[1, c].astype(F32)

    def drain():
        for k in range(n - 1):

            @pl.when(c < n - 1 - k)
            def _():
                right(k).wait_send()

            @pl.when(c > k)
            def _():
                left(k).wait_send()

    return slot, total, drain


def chain_scratch(n, rows):
    return [
        pltpu.VMEM((2, n - 1, rows, D), BF),
        pltpu.VMEM((2, n - 1, rows, D), BF),
        pltpu.SemaphoreType.DMA((2, n - 1)),
        pltpu.SemaphoreType.DMA((2, n - 1)),
    ]


def slot_rows(tsr_ref, e, capacity):
    rows = tsr_ref.shape[1]
    spots = lax.broadcasted_iota(jnp.int32, (capacity, rows), 0)
    return jnp.where(spots == tsr_ref[pl.ds(e, 1)], 1.0, 0.0).astype(BF)


def slot_column(meta_ref, e):
    picked = jnp.where(lane_iota(meta_ref.shape) == e, meta_ref[...], 0.0)
    return jnp.sum(picked, axis=1, keepdims=True).astype(jnp.int32)


def full_weight(w_ref, t):
    ranks, _, _, depth, ff = w_ref.shape
    return w_ref[:, t, 0].reshape(ranks * depth, ff)


COMBINE = 256


def experts_forward_kernel(
    cols,
    capacity,
    n2_ref,
    prev_ref,
    cot_ref,
    rw_ref,
    carry_ref,
    tsr_ref,
    meta_ref,
    w_ref,
    x_ref,
    gu_ref,
    mix_ref,
    gates_ref,
    cotw_ref,
    mix_acc,
    send,
    recv,
    local_sem,
):
    e = pl.program_id(0)
    experts = pl.num_programs(0)
    r, c = place()
    rows = n2_ref.shape[0]
    local = rows // cols
    step, drain = gather_chain(cot_ref, cotw_ref, send, recv, cols)
    own_copy = pltpu.make_async_copy(cot_ref, cotw_ref.at[c], local_sem.at[0])

    @pl.when(e == 0)
    def _():
        greet(col_peers(cols))
        own_copy.start()
        step(0)
        prev = jnp.concatenate([mm(prev_ref[i], carry_ref[...], TN) for i in range(cols)], axis=0)
        g = gate_lanes(mm(n2_ref[...], rw_ref[...], NT) + prev, meta_ref[...])
        high = g.astype(BF)
        gates_ref[:, :LANES] = high
        gates_ref[:, LANES:] = (g - high.astype(F32)).astype(BF)
        mix_acc[...] = jnp.zeros_like(mix_acc)

    @pl.when(e == 3)
    def _():
        step(1)

    one = slot_rows(tsr_ref, e, capacity)
    x = mm(one, n2_ref[...]).astype(BF)
    x_ref[0] = x
    sg = mm(one, gates_ref[...])
    sg = jnp.sum(jnp.where(lane_iota(sg.shape) % LANES == e, sg, 0.0), axis=1, keepdims=True)
    g = mm(x, full_weight(w_ref, 0))
    u = mm(x, full_weight(w_ref, 1))
    gu_ref[0, 0] = g.astype(BF)
    gu_ref[0, 1] = u.astype(BF)
    gh = (g * jax.nn.sigmoid(g) * u * sg).astype(BF)
    y = mm(gh, full_weight(w_ref, 2), NT).astype(BF)
    tsc = slot_column(meta_ref, e)
    for b in range(rows // COMBINE):
        rs = slice(b * COMBINE, (b + 1) * COMBINE)
        one_t = jnp.where(lane_iota((COMBINE, capacity)) == tsc[rs], 1.0, 0.0).astype(BF)
        mix_acc[rs] += mm(one_t, y)

    @pl.when(e == experts - 1)
    def _():
        for k in range(2, cols):
            step(k)
        for d in range(cols):
            mix_ref[d] = mix_acc[d * local : (d + 1) * local].astype(BF)
        drain()
        own_copy.wait()


def experts_forward(cols, n2, prev, cot, rw, carry, meta, slots, w_all):
    rows = n2.shape[0]
    capacity = rows // 4
    ranks, three, experts, depth, ff = w_all.shape
    local = rows // cols
    return pl.pallas_call(
        functools.partial(experts_forward_kernel, cols, capacity),
        grid=(experts,),
        out_shape=(
            jax.ShapeDtypeStruct((experts, capacity, D), BF),
            jax.ShapeDtypeStruct((experts, 2, capacity, ff), BF),
            jax.ShapeDtypeStruct((cols, local, D), BF),
            jax.ShapeDtypeStruct((rows, 2 * LANES), BF),
            jax.ShapeDtypeStruct((cols, local, D), BF),
        ),
        in_specs=[
            whole((rows, D)),
            whole((cols, 16, local)),
            whole((local, D)),
            whole((LANES, D)),
            whole((16, LANES)),
            whole((experts, rows)),
            whole((rows, LANES)),
            pl.BlockSpec((ranks, three, 1, depth, ff), lambda e: (0, 0, e, 0, 0)),
        ],
        out_specs=(
            pl.BlockSpec((1, capacity, D), lambda e: (e, 0, 0)),
            pl.BlockSpec((1, 2, capacity, ff), lambda e: (e, 0, 0, 0)),
            whole((cols, local, D)),
            whole((rows, 2 * LANES)),
            ANY,
        ),
        scratch_shapes=[
            pltpu.VMEM((rows, D), F32),
            pltpu.SemaphoreType.DMA((2, cols - 1)),
            pltpu.SemaphoreType.DMA((2, cols - 1)),
            pltpu.SemaphoreType.DMA((1,)),
        ],
        compiler_params=pltpu.CompilerParams(
            vmem_limit_bytes=60 * MIB, collective_id=1, has_side_effects=True
        ),
        cost_estimate=pl.CostEstimate(
            flops=experts * capacity * 4 * D * (2 * ff + rows),
            bytes_accessed=40 * MIB,
            transcendentals=experts * capacity * ff,
        ),
        name="experts_forward",
    )(n2, prev, cot, rw, carry, slots, meta, w_all)


def experts_backward_kernel(
    cols,
    capacity,
    cot_ref,
    mix_ref,
    gates_ref,
    tsr_ref,
    meta_ref,
    w_ref,
    x_ref,
    gu_ref,
    gt_ref,
    dots_ref,
    mixsum_ref,
    gown_ref,
    sib_ref,
    gt_acc,
    gbuf,
    out,
    arrived,
    send,
    recv,
    own_sem,
    sib_send,
    sib_recv,
):
    e = pl.program_id(0)
    experts = pl.num_programs(0)
    r, c = place()
    core = r % 2
    rows = cot_ref.shape[0]
    local = rows // cols
    place_now = lax.rem(e, 2)
    slot, total, drain = reduce_chain(lambda d: mix_ref[d], out, arrived, send, recv, cols)

    def own_copy(expert, at):
        return pltpu.make_async_copy(gbuf.at[at, :, :, core], gown_ref.at[expert], own_sem.at[at])

    def sib_copy(expert, at):
        return send_to(
            gbuf.at[at, :, :, 1 - core],
            sib_ref.at[expert],
            sib_send.at[at],
            sib_recv.at[expert],
            (flip(r, 1), c),
        )

    @pl.when(e == 0)
    def _():
        greet(col_peers(cols) + [(flip(r, 1), c)])
        slot(0)
        gt_acc[...] = jnp.zeros_like(gt_acc)

    @pl.when(e == 2)
    def _():
        slot(1)

    @pl.when(e == 5)
    def _():
        slot(2)

    one = slot_rows(tsr_ref, e, capacity)
    ct = mm(one, cot_ref[...]).astype(BF)
    sg = mm(one, gates_ref[...])
    sg = jnp.sum(jnp.where(lane_iota(sg.shape) % LANES == e, sg, 0.0), axis=1, keepdims=True)
    x = x_ref[0]
    g, u = gu_ref[0, 0].astype(F32), gu_ref[0, 1].astype(F32)
    wg, wu = full_weight(w_ref, 0), full_weight(w_ref, 1)
    v = mm(ct, full_weight(w_ref, 2))
    sig = jax.nn.sigmoid(g)
    act = g * sig
    h = act * u
    dot = jnp.sum(h * v, axis=1, keepdims=True)
    dots_ref[pl.ds(e, 1)] = jnp.sum(one.astype(F32) * dot, axis=0, keepdims=True)
    gh = (h * sg).astype(BF)
    gv = v * sg
    dg = (gv * u * (sig * (1.0 + g * (1.0 - sig)))).astype(BF)
    du = (gv * act).astype(BF)
    dx = (mm(dg, wg, NT) + mm(du, wu, NT)).astype(BF)
    tsc = slot_column(meta_ref, e)
    for b in range(rows // COMBINE):
        rs = slice(b * COMBINE, (b + 1) * COMBINE)
        one_t = jnp.where(lane_iota((COMBINE, capacity)) == tsc[rs], 1.0, 0.0).astype(BF)
        gt_acc[rs] += mm(one_t, dx)

    @pl.when(e >= 2)
    def _():
        own_copy(e - 2, place_now).wait()
        sib_copy(e - 2, place_now).wait_send()

    shape = gbuf.shape[2:]
    gbuf[place_now, 0] = mm(x, dg, TN).astype(BF).reshape(shape)
    gbuf[place_now, 1] = mm(x, du, TN).astype(BF).reshape(shape)
    gbuf[place_now, 2] = mm(ct, gh, TN).astype(BF).reshape(shape)
    own_copy(e, place_now).start()
    sib_copy(e, place_now).start()

    @pl.when(e == experts - 1)
    def _():
        for d in range(cols):
            gt_ref[d] = gt_acc[d * local : (d + 1) * local].astype(BF)
        for s in range(3, cols):
            slot(s)
        total(mixsum_ref)
        drain()
        for back in (1, 0):
            own_copy(e - back, lax.rem(e - back, 2)).wait()
            sib_copy(e - back, lax.rem(e - back, 2)).wait_send()
        for i in range(8):
            sib_copy(i, i % 2).wait_recv()


def experts_backward(cols, cot, mix, gates, meta, slots, w_all, x, gu):
    rows = cot.shape[0]
    capacity = rows // 4
    ranks, three, experts, depth, ff = w_all.shape
    local = rows // cols
    chips = ranks // 2
    half = jax.ShapeDtypeStruct((experts, three, chips, depth, ff), BF)
    return pl.pallas_call(
        functools.partial(experts_backward_kernel, cols, capacity),
        grid=(experts,),
        out_shape=(
            jax.ShapeDtypeStruct((cols, local, D), BF),
            jax.ShapeDtypeStruct((experts, rows), F32),
            jax.ShapeDtypeStruct((local, D), F32),
            half,
            half,
        ),
        in_specs=[
            whole((rows, D)),
            whole((cols, local, D)),
            whole((rows, 2 * LANES)),
            whole((experts, rows)),
            whole((rows, LANES)),
            pl.BlockSpec((ranks, three, 1, depth, ff), lambda e: (0, 0, e, 0, 0)),
            pl.BlockSpec((1, capacity, D), lambda e: (e, 0, 0)),
            pl.BlockSpec((1, 2, capacity, ff), lambda e: (e, 0, 0, 0)),
        ],
        out_specs=(
            whole((cols, local, D)),
            whole((experts, rows)),
            whole((local, D)),
            ANY,
            ANY,
        ),
        scratch_shapes=[
            pltpu.VMEM((rows, D), F32),
            pltpu.VMEM((2, three, chips, 2, depth, ff), BF),
            *chain_scratch(cols, local),
            pltpu.SemaphoreType.DMA((2,)),
            pltpu.SemaphoreType.DMA((2,)),
            pltpu.SemaphoreType.DMA((experts,)),
        ],
        compiler_params=pltpu.CompilerParams(
            vmem_limit_bytes=60 * MIB, collective_id=2, has_side_effects=True
        ),
        cost_estimate=pl.CostEstimate(
            flops=experts * capacity * 4 * D * (3 * ff + rows),
            bytes_accessed=60 * MIB,
            transcendentals=experts * capacity * ff,
        ),
        name="experts_backward",
    )(cot, mix, gates, slots, meta, w_all, x, gu)


def pack_heads(dst, value):
    rows = value.shape[0]
    half = rows // 2
    dst[:rows] = value[:, :LANES]
    dst[rows:] = jnp.concatenate([value[:half, LANES:], value[half:, LANES:]], axis=1)


def unpack_heads(packed, rows):
    top, rest = packed[:rows], packed[rows:]
    return (
        top[:, :HEAD_DIM],
        top[:, HEAD_DIM:],
        jnp.concatenate([rest[:, :HEAD_DIM], rest[:, HEAD_DIM:]], axis=0),
    )


def to_rows(src_of, dst, send, recv, ranks):
    r, c = place()
    copies = []
    for m in range(1, ranks):
        there = flip(r, m)
        copies.append(send_to(src_of(there), dst.at[r], send.at[m - 1], recv.at[m - 1], (there, c)))
    return copies


def to_cols(src_of, dst, send, recv, n):
    r, c = place()
    copies = []
    for k in range(1, n):
        there = (c + k) % n
        copies.append(send_to(src_of(there), dst.at[c], send.at[k - 1], recv.at[k - 1], (r, there)))
    return copies


def all_sum(ref, count):
    total = ref[0].astype(F32)
    for i in range(1, count):
        total = total + ref[i].astype(F32)
    return total


def send_weight_grads(first, count, gown, sib, hin, lbuf, hbuf, load_sem, send, recv):
    r, c = place()
    chip = r // 2

    def loads(i):
        at = lax.rem(i, 2)
        return [
            pltpu.make_async_copy(ref.at[first + i], lbuf.at[at, j], load_sem.at[at, j])
            for j, ref in enumerate((gown, sib))
        ]

    def sends(i):
        return [
            send_to(
                hbuf.at[i, :, flip(chip, k)],
                hin.at[i, k - 1],
                send.at[i, k - 1],
                recv.at[i, k - 1],
                (flip(r, 2 * k), c),
            )
            for k in range(1, 4)
        ]

    for copy in loads(0):
        copy.start()

    def body(i, carry):
        @pl.when(i + 1 < count)
        def _():
            for copy in loads(i + 1):
                copy.start()

        for copy in loads(i):
            copy.wait()
        at = lax.rem(i, 2)
        hbuf[i] = (lbuf[at, 0].astype(F32) + lbuf[at, 1].astype(F32)).astype(BF)
        for copy in sends(i):
            copy.start()
        return carry

    lax.fori_loop(0, count, body, 0)

    def finish():
        def wait(i, carry):
            for copy in sends(i):
                copy.wait()
            return carry

        lax.fori_loop(0, count, wait, 0)

    return finish


def weight_scratch(count, block):
    three, chips, depth, ff = block
    return [
        pltpu.VMEM((2, 2, three, chips, depth, ff), BF),
        pltpu.VMEM((count, three, chips, depth, ff), BF),
        pltpu.SemaphoreType.DMA((2, 2)),
        pltpu.SemaphoreType.DMA((count, 3)),
        pltpu.SemaphoreType.DMA((count, 3)),
    ]


def resid_kernel(
    cols,
    count,
    gt_ref,
    dots_ref,
    mixsum_ref,
    n2_ref,
    middle_ref,
    cot_ref,
    meta_ref,
    prev_ref,
    rw_ref,
    carry_ref,
    gain_ref,
    out_t_ref,
    mixed_ref,
    gown_ref,
    sib_ref,
    layer_ref,
    resid_ref,
    gm_ref,
    og_ref,
    small_ref,
    pg_ref,
    hin_ref,
    out,
    arrived,
    send,
    recv,
    dots_in,
    dsend,
    drecv,
    grad,
    gm_out,
    gsend,
    grecv,
    gm_sem,
    *weight_refs,
):
    r, c = place()
    local = n2_ref.shape[0]
    greet(col_peers(cols) + [(flip(r, 2 * k), c) for k in range(1, 4)])
    slot, total, drain = reduce_chain(lambda d: gt_ref[d], out, arrived, send, recv, cols)

    def dots_of(d):
        return dots_ref.at[:, pl.ds(pl.multiple_of(d * local, LANES), local)]

    dot_copies = to_cols(dots_of, dots_in, dsend, drecv, cols)
    for copy in dot_copies:
        copy.start()
    dots_in[c] = dots_of(c)[...]
    slot(0)
    finish = send_weight_grads(0, count, gown_ref, sib_ref, hin_ref, *weight_refs)
    slot(1)

    meta = meta_ref[pl.ds(pl.multiple_of(c * local, LANES), local)]
    n2, cot = n2_ref[...], cot_ref[...]
    n2f, cotf = n2.astype(F32), cot.astype(F32)
    middle = middle_ref[...]
    rw = rw_ref[...]
    lin = mm(n2, rw, NT)
    prev = prev_ref[...]
    gates = gate_lanes(lin + mm(prev, carry_ref[...], TN), meta)
    lane = lane_iota((local, LANES))
    cot_lin = mm(cot, rw, NT)
    dot_keep = jnp.sum(cotf * n2f, axis=1, keepdims=True)
    for copy in dot_copies:
        copy.wait()
    d = jnp.concatenate([all_sum(dots_in, cols), jnp.zeros((LANES - EXPERTS, local), F32)], axis=0).T
    g_gates = jnp.where(lane == EXPERTS + 1, dot_keep, d)
    keep = gates[:, EXPERTS + 1 : EXPERTS + 2]
    mixes, packs = [], jnp.zeros((local, LANES), F32)
    for j in range(2):
        l0 = lin[:, ROW_CONST + 2 * j : ROW_CONST + 2 * j + 1]
        l1 = lin[:, ROW_CONST + 2 * j + 1 : ROW_CONST + 2 * j + 2]
        top = jnp.maximum(l0, l1)
        e0, e1 = jnp.exp(l0 - top), jnp.exp(l1 - top)
        a0, a1 = e0 / (e0 + e1), e1 / (e0 + e1)
        share = gates[:, EXPERTS + 2 + j : EXPERTS + 3 + j]
        dot_vec = cot_lin[:, ROW_VEC + j : ROW_VEC + j + 1]
        keep = keep + share * a0
        mixes.append(share * a1)
        g_gates = jnp.where(lane == EXPERTS + 2 + j, a0 * dot_keep + a1 * dot_vec, g_gates)
        gk, gv = share * dot_keep, share * dot_vec
        mean = a0 * gk + a1 * gv
        packs = packs + jnp.where(lane == ROW_CONST + 2 * j, a0 * (gk - mean), 0.0)
        packs = packs + jnp.where(lane == ROW_CONST + 2 * j + 1, a1 * (gv - mean), 0.0)
        packs = packs + jnp.where(lane == ROW_VEC + j, share * a1, 0.0)
    packs = packs + gates * (g_gates - jnp.sum(gates * g_gates, axis=1, keepdims=True))
    vec = rw[ROW_VEC : ROW_VEC + 2].astype(F32)
    layer = middle + mixsum_ref[...] + keep * n2f + mixes[0] * vec[0:1] + mixes[1] * vec[1:2]
    layer_ref[...] = layer.astype(BF)

    high = packs.astype(BF)
    low = (packs - high.astype(F32)).astype(BF)
    back = lane < ROW_VEC
    high_b = jnp.where(back, packs, 0.0).astype(BF)
    low_b = jnp.where(back, packs - high.astype(F32), 0.0).astype(BF)
    grad_local = keep * cotf + mm(high_b, rw) + mm(low_b, rw)
    by_n2 = mm(high, n2, TN) + mm(low, n2, TN)
    by_cot = mm(high, cot, TN) + mm(low, cot, TN)
    by_prev = mm(prev, high) + mm(prev, low)
    pg = mm(carry_ref[...], high_b, NT) + mm(carry_ref[...], low_b, NT)
    pg_ref[...] = pg[:ROUTES]
    sub = lax.broadcasted_iota(jnp.int32, (SMALL_ROWS, D), 0)
    small_ref[:, :D] = jnp.where(sub < ROW_VEC, by_n2[:SMALL_ROWS], by_cot[:SMALL_ROWS])
    small_ref[:16, D:] = by_prev
    small_ref[16:, D:] = jnp.zeros((SMALL_ROWS - 16, LANES), F32)

    for s in range(2, cols):
        slot(s)
    total(grad)
    grad_normed = grad[...] + grad_local
    scale = norm_rows(middle)
    gained = grad_normed * gain_ref[...]
    mid_dot = jnp.sum(gained * middle, axis=1, keepdims=True)
    resid = cotf + scale * gained - middle * (scale * scale * scale * (mid_dot * (1.0 / D)))
    resid_ref[...] = resid
    cut = resid.astype(BF)
    gm = (mm(cut, out_t_ref[...]) * meta[:, META_VALID : META_VALID + 1]).astype(BF)
    width = D // cols
    for i in range(cols):
        pack_heads(gm_out.at[i], gm[:, i * width : (i + 1) * width])
    gm_copies = to_cols(lambda i: gm_out.at[i], gm_ref, gsend, grecv, cols)
    for copy in gm_copies:
        copy.start()
    keep_own = pltpu.make_async_copy(gm_out.at[c], gm_ref.at[c], gm_sem.at[0])
    keep_own.start()
    small_ref[ROW_GAIN : ROW_GAIN + 1, :D] = jnp.sum(grad_normed * middle * scale, axis=0, keepdims=True)
    og_ref[...] = mm(cut, mixed_ref[...], TN).astype(BF)
    keep_own.wait()
    for copy in gm_copies:
        copy.wait()
    drain()
    finish()


def resid_step(cols, count, gt, dots, mixsum, n2, middle, cot, meta, prev, rw, carry, gain, out_t, mixed, gown, sib):
    local = n2.shape[0]
    experts, three, chips, depth, ff = gown.shape
    vm = pl.BlockSpec(memory_space=pltpu.VMEM)
    return pl.pallas_call(
        functools.partial(resid_kernel, cols, count),
        out_shape=(
            jax.ShapeDtypeStruct((local, D), BF),
            jax.ShapeDtypeStruct((local, D), F32),
            jax.ShapeDtypeStruct((cols, local * 3 // 2, LANES), BF),
            jax.ShapeDtypeStruct((D, D), BF),
            jax.ShapeDtypeStruct((SMALL_ROWS, D + LANES), F32),
            jax.ShapeDtypeStruct((ROUTES, local), F32),
            jax.ShapeDtypeStruct((count, 3, three, depth, ff), BF),
        ),
        in_specs=[vm] * 13 + [ANY, ANY],
        out_specs=(vm, vm, ANY, vm, vm, vm, ANY),
        scratch_shapes=[
            *chain_scratch(cols, local),
            pltpu.VMEM((cols, EXPERTS, local), F32),
            pltpu.SemaphoreType.DMA((cols - 1,)),
            pltpu.SemaphoreType.DMA((cols - 1,)),
            pltpu.VMEM((local, D), F32),
            pltpu.VMEM((cols, local * 3 // 2, LANES), BF),
            pltpu.SemaphoreType.DMA((cols - 1,)),
            pltpu.SemaphoreType.DMA((cols - 1,)),
            pltpu.SemaphoreType.DMA((1,)),
            *weight_scratch(count, (three, chips, depth, ff)),
        ],
        compiler_params=pltpu.CompilerParams(
            vmem_limit_bytes=60 * MIB, collective_id=3, has_side_effects=True
        ),
        cost_estimate=pl.CostEstimate(flops=6 * local * D * D, bytes_accessed=40 * MIB, transcendentals=0),
        name="resid_step",
    )(gt, dots, mixsum, n2, middle, cot, meta, prev, rw, carry, gain, out_t, mixed, gown, sib)


def finish_kernel(
    cols,
    ranks,
    first,
    count,
    gm_ref,
    qkv_ref,
    meta_ref,
    o_ref,
    lse_ref,
    x_ref,
    gain_ref,
    w_ref,
    cos_ref,
    sin_ref,
    small_ref,
    og_ref,
    resid_ref,
    xown_ref,
    gown_ref,
    sib_ref,
    ig_ref,
    small_out,
    gain_out,
    qg_out,
    og_out,
    hin_ref,
    do_s,
    dq_s,
    dk_s,
    dv_s,
    gn_s,
    qg_acc,
    qg_cut,
    out,
    arrived,
    send,
    recv,
    small_rows,
    small_cols,
    og_rows,
    og_parts,
    og_cols,
    gain_rows,
    gain_cols,
    qg_rows,
    q_parts,
    q_land,
    total_s,
    row_send,
    row_recv,
    col_send,
    col_recv,
    *weight_refs,
):
    r, c = place()
    heads = 3
    rows = x_ref.shape[0]
    local = rows // cols
    depth = D // ranks
    width = heads * HEAD_DIM
    score_scale = 1.0 / math.sqrt(HEAD_DIM)
    greet(col_peers(cols) + [(flip(r, m), c) for m in range(1, ranks)])

    def rows_of(ref, d):
        return ref.at[pl.ds(pl.multiple_of(d * depth, 16), depth)]

    small_to_rows = to_rows(lambda d: small_ref, small_rows, row_send.at[0], row_recv.at[0], ranks)
    og_to_rows = to_rows(lambda d: rows_of(og_ref, d), og_rows, row_send.at[1], row_recv.at[1], ranks)
    for copy in small_to_rows + og_to_rows:
        copy.start()
    small_rows[r] = small_ref[...]
    og_rows[r] = rows_of(og_ref, r)[...]
    finish = send_weight_grads(first, count, gown_ref, sib_ref, hin_ref, *weight_refs)

    for d in range(cols):
        at = slice(d * local, (d + 1) * local)
        for h, value in enumerate(unpack_heads(gm_ref[d], local)):
            do_s[h, at] = value

    blocks = rows // Q_ROWS

    def one_head(h, carry):
        for i in reversed(range(blocks)):
            at = slice(i * Q_ROWS, (i + 1) * Q_ROWS)
            length = (i + 1) * Q_ROWS
            q, do = qkv_ref[h, at], do_s[h, at]
            k, v = qkv_ref[heads + h, :length], qkv_ref[2 * heads + h, :length]
            delta = jnp.sum(do.astype(F32) * o_ref[h, at].astype(F32), axis=1, keepdims=True)
            s = mm(q, k, NT)
            ok = seen(column(meta_ref, at, META_BEGIN).astype(jnp.int32), i * Q_ROWS, Q_ROWS, length)
            p = jnp.where(ok, jnp.exp(s - lse_ref[h, at]), 0.0)
            ds = (p * (mm(do, v, NT) - delta)).astype(BF)
            dq_s[h, at] = mm(ds, k) * score_scale
            dk, dv = mm(ds, q, TN), mm(p.astype(BF), do, TN)
            if i == blocks - 1:
                dk_s[h], dv_s[h] = dk, dv
            else:
                dk_s[h, :length] += dk
                dv_s[h, :length] += dv
        return carry

    lax.fori_loop(0, 2, one_head, 0)
    for copy in small_to_rows + og_to_rows:
        copy.wait()
    small_cols[c] = all_sum(small_rows, ranks)
    og_sum = all_sum(og_rows, ranks)
    for i in range(cols):
        og_parts[i] = og_sum[:, i * width : (i + 1) * width]
    small_to_cols = to_cols(lambda d: small_cols.at[c], small_cols, col_send.at[0], col_recv.at[0], cols)
    og_to_cols = to_cols(lambda d: og_parts.at[d], og_cols, col_send.at[1], col_recv.at[1], cols)
    for copy in small_to_cols + og_to_cols:
        copy.start()
    og_cols[c] = og_parts[c]
    lax.fori_loop(2, 3, one_head, 0)

    slot, total, drain = reduce_chain(lambda d: gn_s[d], out, arrived, send, recv, cols)
    gain_total = jnp.zeros((1, D), F32)
    weight = w_ref[...]
    for n, d in enumerate((3, 0, 2, 1)):
        at = slice(d * local, (d + 1) * local)
        cosine, sines = cos_ref[at], sin_ref[at]
        turned = [dq_s[h, at] for h in range(heads)] + [dk_s[h, at] for h in range(heads)]
        parts = []
        for part in range(heads):
            v = jnp.concatenate(turned[2 * part : 2 * part + 2], axis=1)
            parts.append((v * cosine - swap_pairs(v) * sines).astype(BF))
        parts += [dv_s[h, at].astype(BF) for h in range(heads)]
        gp = jnp.concatenate(parts, axis=1)
        x = x_ref[at].astype(F32)
        xs = x * norm_rows(x)
        gn = mm(gp, weight, NT)
        gn_s[d] = gn.astype(BF)
        gain_total = gain_total + jnp.sum(gn * xs, axis=0, keepdims=True)
        grad = mm((xs * gain_ref[...]).astype(BF), gp, TN)
        if n == 0:
            qg_acc[...] = grad
        else:
            qg_acc[...] += grad
        if n == 1:
            slot(0)
        if n == 3:
            slot(1)
    qg_cut[...] = qg_acc[...].astype(BF)
    gain_rows[r] = jnp.broadcast_to(gain_total, (8, D))
    qg_to_rows = to_rows(lambda d: rows_of(qg_cut, d), qg_rows, row_send.at[2], row_recv.at[2], ranks)
    gain_to_rows = to_rows(lambda d: gain_rows.at[r], gain_rows, row_send.at[3], row_recv.at[3], ranks)
    for copy in gain_to_rows + qg_to_rows:
        copy.start()
    qg_rows[r] = rows_of(qg_cut, r)[...]
    for s in range(2, cols - 1):
        slot(s)
    for copy in gain_to_rows + qg_to_rows:
        copy.wait()
    gain_cols[c] = all_sum(gain_rows, ranks)
    q_sum = all_sum(qg_rows, ranks)
    for i in range(3):
        q_parts[i] = q_sum[:, i * width : (i + 1) * width]
    gain_to_cols = to_cols(lambda d: gain_cols.at[c], gain_cols, col_send.at[2], col_recv.at[2], cols)
    odd, high = c % 2, c // 2
    q_copies = [
        send_to(
            q_parts.at[1 - odd + high],
            q_land.at[1],
            col_send.at[3, 0],
            col_recv.at[3, 0],
            (r, flip(c, 1)),
        ),
        send_to(
            q_parts.at[2 - 2 * high],
            q_land.at[2 - 2 * odd],
            col_send.at[3, 1],
            col_recv.at[3, 1],
            (r, flip(c, 2)),
        ),
    ]
    for copy in gain_to_cols + q_copies:
        copy.start()
    q_land[2 * odd] = q_parts[(c + 1) // 2]
    slot(cols - 1)
    total(total_s)
    gn = total_s[...]
    x = xown_ref[...].astype(F32)
    scale = norm_rows(x)
    gained = gn * gain_ref[...]
    x_dot = jnp.sum(gained * x, axis=1, keepdims=True)
    ig_ref[...] = resid_ref[...] + scale * gained - x * (scale * scale * scale * (x_dot * (1.0 / D)))
    for copy in small_to_cols + og_to_cols + gain_to_cols + q_copies:
        copy.wait()
    small_out[...] = all_sum(small_cols, cols)
    og_out[...] = all_sum(og_cols, cols)
    gain_out[...] = all_sum(gain_cols, cols)
    qg_out[...] = q_land[...]
    drain()
    finish()


def finish_step(cols, ranks, first, gm, qkv, meta, o, lse, x, gain, w, cosine, sines, small, og, resid, xown, gown, sib):
    rows = x.shape[0]
    local = rows // cols
    experts, three, chips, depth, ff = gown.shape
    count = experts - first
    heads, width = 3, 3 * HEAD_DIM
    vm = pl.BlockSpec(memory_space=pltpu.VMEM)
    wide = D + LANES
    return pl.pallas_call(
        functools.partial(finish_kernel, cols, ranks, first, count),
        out_shape=(
            jax.ShapeDtypeStruct((local, D), F32),
            jax.ShapeDtypeStruct((SMALL_ROWS, wide), F32),
            jax.ShapeDtypeStruct((8, D), F32),
            jax.ShapeDtypeStruct((3, depth, width), F32),
            jax.ShapeDtypeStruct((depth, width), F32),
            jax.ShapeDtypeStruct((count, 3, three, depth, ff), BF),
        ),
        in_specs=[vm] * 14 + [ANY, ANY],
        out_specs=(vm, vm, vm, vm, vm, ANY),
        scratch_shapes=[
            pltpu.VMEM((heads, rows, HEAD_DIM), BF),
            pltpu.VMEM((heads, rows, HEAD_DIM), F32),
            pltpu.VMEM((heads, rows, HEAD_DIM), F32),
            pltpu.VMEM((heads, rows, HEAD_DIM), F32),
            pltpu.VMEM((cols, local, D), BF),
            pltpu.VMEM((D, 3 * width), F32),
            pltpu.VMEM((D, 3 * width), BF),
            *chain_scratch(cols, local),
            pltpu.VMEM((ranks, SMALL_ROWS, wide), F32),
            pltpu.VMEM((cols, SMALL_ROWS, wide), F32),
            pltpu.VMEM((ranks, depth, D), BF),
            pltpu.VMEM((cols, depth, width), F32),
            pltpu.VMEM((cols, depth, width), F32),
            pltpu.VMEM((ranks, 8, D), F32),
            pltpu.VMEM((cols, 8, D), F32),
            pltpu.VMEM((ranks, depth, 3 * width), BF),
            pltpu.VMEM((3, depth, width), F32),
            pltpu.VMEM((3, depth, width), F32),
            pltpu.VMEM((local, D), F32),
            pltpu.SemaphoreType.DMA((4, ranks - 1)),
            pltpu.SemaphoreType.DMA((4, ranks - 1)),
            pltpu.SemaphoreType.DMA((4, cols - 1)),
            pltpu.SemaphoreType.DMA((4, cols - 1)),
            *weight_scratch(count, (three, chips, depth, ff)),
        ],
        compiler_params=pltpu.CompilerParams(
            vmem_limit_bytes=62 * MIB, collective_id=4, has_side_effects=True
        ),
        cost_estimate=pl.CostEstimate(
            flops=20 * heads * rows * rows * HEAD_DIM, bytes_accessed=40 * MIB, transcendentals=heads * rows * rows
        ),
        name="finish_step",
    )(gm, qkv, meta, o, lse, x, gain, w, cosine, sines, small, og, resid, xown, gown, sib)


META_HIT, META_BEGIN, META_VALID = 8, 20, 21


def column(ref, at, lane):
    return ref[at, lane : lane + 1]


def tokens_meta(routes_ref, lengths_ref, rows, experts):
    kinds = lax.broadcasted_iota(jnp.int32, (16, rows), 0)
    hits = jnp.where((kinds == routes_ref[0:1]) | (kinds == routes_ref[1:2]), 1.0, 0.0)
    step = 256
    earlier = lax.broadcasted_iota(jnp.int32, (step, step), 0) < lax.broadcasted_iota(
        jnp.int32, (step, step), 1
    )
    earlier = jnp.where(earlier, 1.0, 0.0).astype(BF)
    counts, running = [], jnp.zeros((16, 1), F32)
    for b in range(rows // step):
        block = hits[:, b * step : (b + 1) * step]
        counts.append(mm(block.astype(BF), earlier) + running)
        running = running + jnp.sum(block, axis=1, keepdims=True)
    slots = jnp.where(hits > 0.0, jnp.concatenate(counts, axis=1), -1.0)[:experts]
    spot = lax.broadcasted_iota(jnp.int32, (8, rows), 1)
    begin, end = jnp.zeros((8, rows), F32), 0
    for i in range(lengths_ref.shape[1]):
        end = end + lengths_ref[0, i]
        begin = jnp.where(spot >= end, end.astype(F32), begin)
    valid = jnp.where(spot < end, 1.0, 0.0)
    tail = jnp.where(lax.broadcasted_iota(jnp.int32, (8, rows), 0) == 0, begin, valid)
    spare = jnp.zeros((LANES - experts - 12 - 8, rows), F32)
    meta = jnp.concatenate([slots, hits[:12], tail, spare], axis=0).T
    return slots.astype(jnp.int32), meta


def first_kernel(
    cols,
    ranks,
    x_ref,
    again_ref,
    fgain_ref,
    wq_ref,
    wo_ref,
    prev_ref,
    routes_ref,
    lengths_ref,
    cos_ref,
    sin_ref,
    freq_ref,
    gate_ref,
    up_ref,
    down_ref,
    wall_ref,
    qkv_ref,
    o_ref,
    lse_ref,
    xw_ref,
    wq_out,
    wo_out,
    cos_out,
    sin_out,
    meta_ref,
    slots_ref,
    mixed_ref,
    middle_ref,
    n2_ref,
    n2w_ref,
    prevw_ref,
    xw,
    q_parts,
    q_land,
    o_parts,
    o_land,
    wq,
    wo,
    a_out,
    a_in,
    prevw,
    local_sem,
    x_send,
    x_recv,
    n_send,
    n_recv,
    q_send,
    q_recv,
    c_send,
    c_recv,
    r_send,
    r_recv,
    e_send,
    e_recv,
    s_send,
    s_recv,
):
    r, c = place()
    heads = 3
    local = x_ref.shape[0]
    rows = local * cols
    width = heads * HEAD_DIM
    depth = D // ranks
    odd, high = c % 2, c // 2
    greet(col_peers(cols) + [(flip(r, m), c) for m in range(1, ranks)])

    for s in range(3):
        q_parts[s] = wq_ref[:, s * width : (s + 1) * width]
    q_copies = [
        send_to(q_parts.at[1], q_land.at[(c + 1) // 2], q_send.at[0], q_recv.at[0], (r, flip(c, 1))),
        send_to(q_parts.at[2 - 2 * odd], q_land.at[2 * high], q_send.at[1], q_recv.at[1], (r, flip(c, 2))),
    ]
    for copy in q_copies:
        copy.start()
    o_parts[...] = wo_ref[...]
    o_copies = to_cols(lambda d: o_parts, o_land, c_send.at[0], c_recv.at[0], cols)
    prev_copies = to_cols(lambda d: prev_ref, prevw, c_send.at[1], c_recv.at[1], cols)
    x_step, x_drain = gather_chain(x_ref, xw, x_send, x_recv, cols)
    x_step(0)
    for copy in o_copies + prev_copies:
        copy.start()
    q_land[(c + 1) // 2] = q_parts[2 * odd]
    o_land[c] = wo_ref[...]
    prevw[c] = prev_ref[...]
    xw[c] = x_ref[...]

    def rows_of(ref, d):
        return ref.at[pl.ds(pl.multiple_of(d * depth, 16), depth)]

    def push_rows(ref, at):
        copies = []
        for m in range(1, ranks):
            there = flip(r, m)
            copies.append(
                send_to(rows_of(ref, r), rows_of(ref, r), r_send.at[at, m - 1], r_recv.at[at, m - 1], (there, c))
            )
        return copies

    for copy in q_copies:
        copy.wait()
    rows_of(wq, r)[...] = jnp.concatenate([q_land[i] for i in range(3)], axis=1)
    wq_copies = push_rows(wq, 0)
    for copy in wq_copies:
        copy.start()
    for copy in o_copies:
        copy.wait()
    rows_of(wo, r)[...] = jnp.concatenate([o_land[i] for i in range(cols)], axis=1)
    wo_copies = push_rows(wo, 1)
    for copy in wo_copies:
        copy.start()

    weights = (gate_ref, up_ref, down_ref)
    kept = [pltpu.make_async_copy(ref, wall_ref.at[r, t], local_sem.at[t]) for t, ref in enumerate(weights)]
    chip_copies = [
        [
            send_to(ref, wall_ref.at[r, t], e_send.at[t, k - 1], e_recv.at[t, k - 1], (flip(r, 2 * k), c))
            for k in range(1, 4)
        ]
        for t, ref in enumerate(weights)
    ]
    for copies in chip_copies:
        for copy in copies:
            copy.start()
    for copy in kept:
        copy.start()

    def pass_on(t):
        copies = []
        for k in range(4):
            there = flip(r, 2 * k)
            src = weights[t] if k == 0 else wall_ref.at[there, t]
            copies.append(send_to(src, wall_ref.at[there, t], s_send.at[t, k], s_recv.at[t, k], (flip(r, 1), c)))
        return copies

    def forward(t):
        for k, copy in enumerate(pass_on(t)):
            if k:
                chip_copies[t][k - 1].wait_recv()
            copy.start()

    slots, meta = tokens_meta(routes_ref, lengths_ref, rows, EXPERTS)
    slots_ref[...] = slots
    meta_ref[...] = meta
    sub = lax.broadcasted_iota(jnp.int32, (8, LANES), 0)
    firsts, end, ends = jnp.zeros((8, LANES), F32), 0, []
    for i in range(lengths_ref.shape[1]):
        firsts = jnp.where(sub == i, jnp.asarray(end, jnp.int32).astype(F32), firsts)
        end = end + lengths_ref[0, i]
        ends.append(end)
    angle = firsts * freq_ref[...]
    cos_first, sin_first = jnp.cos(angle), jnp.sin(angle)
    spot = lax.broadcasted_iota(jnp.int32, (rows, LANES), 0)
    cb, sb = jnp.ones((rows, LANES), F32), jnp.zeros((rows, LANES), F32)
    for i in range(1, len(ends)):
        cb = jnp.where(spot >= ends[i - 1], cos_first[i : i + 1], cb)
        sb = jnp.where(spot >= ends[i - 1], sin_first[i : i + 1], sb)
    cb, sb = jnp.where(spot >= end, 1.0, cb), jnp.where(spot >= end, 0.0, sb)
    sign = jnp.where(lane_iota((rows, LANES)) % 2 == 0, -1.0, 1.0)
    cos_out[...] = cos_ref[...] * cb + sin_ref[...] * sb
    sin_out[...] = (sin_ref[...] * cb - cos_ref[...] * sb) * sign

    def project(d):
        at = pl.ds(pl.multiple_of(d * local, LANES), local)
        x = xw[d].astype(F32)
        normed = (x * norm_rows(x) * again_ref[...]).astype(BF)
        proj = mm(normed, wq[...])
        cosine, sines = cos_out[at], sin_out[at]
        for part in range(2 * width // LANES):
            v = proj[:, part * LANES : (part + 1) * LANES]
            t = v * cosine + swap_pairs(v) * sines
            for half in range(2):
                head = 2 * part + half
                piece = t[:, half * HEAD_DIM : (half + 1) * HEAD_DIM].astype(BF)
                if head < heads:
                    piece = piece * jnp.asarray(1.0 / math.sqrt(HEAD_DIM), BF)
                qkv_ref[head, at] = piece
        for head in range(2 * heads, 3 * heads):
            qkv_ref[head, at] = proj[:, head * HEAD_DIM : (head + 1) * HEAD_DIM].astype(BF)

    x_step(1)
    for copy in wq_copies:
        copy.wait()
    for k in range(cols):
        if k > 1:
            x_step(k)

        def side(way, carry, k=k):
            d = c + k * (2 * way - 1)

            @pl.when((d >= 0) & (d < cols))
            def _():
                project(jnp.clip(d, 0, cols - 1))

            return carry

        lax.fori_loop(0, 2 if k else 1, side, 0)

    blocks = rows // Q_ROWS

    def one_head(h, carry):
        for i in range(blocks):
            at = slice(i * Q_ROWS, (i + 1) * Q_ROWS)
            length = (i + 1) * Q_ROWS
            s = mm(qkv_ref[h, at], qkv_ref[heads + h, :length], NT)
            begin = column(meta_ref, at, META_BEGIN).astype(jnp.int32)
            s = jnp.where(seen(begin, i * Q_ROWS, Q_ROWS, length), s, NEG)
            top = jnp.max(s, axis=1, keepdims=True)
            p = jnp.exp(s - top)
            total = jnp.sum(p, axis=1, keepdims=True)
            o = mm(p.astype(BF), qkv_ref[2 * heads + h, :length]) * (column(meta_ref, at, META_VALID) / total)
            o_ref[h, at] = o.astype(BF)
            lse_ref[h, at] = top + jnp.log(total)
        return carry

    lax.fori_loop(0, heads, one_head, 0)
    for d in range(cols):
        at = slice(d * local, (d + 1) * local)
        pack_heads(a_out.at[d], jnp.concatenate([o_ref[h, at] for h in range(heads)], axis=1))
    a_copies = to_cols(lambda d: a_out.at[d], a_in, c_send.at[2], c_recv.at[2], cols)
    for copy in a_copies:
        copy.start()
    a_in[c] = a_out[c]
    kept_out = [
        pltpu.make_async_copy(xw, xw_ref, local_sem.at[3]),
        pltpu.make_async_copy(wq, wq_out, local_sem.at[4]),
    ]
    for copy in kept_out:
        copy.start()
    for copy in wo_copies:
        copy.wait()
    forward(0)
    for copy in a_copies:
        copy.wait()
    parts = []
    for i in range(cols):
        parts.extend(unpack_heads(a_in[i], local))
    mixed = jnp.concatenate(parts, axis=1)
    mixed_ref[...] = mixed
    middle = x_ref[...].astype(F32) + mm(mixed, wo[...], NT)
    middle_ref[...] = middle
    n2_ref[...] = (middle * norm_rows(middle) * fgain_ref[...]).astype(BF)
    n_step, n_drain = gather_chain(n2_ref, n2w_ref, n_send, n_recv, cols)
    n_step(0)
    kept_late = [
        pltpu.make_async_copy(n2_ref, n2w_ref.at[c], local_sem.at[5]),
        pltpu.make_async_copy(wo, wo_out, local_sem.at[6]),
    ]
    for copy in kept_late:
        copy.start()
    for copy in prev_copies:
        copy.wait()
    prevw_ref[...] = prevw[...]
    n_step(1)
    forward(1)
    for k in range(2, cols):
        n_step(k)
    forward(2)
    x_drain()
    n_drain()
    for copies in chip_copies:
        for copy in copies:
            copy.wait_send()
    for t in range(3):
        for copy in pass_on(t):
            copy.wait()
    for copy in kept + kept_out + kept_late:
        copy.wait()


def first_step(cols, ranks, x, again, fgain, wq, wo, prev, routes, lengths, gate, up, down):
    local = x.shape[0]
    rows = local * cols
    heads, width = 3, 3 * HEAD_DIM
    experts, depth, ff = gate.shape
    spots = np.arange(rows, dtype=np.float64)[:, None]
    pair = np.arange(LANES) % HEAD_DIM // 2
    freq = np.exp(-(2.0 * pair / HEAD_DIM) * math.log(BASE))[None, :]
    tables = [np.cos(spots * freq), np.sin(spots * freq), freq]
    tables = [jnp.asarray(value.astype(np.float32)) for value in tables]
    vm = pl.BlockSpec(memory_space=pltpu.VMEM)
    dma = pltpu.SemaphoreType.DMA
    return pl.pallas_call(
        functools.partial(first_kernel, cols, ranks),
        out_shape=(
            jax.ShapeDtypeStruct((ranks, 3, experts, depth, ff), BF),
            jax.ShapeDtypeStruct((3 * heads, rows, HEAD_DIM), BF),
            jax.ShapeDtypeStruct((heads, rows, HEAD_DIM), BF),
            jax.ShapeDtypeStruct((heads, rows, 1), F32),
            jax.ShapeDtypeStruct((cols, local, D), BF),
            jax.ShapeDtypeStruct((D, 3 * width), BF),
            jax.ShapeDtypeStruct((D, D), BF),
            jax.ShapeDtypeStruct((rows, LANES), F32),
            jax.ShapeDtypeStruct((rows, LANES), F32),
            jax.ShapeDtypeStruct((rows, LANES), F32),
            jax.ShapeDtypeStruct((experts, rows), jnp.int32),
            jax.ShapeDtypeStruct((local, D), BF),
            jax.ShapeDtypeStruct((local, D), F32),
            jax.ShapeDtypeStruct((local, D), BF),
            jax.ShapeDtypeStruct((cols, local, D), BF),
            jax.ShapeDtypeStruct((cols, 16, local), BF),
        ),
        in_specs=[vm] * 7 + [pl.BlockSpec(memory_space=pltpu.SMEM)] + [vm] * 3 + [ANY] * 3,
        out_specs=(ANY, vm, vm, vm, ANY, ANY, ANY, vm, vm, vm, vm, vm, vm, vm, ANY, vm),
        scratch_shapes=[
            pltpu.VMEM((cols, local, D), BF),
            pltpu.VMEM((3, depth, width), BF),
            pltpu.VMEM((3, depth, width), BF),
            pltpu.VMEM((depth, width), BF),
            pltpu.VMEM((cols, depth, width), BF),
            pltpu.VMEM((D, 3 * width), BF),
            pltpu.VMEM((D, D), BF),
            pltpu.VMEM((cols, local * 3 // 2, LANES), BF),
            pltpu.VMEM((cols, local * 3 // 2, LANES), BF),
            pltpu.VMEM((cols, 16, local), BF),
            dma((7,)),
            dma((2, cols - 1)),
            dma((2, cols - 1)),
            dma((2, cols - 1)),
            dma((2, cols - 1)),
            dma((2,)),
            dma((2,)),
            dma((3, cols - 1)),
            dma((3, cols - 1)),
            dma((2, ranks - 1)),
            dma((2, ranks - 1)),
            dma((3, 3)),
            dma((3, 3)),
            dma((3, 4)),
            dma((3, 4)),
        ],
        compiler_params=pltpu.CompilerParams(
            vmem_limit_bytes=60 * MIB, collective_id=5, has_side_effects=True
        ),
        cost_estimate=pl.CostEstimate(
            flops=8 * heads * rows * rows * HEAD_DIM, bytes_accessed=40 * MIB, transcendentals=heads * rows * rows
        ),
        name="first_step",
    )(x, again, fgain, wq, wo, prev, routes, lengths, *tables, gate, up, down)


SENT_FIRST = 5


def on_device_heads(
    sizes,
    inputs,
    attn_gain,
    qkv_weight,
    out_weight,
    ffn_gain,
    router_weight,
    carry_weight,
    const_weight,
    const_vector,
    gate_weight,
    up_weight,
    down_weight,
    prev_logits,
    seq_lengths,
    expert_routes,
    cotangent,
):
    ranks, cols = sizes
    heads = HEADS // cols
    width = heads * HEAD_DIM
    row_index = lax.axis_index("row")
    row_total = expert_routes.shape[0]
    rw = jnp.concatenate(
        [
            router_weight.T,
            const_weight.transpose(0, 2, 1).reshape(4, D),
            const_vector,
            jnp.zeros((LANES - ROW_GAIN, D), BF),
        ],
        axis=0,
    )
    carry = jnp.pad(carry_weight, ((0, 16 - ROUTES), (0, LANES - ROUTES)))
    prev = jnp.pad(prev_logits, ((0, 16 - ROUTES), (0, 0)))
    attn_gain_row = attn_gain.astype(F32)[None, :]
    ffn_gain_row = ffn_gain.astype(F32)[None, :]

    (
        w_all,
        qkv,
        mixed_heads,
        lse,
        whole_in,
        qkv_own,
        out_t,
        cosine,
        sines,
        meta,
        slots,
        mixed,
        middle,
        n2,
        n2_whole,
        prev_whole,
    ) = first_step(
        cols,
        ranks,
        inputs,
        attn_gain_row,
        ffn_gain_row,
        qkv_weight,
        out_weight.T,
        prev,
        expert_routes.T,
        seq_lengths,
        gate_weight,
        up_weight,
        down_weight.transpose(0, 2, 1),
    )
    x, gu, mix, gates, cot_whole = experts_forward(
        cols, n2_whole.reshape(row_total, D), prev_whole, cotangent, rw, carry, meta, slots, w_all
    )
    gt, dots, mixsum, gown, sib = experts_backward(
        cols, cot_whole.reshape(row_total, D), mix, gates, meta, slots, w_all, x, gu
    )
    layer_out, resid, gm, og, small, prev_grad, hin0 = resid_step(
        cols,
        SENT_FIRST,
        gt,
        dots,
        mixsum,
        n2,
        middle,
        cotangent,
        meta,
        prev,
        rw,
        carry,
        ffn_gain_row,
        out_t,
        mixed,
        gown,
        sib,
    )
    input_grad, small_all, gain_all, qg, og_own, hin1 = finish_step(
        cols,
        ranks,
        SENT_FIRST,
        gm,
        qkv,
        meta,
        mixed_heads,
        lse,
        whole_in.reshape(row_total, D),
        attn_gain_row,
        qkv_own,
        cosine,
        sines,
        small,
        og,
        resid,
        inputs,
        gown,
        sib,
    )
    chip = row_index // 2
    grads = lax.dynamic_index_in_dim(gown, chip, 2, keepdims=False).astype(F32)
    grads = grads + lax.dynamic_index_in_dim(sib, chip, 2, keepdims=False).astype(F32)
    hin = jnp.concatenate([hin0, hin1], axis=0)
    grads = grads + jnp.sum(hin.astype(F32), axis=1)
    depth = qkv_weight.shape[0]
    return (
        layer_out,
        input_grad,
        gain_all[0],
        qg.transpose(1, 0, 2).reshape(depth, 3 * width),
        og_own.T,
        small_all[ROW_GAIN, :D],
        small_all[:ROUTES, :D].T,
        small_all[:ROUTES, D : D + ROUTES],
        small_all[ROW_CONST:ROW_VEC, :D].reshape(2, 2, D).transpose(0, 2, 1),
        small_all[ROW_VEC:ROW_GAIN, :D],
        grads[:, 0],
        grads[:, 1],
        grads[:, 2].transpose(0, 2, 1),
        prev_grad,
    )


def solution(mesh):
    sizes = (mesh.shape["row"], mesh.shape["col"])
    body = functools.partial(on_device_heads, sizes) if sizes == (8, 4) else on_device
    placed = (
        P(("row", "col"), None),
        P(),
        P("row", "col"),
        P("col", "row"),
        P(),
        P(),
        P(),
        P(),
        P(),
        P(None, "row", "col"),
        P(None, "row", "col"),
        P(None, "col", "row"),
        P(None, ("row", "col")),
        P("row", None),
        P("row", None),
        P(("row", "col"), None),
    )
    return jax.shard_map(
        body,
        mesh=mesh,
        in_specs=placed,
        out_specs=(
            P(("row", "col"), None),
            P(("row", "col"), None),
            P(),
            P("row", "col"),
            P("col", "row"),
            P(),
            P(),
            P(),
            P(),
            P(),
            P(None, "row", "col"),
            P(None, "row", "col"),
            P(None, "col", "row"),
            P(None, ("row", "col")),
        ),
        check_vma=False,
    )
```

```python
import functools
import math

import jax
import jax.numpy as jnp
import numpy as np
from jax import lax
from jax.experimental import pallas as pl
from jax.experimental.pallas import tpu as pltpu
from jax.sharding import PartitionSpec as P

D = 768
HEADS = 12
HEAD_DIM = 64
EXPERTS = 8
ROUTES = 12


EPS = 1e-06
BASE = 10000.0
NEG = -1e30
HIGH = lax.Precision.HIGHEST
CONTRACT_FIRST = (((0,), (0,)), ((), ()))
CONTRACT_LAST = (((1,), (1,)), ((), ()))


def rotate(block_value, positions, first_col, direction):
    row_count, col_count = block_value.shape
    column = first_col + jnp.arange(0, col_count, 2, dtype=jnp.int32)
    inner_col = column % D
    section = column // D
    head_pair = inner_col % HEAD_DIM // 2
    exponent = (2 * head_pair).astype(jnp.float32) / HEAD_DIM
    frequency = jnp.exp(-exponent * math.log(BASE))
    turned_on = (section < 2).astype(jnp.float32)
    angles = positions.astype(jnp.float32)[:, None] * (frequency * turned_on)[None, :]
    cosine = jnp.cos(angles)
    sines = direction * jnp.sin(angles)
    paired = block_value.reshape(row_count, col_count // 2, 2)
    first_part = paired[:, :, 0]
    second_part = paired[:, :, 1]
    rotated = jnp.stack(
        [first_part * cosine - second_part * sines, second_part * cosine + first_part * sines],
        axis=2,
    )
    return rotated.reshape(row_count, col_count)


def sequence_info(lengths_row, row_total):
    seq_count = lengths_row.shape[0]
    ends = jnp.cumsum(lengths_row)
    starts = ends - lengths_row
    token_place = jnp.arange(row_total, dtype=jnp.int32)
    seq_index = jnp.sum((token_place[:, None] >= ends[None, :]).astype(jnp.int32), axis=1)
    member = seq_index[:, None] == jnp.arange(seq_count, dtype=jnp.int32)[None, :]
    begin = jnp.sum(jnp.where(member, starts[None, :], 0), axis=1)
    return (seq_index, token_place - begin, seq_index < seq_count)


def partial_sums(term_value):
    return lax.psum_scatter(
        term_value.astype(jnp.bfloat16), "col", scatter_dimension=0, tiled=True
    ).astype(jnp.float32)


def whole_columns(part_value):
    return lax.all_gather(part_value, "col", axis=0, tiled=True)


def to_heads(block_value):
    return lax.all_to_all(block_value, "col", split_axis=0, concat_axis=1, tiled=True)


def to_features(block_value):
    return lax.all_to_all(block_value, "col", split_axis=1, concat_axis=0, tiled=True)


def key_scores(query_heads, key_block, query_seq, query_place, key_seq, key_place, score_scale):
    raw_scores = (
        jnp.einsum("qhd,khd->hqk", query_heads, key_block, preferred_element_type=jnp.float32)
        * score_scale
    )
    allowed = (query_seq[:, None] == key_seq[None, :]) & (
        key_place[None, :] <= query_place[:, None]
    )
    return (jnp.where(allowed[None], raw_scores, NEG), allowed)


def split_keys(key_values, seq_index, token_place, block_rows):
    count_blocks = key_values.shape[0] // block_rows
    blocks_kv = key_values.reshape(count_blocks, block_rows, 2, HEADS, HEAD_DIM)
    return (
        blocks_kv,
        seq_index.reshape(count_blocks, block_rows),
        token_place.reshape(count_blocks, block_rows),
    )


def attend_forward(
    queries, key_values, query_seq, query_place, seq_index, token_place, block_rows, score_scale
):
    local_rows = queries.shape[0]
    query_heads = queries.reshape(local_rows, HEADS, HEAD_DIM)
    key_items = split_keys(key_values, seq_index, token_place, block_rows)

    def max_step(running, block_items):
        running_max, running_sum = running
        kv_block, key_seq, key_place = block_items
        scores, allowed = key_scores(
            query_heads, kv_block[:, 0], query_seq, query_place, key_seq, key_place, score_scale
        )
        new_max = jnp.maximum(running_max, jnp.max(scores, axis=2))
        shifted = jnp.where(allowed[None], jnp.exp(scores - new_max[:, :, None]), 0.0)
        new_sum = running_sum * jnp.exp(running_max - new_max) + jnp.sum(shifted, axis=2)
        return ((new_max, new_sum), None)

    start_state = (
        jnp.full((HEADS, local_rows), NEG, jnp.float32),
        jnp.zeros((HEADS, local_rows), jnp.float32),
    )
    (final_max, final_sum), unused = lax.scan(max_step, start_state, key_items)
    log_total = final_max + jnp.log(final_sum)

    def out_step(running, block_items):
        kv_block, key_seq, key_place = block_items
        scores, allowed = key_scores(
            query_heads, kv_block[:, 0], query_seq, query_place, key_seq, key_place, score_scale
        )
        probs_low = jnp.exp(scores - log_total[:, :, None]).astype(jnp.bfloat16)
        return (
            running
            + jnp.einsum(
                "hqk,khd->qhd", probs_low, kv_block[:, 1], preferred_element_type=jnp.float32
            ),
            None,
        )

    attended, unused = lax.scan(
        out_step, jnp.zeros((local_rows, HEADS, HEAD_DIM), jnp.float32), key_items
    )
    return (attended.reshape(local_rows, D), log_total)


def attend_backward(
    queries,
    key_values,
    log_total,
    row_delta,
    grad_heads_in,
    query_seq,
    query_place,
    seq_index,
    token_place,
    block_rows,
    score_scale,
):
    local_rows = queries.shape[0]
    query_heads = queries.reshape(local_rows, HEADS, HEAD_DIM)
    grad_heads = grad_heads_in.reshape(local_rows, HEADS, HEAD_DIM)
    key_items = split_keys(key_values, seq_index, token_place, block_rows)

    def grad_step(running, block_items):
        kv_block, key_seq, key_place = block_items
        scores, allowed = key_scores(
            query_heads, kv_block[:, 0], query_seq, query_place, key_seq, key_place, score_scale
        )
        probs_full = jnp.exp(scores - log_total[:, :, None])
        probs_low = probs_full.astype(jnp.bfloat16)
        grad_probs = jnp.einsum(
            "qhd,khd->hqk", grad_heads, kv_block[:, 1], preferred_element_type=jnp.float32
        )
        grad_scores = (probs_full * (grad_probs - row_delta[:, :, None])).astype(jnp.bfloat16)
        new_running = (
            running
            + jnp.einsum(
                "hqk,khd->qhd", grad_scores, kv_block[:, 0], preferred_element_type=jnp.float32
            )
            * score_scale
        )
        grad_keys = (
            jnp.einsum("hqk,qhd->khd", grad_scores, query_heads, preferred_element_type=jnp.float32)
            * score_scale
        )
        grad_values = jnp.einsum(
            "hqk,qhd->khd", probs_low, grad_heads, preferred_element_type=jnp.float32
        )
        return (new_running, jnp.stack([grad_keys, grad_values], axis=1))

    grad_queries, grad_kv = lax.scan(
        grad_step, jnp.zeros((local_rows, HEADS, HEAD_DIM), jnp.float32), key_items
    )
    return (grad_queries.reshape(local_rows, D), grad_kv.reshape(key_values.shape[0], 2 * D))


def on_device(
    inputs,
    attn_gain,
    qkv_weight,
    out_weight,
    ffn_gain,
    router_weight,
    carry_weight,
    const_weight,
    const_vector,
    gate_weight,
    up_weight,
    down_weight,
    prev_logits,
    seq_lengths,
    expert_routes,
    cotangent,
):
    col_index = lax.axis_index("col")
    row_total = expert_routes.shape[0]
    local_rows = inputs.shape[0]
    capacity = row_total // 4
    block_rows = min(row_total, 512)
    score_scale = 1.0 / math.sqrt(HEAD_DIM)
    full_weights = (
        lax.all_gather(qkv_weight, "row", axis=0, tiled=True),
        lax.all_gather(out_weight, "row", axis=1, tiled=True),
        lax.all_gather(gate_weight, "row", axis=1, tiled=True),
        lax.all_gather(up_weight, "row", axis=1, tiled=True),
        lax.all_gather(down_weight, "row", axis=2, tiled=True),
    )
    qkv_full, out_full, gate_full, up_full, down_full = full_weights
    whole_in, whole_cot, whole_prev = (
        lax.all_gather(inputs, "col", axis=0, tiled=True),
        lax.all_gather(cotangent, "col", axis=0, tiled=True),
        lax.all_gather(prev_logits, "col", axis=1, tiled=True),
    )
    seq_index, positions, valid_all = sequence_info(seq_lengths[0], row_total)
    token_place = jnp.arange(row_total, dtype=jnp.int32)
    first_row = col_index * local_rows

    def own_rows(whole_value):
        return lax.dynamic_slice_in_dim(whole_value, first_row, local_rows, 0)

    query_seq = own_rows(seq_index)
    query_place = own_rows(token_place)
    query_pos = own_rows(positions)
    query_valid = own_rows(valid_all).astype(jnp.float32)[:, None]
    input_rows = whole_in.astype(jnp.float32)
    attn_gain_full = attn_gain.astype(jnp.float32)
    scale_attn = lax.rsqrt(jnp.mean(input_rows * input_rows, axis=1, keepdims=True) + EPS)
    normed1 = (input_rows * scale_attn * attn_gain_full).astype(jnp.bfloat16)
    projected = jnp.dot(normed1, qkv_full, preferred_element_type=jnp.float32)
    turned = rotate(projected, positions, col_index * projected.shape[1], 1.0).astype(jnp.bfloat16)
    token_qkv = to_heads(turned)
    queries = token_qkv[:, :D]
    key_values = lax.all_gather(token_qkv[:, D:], "col", axis=0, tiled=True)
    attended, log_total = attend_forward(
        queries, key_values, query_seq, query_place, seq_index, token_place, block_rows, score_scale
    )
    attn_tok = (attended * query_valid).astype(jnp.bfloat16)
    attn_feat = to_features(attn_tok)
    attn_out = partial_sums(jnp.dot(attn_feat, out_full, preferred_element_type=jnp.float32))
    input_local = inputs.astype(jnp.float32)
    middle = input_local + attn_out
    scale_ffn = lax.rsqrt(jnp.mean(middle * middle, axis=1, keepdims=True) + EPS)
    ffn_gain_full = ffn_gain.astype(jnp.float32)
    normed2_local = (middle * scale_ffn * ffn_gain_full).astype(jnp.bfloat16)
    normed2 = whole_columns(normed2_local)
    carry_full = carry_weight.astype(jnp.float32)
    prev_rows = whole_prev.astype(jnp.float32).T
    route_hot = (
        expert_routes[:, :, None] == jnp.arange(ROUTES, dtype=jnp.int32)[None, None, :]
    ).astype(jnp.float32)
    logits = jnp.dot(normed2, router_weight, preferred_element_type=jnp.float32) + jnp.dot(
        prev_rows, carry_full, precision=HIGH
    )
    picked = jnp.sum(route_hot * logits[:, None, :], axis=2)
    gate_values = jax.nn.softmax(picked, axis=1)
    flat_route = expert_routes.reshape(-1)
    route_hits = (flat_route[:, None] == jnp.arange(EXPERTS, dtype=jnp.int32)[None, :]).astype(
        jnp.int32
    )
    slot_index = jnp.sum((jnp.cumsum(route_hits, axis=0) - 1) * route_hits, axis=1)
    dump_slot = EXPERTS * capacity
    target = jnp.where(flat_route < EXPERTS, flat_route * capacity + slot_index, dump_slot)
    slot_owner = (
        jnp.full((dump_slot + 1,), row_total, jnp.int32)
        .at[target]
        .set(jnp.arange(2 * row_total, dtype=jnp.int32) // 2)[:dump_slot]
    )
    slot_gate = (
        jnp.zeros((dump_slot + 1,), jnp.float32)
        .at[target]
        .set(gate_values.reshape(-1))[:dump_slot]
        .reshape(EXPERTS, capacity, 1)
    )
    zero_row = jnp.zeros((1, D), jnp.bfloat16)
    expert_in = jnp.concatenate([normed2, zero_row], axis=0)[slot_owner].reshape(
        EXPERTS, capacity, D
    )
    gate_pre = jnp.einsum("ecd,edf->ecf", expert_in, gate_full, preferred_element_type=jnp.float32)
    up_pre = jnp.einsum("ecd,edf->ecf", expert_in, up_full, preferred_element_type=jnp.float32)
    sigmoid_gate = jax.nn.sigmoid(gate_pre)
    activated = gate_pre * sigmoid_gate
    hidden = (activated * up_pre).astype(jnp.bfloat16)
    expert_out = jnp.einsum("ecf,efd->ecd", hidden, down_full, preferred_element_type=jnp.float32)
    out_rows = jnp.concatenate(
        [expert_out.reshape(dump_slot, D), jnp.zeros((1, D), jnp.float32)], axis=0
    )
    chosen_out = out_rows[target].reshape(row_total, 2, D)
    cot_rows = whole_cot.astype(jnp.float32)
    ffn_mix = jnp.sum(gate_values[:, :, None] * chosen_out, axis=1)
    ffn_dots = jnp.sum(cot_rows[:, None, :] * chosen_out, axis=2)
    mix_local = partial_sums(ffn_mix)
    normed_local = normed2_local.astype(jnp.float32)
    vector_full = const_vector.astype(jnp.float32)
    routes_local = own_rows(expert_routes)
    gates_local = own_rows(gate_values)
    hot_local = own_rows(route_hot)
    copy_hit = (routes_local == EXPERTS + 1).astype(jnp.float32)
    const_hit = (
        routes_local[:, :, None] == (EXPERTS + 2 + jnp.arange(2, dtype=jnp.int32))[None, None, :]
    ).astype(jnp.float32)
    copy_share = jnp.sum(gates_local * copy_hit, axis=1)
    const_share = jnp.sum(gates_local[:, :, None] * const_hit, axis=1)
    const_alpha = jax.nn.softmax(
        jnp.einsum("td,jdk->tjk", normed2_local, const_weight, preferred_element_type=jnp.float32),
        axis=2,
    )
    keep_share = copy_share + jnp.sum(const_share * const_alpha[:, :, 0], axis=1)
    local_mix = keep_share[:, None] * normed_local + jnp.dot(
        const_share * const_alpha[:, :, 1], vector_full, precision=HIGH
    )
    layer_out = (middle + mix_local + local_mix).astype(jnp.bfloat16)
    qkv_full, out_full, gate_full, up_full, down_full = full_weights
    ffn_total = lax.psum(ffn_dots, "col")
    ffn_local = own_rows(ffn_total)
    cot_local = cotangent.astype(jnp.float32)
    dot_keep = jnp.sum(cot_local * normed_local, axis=1)
    dot_vector = jnp.dot(cot_local, vector_full.T, precision=HIGH)
    const_dots = const_alpha[:, :, 0] * dot_keep[:, None] + const_alpha[:, :, 1] * dot_vector
    grad_gates = (
        ffn_local
        + copy_hit * dot_keep[:, None]
        + jnp.sum(const_hit * const_dots[:, None, :], axis=2)
    )
    grad_picked = gates_local * (
        grad_gates - jnp.sum(gates_local * grad_gates, axis=1, keepdims=True)
    )
    grad_logits = jnp.sum(hot_local * grad_picked[:, :, None], axis=1)
    prev_local = prev_logits.astype(jnp.float32).T
    router_grad = lax.dot_general(normed_local, grad_logits, CONTRACT_FIRST, precision=HIGH)
    carry_grad = lax.dot_general(prev_local, grad_logits, CONTRACT_FIRST, precision=HIGH)
    prev_grad = lax.dot_general(carry_full, grad_logits, CONTRACT_LAST, precision=HIGH)
    grad_alpha_keep = const_share * dot_keep[:, None]
    grad_alpha_vector = const_share * dot_vector
    alpha_mean = const_alpha[:, :, 0] * grad_alpha_keep + const_alpha[:, :, 1] * grad_alpha_vector
    grad_alpha_logits = jnp.stack(
        [
            const_alpha[:, :, 0] * (grad_alpha_keep - alpha_mean),
            const_alpha[:, :, 1] * (grad_alpha_vector - alpha_mean),
        ],
        axis=2,
    )
    const_grad = jnp.einsum("td,tjk->jdk", normed_local, grad_alpha_logits, precision=HIGH)
    vector_grad = lax.dot_general(
        const_share * const_alpha[:, :, 1], cot_local, CONTRACT_FIRST, precision=HIGH
    )
    router_full = router_weight.astype(jnp.float32)
    const_full = const_weight.astype(jnp.float32)
    grad_normed_local = (
        keep_share[:, None] * cot_local
        + lax.dot_general(grad_logits, router_full, CONTRACT_LAST, precision=HIGH)
        + jnp.einsum("tjk,jdk->td", grad_alpha_logits, const_full, precision=HIGH)
    )
    cot_in = jnp.concatenate([whole_cot, zero_row], axis=0)[slot_owner].reshape(
        EXPERTS, capacity, D
    )
    grad_expert = (slot_gate * cot_in.astype(jnp.float32)).astype(jnp.bfloat16)
    down_grad = jnp.einsum("ecf,ecd->efd", hidden, grad_expert, preferred_element_type=jnp.float32)
    grad_hidden = jnp.einsum(
        "ecd,efd->ecf", grad_expert, down_full, preferred_element_type=jnp.float32
    )
    grad_gate_pre = (
        grad_hidden * up_pre * sigmoid_gate * (1.0 + gate_pre * (1.0 - sigmoid_gate))
    ).astype(jnp.bfloat16)
    grad_up_pre = (grad_hidden * activated).astype(jnp.bfloat16)
    gate_grad = jnp.einsum(
        "ecd,ecf->edf", expert_in, grad_gate_pre, preferred_element_type=jnp.float32
    )
    up_grad = jnp.einsum("ecd,ecf->edf", expert_in, grad_up_pre, preferred_element_type=jnp.float32)
    grad_expert_in = jnp.einsum(
        "ecf,edf->ecd", grad_gate_pre, gate_full, preferred_element_type=jnp.float32
    ) + jnp.einsum("ecf,edf->ecd", grad_up_pre, up_full, preferred_element_type=jnp.float32)
    grad_slots = jnp.concatenate(
        [grad_expert_in.reshape(dump_slot, D), jnp.zeros((1, D), jnp.float32)], axis=0
    )
    grad_tokens = jnp.sum(grad_slots[target].reshape(row_total, 2, D), axis=1)
    grad_normed = partial_sums(grad_tokens) + grad_normed_local
    gained_ffn = grad_normed * ffn_gain_full
    ffn_dots_rows = jnp.sum(gained_ffn * middle, axis=1, keepdims=True)
    grad_middle = scale_ffn * gained_ffn - middle * scale_ffn**3 * (ffn_dots_rows / D)
    ffn_gain_grad = jnp.sum(grad_normed * middle * scale_ffn, axis=0)
    grad_resid = cot_local + grad_middle
    branch_cot = whole_columns(grad_resid.astype(jnp.bfloat16))
    out_grad = lax.dot_general(
        attn_feat, branch_cot, CONTRACT_FIRST, preferred_element_type=jnp.float32
    )
    grad_mixed = lax.dot_general(
        branch_cot, out_full, CONTRACT_LAST, preferred_element_type=jnp.float32
    )
    grad_tok = to_heads(grad_mixed.astype(jnp.bfloat16))
    grad_heads_in = (grad_tok.astype(jnp.float32) * query_valid).astype(jnp.bfloat16)
    row_delta = jnp.sum(
        grad_heads_in.astype(jnp.float32).reshape(local_rows, HEADS, HEAD_DIM)
        * attended.reshape(local_rows, HEADS, HEAD_DIM),
        axis=2,
    ).T
    grad_queries, grad_kv = attend_backward(
        queries,
        key_values,
        log_total,
        row_delta,
        grad_heads_in,
        query_seq,
        query_place,
        seq_index,
        token_place,
        block_rows,
        score_scale,
    )
    grad_kv_local = lax.psum_scatter(
        grad_kv.astype(jnp.bfloat16), "col", scatter_dimension=0, tiled=True
    ).astype(jnp.float32)
    grad_turned = jnp.concatenate([grad_queries, grad_kv_local], axis=1)
    grad_proj_tok = rotate(grad_turned, query_pos, 0, -1.0).astype(jnp.bfloat16)
    grad_projected = to_features(grad_proj_tok)
    qkv_grad = lax.dot_general(
        normed1, grad_projected, CONTRACT_FIRST, preferred_element_type=jnp.float32
    )
    grad_normed1 = partial_sums(
        lax.dot_general(grad_projected, qkv_full, CONTRACT_LAST, preferred_element_type=jnp.float32)
    )
    scale_attn_local = own_rows(scale_attn)
    gained_attn = grad_normed1 * attn_gain_full
    attn_dots_rows = jnp.sum(gained_attn * input_local, axis=1, keepdims=True)
    input_grad = (
        grad_resid
        + scale_attn_local * gained_attn
        - input_local * scale_attn_local**3 * (attn_dots_rows / D)
    )
    attn_gain_grad = jnp.sum(grad_normed1 * input_local * scale_attn_local, axis=0)
    qkv_grad, out_grad, gate_grad, up_grad, down_grad = (
        lax.psum_scatter(
            qkv_grad.astype(jnp.bfloat16), "row", scatter_dimension=0, tiled=True
        ).astype(jnp.float32),
        lax.psum_scatter(
            out_grad.astype(jnp.bfloat16), "row", scatter_dimension=1, tiled=True
        ).astype(jnp.float32),
        lax.psum_scatter(
            gate_grad.astype(jnp.bfloat16), "row", scatter_dimension=1, tiled=True
        ).astype(jnp.float32),
        lax.psum_scatter(
            up_grad.astype(jnp.bfloat16), "row", scatter_dimension=1, tiled=True
        ).astype(jnp.float32),
        lax.psum_scatter(
            down_grad.astype(jnp.bfloat16), "row", scatter_dimension=2, tiled=True
        ).astype(jnp.float32),
    )
    attn_gain_grad, ffn_gain_grad, router_grad, carry_grad, const_grad, vector_grad = lax.psum(
        (attn_gain_grad, ffn_gain_grad, router_grad, carry_grad, const_grad, vector_grad),
        ("row", "col"),
    )
    return (
        layer_out,
        input_grad,
        attn_gain_grad,
        qkv_grad,
        out_grad,
        ffn_gain_grad,
        router_grad,
        carry_grad,
        const_grad,
        vector_grad,
        gate_grad,
        up_grad,
        down_grad,
        prev_grad,
    )


BF = jnp.bfloat16
F32 = jnp.float32
LANES = 128
NN = (((1,), (0,)), ((), ()))
NT = (((1,), (1,)), ((), ()))
TN = (((0,), (0,)), ((), ()))
ROW_CONST = 12
ROW_VEC = 16
ROW_GAIN = 18
SMALL_ROWS = 24
Q_ROWS = 256
MIB = 1 << 20


def mm(a, b, dims=NN):
    return lax.dot_general(a, b, dims, preferred_element_type=F32)


def lane_iota(shape):
    return lax.broadcasted_iota(jnp.int32, shape, len(shape) - 1)


def whole(shape):
    return pl.BlockSpec(tuple(shape), lambda *_: (0,) * len(shape), pipeline_mode=pl.Buffered(1))


def swap_pairs(v):
    even = lane_iota(v.shape) % 2 == 0
    return jnp.where(even, pltpu.roll(v, LANES - 1, 1), pltpu.roll(v, 1, 1))


def norm_rows(x):
    return lax.rsqrt(jnp.mean(x * x, axis=1, keepdims=True) + EPS)


def seen(begin, first, rows, length):
    u = lax.broadcasted_iota(jnp.int32, (rows, length), 1)
    t = lax.broadcasted_iota(jnp.int32, (rows, length), 0) + first
    return (u >= begin) & (u <= t)


def gate_lanes(logits, meta):
    lane = lane_iota(logits.shape)
    hit = (pltpu.roll(meta, LANES - META_HIT, 1) > 0.0) & (lane < ROUTES)
    held = jnp.where(hit, logits, NEG)
    e = jnp.where(hit, jnp.exp(held - jnp.max(held, axis=1, keepdims=True)), 0.0)
    return e / jnp.sum(e, axis=1, keepdims=True)


MESH = pl.DeviceIdType.MESH
ANY = pl.BlockSpec(memory_space=pl.ANY)


def place():
    return lax.axis_index("row"), lax.axis_index("col")


def flip(index, mask):
    for bit in (1, 2, 4):
        if mask & bit:
            index = index + bit - 2 * bit * (index // bit % 2)
    return index


def greet(devices):
    barrier = pltpu.get_barrier_semaphore()
    for device in devices:
        pl.semaphore_signal(barrier, inc=1, device_id=device, device_id_type=MESH)
    pl.semaphore_wait(barrier, len(devices))


def send_to(src, dst, send, recv, device):
    return pltpu.make_async_remote_copy(
        src_ref=src, dst_ref=dst, send_sem=send, recv_sem=recv, device_id=device, device_id_type=MESH
    )


def col_peers(n):
    r, c = place()
    return [(r, (c + k) % n) for k in range(1, n)]


def gather_chain(own, dst, send, recv, n):
    r, c = place()

    def right(k):
        i = jnp.maximum(c - k, 0)
        src = own if k == 0 else dst.at[i]
        return send_to(src, dst.at[i], send.at[0, k], recv.at[0, k], (r, jnp.minimum(c + 1, n - 1)))

    def left(k):
        i = jnp.minimum(c + k, n - 1)
        src = own if k == 0 else dst.at[i]
        return send_to(src, dst.at[i], send.at[1, k], recv.at[1, k], (r, jnp.maximum(c - 1, 0)))

    def step(k):
        if k > 0:

            @pl.when(c >= k)
            def _():
                right(k - 1).wait_recv()

            @pl.when(c + k < n)
            def _():
                left(k - 1).wait_recv()

        if k < n - 1:

            @pl.when((c >= k) & (c + 1 < n))
            def _():
                right(k).start()

            @pl.when((c + k < n) & (c >= 1))
            def _():
                left(k).start()

    def drain():
        for k in range(n - 1):

            @pl.when((c >= k) & (c + 1 < n))
            def _():
                right(k).wait_send()

            @pl.when((c + k < n) & (c >= 1))
            def _():
                left(k).wait_send()

    return step, drain


def reduce_chain(own, out, arrived, send, recv, n):
    r, c = place()

    def right(k):
        return send_to(out.at[0, k], arrived.at[0, k], send.at[0, k], recv.at[0, k], (r, jnp.minimum(c + 1, n - 1)))

    def left(k):
        return send_to(out.at[1, k], arrived.at[1, k], send.at[1, k], recv.at[1, k], (r, jnp.maximum(c - 1, 0)))

    def slot(s):
        if s == n - 1:

            @pl.when(c >= 1)
            def _():
                right(n - 1 - c).wait_recv()

            @pl.when(c <= n - 2)
            def _():
                left(c).wait_recv()

            return

        @pl.when(c <= s)
        def _():
            k = jnp.maximum(s - c, 0)

            @pl.when(c >= 1)
            def _():
                right(k).wait_recv()
                out[0, k] = (own(n - 1 - k).astype(F32) + arrived[0, k].astype(F32)).astype(BF)

            @pl.when(c == 0)
            def _():
                out[0, k] = own(n - 1 - k).astype(BF)

            right(k).start()

        @pl.when(n - 1 - c <= s)
        def _():
            k = jnp.maximum(s - (n - 1 - c), 0)

            @pl.when(c <= n - 2)
            def _():
                left(k).wait_recv()
                out[1, k] = (own(k).astype(F32) + arrived[1, k].astype(F32)).astype(BF)

            @pl.when(c == n - 1)
            def _():
                out[1, k] = own(k).astype(BF)

            left(k).start()

    def total(dst):
        dst[...] = own(c).astype(F32)

        @pl.when(c >= 1)
        def _():
            dst[...] += arrived[0, n - 1 - c].astype(F32)

        @pl.when(c <= n - 2)
        def _():
            dst[...] += arrived[1, c].astype(F32)

    def drain():
        for k in range(n - 1):

            @pl.when(c < n - 1 - k)
            def _():
                right(k).wait_send()

            @pl.when(c > k)
            def _():
                left(k).wait_send()

    return slot, total, drain


def chain_scratch(n, rows):
    return [
        pltpu.VMEM((2, n - 1, rows, D), BF),
        pltpu.VMEM((2, n - 1, rows, D), BF),
        pltpu.SemaphoreType.DMA((2, n - 1)),
        pltpu.SemaphoreType.DMA((2, n - 1)),
    ]


def slot_rows(slots_ref, e, capacity):
    rows = slots_ref.shape[1]
    spots = lax.broadcasted_iota(jnp.int32, (capacity, rows), 0)
    return jnp.where(spots == slots_ref[pl.ds(e, 1)], 1.0, 0.0).astype(BF)


def slot_gates(one, gates_ref, e):
    sg = mm(one, gates_ref[...])
    return jnp.sum(jnp.where(lane_iota(sg.shape) % LANES == e, sg, 0.0), axis=1, keepdims=True)


def combine(meta_ref, y_ref, d, local):
    experts, capacity, width = y_ref.shape
    at = slice(d * local, (d + 1) * local)
    lane = lane_iota((local, capacity)).astype(F32)
    ones = [jnp.where(lane == column(meta_ref, at, e), 1.0, 0.0).astype(BF) for e in range(experts)]
    return mm(jnp.concatenate(ones, axis=1), y_ref[...].reshape(experts * capacity, width)).astype(BF)


META_HIT, META_BEGIN, META_VALID = 8, 20, 21
EARLY = 3
SENT_SOON, SENT_NEXT = 2, 3


def column(ref, at, lane):
    return ref[at, lane : lane + 1]


def start_all(copies):
    for copy in copies:
        copy.start()


def wait_all(copies):
    for copy in copies:
        copy.wait()


def moves(pairs, sem):
    return [pltpu.make_async_copy(src, dst, sem.at[i]) for i, (src, dst) in enumerate(pairs)]


def pack_head(value):
    half = value.shape[0] // 2
    return jnp.concatenate([value[:half], value[half:]], axis=1)


def unpack_head(packed):
    return jnp.concatenate([packed[:, :HEAD_DIM], packed[:, HEAD_DIM:]], axis=0)


def to_rows(src_of, dst, send, recv, ranks):
    r, c = place()
    copies = []
    for m in range(1, ranks):
        there = flip(r, m)
        copies.append(send_to(src_of(there), dst.at[r], send.at[m - 1], recv.at[m - 1], (there, c)))
    return copies


def to_cols(src_of, dst, send, recv, n):
    r, c = place()
    copies = []
    for k in range(1, n):
        there = (c + k) % n
        copies.append(send_to(src_of(there), dst.at[c], send.at[k - 1], recv.at[k - 1], (r, there)))
    return copies


def to_chips(src_of, dst, send, recv):
    r, c = place()
    return [
        send_to(src_of(flip(r // 2, k)), dst.at[k - 1], send.at[k - 1], recv.at[k - 1], (flip(r, 2 * k), c))
        for k in range(1, 4)
    ]


def all_sum(ref, count):
    total = ref[0].astype(F32)
    for i in range(1, count):
        total = total + ref[i].astype(F32)
    return total


def tokens_meta(routes_ref, lengths_ref, rows, experts):
    kinds = lax.broadcasted_iota(jnp.int32, (16, rows), 0)
    hits = jnp.where((kinds == routes_ref[0:1]) | (kinds == routes_ref[1:2]), 1.0, 0.0)
    step = 256
    earlier = lax.broadcasted_iota(jnp.int32, (step, step), 0) < lax.broadcasted_iota(
        jnp.int32, (step, step), 1
    )
    earlier = jnp.where(earlier, 1.0, 0.0).astype(BF)
    counts, running = [], jnp.zeros((16, 1), F32)
    for b in range(rows // step):
        block = hits[:, b * step : (b + 1) * step]
        counts.append(mm(block.astype(BF), earlier) + running)
        running = running + jnp.sum(block, axis=1, keepdims=True)
    slots = jnp.where(hits > 0.0, jnp.concatenate(counts, axis=1), -1.0)[:experts]
    spot = lax.broadcasted_iota(jnp.int32, (8, rows), 1)
    begin, end = jnp.zeros((8, rows), F32), 0
    for i in range(lengths_ref.shape[1]):
        end = end + lengths_ref[0, i]
        begin = jnp.where(spot >= end, end.astype(F32), begin)
    valid = jnp.where(spot < end, 1.0, 0.0)
    tail = jnp.where(lax.broadcasted_iota(jnp.int32, (8, rows), 0) == 0, begin, valid)
    spare = jnp.zeros((LANES - experts - 12 - 8, rows), F32)
    meta = jnp.concatenate([slots, hits[:12], tail, spare], axis=0).T
    return slots.astype(jnp.int32), meta


def first_kernel(
    cols,
    ranks,
    x_ref,
    cot_ref,
    router_ref,
    const_ref,
    vector_ref,
    again_ref,
    fgain_ref,
    carry_ref,
    wq_ref,
    wo_ref,
    prev_ref,
    routes_ref,
    lengths_ref,
    cos_ref,
    sin_ref,
    freq_ref,
    gate_ref,
    up_ref,
    down_ref,
    wall_ref,
    qkv_out,
    o_out,
    lse_out,
    xw_out,
    wq_out,
    wo_out,
    cos_out,
    sin_out,
    meta_out,
    slots_ref,
    mixed_out,
    middle_out,
    n2w_ref,
    prevw_out,
    cota_ref,
    rw_out,
    carry_out,
    xw,
    q_parts,
    q_land,
    o_parts,
    o_land,
    wq,
    wo,
    a_send,
    a_land,
    prev_s,
    prevw,
    qkv_s,
    o_s,
    lse_s,
    cos_s,
    sin_s,
    meta_s,
    mixed_s,
    middle_s,
    n2_s,
    w_s,
    local_sem,
    x_send,
    x_recv,
    n_send,
    n_recv,
    t_send,
    t_recv,
    q_send,
    q_recv,
    c_send,
    c_recv,
    r_send,
    r_recv,
    e_send,
    e_recv,
    d_send,
    d_recv,
    s_send,
    s_recv,
    h_send,
    h_recv,
):
    r, c = place()
    heads = 3
    local = x_ref.shape[0]
    rows = local * cols
    width = heads * HEAD_DIM
    depth = D // ranks
    odd, high = c % 2, c // 2
    again = again_ref[...].astype(F32).reshape(1, D)
    fgain = fgain_ref[...].astype(F32).reshape(1, D)
    greet(col_peers(cols) + [(flip(r, m), c) for m in (1, 2, 4, 6)])

    for s in range(3):
        q_parts[s] = wq_ref[:, s * width : (s + 1) * width]
    q_copies = [
        send_to(q_parts.at[1], q_land.at[(c + 1) // 2], q_send.at[0], q_recv.at[0], (r, flip(c, 1))),
        send_to(q_parts.at[2 - 2 * odd], q_land.at[2 * high], q_send.at[1], q_recv.at[1], (r, flip(c, 2))),
    ]
    start_all(q_copies)
    o_parts[...] = wo_ref[...].astype(F32).T.astype(BF)
    prev_s[...] = jnp.concatenate([prev_ref[...].astype(F32), jnp.zeros((16 - ROUTES, local), F32)], axis=0).astype(BF)
    o_copies = to_cols(lambda d: o_parts, o_land, c_send.at[0], c_recv.at[0], cols)
    prev_copies = to_cols(lambda d: prev_s, prevw, c_send.at[1], c_recv.at[1], cols)
    x_step, x_drain = gather_chain(x_ref, xw, x_send, x_recv, cols)
    x_step(0)
    start_all(o_copies + prev_copies)
    q_land[(c + 1) // 2] = q_parts[2 * odd]
    o_land[c] = o_parts[...]
    prevw[c] = prev_s[...]
    xw[c] = x_ref[...]

    def rows_at(d):
        return pl.ds(pl.multiple_of(d * depth, 16), depth)

    def push(ref, at):
        here = ref.at[rows_at(r)]
        return [
            send_to(here, here, r_send.at[at, k - 1], r_recv.at[at, k - 1], (flip(r, 2 * k), c))
            for k in range(1, 4)
        ]

    def hand(ref, at):
        copies = []
        for k in range(4):
            here = ref.at[rows_at(flip(r, 2 * k))]
            copies.append(send_to(here, here, r_send.at[at, 3 + k], r_recv.at[at, 3 + k], (flip(r, 1), c)))
        return copies

    wait_all(q_copies)
    wq[rows_at(r)] = jnp.concatenate([q_land[i] for i in range(3)], axis=1)
    wq_push, wq_hand = push(wq, 0), hand(wq, 0)
    start_all(wq_push)
    wait_all(o_copies)
    wo[rows_at(r)] = jnp.concatenate([o_land[i] for i in range(cols)], axis=1)
    wo_push, wo_hand = push(wo, 1), hand(wo, 1)
    start_all(wo_push)

    weights = (gate_ref, up_ref, down_ref)
    half = gate_ref.shape[0] // 2
    held = moves([(ref, w_s.at[t]) for t, ref in enumerate(weights)], local_sem)
    kept = moves([(w_s.at[t], wall_ref.at[t, :, rows_at(r)]) for t in range(3)], local_sem)

    def to_near(t):
        dst = wall_ref.at[t, :, rows_at(r)]
        return [
            send_to(weights[t], dst, e_send.at[t, k - 1], e_recv.at[t, k - 1], (flip(r, 2 * k), c))
            for k in (1, 2)
        ]

    def to_far(t):
        copies = []
        for k in (1, 2):
            here = wall_ref.at[t, pl.ds((k - 1) * half, half), rows_at(flip(r, 2 * k))]
            copies.append(send_to(here, here, d_send.at[t, k - 1], d_recv.at[t, k - 1], (flip(r, 6 - 2 * k), c)))
        return copies

    def to_other_core(t):
        copies = []
        for k in range(4):
            here = wall_ref.at[t, :, rows_at(flip(r, 2 * k))]
            src = weights[t] if k == 0 else here
            copies.append(send_to(src, here, s_send.at[t, k], s_recv.at[t, k], (flip(r, 1), c)))
        return copies

    def relay(t):
        for near, far in zip(to_near(t), to_far(t)):
            near.wait_recv()
            far.start()

    def hand_over(t):
        for far in to_far(t):
            far.wait_recv()
        start_all(to_other_core(t))

    for t in range(3):
        start_all(to_near(t))
    start_all(held)

    small = [ref[...].astype(F32) for ref in (router_ref, const_ref.at[0], const_ref.at[1], vector_ref)]
    small += [again, fgain, jnp.zeros((LANES - ROW_GAIN - 2, D), F32)]
    rw_out[...] = jnp.concatenate(small, axis=0).astype(BF)
    carry = jnp.concatenate([carry_ref[...].astype(F32), jnp.zeros((ROUTES, LANES - ROUTES), F32)], axis=1)
    carry_out[...] = jnp.concatenate([carry, jnp.zeros((16 - ROUTES, LANES), F32)], axis=0).astype(BF)
    slots, meta = tokens_meta(routes_ref, lengths_ref, rows, EXPERTS)
    slots_ref[...] = slots
    meta_s[...] = meta
    sub = lax.broadcasted_iota(jnp.int32, (8, LANES), 0)
    firsts, end, ends = jnp.zeros((8, LANES), F32), 0, []
    for i in range(lengths_ref.shape[1]):
        firsts = jnp.where(sub == i, jnp.asarray(end, jnp.int32).astype(F32), firsts)
        end = end + lengths_ref[0, i]
        ends.append(end)
    angle = firsts * freq_ref[...]
    cos_first, sin_first = jnp.cos(angle), jnp.sin(angle)
    spot = lax.broadcasted_iota(jnp.int32, (rows, LANES), 0)
    cb, sb = jnp.ones((rows, LANES), F32), jnp.zeros((rows, LANES), F32)
    for i in range(1, len(ends)):
        cb = jnp.where(spot >= ends[i - 1], cos_first[i : i + 1], cb)
        sb = jnp.where(spot >= ends[i - 1], sin_first[i : i + 1], sb)
    cb, sb = jnp.where(spot >= end, 1.0, cb), jnp.where(spot >= end, 0.0, sb)
    sign = jnp.where(lane_iota((rows, LANES)) % 2 == 0, -1.0, 1.0)
    cos_s[...] = cos_ref[...] * cb + sin_ref[...] * sb
    sin_s[...] = (sin_ref[...] * cb - cos_ref[...] * sb) * sign
    lse_s[...] = jnp.zeros_like(lse_s)

    def project(d):
        at = pl.ds(pl.multiple_of(d * local, LANES), local)
        x = xw[d].astype(F32)
        normed = (x * norm_rows(x) * again).astype(BF)
        proj = mm(normed, wq[...])
        cosine, sines = cos_s[at], sin_s[at]
        for part in range(2 * width // LANES):
            v = proj[:, part * LANES : (part + 1) * LANES]
            t = v * cosine + swap_pairs(v) * sines
            for side in range(2):
                head = 2 * part + side
                piece = t[:, side * HEAD_DIM : (side + 1) * HEAD_DIM].astype(BF)
                if head < heads:
                    piece = piece * jnp.asarray(1.0 / math.sqrt(HEAD_DIM), BF)
                qkv_s[head, at] = piece
        for head in range(2 * heads, 3 * heads):
            qkv_s[head, at] = proj[:, head * HEAD_DIM : (head + 1) * HEAD_DIM].astype(BF)

    def project_at(k):
        def side(way, carry):
            d = c + k * (2 * way - 1)

            @pl.when((d >= 0) & (d < cols))
            def _():
                project(jnp.clip(d, 0, cols - 1))

            return carry

        lax.fori_loop(0, 2 if k else 1, side, 0)

    early = local // EARLY
    cot_step, cot_drain = gather_chain(cot_ref.at[pl.ds(0, early)], cota_ref, t_send, t_recv, cols)
    cot_kept = moves([(cot_ref.at[pl.ds(0, early)], cota_ref.at[c])], local_sem.at[pl.ds(3, 1)])

    wait_all(held)
    start_all(kept)
    x_step(1)
    for copy in wq_push:
        copy.wait_recv()
    start_all(wq_hand)
    x_step(2)
    for copy in wo_push:
        copy.wait_recv()
    start_all(wo_hand)
    wait_all(wq_hand)
    project_at(0)
    project_at(1)
    project_at(2)
    relay(0)
    x_step(3)
    cot_step(0)
    start_all(cot_kept)
    project_at(3)
    cot_step(1)

    blocks = rows // Q_ROWS

    def head_copies(h):
        copies = []
        for k in range(1, cols):
            there = (c + k) % cols
            copies.append(
                send_to(a_send.at[there, h], a_land.at[c, h], h_send.at[h, k - 1], h_recv.at[h, k - 1], (r, there))
            )
        return copies

    def one_head(h, carry):
        for i in range(blocks):
            at = slice(i * Q_ROWS, (i + 1) * Q_ROWS)
            length = (i + 1) * Q_ROWS
            s = mm(qkv_s[h, at], qkv_s[heads + h, :length], NT)
            begin = column(meta_s, at, META_BEGIN).astype(jnp.int32)
            s = jnp.where(seen(begin, i * Q_ROWS, Q_ROWS, length), s, NEG)
            top = jnp.max(s, axis=1, keepdims=True)
            p = jnp.exp(s - top)
            total = jnp.sum(p, axis=1, keepdims=True)
            o = mm(p.astype(BF), qkv_s[2 * heads + h, :length]) * (column(meta_s, at, META_VALID) / total)
            o_s[h, at] = o.astype(BF)
            lse_s[at] = jnp.where(lane_iota((Q_ROWS, LANES)) == h, top + jnp.log(total), lse_s[at])
        for d in range(cols):
            a_send[d, h] = pack_head(o_s[h, d * local : (d + 1) * local])
        start_all(head_copies(h))
        return carry

    lax.fori_loop(0, 1, one_head, 0)
    cot_step(2)
    relay(1)
    lax.fori_loop(1, heads, one_head, 0)
    a_land[c] = a_send[c]
    stored = moves(
        [
            (xw, xw_out),
            (wq, wq_out),
            (qkv_s, qkv_out),
            (o_s, o_out),
            (lse_s, lse_out),
            (cos_s, cos_out),
            (sin_s, sin_out),
            (meta_s, meta_out),
        ],
        local_sem.at[pl.ds(4, 8)],
    )
    start_all(stored)
    cot_step(3)
    wait_all(wo_hand)
    hand_over(0)
    for h in range(heads):
        wait_all(head_copies(h))
    mixed = jnp.concatenate([unpack_head(a_land[i, h]) for i in range(cols) for h in range(heads)], axis=1)
    mixed_s[...] = mixed
    middle = x_ref[...].astype(F32) + mm(mixed, wo[...], NT)
    middle_s[...] = middle
    n2_s[...] = (middle * norm_rows(middle) * fgain).astype(BF)
    n_step, n_drain = gather_chain(n2_s, n2w_ref, n_send, n_recv, cols)
    n_step(0)
    wait_all(prev_copies)
    stored_late = moves(
        [(n2_s, n2w_ref.at[c]), (wo, wo_out), (mixed_s, mixed_out), (middle_s, middle_out), (prevw, prevw_out)],
        local_sem.at[pl.ds(12, 5)],
    )
    start_all(stored_late)
    relay(2)
    n_step(1)
    hand_over(1)
    n_step(2)
    hand_over(2)
    n_step(3)
    x_drain()
    n_drain()
    cot_drain()
    for copy in wq_push + wo_push:
        copy.wait_send()
    for t in range(3):
        for copy in to_near(t) + to_far(t):
            copy.wait_send()
        wait_all(to_other_core(t))
    wait_all(kept + cot_kept + stored + stored_late)


def first_step(cols, ranks, x, cot, router, const, vector, again, fgain, carry, wq, wo, prev, routes, lengths, gate, up, down):
    local = x.shape[0]
    rows = local * cols
    heads, width = 3, 3 * HEAD_DIM
    experts, depth, ff = gate.shape
    spots = np.arange(rows, dtype=np.float64)[:, None]
    pair = np.arange(LANES) % HEAD_DIM // 2
    freq = np.exp(-(2.0 * pair / HEAD_DIM) * math.log(BASE))[None, :]
    tables = [np.cos(spots * freq), np.sin(spots * freq), freq]
    tables = [jnp.asarray(value.astype(np.float32)) for value in tables]
    vm = pl.BlockSpec(memory_space=pltpu.VMEM)
    dma = pltpu.SemaphoreType.DMA
    return pl.pallas_call(
        functools.partial(first_kernel, cols, ranks),
        out_shape=(
            jax.ShapeDtypeStruct((3, experts, D, ff), BF),
            jax.ShapeDtypeStruct((3 * heads, rows, HEAD_DIM), BF),
            jax.ShapeDtypeStruct((heads, rows, HEAD_DIM), BF),
            jax.ShapeDtypeStruct((rows, LANES), F32),
            jax.ShapeDtypeStruct((cols, local, D), BF),
            jax.ShapeDtypeStruct((D, 3 * width), BF),
            jax.ShapeDtypeStruct((D, D), BF),
            jax.ShapeDtypeStruct((rows, LANES), F32),
            jax.ShapeDtypeStruct((rows, LANES), F32),
            jax.ShapeDtypeStruct((rows, LANES), F32),
            jax.ShapeDtypeStruct((experts, rows), jnp.int32),
            jax.ShapeDtypeStruct((local, D), BF),
            jax.ShapeDtypeStruct((local, D), F32),
            jax.ShapeDtypeStruct((cols, local, D), BF),
            jax.ShapeDtypeStruct((cols, 16, local), BF),
            jax.ShapeDtypeStruct((cols, local // EARLY, D), BF),
            jax.ShapeDtypeStruct((LANES, D), BF),
            jax.ShapeDtypeStruct((16, LANES), BF),
        ),
        in_specs=[vm] * 12 + [pl.BlockSpec(memory_space=pltpu.SMEM)] + [vm] * 3 + [ANY] * 3,
        out_specs=(ANY,) * 10 + (vm,) + (ANY,) * 5 + (vm, vm),
        scratch_shapes=[
            pltpu.VMEM((cols, local, D), BF),
            pltpu.VMEM((3, depth, width), BF),
            pltpu.VMEM((3, depth, width), BF),
            pltpu.VMEM((depth, width), BF),
            pltpu.VMEM((cols, depth, width), BF),
            pltpu.VMEM((D, 3 * width), BF),
            pltpu.VMEM((D, D), BF),
            pltpu.VMEM((cols, heads, local // 2, LANES), BF),
            pltpu.VMEM((cols, heads, local // 2, LANES), BF),
            pltpu.VMEM((16, local), BF),
            pltpu.VMEM((cols, 16, local), BF),
            pltpu.VMEM((3 * heads, rows, HEAD_DIM), BF),
            pltpu.VMEM((heads, rows, HEAD_DIM), BF),
            pltpu.VMEM((rows, LANES), F32),
            pltpu.VMEM((rows, LANES), F32),
            pltpu.VMEM((rows, LANES), F32),
            pltpu.VMEM((rows, LANES), F32),
            pltpu.VMEM((local, D), BF),
            pltpu.VMEM((local, D), F32),
            pltpu.VMEM((local, D), BF),
            pltpu.VMEM((3, experts, depth, ff), BF),
            dma((17,)),
            dma((2, cols - 1)),
            dma((2, cols - 1)),
            dma((2, cols - 1)),
            dma((2, cols - 1)),
            dma((2, cols - 1)),
            dma((2, cols - 1)),
            dma((2,)),
            dma((2,)),
            dma((2, cols - 1)),
            dma((2, cols - 1)),
            dma((2, 7)),
            dma((2, 7)),
            dma((3, 2)),
            dma((3, 2)),
            dma((3, 2)),
            dma((3, 2)),
            dma((3, 4)),
            dma((3, 4)),
            dma((heads, cols - 1)),
            dma((heads, cols - 1)),
        ],
        compiler_params=pltpu.CompilerParams(
            vmem_limit_bytes=60 * MIB, collective_id=5, has_side_effects=True
        ),
        cost_estimate=pl.CostEstimate(
            flops=8 * heads * rows * rows * HEAD_DIM, bytes_accessed=40 * MIB, transcendentals=heads * rows * rows
        ),
        name="first_step",
    )(x, cot, router, const, vector, again, fgain, carry, wq, wo, prev, routes, lengths, *tables, gate, up, down)


def experts_forward_kernel(
    cols,
    capacity,
    n2_ref,
    prev_ref,
    cot_ref,
    rw_ref,
    carry_ref,
    slots_ref,
    meta_ref,
    w_ref,
    x_ref,
    gu_ref,
    y_ref,
    gates_ref,
    cotb_ref,
    send,
    recv,
    local_sem,
):
    e = pl.program_id(0)
    experts = pl.num_programs(0)
    r, c = place()
    early = cot_ref.shape[0] // EARLY
    late = cot_ref.at[pl.ds(early, cot_ref.shape[0] - early)]
    step, drain = gather_chain(late, cotb_ref, send, recv, cols)
    own_copy = pltpu.make_async_copy(late, cotb_ref.at[c], local_sem.at[0])

    @pl.when(e == 0)
    def _():
        greet(col_peers(cols))
        own_copy.start()
        step(0)
        prev = jnp.concatenate([mm(prev_ref[i], carry_ref[...], TN) for i in range(cols)], axis=0)
        g = gate_lanes(mm(n2_ref[...], rw_ref[...], NT) + prev, meta_ref[...])
        high = g.astype(BF)
        gates_ref[:, :LANES] = high
        gates_ref[:, LANES:] = (g - high.astype(F32)).astype(BF)

    @pl.when(e == 3)
    def _():
        step(1)

    @pl.when(e == 6)
    def _():
        step(2)

    one = slot_rows(slots_ref, e, capacity)
    x = mm(one, n2_ref[...]).astype(BF)
    x_ref[0] = x
    sg = slot_gates(one, gates_ref, e)
    g = mm(x, w_ref[0, 0])
    u = mm(x, w_ref[1, 0])
    gu_ref[0, 0] = g.astype(BF)
    gu_ref[0, 1] = u.astype(BF)
    gh = (g * jax.nn.sigmoid(g) * u * sg).astype(BF)
    y_ref[0] = mm(gh, w_ref[2, 0], NT).astype(BF)

    @pl.when(e == experts - 1)
    def _():
        for k in range(3, cols):
            step(k)
        drain()
        own_copy.wait()


def experts_forward(cols, n2, prev, cot, rw, carry, meta, slots, w_all):
    rows = n2.shape[0]
    capacity = rows // 4
    three, experts, deep, ff = w_all.shape
    local = rows // cols
    rest = local - local // EARLY
    return pl.pallas_call(
        functools.partial(experts_forward_kernel, cols, capacity),
        grid=(experts,),
        out_shape=(
            jax.ShapeDtypeStruct((experts, capacity, D), BF),
            jax.ShapeDtypeStruct((experts, 2, capacity, ff), BF),
            jax.ShapeDtypeStruct((experts, capacity, D), BF),
            jax.ShapeDtypeStruct((rows, 2 * LANES), BF),
            jax.ShapeDtypeStruct((cols, rest, D), BF),
        ),
        in_specs=[
            whole((rows, D)),
            whole((cols, 16, local)),
            whole((local, D)),
            whole((LANES, D)),
            whole((16, LANES)),
            whole((experts, rows)),
            whole((rows, LANES)),
            pl.BlockSpec((three, 1, deep, ff), lambda e: (0, e, 0, 0)),
        ],
        out_specs=(
            pl.BlockSpec((1, capacity, D), lambda e: (e, 0, 0)),
            pl.BlockSpec((1, 2, capacity, ff), lambda e: (e, 0, 0, 0)),
            pl.BlockSpec((1, capacity, D), lambda e: (e, 0, 0)),
            whole((rows, 2 * LANES)),
            ANY,
        ),
        scratch_shapes=[
            pltpu.SemaphoreType.DMA((2, cols - 1)),
            pltpu.SemaphoreType.DMA((2, cols - 1)),
            pltpu.SemaphoreType.DMA((1,)),
        ],
        compiler_params=pltpu.CompilerParams(
            vmem_limit_bytes=60 * MIB, collective_id=1, has_side_effects=True
        ),
        cost_estimate=pl.CostEstimate(
            flops=experts * capacity * 2 * D * (3 * ff + rows),
            bytes_accessed=40 * MIB,
            transcendentals=experts * capacity * ff,
        ),
        name="experts_forward",
    )(n2, prev, cot, rw, carry, slots, meta, w_all)


def experts_backward_kernel(
    cols,
    capacity,
    cota_ref,
    cotb_ref,
    y_ref,
    gates_ref,
    slots_ref,
    meta_ref,
    w_ref,
    x_ref,
    gu_ref,
    dx_ref,
    dots_ref,
    mixsum_ref,
    gown_ref,
    sib_ref,
    hin_ref,
    cot_s,
    mix_s,
    gbuf,
    out,
    arrived,
    send,
    recv,
    own_sem,
    sib_send,
    sib_recv,
    cot_sem,
    lbuf,
    hbuf,
    l_sem,
    hsend,
    hrecv,
):
    e = pl.program_id(0)
    experts = pl.num_programs(0)
    r, c = place()
    core = r % 2
    local = mix_s.shape[1]
    early = cota_ref.shape[1]
    place_now = lax.rem(e, 2)
    slot, total, drain = reduce_chain(lambda d: mix_s[d], out, arrived, send, recv, cols)

    def own_copy(expert, at):
        return pltpu.make_async_copy(gbuf.at[at, :, :, core], gown_ref.at[expert], own_sem.at[at])

    def sib_copy(expert, at):
        return send_to(
            gbuf.at[at, :, :, 1 - core],
            sib_ref.at[expert],
            sib_send.at[at],
            sib_recv.at[expert],
            (flip(r, 1), c),
        )

    cot_loads = moves(
        [(cota_ref.at[d], cot_s.at[pl.ds(d * local, early)]) for d in range(cols)]
        + [(cotb_ref.at[d], cot_s.at[pl.ds(d * local + early, local - early)]) for d in range(cols)],
        cot_sem,
    )
    before = jnp.maximum(e - 1, 0)
    sib_load = pltpu.make_async_copy(sib_ref.at[before], lbuf, l_sem.at[0])
    sends_now = (e >= 1) & (e <= SENT_SOON)

    def h_sends(i):
        return to_chips(lambda there: hbuf.at[i, :, there], hin_ref.at[i], hsend.at[i], hrecv.at[i])

    @pl.when(e == 0)
    def _():
        start_all(cot_loads)
        greet(col_peers(cols) + [(flip(r, m), c) for m in (1, 2, 4, 6)])
        for n, d in enumerate((3, 0, 2, 1)):
            mix_s[d] = combine(meta_ref, y_ref, d, local)
            if n == 1:
                slot(0)
        wait_all(cot_loads)

    @pl.when(e == 2)
    def _():
        slot(1)

    @pl.when(e == 5)
    def _():
        slot(2)

    one = slot_rows(slots_ref, e, capacity)
    ct = mm(one, cot_s[...]).astype(BF)
    sg = slot_gates(one, gates_ref, e)
    x = x_ref[0]

    @pl.when(sends_now)
    def _():
        sib_copy(before, 1 - place_now).wait_recv()
        sib_load.start()

    g, u = gu_ref[0, 0].astype(F32), gu_ref[0, 1].astype(F32)
    v = mm(ct, w_ref[2, 0])
    sig = jax.nn.sigmoid(g)
    act = g * sig
    h = act * u
    dot = jnp.sum(h * v, axis=1, keepdims=True)
    dots_ref[pl.ds(e, 1)] = jnp.sum(one.astype(F32) * dot, axis=0, keepdims=True)
    gh = (h * sg).astype(BF)
    gv = v * sg
    dg = (gv * u * (sig * (1.0 + g * (1.0 - sig)))).astype(BF)
    du = (gv * act).astype(BF)
    dx_ref[0] = (mm(dg, w_ref[0, 0], NT) + mm(du, w_ref[1, 0], NT)).astype(BF)

    @pl.when(e >= 2)
    def _():
        own_copy(e - 2, place_now).wait()
        sib_copy(e - 2, place_now).wait_send()

    shape = gbuf.shape[2:]
    gbuf[place_now, 0] = mm(x, dg, TN).astype(BF).reshape(shape)
    gbuf[place_now, 1] = mm(x, du, TN).astype(BF).reshape(shape)
    gbuf[place_now, 2] = mm(ct, gh, TN).astype(BF).reshape(shape)
    own_copy(e, place_now).start()
    sib_copy(e, place_now).start()

    @pl.when(sends_now)
    def _():
        sib_load.wait()
        hbuf[before] = (gbuf[1 - place_now, :, :, core].astype(F32) + lbuf[...].astype(F32)).astype(BF)
        start_all(h_sends(before))

    @pl.when(e == experts - 1)
    def _():
        for s in range(3, cols):
            slot(s)
        total(mixsum_ref)
        drain()
        for back in (1, 0):
            own_copy(e - back, lax.rem(e - back, 2)).wait()
            sib_copy(e - back, lax.rem(e - back, 2)).wait_send()
        for i in range(SENT_SOON, EXPERTS):
            sib_copy(i, i % 2).wait_recv()
        for i in range(SENT_SOON):
            wait_all(h_sends(i))


def experts_backward(cols, ranks, cota, cotb, y, gates, meta, slots, w_all, x, gu):
    experts, capacity, _ = y.shape
    rows = slots.shape[1]
    three, _, deep, ff = w_all.shape
    local = rows // cols
    chips = ranks // 2
    depth = deep // ranks
    half = jax.ShapeDtypeStruct((experts, three, chips, depth, ff), BF)
    return pl.pallas_call(
        functools.partial(experts_backward_kernel, cols, capacity),
        grid=(experts,),
        out_shape=(
            jax.ShapeDtypeStruct((experts, capacity, D), BF),
            jax.ShapeDtypeStruct((experts, rows), F32),
            jax.ShapeDtypeStruct((local, D), F32),
            half,
            half,
            jax.ShapeDtypeStruct((SENT_SOON, 3, three, depth, ff), BF),
        ),
        in_specs=[
            ANY,
            ANY,
            whole((experts, capacity, D)),
            whole((rows, 2 * LANES)),
            whole((experts, rows)),
            whole((rows, LANES)),
            pl.BlockSpec((three, 1, deep, ff), lambda e: (0, e, 0, 0)),
            pl.BlockSpec((1, capacity, D), lambda e: (e, 0, 0)),
            pl.BlockSpec((1, 2, capacity, ff), lambda e: (e, 0, 0, 0)),
        ],
        out_specs=(
            pl.BlockSpec((1, capacity, D), lambda e: (e, 0, 0)),
            whole((experts, rows)),
            whole((local, D)),
            ANY,
            ANY,
            ANY,
        ),
        scratch_shapes=[
            pltpu.VMEM((rows, D), BF),
            pltpu.VMEM((cols, local, D), BF),
            pltpu.VMEM((2, three, chips, 2, depth, ff), BF),
            *chain_scratch(cols, local),
            pltpu.SemaphoreType.DMA((2,)),
            pltpu.SemaphoreType.DMA((2,)),
            pltpu.SemaphoreType.DMA((experts,)),
            pltpu.SemaphoreType.DMA((2 * cols,)),
            pltpu.VMEM((three, chips, depth, ff), BF),
            pltpu.VMEM((SENT_SOON, three, chips, depth, ff), BF),
            pltpu.SemaphoreType.DMA((1,)),
            pltpu.SemaphoreType.DMA((SENT_SOON, 3)),
            pltpu.SemaphoreType.DMA((SENT_SOON, 3)),
        ],
        compiler_params=pltpu.CompilerParams(
            vmem_limit_bytes=60 * MIB, collective_id=2, has_side_effects=True
        ),
        cost_estimate=pl.CostEstimate(
            flops=experts * capacity * 4 * D * (3 * ff + rows),
            bytes_accessed=60 * MIB,
            transcendentals=experts * capacity * ff,
        ),
        name="experts_backward",
    )(cota, cotb, y, gates, slots, meta, w_all, x, gu)


def resid_kernel(
    cols,
    count,
    dx_ref,
    meta_ref,
    dots_ref,
    rw_ref,
    prev_ref,
    carry_ref,
    cot_ref,
    mixsum_in,
    n2w_in,
    middle_in,
    out_t_in,
    mixed_in,
    gown_ref,
    sib_ref,
    layer_ref,
    resid_ref,
    gm_ref,
    og_ref,
    small_ref,
    pg_ref,
    hin_ref,
    hrest_ref,
    mixsum,
    n2_s,
    middle_s,
    out_t,
    mixed_s,
    resid_s,
    load_sem,
    gt_s,
    out,
    arrived,
    send,
    recv,
    dots_in,
    dsend,
    drecv,
    grad,
    gm_out,
    gsend,
    grecv,
    gm_sem,
    lbuf,
    hbuf,
    hload,
    hsend,
    hrecv,
    hkeep,
):
    r, c = place()
    chip = r // 2
    local = cot_ref.shape[0]
    held = hbuf.shape[0]
    loads = moves(
        [
            (n2w_in.at[c], n2_s),
            (middle_in, middle_s),
            (mixsum_in, mixsum),
            (out_t_in, out_t),
            (mixed_in, mixed_s),
        ],
        load_sem,
    )
    greet(col_peers(cols) + [(flip(r, 2 * k), c) for k in range(1, 4)])
    slot, total, drain = reduce_chain(lambda d: gt_s[d], out, arrived, send, recv, cols)

    def dots_of(d):
        return dots_ref.at[:, pl.ds(pl.multiple_of(d * local, LANES), local)]

    dot_copies = to_cols(dots_of, dots_in, dsend, drecv, cols)
    start_all(dot_copies)
    dots_in[c] = dots_of(c)[...]
    for n, d in enumerate((3, 0, 2, 1)):
        gt_s[d] = combine(meta_ref, dx_ref, d, local)
        if n == 1:
            slot(0)

    def h_loads(i):
        at = lax.rem(i, 2)
        return [
            pltpu.make_async_copy(ref.at[SENT_SOON + i], lbuf.at[at, j], hload.at[at, j])
            for j, ref in enumerate((gown_ref, sib_ref))
        ]

    def h_sends(i):
        return to_chips(lambda there: hbuf.at[i, :, there], hin_ref.at[i], hsend.at[i], hrecv.at[i])

    def h_keeps(i):
        return moves(
            [(hbuf.at[i, :, flip(chip, k)], hrest_ref.at[i - count, k - 1]) for k in range(1, 4)],
            hkeep.at[i - count],
        )

    start_all(h_loads(0))

    def add_cores(i, carry):
        @pl.when(i + 1 < held)
        def _():
            start_all(h_loads(i + 1))

        wait_all(h_loads(i))
        at = lax.rem(i, 2)
        hbuf[i] = (lbuf[at, 0].astype(F32) + lbuf[at, 1].astype(F32)).astype(BF)

        @pl.when(i < count)
        def _():
            start_all(h_sends(i))

        @pl.when(i >= count)
        def _():
            start_all(h_keeps(jnp.maximum(i, count)))

        return carry

    lax.fori_loop(0, held, add_cores, 0)
    start_all(loads)
    slot(1)
    wait_all(loads)

    meta = meta_ref[pl.ds(pl.multiple_of(c * local, LANES), local)]
    n2, cot = n2_s[...], cot_ref[...]
    n2f, cotf = n2.astype(F32), cot.astype(F32)
    middle = middle_s[...]
    rw = rw_ref[...]
    lin = mm(n2, rw, NT)
    prev = prev_ref[c]
    gates = gate_lanes(lin + mm(prev, carry_ref[...], TN), meta)
    lane = lane_iota((local, LANES))
    cot_lin = mm(cot, rw, NT)
    dot_keep = jnp.sum(cotf * n2f, axis=1, keepdims=True)
    wait_all(dot_copies)
    d = jnp.concatenate([all_sum(dots_in, cols), jnp.zeros((LANES - EXPERTS, local), F32)], axis=0).T
    g_gates = jnp.where(lane == EXPERTS + 1, dot_keep, d)
    keep = gates[:, EXPERTS + 1 : EXPERTS + 2]
    mixes, packs = [], jnp.zeros((local, LANES), F32)
    for j in range(2):
        l0 = lin[:, ROW_CONST + 2 * j : ROW_CONST + 2 * j + 1]
        l1 = lin[:, ROW_CONST + 2 * j + 1 : ROW_CONST + 2 * j + 2]
        top = jnp.maximum(l0, l1)
        e0, e1 = jnp.exp(l0 - top), jnp.exp(l1 - top)
        a0, a1 = e0 / (e0 + e1), e1 / (e0 + e1)
        share = gates[:, EXPERTS + 2 + j : EXPERTS + 3 + j]
        dot_vec = cot_lin[:, ROW_VEC + j : ROW_VEC + j + 1]
        keep = keep + share * a0
        mixes.append(share * a1)
        g_gates = jnp.where(lane == EXPERTS + 2 + j, a0 * dot_keep + a1 * dot_vec, g_gates)
        gk, gv = share * dot_keep, share * dot_vec
        mean = a0 * gk + a1 * gv
        packs = packs + jnp.where(lane == ROW_CONST + 2 * j, a0 * (gk - mean), 0.0)
        packs = packs + jnp.where(lane == ROW_CONST + 2 * j + 1, a1 * (gv - mean), 0.0)
        packs = packs + jnp.where(lane == ROW_VEC + j, share * a1, 0.0)
    packs = packs + gates * (g_gates - jnp.sum(gates * g_gates, axis=1, keepdims=True))
    vec = rw[ROW_VEC : ROW_VEC + 2].astype(F32)
    layer = middle + mixsum[...] + keep * n2f + mixes[0] * vec[0:1] + mixes[1] * vec[1:2]
    layer_ref[...] = layer.astype(BF)

    high = packs.astype(BF)
    low = (packs - high.astype(F32)).astype(BF)
    back = lane < ROW_VEC
    high_b = jnp.where(back, packs, 0.0).astype(BF)
    low_b = jnp.where(back, packs - high.astype(F32), 0.0).astype(BF)
    grad_local = keep * cotf + mm(high_b, rw) + mm(low_b, rw)
    by_n2 = mm(high, n2, TN) + mm(low, n2, TN)
    by_cot = mm(high, cot, TN) + mm(low, cot, TN)
    by_prev = mm(prev, high) + mm(prev, low)
    pg = mm(carry_ref[...], high_b, NT) + mm(carry_ref[...], low_b, NT)
    pg_ref[...] = pg[:ROUTES]
    sub = lax.broadcasted_iota(jnp.int32, (SMALL_ROWS, D), 0)
    small_ref[:, :D] = jnp.where(sub < ROW_VEC, by_n2[:SMALL_ROWS], by_cot[:SMALL_ROWS])
    small_ref[:16, D : D + LANES] = by_prev
    small_ref[16:, D : D + LANES] = jnp.zeros((SMALL_ROWS - 16, LANES), F32)
    small_ref[:, D + LANES :] = jnp.zeros((SMALL_ROWS, LANES), F32)
    fgain = rw[ROW_GAIN + 1 : ROW_GAIN + 2].astype(F32)
    scale = norm_rows(middle)

    for s in range(2, cols):
        slot(s)
    total(grad)
    grad_normed = grad[...] + grad_local
    gained = grad_normed * fgain
    mid_dot = jnp.sum(gained * middle, axis=1, keepdims=True)
    resid = cotf + scale * gained - middle * (scale * scale * scale * (mid_dot * (1.0 / D)))
    cut = resid.astype(BF)
    gm = (mm(cut, out_t[...]) * meta[:, META_VALID : META_VALID + 1]).astype(BF)
    width = D // cols
    for i in range(cols):
        for h in range(width // HEAD_DIM):
            at = i * width + h * HEAD_DIM
            gm_out[i, h] = pack_head(gm[:, at : at + HEAD_DIM])
    gm_copies = to_cols(lambda i: gm_out.at[i], gm_ref, gsend, grecv, cols)
    start_all(gm_copies)
    resid_s[...] = resid
    stored = moves([(gm_out.at[c], gm_ref.at[c]), (resid_s, resid_ref)], gm_sem)
    start_all(stored)
    small_ref[ROW_GAIN : ROW_GAIN + 1, :D] = jnp.sum(grad_normed * middle * scale, axis=0, keepdims=True)
    og_ref[...] = mm(cut, mixed_s[...], TN).astype(BF)
    wait_all(stored + gm_copies)
    drain()

    def end(i, carry):
        @pl.when(i < count)
        def _():
            wait_all(h_sends(i))

        @pl.when(i >= count)
        def _():
            wait_all(h_keeps(jnp.maximum(i, count)))

        return carry

    lax.fori_loop(0, held, end, 0)


def resid_step(cols, dx, meta, dots, rw, prev, carry, cot, mixsum, n2w, middle, out_t, mixed, gown, sib):
    local = cot.shape[0]
    experts, three, chips, depth, ff = gown.shape
    count, held = SENT_NEXT, experts - SENT_SOON
    vm = pl.BlockSpec(memory_space=pltpu.VMEM)
    dma = pltpu.SemaphoreType.DMA
    return pl.pallas_call(
        functools.partial(resid_kernel, cols, count),
        out_shape=(
            jax.ShapeDtypeStruct((local, D), BF),
            jax.ShapeDtypeStruct((local, D), F32),
            jax.ShapeDtypeStruct((cols, 3, local // 2, LANES), BF),
            jax.ShapeDtypeStruct((D, D), BF),
            jax.ShapeDtypeStruct((SMALL_ROWS, D + 2 * LANES), F32),
            jax.ShapeDtypeStruct((ROUTES, local), F32),
            jax.ShapeDtypeStruct((count, 3, three, depth, ff), BF),
            jax.ShapeDtypeStruct((held - count, 3, three, depth, ff), BF),
        ),
        in_specs=[vm] * 7 + [ANY] * 7,
        out_specs=(vm, ANY, ANY, vm, vm, vm, ANY, ANY),
        scratch_shapes=[
            pltpu.VMEM((local, D), F32),
            pltpu.VMEM((local, D), BF),
            pltpu.VMEM((local, D), F32),
            pltpu.VMEM((D, D), BF),
            pltpu.VMEM((local, D), BF),
            pltpu.VMEM((local, D), F32),
            dma((5,)),
            pltpu.VMEM((cols, local, D), BF),
            *chain_scratch(cols, local),
            pltpu.VMEM((cols, EXPERTS, local), F32),
            dma((cols - 1,)),
            dma((cols - 1,)),
            pltpu.VMEM((local, D), F32),
            pltpu.VMEM((cols, 3, local // 2, LANES), BF),
            dma((cols - 1,)),
            dma((cols - 1,)),
            dma((2,)),
            pltpu.VMEM((2, 2, three, chips, depth, ff), BF),
            pltpu.VMEM((held, three, chips, depth, ff), BF),
            dma((2, 2)),
            dma((count, 3)),
            dma((count, 3)),
            dma((held - count, 3)),
        ],
        compiler_params=pltpu.CompilerParams(
            vmem_limit_bytes=60 * MIB, collective_id=3, has_side_effects=True
        ),
        cost_estimate=pl.CostEstimate(flops=6 * local * D * D, bytes_accessed=40 * MIB, transcendentals=0),
        name="resid_step",
    )(dx, meta, dots, rw, prev, carry, cot, mixsum, n2w, middle, out_t, mixed, gown, sib)


def finish_kernel(
    cols,
    ranks,
    gm_ref,
    meta_ref,
    lse_ref,
    small_ref,
    og_ref,
    xown_ref,
    rw_ref,
    qkv_in,
    o_in,
    x_in,
    w_in,
    cos_in,
    sin_in,
    resid_in,
    gown_ref,
    sib_ref,
    hsoon_ref,
    hin0_ref,
    hrest_ref,
    ig_ref,
    small_out,
    qg_out,
    og_out,
    gg_ref,
    ug_ref,
    dg_ref,
    hin_ref,
    qkv_s,
    o_s,
    x_s,
    w_s,
    cos_s,
    sin_s,
    resid_s,
    head_sem,
    load_sem,
    do_s,
    dq_s,
    dk_s,
    dv_s,
    gn_s,
    qg_acc,
    qg_cut,
    out,
    arrived,
    send,
    recv,
    small_s,
    small_rows,
    small_cols,
    small_all,
    og_sib,
    og_half,
    og_chips,
    og_parts,
    og_cols,
    qg_sib,
    qg_half,
    qg_chips,
    q_parts,
    q_land,
    total_s,
    fbuf,
    fsem,
    row_send,
    row_recv,
    chip_send,
    chip_recv,
    sib_send,
    sib_recv,
    col_send,
    col_recv,
    hsend,
    hrecv,
):
    r, c = place()
    chip, core = r // 2, r % 2
    heads = 3
    rows = meta_ref.shape[0]
    local = rows // cols
    width = heads * HEAD_DIM
    rest = hrest_ref.shape[0]
    first = gown_ref.shape[0] - rest
    score_scale = 1.0 / math.sqrt(HEAD_DIM)

    def head_loads(h):
        pairs = [(qkv_in.at[i * heads + h], qkv_s.at[i * heads + h]) for i in range(3)]
        return moves(pairs + [(o_in.at[h], o_s.at[h])], head_sem.at[h])

    loads = moves(
        [(x_in, x_s), (w_in, w_s), (cos_in, cos_s), (sin_in, sin_s), (resid_in, resid_s)], load_sem
    )
    start_all(head_loads(0))
    greet(col_peers(cols) + [(flip(r, m), c) for m in range(1, ranks)])
    for h in range(1, heads):
        start_all(head_loads(h))
    start_all(loads)

    def to_sibling(src, dst, at):
        return send_to(src.at[:, 1 - core], dst, sib_send.at[at], sib_recv.at[at], (flip(r, 1), c))

    og_across = to_sibling(og_ref, og_sib, 0)
    og_across.start()

    for d in range(cols):
        at = slice(d * local, (d + 1) * local)
        for h in range(heads):
            do_s[h, at] = unpack_head(gm_ref[d, h])

    def halves(ref, sib, half):
        for k in range(ranks // 2):
            half[k] = (ref[k, core].astype(F32) + sib[k].astype(F32)).astype(BF)

    og_across.wait()
    halves(og_ref, og_sib, og_half)
    og_to_chips = to_chips(lambda there: og_half.at[there], og_chips, chip_send.at[0], chip_recv.at[0])
    start_all(og_to_chips)

    def h_sends(i):
        r_, c_ = place()
        return [
            send_to(
                hrest_ref.at[i, k - 1],
                hin_ref.at[i, k - 1],
                hsend.at[i, k - 1],
                hrecv.at[i, k - 1],
                (flip(r_, 2 * k), c_),
            )
            for k in range(1, 4)
        ]

    def start_sends(i, carry):
        start_all(h_sends(i))
        return carry

    lax.fori_loop(0, rest, start_sends, 0)

    blocks = rows // Q_ROWS

    def one_head(h, carry):
        wait_all(head_loads(h))
        for i in reversed(range(blocks)):
            at = slice(i * Q_ROWS, (i + 1) * Q_ROWS)
            length = (i + 1) * Q_ROWS
            q, do = qkv_s[h, at], do_s[h, at]
            k, v = qkv_s[heads + h, :length], qkv_s[2 * heads + h, :length]
            delta = jnp.sum(do.astype(F32) * o_s[h, at].astype(F32), axis=1, keepdims=True)
            lse = jnp.sum(jnp.where(lane_iota((Q_ROWS, LANES)) == h, lse_ref[at], 0.0), axis=1, keepdims=True)
            s = mm(q, k, NT)
            ok = seen(column(meta_ref, at, META_BEGIN).astype(jnp.int32), i * Q_ROWS, Q_ROWS, length)
            p = jnp.where(ok, jnp.exp(s - lse), 0.0)
            ds = (p * (mm(do, v, NT) - delta)).astype(BF)
            dq_s[h, at] = mm(ds, k) * score_scale
            dk, dv = mm(ds, q, TN), mm(p.astype(BF), do, TN)
            if i == blocks - 1:
                dk_s[h], dv_s[h] = dk, dv
            else:
                dk_s[h, :length] += dk
                dv_s[h, :length] += dv
        return carry

    lax.fori_loop(0, heads, one_head, 0)

    slot, total, drain = reduce_chain(lambda d: gn_s[d], out, arrived, send, recv, cols)
    wait_all(loads)
    gain_total = jnp.zeros((1, D), F32)
    weight = w_s[...]
    again = rw_ref[ROW_GAIN : ROW_GAIN + 1].astype(F32)
    for n, d in enumerate((3, 0, 2, 1)):
        at = slice(d * local, (d + 1) * local)
        cosine, sines = cos_s[at], sin_s[at]
        turned = [dq_s[h, at] for h in range(heads)] + [dk_s[h, at] for h in range(heads)]
        parts = []
        for part in range(heads):
            v = jnp.concatenate(turned[2 * part : 2 * part + 2], axis=1)
            parts.append((v * cosine - swap_pairs(v) * sines).astype(BF))
        parts += [dv_s[h, at].astype(BF) for h in range(heads)]
        gp = jnp.concatenate(parts, axis=1)
        x = x_s[d].astype(F32)
        xs = x * norm_rows(x)
        gn = mm(gp, weight, NT)
        gn_s[d] = gn.astype(BF)
        if n == 1:
            slot(0)
        gain_total = gain_total + jnp.sum(gn * xs, axis=0, keepdims=True)
        grad = mm((xs * again).astype(BF), gp, TN)
        if n == 0:
            qg_acc[...] = grad
        else:
            qg_acc[...] += grad
    qg_cut[...] = qg_acc[...].astype(BF).reshape(qg_cut.shape)
    qg_across = to_sibling(qg_cut, qg_sib, 1)
    qg_across.start()

    sub = lax.broadcasted_iota(jnp.int32, (SMALL_ROWS, D), 0)
    for i in range(ranks):
        block = small_ref[:, i * LANES : (i + 1) * LANES]
        if i < D // LANES:
            own = sub[:, :LANES] == ROW_GAIN + 1
            block = jnp.where(own, gain_total[:, i * LANES : (i + 1) * LANES], block)
        small_s[i] = block
    small_to_rows = to_rows(lambda d: small_s.at[d], small_rows, row_send.at[0], row_recv.at[0], ranks)
    start_all(small_to_rows)
    small_rows[r] = small_s[r]
    slot(1)

    def sum_grads(low, high, hin, base):
        def f_loads(i):
            at = lax.rem(i, 2)
            return moves(
                [
                    (gown_ref.at[i, :, chip], fbuf.at[at, 0]),
                    (sib_ref.at[i, :, chip], fbuf.at[at, 1]),
                    (hin.at[i - base], fbuf.at[at, pl.ds(2, 3)]),
                ],
                fsem.at[at],
            )

        start_all(f_loads(low))

        def body(i, carry):
            @pl.when(i + 1 < high)
            def _():
                start_all(f_loads(jnp.minimum(i + 1, high - 1)))

            wait_all(f_loads(i))
            at = lax.rem(i, 2)
            total_grad = fbuf[at, 0].astype(F32)
            for j in range(1, 5):
                total_grad = total_grad + fbuf[at, j].astype(F32)
            gg_ref[i] = total_grad[0]
            ug_ref[i] = total_grad[1]
            dg_ref[i] = total_grad[2]
            return carry

        lax.fori_loop(low, high, body, 0)

    qg_across.wait()
    halves(qg_cut, qg_sib, qg_half)
    qg_to_chips = to_chips(lambda there: qg_half.at[there], qg_chips, chip_send.at[1], chip_recv.at[1])
    start_all(qg_to_chips)
    wait_all(small_to_rows)
    small_cols[c] = all_sum(small_rows, ranks)
    small_to_cols = to_cols(lambda d: small_cols.at[c], small_cols, col_send.at[0], col_recv.at[0], cols)
    start_all(small_to_cols)
    wait_all(og_to_chips)
    og_sum = og_ref[chip, core].astype(F32) + og_sib[chip].astype(F32) + all_sum(og_chips, 3)
    for i in range(cols):
        og_parts[i] = og_sum[:, i * width : (i + 1) * width]
    og_to_cols = to_cols(lambda d: og_parts.at[d], og_cols, col_send.at[1], col_recv.at[1], cols)
    start_all(og_to_cols)
    og_cols[c] = og_parts[c]
    sum_grads(0, SENT_SOON, hsoon_ref, 0)
    sum_grads(SENT_SOON, first, hin0_ref, SENT_SOON)
    slot(2)
    wait_all(qg_to_chips)
    q_sum = qg_cut[chip, core].astype(F32) + qg_sib[chip].astype(F32) + all_sum(qg_chips, 3)
    for i in range(3):
        q_parts[i] = q_sum[:, i * width : (i + 1) * width]
    odd, high = c % 2, c // 2
    q_copies = [
        send_to(
            q_parts.at[1 - odd + high],
            q_land.at[1],
            col_send.at[2, 0],
            col_recv.at[2, 0],
            (r, flip(c, 1)),
        ),
        send_to(
            q_parts.at[2 - 2 * high],
            q_land.at[2 - 2 * odd],
            col_send.at[2, 1],
            col_recv.at[2, 1],
            (r, flip(c, 2)),
        ),
    ]
    start_all(q_copies)
    q_land[2 * odd] = q_parts[(c + 1) // 2]
    wait_all(small_to_cols)
    small_all[r] = all_sum(small_cols, cols)
    small_back = to_rows(lambda d: small_all.at[r], small_all, row_send.at[1], row_recv.at[1], ranks)
    start_all(small_back)

    def end_sends(i, carry):
        wait_all(h_sends(i))
        return carry

    lax.fori_loop(0, rest, end_sends, 0)
    sum_grads(first, first + rest, hin_ref, first)
    wait_all(og_to_cols + q_copies + small_back)
    og_out[...] = all_sum(og_cols, cols)
    for i in range(3):
        qg_out[:, i * width : (i + 1) * width] = q_land[i]
    for i in range(ranks):
        small_out[:, i * LANES : (i + 1) * LANES] = small_all[i]
    slot(3)
    total(total_s)
    gn = total_s[...]
    x = xown_ref[...].astype(F32)
    scale = norm_rows(x)
    gained = gn * again
    x_dot = jnp.sum(gained * x, axis=1, keepdims=True)
    ig_ref[...] = resid_s[...] + scale * gained - x * (scale * scale * scale * (x_dot * (1.0 / D)))
    drain()


def finish_step(cols, ranks, gm, meta, lse, small, og, xown, rw, qkv, o, x, w, cosine, sines, resid, gown, sib, hsoon, hin0, hrest):
    rows = meta.shape[0]
    local = rows // cols
    experts, three, chips, depth, ff = gown.shape
    rest = hrest.shape[0]
    heads, width = 3, 3 * HEAD_DIM
    vm = pl.BlockSpec(memory_space=pltpu.VMEM)
    dma = pltpu.SemaphoreType.DMA
    wide = D + 2 * LANES
    weight_grad = jax.ShapeDtypeStruct((experts, depth, ff), F32)
    return pl.pallas_call(
        functools.partial(finish_kernel, cols, ranks),
        out_shape=(
            jax.ShapeDtypeStruct((local, D), F32),
            jax.ShapeDtypeStruct((SMALL_ROWS, wide), F32),
            jax.ShapeDtypeStruct((depth, 3 * width), F32),
            jax.ShapeDtypeStruct((depth, width), F32),
            weight_grad,
            weight_grad,
            weight_grad,
            jax.ShapeDtypeStruct((rest, 3, three, depth, ff), BF),
        ),
        in_specs=[vm] * 7 + [ANY] * 12,
        out_specs=(vm,) * 7 + (ANY,),
        scratch_shapes=[
            pltpu.VMEM((3 * heads, rows, HEAD_DIM), BF),
            pltpu.VMEM((heads, rows, HEAD_DIM), BF),
            pltpu.VMEM((cols, local, D), BF),
            pltpu.VMEM((D, 3 * width), BF),
            pltpu.VMEM((rows, LANES), F32),
            pltpu.VMEM((rows, LANES), F32),
            pltpu.VMEM((local, D), F32),
            dma((heads, 4)),
            dma((5,)),
            pltpu.VMEM((heads, rows, HEAD_DIM), BF),
            pltpu.VMEM((heads, rows, HEAD_DIM), F32),
            pltpu.VMEM((heads, rows, HEAD_DIM), F32),
            pltpu.VMEM((heads, rows, HEAD_DIM), F32),
            pltpu.VMEM((cols, local, D), BF),
            pltpu.VMEM((D, 3 * width), F32),
            pltpu.VMEM((chips, 2, depth, 3 * width), BF),
            *chain_scratch(cols, local),
            pltpu.VMEM((ranks, SMALL_ROWS, LANES), F32),
            pltpu.VMEM((ranks, SMALL_ROWS, LANES), F32),
            pltpu.VMEM((cols, SMALL_ROWS, LANES), F32),
            pltpu.VMEM((ranks, SMALL_ROWS, LANES), F32),
            pltpu.VMEM((chips, depth, D), BF),
            pltpu.VMEM((chips, depth, D), BF),
            pltpu.VMEM((3, depth, D), BF),
            pltpu.VMEM((cols, depth, width), F32),
            pltpu.VMEM((cols, depth, width), F32),
            pltpu.VMEM((chips, depth, 3 * width), BF),
            pltpu.VMEM((chips, depth, 3 * width), BF),
            pltpu.VMEM((3, depth, 3 * width), BF),
            pltpu.VMEM((3, depth, width), F32),
            pltpu.VMEM((3, depth, width), F32),
            pltpu.VMEM((local, D), F32),
            pltpu.VMEM((2, 5, three, depth, ff), BF),
            dma((2, 3)),
            dma((2, ranks - 1)),
            dma((2, ranks - 1)),
            dma((2, 3)),
            dma((2, 3)),
            dma((2,)),
            dma((2,)),
            dma((3, cols - 1)),
            dma((3, cols - 1)),
            dma((rest, 3)),
            dma((rest, 3)),
        ],
        compiler_params=pltpu.CompilerParams(
            vmem_limit_bytes=62 * MIB, collective_id=4, has_side_effects=True
        ),
        cost_estimate=pl.CostEstimate(
            flops=20 * heads * rows * rows * HEAD_DIM, bytes_accessed=40 * MIB, transcendentals=heads * rows * rows
        ),
        name="finish_step",
    )(gm, meta, lse, small, og, xown, rw, qkv, o, x, w, cosine, sines, resid, gown, sib, hsoon, hin0, hrest)


def place_kernel(
    small_ref,
    qg_ref,
    og_ref,
    pg_ref,
    layer_in,
    ig_in,
    gg_in,
    ug_in,
    dg_in,
    layer_ref,
    ig_ref,
    gg_ref,
    ug_ref,
    dg_ref,
    again_ref,
    qkv_ref,
    out_ref,
    fgain_ref,
    router_ref,
    carry_ref,
    const_ref,
    vector_ref,
    prev_ref,
):
    for src, dst in ((gg_in, gg_ref), (ug_in, ug_ref), (dg_in, dg_ref), (ig_in, ig_ref), (layer_in, layer_ref)):
        dst[...] = src[...]
    again_ref[...] = small_ref[ROW_GAIN + 1 : ROW_GAIN + 2, :D].reshape(D)
    fgain_ref[...] = small_ref[ROW_GAIN : ROW_GAIN + 1, :D].reshape(D)
    qkv_ref[...] = qg_ref[...]
    out_ref[...] = og_ref[...].T
    router_ref[...] = small_ref[:ROUTES, :D]
    carry_ref[...] = small_ref[:ROUTES, D : D + ROUTES]
    for j in range(2):
        const_ref[j] = small_ref[ROW_CONST + 2 * j : ROW_CONST + 2 * j + 2, :D]
    vector_ref[...] = small_ref[ROW_VEC : ROW_VEC + 2, :D]
    prev_ref[...] = pg_ref[...]


def place_outputs(small, qg, og, pg, layer, ig, gg, ug, dg):
    vm = pl.BlockSpec(memory_space=pltpu.VMEM)
    shapes = [layer.shape, ig.shape, gg.shape, ug.shape, dg.shape]
    shapes += [(D,), qg.shape, og.shape[::-1], (D,), (ROUTES, D), (ROUTES, ROUTES), (2, 2, D), (2, D), pg.shape]
    return pl.pallas_call(
        place_kernel,
        out_shape=[jax.ShapeDtypeStruct(shape, F32 if i else BF) for i, shape in enumerate(shapes)],
        in_specs=[vm] * 9,
        out_specs=[vm] * 14,
        compiler_params=pltpu.CompilerParams(vmem_limit_bytes=48 * MIB),
        cost_estimate=pl.CostEstimate(flops=0, bytes_accessed=16 * MIB, transcendentals=0),
        name="place_outputs",
    )(small, qg, og, pg, layer, ig, gg, ug, dg)


def on_device_heads(
    sizes,
    inputs,
    attn_gain,
    qkv_weight,
    out_weight,
    ffn_gain,
    router_weight,
    carry_weight,
    const_weight,
    const_vector,
    gate_weight,
    up_weight,
    down_weight,
    prev_logits,
    seq_lengths,
    expert_routes,
    cotangent,
):
    ranks, cols = sizes
    row_total = expert_routes.shape[0]
    depth = qkv_weight.shape[0]

    (
        w_all,
        qkv,
        mixed_heads,
        lse,
        whole_in,
        qkv_own,
        out_t,
        cosine,
        sines,
        meta,
        slots,
        mixed,
        middle,
        n2_whole,
        prev_whole,
        cot_early,
        rw,
        carry,
    ) = first_step(
        cols,
        ranks,
        inputs,
        cotangent,
        router_weight.T,
        const_weight.transpose(0, 2, 1),
        const_vector,
        attn_gain,
        ffn_gain,
        carry_weight,
        qkv_weight,
        out_weight,
        prev_logits,
        expert_routes.T,
        seq_lengths,
        gate_weight,
        up_weight,
        down_weight.transpose(0, 2, 1),
    )
    x, gu, y, gates, cot_late = experts_forward(
        cols, n2_whole.reshape(row_total, D), prev_whole, cotangent, rw, carry, meta, slots, w_all
    )
    dx, dots, mixsum, gown, sib, hsoon = experts_backward(
        cols, ranks, cot_early, cot_late, y, gates, meta, slots, w_all, x, gu
    )
    layer_out, resid, gm, og, small, prev_grad, hin0, hrest = resid_step(
        cols, dx, meta, dots, rw, prev_whole, carry, cotangent, mixsum, n2_whole, middle, out_t, mixed, gown, sib
    )
    input_grad, small_all, qkv_grad, og_own, gate_grad, up_grad, down_grad, _ = finish_step(
        cols,
        ranks,
        gm,
        meta,
        lse,
        small,
        og.reshape(ranks // 2, 2, depth, D),
        inputs,
        rw,
        qkv,
        mixed_heads,
        whole_in,
        qkv_own,
        cosine,
        sines,
        resid,
        gown,
        sib,
        hsoon,
        hin0,
        hrest,
    )
    layer_out, input_grad, gate_grad, up_grad, down_grad, again, qkv_grad, out_grad, fgain, router, carry, const, vector, prev = (
        place_outputs(small_all, qkv_grad, og_own, prev_grad, layer_out, input_grad, gate_grad, up_grad, down_grad)
    )
    return (
        layer_out,
        input_grad,
        again,
        qkv_grad,
        out_grad,
        fgain,
        router.T,
        carry,
        const.transpose(0, 2, 1),
        vector,
        gate_grad,
        up_grad,
        down_grad.transpose(0, 2, 1),
        prev,
    )


def solution(mesh):
    sizes = (mesh.shape["row"], mesh.shape["col"])
    body = functools.partial(on_device_heads, sizes) if sizes == (8, 4) else on_device
    placed = (
        P(("row", "col"), None),
        P(),
        P("row", "col"),
        P("col", "row"),
        P(),
        P(),
        P(),
        P(),
        P(),
        P(None, "row", "col"),
        P(None, "row", "col"),
        P(None, "col", "row"),
        P(None, ("row", "col")),
        P("row", None),
        P("row", None),
        P(("row", "col"), None),
    )
    return jax.shard_map(
        body,
        mesh=mesh,
        in_specs=placed,
        out_specs=(
            P(("row", "col"), None),
            P(("row", "col"), None),
            P(),
            P("row", "col"),
            P("col", "row"),
            P(),
            P(),
            P(),
            P(),
            P(),
            P(None, "row", "col"),
            P(None, "row", "col"),
            P(None, "col", "row"),
            P(None, ("row", "col")),
        ),
        check_vma=False,
    )
```

```python
import functools
import math

import jax
import jax.numpy as jnp
import numpy as np
from jax import lax
from jax.experimental import pallas as pl
from jax.experimental.pallas import tpu as pltpu
from jax.sharding import PartitionSpec as P

D = 768
HEADS = 12
HEAD_DIM = 64
EXPERTS = 8
ROUTES = 12


EPS = 1e-06
BASE = 10000.0
NEG = -1e30
HIGH = lax.Precision.HIGHEST
CONTRACT_FIRST = (((0,), (0,)), ((), ()))
CONTRACT_LAST = (((1,), (1,)), ((), ()))


def rotate(block_value, positions, first_col, direction):
    row_count, col_count = block_value.shape
    column = first_col + jnp.arange(0, col_count, 2, dtype=jnp.int32)
    inner_col = column % D
    section = column // D
    head_pair = inner_col % HEAD_DIM // 2
    exponent = (2 * head_pair).astype(jnp.float32) / HEAD_DIM
    frequency = jnp.exp(-exponent * math.log(BASE))
    turned_on = (section < 2).astype(jnp.float32)
    angles = positions.astype(jnp.float32)[:, None] * (frequency * turned_on)[None, :]
    cosine = jnp.cos(angles)
    sines = direction * jnp.sin(angles)
    paired = block_value.reshape(row_count, col_count // 2, 2)
    first_part = paired[:, :, 0]
    second_part = paired[:, :, 1]
    rotated = jnp.stack(
        [first_part * cosine - second_part * sines, second_part * cosine + first_part * sines],
        axis=2,
    )
    return rotated.reshape(row_count, col_count)


def sequence_info(lengths_row, row_total):
    seq_count = lengths_row.shape[0]
    ends = jnp.cumsum(lengths_row)
    starts = ends - lengths_row
    token_place = jnp.arange(row_total, dtype=jnp.int32)
    seq_index = jnp.sum((token_place[:, None] >= ends[None, :]).astype(jnp.int32), axis=1)
    member = seq_index[:, None] == jnp.arange(seq_count, dtype=jnp.int32)[None, :]
    begin = jnp.sum(jnp.where(member, starts[None, :], 0), axis=1)
    return (seq_index, token_place - begin, seq_index < seq_count)


def partial_sums(term_value):
    return lax.psum_scatter(
        term_value.astype(jnp.bfloat16), "col", scatter_dimension=0, tiled=True
    ).astype(jnp.float32)


def whole_columns(part_value):
    return lax.all_gather(part_value, "col", axis=0, tiled=True)


def to_heads(block_value):
    return lax.all_to_all(block_value, "col", split_axis=0, concat_axis=1, tiled=True)


def to_features(block_value):
    return lax.all_to_all(block_value, "col", split_axis=1, concat_axis=0, tiled=True)


def key_scores(query_heads, key_block, query_seq, query_place, key_seq, key_place, score_scale):
    raw_scores = (
        jnp.einsum("qhd,khd->hqk", query_heads, key_block, preferred_element_type=jnp.float32)
        * score_scale
    )
    allowed = (query_seq[:, None] == key_seq[None, :]) & (
        key_place[None, :] <= query_place[:, None]
    )
    return (jnp.where(allowed[None], raw_scores, NEG), allowed)


def split_keys(key_values, seq_index, token_place, block_rows):
    count_blocks = key_values.shape[0] // block_rows
    blocks_kv = key_values.reshape(count_blocks, block_rows, 2, HEADS, HEAD_DIM)
    return (
        blocks_kv,
        seq_index.reshape(count_blocks, block_rows),
        token_place.reshape(count_blocks, block_rows),
    )


def attend_forward(
    queries, key_values, query_seq, query_place, seq_index, token_place, block_rows, score_scale
):
    local_rows = queries.shape[0]
    query_heads = queries.reshape(local_rows, HEADS, HEAD_DIM)
    key_items = split_keys(key_values, seq_index, token_place, block_rows)

    def max_step(running, block_items):
        running_max, running_sum = running
        kv_block, key_seq, key_place = block_items
        scores, allowed = key_scores(
            query_heads, kv_block[:, 0], query_seq, query_place, key_seq, key_place, score_scale
        )
        new_max = jnp.maximum(running_max, jnp.max(scores, axis=2))
        shifted = jnp.where(allowed[None], jnp.exp(scores - new_max[:, :, None]), 0.0)
        new_sum = running_sum * jnp.exp(running_max - new_max) + jnp.sum(shifted, axis=2)
        return ((new_max, new_sum), None)

    start_state = (
        jnp.full((HEADS, local_rows), NEG, jnp.float32),
        jnp.zeros((HEADS, local_rows), jnp.float32),
    )
    (final_max, final_sum), unused = lax.scan(max_step, start_state, key_items)
    log_total = final_max + jnp.log(final_sum)

    def out_step(running, block_items):
        kv_block, key_seq, key_place = block_items
        scores, allowed = key_scores(
            query_heads, kv_block[:, 0], query_seq, query_place, key_seq, key_place, score_scale
        )
        probs_low = jnp.exp(scores - log_total[:, :, None]).astype(jnp.bfloat16)
        return (
            running
            + jnp.einsum(
                "hqk,khd->qhd", probs_low, kv_block[:, 1], preferred_element_type=jnp.float32
            ),
            None,
        )

    attended, unused = lax.scan(
        out_step, jnp.zeros((local_rows, HEADS, HEAD_DIM), jnp.float32), key_items
    )
    return (attended.reshape(local_rows, D), log_total)


def attend_backward(
    queries,
    key_values,
    log_total,
    row_delta,
    grad_heads_in,
    query_seq,
    query_place,
    seq_index,
    token_place,
    block_rows,
    score_scale,
):
    local_rows = queries.shape[0]
    query_heads = queries.reshape(local_rows, HEADS, HEAD_DIM)
    grad_heads = grad_heads_in.reshape(local_rows, HEADS, HEAD_DIM)
    key_items = split_keys(key_values, seq_index, token_place, block_rows)

    def grad_step(running, block_items):
        kv_block, key_seq, key_place = block_items
        scores, allowed = key_scores(
            query_heads, kv_block[:, 0], query_seq, query_place, key_seq, key_place, score_scale
        )
        probs_full = jnp.exp(scores - log_total[:, :, None])
        probs_low = probs_full.astype(jnp.bfloat16)
        grad_probs = jnp.einsum(
            "qhd,khd->hqk", grad_heads, kv_block[:, 1], preferred_element_type=jnp.float32
        )
        grad_scores = (probs_full * (grad_probs - row_delta[:, :, None])).astype(jnp.bfloat16)
        new_running = (
            running
            + jnp.einsum(
                "hqk,khd->qhd", grad_scores, kv_block[:, 0], preferred_element_type=jnp.float32
            )
            * score_scale
        )
        grad_keys = (
            jnp.einsum("hqk,qhd->khd", grad_scores, query_heads, preferred_element_type=jnp.float32)
            * score_scale
        )
        grad_values = jnp.einsum(
            "hqk,qhd->khd", probs_low, grad_heads, preferred_element_type=jnp.float32
        )
        return (new_running, jnp.stack([grad_keys, grad_values], axis=1))

    grad_queries, grad_kv = lax.scan(
        grad_step, jnp.zeros((local_rows, HEADS, HEAD_DIM), jnp.float32), key_items
    )
    return (grad_queries.reshape(local_rows, D), grad_kv.reshape(key_values.shape[0], 2 * D))


def on_device(
    inputs,
    attn_gain,
    qkv_weight,
    out_weight,
    ffn_gain,
    router_weight,
    carry_weight,
    const_weight,
    const_vector,
    gate_weight,
    up_weight,
    down_weight,
    prev_logits,
    seq_lengths,
    expert_routes,
    cotangent,
):
    col_index = lax.axis_index("col")
    row_total = expert_routes.shape[0]
    local_rows = inputs.shape[0]
    capacity = row_total // 4
    block_rows = min(row_total, 512)
    score_scale = 1.0 / math.sqrt(HEAD_DIM)
    full_weights = (
        lax.all_gather(qkv_weight, "row", axis=0, tiled=True),
        lax.all_gather(out_weight, "row", axis=1, tiled=True),
        lax.all_gather(gate_weight, "row", axis=1, tiled=True),
        lax.all_gather(up_weight, "row", axis=1, tiled=True),
        lax.all_gather(down_weight, "row", axis=2, tiled=True),
    )
    qkv_full, out_full, gate_full, up_full, down_full = full_weights
    whole_in, whole_cot, whole_prev = (
        lax.all_gather(inputs, "col", axis=0, tiled=True),
        lax.all_gather(cotangent, "col", axis=0, tiled=True),
        lax.all_gather(prev_logits, "col", axis=1, tiled=True),
    )
    seq_index, positions, valid_all = sequence_info(seq_lengths[0], row_total)
    token_place = jnp.arange(row_total, dtype=jnp.int32)
    first_row = col_index * local_rows

    def own_rows(whole_value):
        return lax.dynamic_slice_in_dim(whole_value, first_row, local_rows, 0)

    query_seq = own_rows(seq_index)
    query_place = own_rows(token_place)
    query_pos = own_rows(positions)
    query_valid = own_rows(valid_all).astype(jnp.float32)[:, None]
    input_rows = whole_in.astype(jnp.float32)
    attn_gain_full = attn_gain.astype(jnp.float32)
    scale_attn = lax.rsqrt(jnp.mean(input_rows * input_rows, axis=1, keepdims=True) + EPS)
    normed1 = (input_rows * scale_attn * attn_gain_full).astype(jnp.bfloat16)
    projected = jnp.dot(normed1, qkv_full, preferred_element_type=jnp.float32)
    turned = rotate(projected, positions, col_index * projected.shape[1], 1.0).astype(jnp.bfloat16)
    token_qkv = to_heads(turned)
    queries = token_qkv[:, :D]
    key_values = lax.all_gather(token_qkv[:, D:], "col", axis=0, tiled=True)
    attended, log_total = attend_forward(
        queries, key_values, query_seq, query_place, seq_index, token_place, block_rows, score_scale
    )
    attn_tok = (attended * query_valid).astype(jnp.bfloat16)
    attn_feat = to_features(attn_tok)
    attn_out = partial_sums(jnp.dot(attn_feat, out_full, preferred_element_type=jnp.float32))
    input_local = inputs.astype(jnp.float32)
    middle = input_local + attn_out
    scale_ffn = lax.rsqrt(jnp.mean(middle * middle, axis=1, keepdims=True) + EPS)
    ffn_gain_full = ffn_gain.astype(jnp.float32)
    normed2_local = (middle * scale_ffn * ffn_gain_full).astype(jnp.bfloat16)
    normed2 = whole_columns(normed2_local)
    carry_full = carry_weight.astype(jnp.float32)
    prev_rows = whole_prev.astype(jnp.float32).T
    route_hot = (
        expert_routes[:, :, None] == jnp.arange(ROUTES, dtype=jnp.int32)[None, None, :]
    ).astype(jnp.float32)
    logits = jnp.dot(normed2, router_weight, preferred_element_type=jnp.float32) + jnp.dot(
        prev_rows, carry_full, precision=HIGH
    )
    picked = jnp.sum(route_hot * logits[:, None, :], axis=2)
    gate_values = jax.nn.softmax(picked, axis=1)
    flat_route = expert_routes.reshape(-1)
    route_hits = (flat_route[:, None] == jnp.arange(EXPERTS, dtype=jnp.int32)[None, :]).astype(
        jnp.int32
    )
    slot_index = jnp.sum((jnp.cumsum(route_hits, axis=0) - 1) * route_hits, axis=1)
    dump_slot = EXPERTS * capacity
    target = jnp.where(flat_route < EXPERTS, flat_route * capacity + slot_index, dump_slot)
    slot_owner = (
        jnp.full((dump_slot + 1,), row_total, jnp.int32)
        .at[target]
        .set(jnp.arange(2 * row_total, dtype=jnp.int32) // 2)[:dump_slot]
    )
    slot_gate = (
        jnp.zeros((dump_slot + 1,), jnp.float32)
        .at[target]
        .set(gate_values.reshape(-1))[:dump_slot]
        .reshape(EXPERTS, capacity, 1)
    )
    zero_row = jnp.zeros((1, D), jnp.bfloat16)
    expert_in = jnp.concatenate([normed2, zero_row], axis=0)[slot_owner].reshape(
        EXPERTS, capacity, D
    )
    gate_pre = jnp.einsum("ecd,edf->ecf", expert_in, gate_full, preferred_element_type=jnp.float32)
    up_pre = jnp.einsum("ecd,edf->ecf", expert_in, up_full, preferred_element_type=jnp.float32)
    sigmoid_gate = jax.nn.sigmoid(gate_pre)
    activated = gate_pre * sigmoid_gate
    hidden = (activated * up_pre).astype(jnp.bfloat16)
    expert_out = jnp.einsum("ecf,efd->ecd", hidden, down_full, preferred_element_type=jnp.float32)
    out_rows = jnp.concatenate(
        [expert_out.reshape(dump_slot, D), jnp.zeros((1, D), jnp.float32)], axis=0
    )
    chosen_out = out_rows[target].reshape(row_total, 2, D)
    cot_rows = whole_cot.astype(jnp.float32)
    ffn_mix = jnp.sum(gate_values[:, :, None] * chosen_out, axis=1)
    ffn_dots = jnp.sum(cot_rows[:, None, :] * chosen_out, axis=2)
    mix_local = partial_sums(ffn_mix)
    normed_local = normed2_local.astype(jnp.float32)
    vector_full = const_vector.astype(jnp.float32)
    routes_local = own_rows(expert_routes)
    gates_local = own_rows(gate_values)
    hot_local = own_rows(route_hot)
    copy_hit = (routes_local == EXPERTS + 1).astype(jnp.float32)
    const_hit = (
        routes_local[:, :, None] == (EXPERTS + 2 + jnp.arange(2, dtype=jnp.int32))[None, None, :]
    ).astype(jnp.float32)
    copy_share = jnp.sum(gates_local * copy_hit, axis=1)
    const_share = jnp.sum(gates_local[:, :, None] * const_hit, axis=1)
    const_alpha = jax.nn.softmax(
        jnp.einsum("td,jdk->tjk", normed2_local, const_weight, preferred_element_type=jnp.float32),
        axis=2,
    )
    keep_share = copy_share + jnp.sum(const_share * const_alpha[:, :, 0], axis=1)
    local_mix = keep_share[:, None] * normed_local + jnp.dot(
        const_share * const_alpha[:, :, 1], vector_full, precision=HIGH
    )
    layer_out = (middle + mix_local + local_mix).astype(jnp.bfloat16)
    qkv_full, out_full, gate_full, up_full, down_full = full_weights
    ffn_total = lax.psum(ffn_dots, "col")
    ffn_local = own_rows(ffn_total)
    cot_local = cotangent.astype(jnp.float32)
    dot_keep = jnp.sum(cot_local * normed_local, axis=1)
    dot_vector = jnp.dot(cot_local, vector_full.T, precision=HIGH)
    const_dots = const_alpha[:, :, 0] * dot_keep[:, None] + const_alpha[:, :, 1] * dot_vector
    grad_gates = (
        ffn_local
        + copy_hit * dot_keep[:, None]
        + jnp.sum(const_hit * const_dots[:, None, :], axis=2)
    )
    grad_picked = gates_local * (
        grad_gates - jnp.sum(gates_local * grad_gates, axis=1, keepdims=True)
    )
    grad_logits = jnp.sum(hot_local * grad_picked[:, :, None], axis=1)
    prev_local = prev_logits.astype(jnp.float32).T
    router_grad = lax.dot_general(normed_local, grad_logits, CONTRACT_FIRST, precision=HIGH)
    carry_grad = lax.dot_general(prev_local, grad_logits, CONTRACT_FIRST, precision=HIGH)
    prev_grad = lax.dot_general(carry_full, grad_logits, CONTRACT_LAST, precision=HIGH)
    grad_alpha_keep = const_share * dot_keep[:, None]
    grad_alpha_vector = const_share * dot_vector
    alpha_mean = const_alpha[:, :, 0] * grad_alpha_keep + const_alpha[:, :, 1] * grad_alpha_vector
    grad_alpha_logits = jnp.stack(
        [
            const_alpha[:, :, 0] * (grad_alpha_keep - alpha_mean),
            const_alpha[:, :, 1] * (grad_alpha_vector - alpha_mean),
        ],
        axis=2,
    )
    const_grad = jnp.einsum("td,tjk->jdk", normed_local, grad_alpha_logits, precision=HIGH)
    vector_grad = lax.dot_general(
        const_share * const_alpha[:, :, 1], cot_local, CONTRACT_FIRST, precision=HIGH
    )
    router_full = router_weight.astype(jnp.float32)
    const_full = const_weight.astype(jnp.float32)
    grad_normed_local = (
        keep_share[:, None] * cot_local
        + lax.dot_general(grad_logits, router_full, CONTRACT_LAST, precision=HIGH)
        + jnp.einsum("tjk,jdk->td", grad_alpha_logits, const_full, precision=HIGH)
    )
    cot_in = jnp.concatenate([whole_cot, zero_row], axis=0)[slot_owner].reshape(
        EXPERTS, capacity, D
    )
    grad_expert = (slot_gate * cot_in.astype(jnp.float32)).astype(jnp.bfloat16)
    down_grad = jnp.einsum("ecf,ecd->efd", hidden, grad_expert, preferred_element_type=jnp.float32)
    grad_hidden = jnp.einsum(
        "ecd,efd->ecf", grad_expert, down_full, preferred_element_type=jnp.float32
    )
    grad_gate_pre = (
        grad_hidden * up_pre * sigmoid_gate * (1.0 + gate_pre * (1.0 - sigmoid_gate))
    ).astype(jnp.bfloat16)
    grad_up_pre = (grad_hidden * activated).astype(jnp.bfloat16)
    gate_grad = jnp.einsum(
        "ecd,ecf->edf", expert_in, grad_gate_pre, preferred_element_type=jnp.float32
    )
    up_grad = jnp.einsum("ecd,ecf->edf", expert_in, grad_up_pre, preferred_element_type=jnp.float32)
    grad_expert_in = jnp.einsum(
        "ecf,edf->ecd", grad_gate_pre, gate_full, preferred_element_type=jnp.float32
    ) + jnp.einsum("ecf,edf->ecd", grad_up_pre, up_full, preferred_element_type=jnp.float32)
    grad_slots = jnp.concatenate(
        [grad_expert_in.reshape(dump_slot, D), jnp.zeros((1, D), jnp.float32)], axis=0
    )
    grad_tokens = jnp.sum(grad_slots[target].reshape(row_total, 2, D), axis=1)
    grad_normed = partial_sums(grad_tokens) + grad_normed_local
    gained_ffn = grad_normed * ffn_gain_full
    ffn_dots_rows = jnp.sum(gained_ffn * middle, axis=1, keepdims=True)
    grad_middle = scale_ffn * gained_ffn - middle * scale_ffn**3 * (ffn_dots_rows / D)
    ffn_gain_grad = jnp.sum(grad_normed * middle * scale_ffn, axis=0)
    grad_resid = cot_local + grad_middle
    branch_cot = whole_columns(grad_resid.astype(jnp.bfloat16))
    out_grad = lax.dot_general(
        attn_feat, branch_cot, CONTRACT_FIRST, preferred_element_type=jnp.float32
    )
    grad_mixed = lax.dot_general(
        branch_cot, out_full, CONTRACT_LAST, preferred_element_type=jnp.float32
    )
    grad_tok = to_heads(grad_mixed.astype(jnp.bfloat16))
    grad_heads_in = (grad_tok.astype(jnp.float32) * query_valid).astype(jnp.bfloat16)
    row_delta = jnp.sum(
        grad_heads_in.astype(jnp.float32).reshape(local_rows, HEADS, HEAD_DIM)
        * attended.reshape(local_rows, HEADS, HEAD_DIM),
        axis=2,
    ).T
    grad_queries, grad_kv = attend_backward(
        queries,
        key_values,
        log_total,
        row_delta,
        grad_heads_in,
        query_seq,
        query_place,
        seq_index,
        token_place,
        block_rows,
        score_scale,
    )
    grad_kv_local = lax.psum_scatter(
        grad_kv.astype(jnp.bfloat16), "col", scatter_dimension=0, tiled=True
    ).astype(jnp.float32)
    grad_turned = jnp.concatenate([grad_queries, grad_kv_local], axis=1)
    grad_proj_tok = rotate(grad_turned, query_pos, 0, -1.0).astype(jnp.bfloat16)
    grad_projected = to_features(grad_proj_tok)
    qkv_grad = lax.dot_general(
        normed1, grad_projected, CONTRACT_FIRST, preferred_element_type=jnp.float32
    )
    grad_normed1 = partial_sums(
        lax.dot_general(grad_projected, qkv_full, CONTRACT_LAST, preferred_element_type=jnp.float32)
    )
    scale_attn_local = own_rows(scale_attn)
    gained_attn = grad_normed1 * attn_gain_full
    attn_dots_rows = jnp.sum(gained_attn * input_local, axis=1, keepdims=True)
    input_grad = (
        grad_resid
        + scale_attn_local * gained_attn
        - input_local * scale_attn_local**3 * (attn_dots_rows / D)
    )
    attn_gain_grad = jnp.sum(grad_normed1 * input_local * scale_attn_local, axis=0)
    qkv_grad, out_grad, gate_grad, up_grad, down_grad = (
        lax.psum_scatter(
            qkv_grad.astype(jnp.bfloat16), "row", scatter_dimension=0, tiled=True
        ).astype(jnp.float32),
        lax.psum_scatter(
            out_grad.astype(jnp.bfloat16), "row", scatter_dimension=1, tiled=True
        ).astype(jnp.float32),
        lax.psum_scatter(
            gate_grad.astype(jnp.bfloat16), "row", scatter_dimension=1, tiled=True
        ).astype(jnp.float32),
        lax.psum_scatter(
            up_grad.astype(jnp.bfloat16), "row", scatter_dimension=1, tiled=True
        ).astype(jnp.float32),
        lax.psum_scatter(
            down_grad.astype(jnp.bfloat16), "row", scatter_dimension=2, tiled=True
        ).astype(jnp.float32),
    )
    attn_gain_grad, ffn_gain_grad, router_grad, carry_grad, const_grad, vector_grad = lax.psum(
        (attn_gain_grad, ffn_gain_grad, router_grad, carry_grad, const_grad, vector_grad),
        ("row", "col"),
    )
    return (
        layer_out,
        input_grad,
        attn_gain_grad,
        qkv_grad,
        out_grad,
        ffn_gain_grad,
        router_grad,
        carry_grad,
        const_grad,
        vector_grad,
        gate_grad,
        up_grad,
        down_grad,
        prev_grad,
    )


BF = jnp.bfloat16
F32 = jnp.float32
LANES = 128
NN = (((1,), (0,)), ((), ()))
NT = (((1,), (1,)), ((), ()))
TN = (((0,), (0,)), ((), ()))
ROW_CONST = 12
ROW_VEC = 16
ROW_GAIN = 18
SMALL_ROWS = 24
Q_ROWS = 256
MIB = 1 << 20


def mm(a, b, dims=NN):
    return lax.dot_general(a, b, dims, preferred_element_type=F32)


def lane_iota(shape):
    return lax.broadcasted_iota(jnp.int32, shape, len(shape) - 1)


def whole(shape):
    return pl.BlockSpec(tuple(shape), lambda *_: (0,) * len(shape), pipeline_mode=pl.Buffered(1))


def swap_pairs(v):
    even = lane_iota(v.shape) % 2 == 0
    return jnp.where(even, pltpu.roll(v, LANES - 1, 1), pltpu.roll(v, 1, 1))


def norm_rows(x):
    return lax.rsqrt(jnp.mean(x * x, axis=1, keepdims=True) + EPS)


def seen(begin, first, rows, length):
    u = lax.broadcasted_iota(jnp.int32, (rows, length), 1)
    t = lax.broadcasted_iota(jnp.int32, (rows, length), 0) + first
    return (u >= begin) & (u <= t)


def gate_lanes(logits, meta):
    lane = lane_iota(logits.shape)
    hit = (pltpu.roll(meta, LANES - META_HIT, 1) > 0.0) & (lane < ROUTES)
    held = jnp.where(hit, logits, NEG)
    e = jnp.where(hit, jnp.exp(held - jnp.max(held, axis=1, keepdims=True)), 0.0)
    return e / jnp.sum(e, axis=1, keepdims=True)


MESH = pl.DeviceIdType.MESH
ANY = pl.BlockSpec(memory_space=pl.ANY)


def place():
    return lax.axis_index("row"), lax.axis_index("col")


def flip(index, mask):
    for bit in (1, 2, 4):
        if mask & bit:
            index = index + bit - 2 * bit * (index // bit % 2)
    return index


def greet(devices):
    barrier = pltpu.get_barrier_semaphore()
    for device in devices:
        pl.semaphore_signal(barrier, inc=1, device_id=device, device_id_type=MESH)
    pl.semaphore_wait(barrier, len(devices))


def send_to(src, dst, send, recv, device):
    return pltpu.make_async_remote_copy(
        src_ref=src, dst_ref=dst, send_sem=send, recv_sem=recv, device_id=device, device_id_type=MESH
    )


def col_peers(n):
    r, c = place()
    return [(r, (c + k) % n) for k in range(1, n)]


def gather_chain(own, dst, send, recv, n):
    r, c = place()

    def right(k):
        i = jnp.maximum(c - k, 0)
        src = own if k == 0 else dst.at[i]
        return send_to(src, dst.at[i], send.at[0, k], recv.at[0, k], (r, jnp.minimum(c + 1, n - 1)))

    def left(k):
        i = jnp.minimum(c + k, n - 1)
        src = own if k == 0 else dst.at[i]
        return send_to(src, dst.at[i], send.at[1, k], recv.at[1, k], (r, jnp.maximum(c - 1, 0)))

    def step(k):
        if k > 0:

            @pl.when(c >= k)
            def _():
                right(k - 1).wait_recv()

            @pl.when(c + k < n)
            def _():
                left(k - 1).wait_recv()

        if k < n - 1:

            @pl.when((c >= k) & (c + 1 < n))
            def _():
                right(k).start()

            @pl.when((c + k < n) & (c >= 1))
            def _():
                left(k).start()

    def drain():
        for k in range(n - 1):

            @pl.when((c >= k) & (c + 1 < n))
            def _():
                right(k).wait_send()

            @pl.when((c + k < n) & (c >= 1))
            def _():
                left(k).wait_send()

    return step, drain


def reduce_chain(own, out, arrived, send, recv, n):
    r, c = place()

    def right(k):
        return send_to(out.at[0, k], arrived.at[0, k], send.at[0, k], recv.at[0, k], (r, jnp.minimum(c + 1, n - 1)))

    def left(k):
        return send_to(out.at[1, k], arrived.at[1, k], send.at[1, k], recv.at[1, k], (r, jnp.maximum(c - 1, 0)))

    def slot(s):
        if s == n - 1:

            @pl.when(c >= 1)
            def _():
                right(n - 1 - c).wait_recv()

            @pl.when(c <= n - 2)
            def _():
                left(c).wait_recv()

            return

        @pl.when(c <= s)
        def _():
            k = jnp.maximum(s - c, 0)

            @pl.when(c >= 1)
            def _():
                right(k).wait_recv()
                out[0, k] = (own(n - 1 - k).astype(F32) + arrived[0, k].astype(F32)).astype(BF)

            @pl.when(c == 0)
            def _():
                out[0, k] = own(n - 1 - k).astype(BF)

            right(k).start()

        @pl.when(n - 1 - c <= s)
        def _():
            k = jnp.maximum(s - (n - 1 - c), 0)

            @pl.when(c <= n - 2)
            def _():
                left(k).wait_recv()
                out[1, k] = (own(k).astype(F32) + arrived[1, k].astype(F32)).astype(BF)

            @pl.when(c == n - 1)
            def _():
                out[1, k] = own(k).astype(BF)

            left(k).start()

    def total(dst):
        dst[...] = own(c).astype(F32)

        @pl.when(c >= 1)
        def _():
            dst[...] += arrived[0, n - 1 - c].astype(F32)

        @pl.when(c <= n - 2)
        def _():
            dst[...] += arrived[1, c].astype(F32)

    def drain():
        for k in range(n - 1):

            @pl.when(c < n - 1 - k)
            def _():
                right(k).wait_send()

            @pl.when(c > k)
            def _():
                left(k).wait_send()

    return slot, total, drain


def chain_scratch(n, rows):
    return [
        pltpu.VMEM((2, n - 1, rows, D), BF),
        pltpu.VMEM((2, n - 1, rows, D), BF),
        pltpu.SemaphoreType.DMA((2, n - 1)),
        pltpu.SemaphoreType.DMA((2, n - 1)),
    ]


def slot_rows(slots_ref, e, capacity):
    rows = slots_ref.shape[1]
    spots = lax.broadcasted_iota(jnp.int32, (capacity, rows), 0)
    return jnp.where(spots == slots_ref[pl.ds(e, 1)], 1.0, 0.0).astype(BF)


def slot_gates(one, gates_ref, e):
    sg = mm(one, gates_ref[...])
    return jnp.sum(jnp.where(lane_iota(sg.shape) % LANES == e, sg, 0.0), axis=1, keepdims=True)


def chain_order(c):
    return [d + (3 - 2 * d) * (c // 2) for d in (3, 2, 0, 1)]


def combine(meta_ref, y_ref, d, local):
    experts, capacity, width = y_ref.shape
    at = pl.ds(pl.multiple_of(d * local, LANES), local)
    lane = lane_iota((local, capacity)).astype(F32)
    ones = [jnp.where(lane == column(meta_ref, at, e), 1.0, 0.0).astype(BF) for e in range(experts)]
    return mm(jnp.concatenate(ones, axis=1), y_ref[...].reshape(experts * capacity, width)).astype(BF)


META_HIT, META_BEGIN, META_VALID = 8, 20, 21
EARLY = 3
SENT_SOON, SENT_NEXT = 2, 3


def column(ref, at, lane):
    return ref[at, lane : lane + 1]


def start_all(copies):
    for copy in copies:
        copy.start()


def wait_all(copies):
    for copy in copies:
        copy.wait()


def moves(pairs, sem):
    return [pltpu.make_async_copy(src, dst, sem.at[i]) for i, (src, dst) in enumerate(pairs)]


def pack_head(value):
    half = value.shape[0] // 2
    return jnp.concatenate([value[:half], value[half:]], axis=1)


def unpack_head(packed):
    return jnp.concatenate([packed[:, :HEAD_DIM], packed[:, HEAD_DIM:]], axis=0)


def to_rows(src_of, dst, send, recv, ranks):
    r, c = place()
    copies = []
    for m in range(1, ranks):
        there = flip(r, m)
        copies.append(send_to(src_of(there), dst.at[r], send.at[m - 1], recv.at[m - 1], (there, c)))
    return copies


def to_cols(src_of, dst, send, recv, n):
    r, c = place()
    copies = []
    for k in range(1, n):
        there = (c + k) % n
        copies.append(send_to(src_of(there), dst.at[c], send.at[k - 1], recv.at[k - 1], (r, there)))
    return copies


def to_chips(src_of, dst, send, recv):
    r, c = place()
    return [
        send_to(src_of(flip(r // 2, k)), dst.at[k - 1], send.at[k - 1], recv.at[k - 1], (flip(r, 2 * k), c))
        for k in range(1, 4)
    ]


def all_sum(ref, count):
    total = ref[0].astype(F32)
    for i in range(1, count):
        total = total + ref[i].astype(F32)
    return total


def tokens_meta(routes_ref, lengths_ref, rows, experts):
    kinds = lax.broadcasted_iota(jnp.int32, (16, rows), 0)
    hits = jnp.where((kinds == routes_ref[0:1]) | (kinds == routes_ref[1:2]), 1.0, 0.0)
    step = 256
    earlier = lax.broadcasted_iota(jnp.int32, (step, step), 0) < lax.broadcasted_iota(
        jnp.int32, (step, step), 1
    )
    earlier = jnp.where(earlier, 1.0, 0.0).astype(BF)
    counts, running = [], jnp.zeros((16, 1), F32)
    for b in range(rows // step):
        block = hits[:, b * step : (b + 1) * step]
        counts.append(mm(block.astype(BF), earlier) + running)
        running = running + jnp.sum(block, axis=1, keepdims=True)
    slots = jnp.where(hits > 0.0, jnp.concatenate(counts, axis=1), -1.0)[:experts]
    spot = lax.broadcasted_iota(jnp.int32, (8, rows), 1)
    begin, end = jnp.zeros((8, rows), F32), 0
    for i in range(lengths_ref.shape[1]):
        end = end + lengths_ref[0, i]
        begin = jnp.where(spot >= end, end.astype(F32), begin)
    valid = jnp.where(spot < end, 1.0, 0.0)
    tail = jnp.where(lax.broadcasted_iota(jnp.int32, (8, rows), 0) == 0, begin, valid)
    spare = jnp.zeros((LANES - experts - 12 - 8, rows), F32)
    meta = jnp.concatenate([slots, hits[:12], tail, spare], axis=0).T
    return slots.astype(jnp.int32), meta


def first_kernel(
    cols,
    ranks,
    x_ref,
    cot_ref,
    router_ref,
    const_ref,
    vector_ref,
    again_ref,
    fgain_ref,
    carry_ref,
    wq_ref,
    wo_ref,
    prev_ref,
    routes_ref,
    lengths_ref,
    cos_ref,
    sin_ref,
    freq_ref,
    gate_ref,
    up_ref,
    down_ref,
    wall_ref,
    qkv_out,
    o_out,
    lse_out,
    xw_out,
    wq_out,
    wo_out,
    cos_out,
    sin_out,
    meta_out,
    slots_ref,
    mixed_out,
    middle_out,
    n2w_ref,
    prevw_out,
    cota_ref,
    rw_out,
    carry_out,
    xw,
    q_parts,
    q_land,
    o_parts,
    o_land,
    wq,
    wo,
    a_send,
    a_land,
    prev_s,
    prevw,
    qkv_s,
    o_s,
    lse_s,
    cos_s,
    sin_s,
    meta_s,
    mixed_s,
    middle_s,
    n2_s,
    w_s,
    local_sem,
    x_send,
    x_recv,
    n_send,
    n_recv,
    t_send,
    t_recv,
    q_send,
    q_recv,
    c_send,
    c_recv,
    r_send,
    r_recv,
    e_send,
    e_recv,
    d_send,
    d_recv,
    s_send,
    s_recv,
    h_send,
    h_recv,
):
    r, c = place()
    heads = 3
    local = x_ref.shape[0]
    rows = local * cols
    width = heads * HEAD_DIM
    depth = D // ranks
    odd, high = c % 2, c // 2
    again = again_ref[...].astype(F32).reshape(1, D)
    fgain = fgain_ref[...].astype(F32).reshape(1, D)
    greet(col_peers(cols) + [(flip(r, m), c) for m in (1, 2, 4, 6)])

    for s in range(3):
        q_parts[s] = wq_ref[:, s * width : (s + 1) * width]
    q_copies = [
        send_to(q_parts.at[1], q_land.at[(c + 1) // 2], q_send.at[0], q_recv.at[0], (r, flip(c, 1))),
        send_to(q_parts.at[2 - 2 * odd], q_land.at[2 * high], q_send.at[1], q_recv.at[1], (r, flip(c, 2))),
    ]
    start_all(q_copies)
    o_parts[...] = wo_ref[...].astype(F32).T.astype(BF)
    prev_s[...] = jnp.concatenate([prev_ref[...].astype(F32), jnp.zeros((16 - ROUTES, local), F32)], axis=0).astype(BF)
    o_copies = to_cols(lambda d: o_parts, o_land, c_send.at[0], c_recv.at[0], cols)
    prev_copies = to_cols(lambda d: prev_s, prevw, c_send.at[1], c_recv.at[1], cols)
    x_step, x_drain = gather_chain(x_ref, xw, x_send, x_recv, cols)
    x_step(0)
    start_all(o_copies + prev_copies)
    q_land[(c + 1) // 2] = q_parts[2 * odd]
    o_land[c] = o_parts[...]
    prevw[c] = prev_s[...]
    xw[c] = x_ref[...]

    def rows_at(d):
        return pl.ds(pl.multiple_of(d * depth, 16), depth)

    def push(ref, at):
        here = ref.at[rows_at(r)]
        return [
            send_to(here, here, r_send.at[at, k - 1], r_recv.at[at, k - 1], (flip(r, 2 * k), c))
            for k in range(1, 4)
        ]

    def hand(ref, at):
        copies = []
        for k in range(4):
            here = ref.at[rows_at(flip(r, 2 * k))]
            copies.append(send_to(here, here, r_send.at[at, 3 + k], r_recv.at[at, 3 + k], (flip(r, 1), c)))
        return copies

    wait_all(q_copies)
    wq[rows_at(r)] = jnp.concatenate([q_land[i] for i in range(3)], axis=1)
    wq_push, wq_hand = push(wq, 0), hand(wq, 0)
    start_all(wq_push)
    wait_all(o_copies)
    wo[rows_at(r)] = jnp.concatenate([o_land[i] for i in range(cols)], axis=1)
    wo_push, wo_hand = push(wo, 1), hand(wo, 1)
    start_all(wo_push)

    weights = (gate_ref, up_ref, down_ref)
    half = gate_ref.shape[0] // 2
    held = moves([(ref, w_s.at[t]) for t, ref in enumerate(weights)], local_sem)
    kept = moves([(w_s.at[t], wall_ref.at[t, :, rows_at(r)]) for t in range(3)], local_sem)

    def to_near(t):
        dst = wall_ref.at[t, :, rows_at(r)]
        return [
            send_to(weights[t], dst, e_send.at[t, k - 1], e_recv.at[t, k - 1], (flip(r, 2 * k), c))
            for k in (1, 2)
        ]

    def to_far(t):
        copies = []
        for k in (1, 2):
            here = wall_ref.at[t, pl.ds((k - 1) * half, half), rows_at(flip(r, 2 * k))]
            copies.append(send_to(here, here, d_send.at[t, k - 1], d_recv.at[t, k - 1], (flip(r, 6 - 2 * k), c)))
        return copies

    def to_other_core(t):
        copies = []
        for k in range(4):
            here = wall_ref.at[t, :, rows_at(flip(r, 2 * k))]
            src = weights[t] if k == 0 else here
            copies.append(send_to(src, here, s_send.at[t, k], s_recv.at[t, k], (flip(r, 1), c)))
        return copies

    def relay(t):
        for near, far, across in zip(to_near(t), to_far(t), to_other_core(t)[1:3]):
            near.wait_recv()
            far.start()
            across.start()

    def hand_over(t):
        for far in to_far(t):
            far.wait_recv()
        to_other_core(t)[3].start()

    for t in range(3):
        start_all(to_near(t))
        to_other_core(t)[0].start()
    start_all(held)

    small = [ref[...].astype(F32) for ref in (router_ref, const_ref.at[0], const_ref.at[1], vector_ref)]
    small += [again, fgain, jnp.zeros((LANES - ROW_GAIN - 2, D), F32)]
    rw_out[...] = jnp.concatenate(small, axis=0).astype(BF)
    carry = jnp.concatenate([carry_ref[...].astype(F32), jnp.zeros((ROUTES, LANES - ROUTES), F32)], axis=1)
    carry_out[...] = jnp.concatenate([carry, jnp.zeros((16 - ROUTES, LANES), F32)], axis=0).astype(BF)
    slots, meta = tokens_meta(routes_ref, lengths_ref, rows, EXPERTS)
    slots_ref[...] = slots
    meta_s[...] = meta
    sub = lax.broadcasted_iota(jnp.int32, (8, LANES), 0)
    firsts, end, ends = jnp.zeros((8, LANES), F32), 0, []
    for i in range(lengths_ref.shape[1]):
        firsts = jnp.where(sub == i, jnp.asarray(end, jnp.int32).astype(F32), firsts)
        end = end + lengths_ref[0, i]
        ends.append(end)
    angle = firsts * freq_ref[...]
    cos_first, sin_first = jnp.cos(angle), jnp.sin(angle)
    spot = lax.broadcasted_iota(jnp.int32, (rows, LANES), 0)
    cb, sb = jnp.ones((rows, LANES), F32), jnp.zeros((rows, LANES), F32)
    for i in range(1, len(ends)):
        cb = jnp.where(spot >= ends[i - 1], cos_first[i : i + 1], cb)
        sb = jnp.where(spot >= ends[i - 1], sin_first[i : i + 1], sb)
    cb, sb = jnp.where(spot >= end, 1.0, cb), jnp.where(spot >= end, 0.0, sb)
    sign = jnp.where(lane_iota((rows, LANES)) % 2 == 0, -1.0, 1.0)
    cos_s[...] = cos_ref[...] * cb + sin_ref[...] * sb
    sin_s[...] = (sin_ref[...] * cb - cos_ref[...] * sb) * sign
    lse_s[...] = jnp.zeros_like(lse_s)

    def project(d):
        at = pl.ds(pl.multiple_of(d * local, LANES), local)
        x = xw[d].astype(F32)
        normed = (x * norm_rows(x) * again).astype(BF)
        proj = mm(normed, wq[...])
        cosine, sines = cos_s[at], sin_s[at]
        for part in range(2 * width // LANES):
            v = proj[:, part * LANES : (part + 1) * LANES]
            t = v * cosine + swap_pairs(v) * sines
            for side in range(2):
                head = 2 * part + side
                piece = t[:, side * HEAD_DIM : (side + 1) * HEAD_DIM].astype(BF)
                if head < heads:
                    piece = piece * jnp.asarray(1.0 / math.sqrt(HEAD_DIM), BF)
                qkv_s[head, at] = piece
        for head in range(2 * heads, 3 * heads):
            qkv_s[head, at] = proj[:, head * HEAD_DIM : (head + 1) * HEAD_DIM].astype(BF)

    def project_at(k):
        def side(way, carry):
            d = c + k * (2 * way - 1)

            @pl.when((d >= 0) & (d < cols))
            def _():
                project(jnp.clip(d, 0, cols - 1))

            return carry

        lax.fori_loop(0, 2 if k else 1, side, 0)

    early = local // EARLY
    cot_step, cot_drain = gather_chain(cot_ref.at[pl.ds(0, early)], cota_ref, t_send, t_recv, cols)
    cot_kept = moves([(cot_ref.at[pl.ds(0, early)], cota_ref.at[c])], local_sem.at[pl.ds(3, 1)])

    wait_all(held)
    start_all(kept)
    x_step(1)
    for copy in wq_push:
        copy.wait_recv()
    start_all(wq_hand)
    x_step(2)
    for copy in wo_push:
        copy.wait_recv()
    start_all(wo_hand)
    wait_all(wq_hand)
    project_at(0)
    project_at(1)
    project_at(2)
    relay(0)
    x_step(3)
    cot_step(0)
    start_all(cot_kept)
    project_at(3)
    cot_step(1)

    blocks = rows // Q_ROWS

    def head_copies(h):
        copies = []
        for k in range(1, cols):
            there = (c + k) % cols
            copies.append(
                send_to(a_send.at[there, h], a_land.at[c, h], h_send.at[h, k - 1], h_recv.at[h, k - 1], (r, there))
            )
        return copies

    def one_head(h, carry):
        for i in range(blocks):
            at = slice(i * Q_ROWS, (i + 1) * Q_ROWS)
            length = (i + 1) * Q_ROWS
            s = mm(qkv_s[h, at], qkv_s[heads + h, :length], NT)
            begin = column(meta_s, at, META_BEGIN).astype(jnp.int32)
            s = jnp.where(seen(begin, i * Q_ROWS, Q_ROWS, length), s, NEG)
            top = jnp.max(s, axis=1, keepdims=True)
            p = jnp.exp(s - top)
            total = jnp.sum(p, axis=1, keepdims=True)
            o = mm(p.astype(BF), qkv_s[2 * heads + h, :length]) * (column(meta_s, at, META_VALID) / total)
            o_s[h, at] = o.astype(BF)
            lse_s[at] = jnp.where(lane_iota((Q_ROWS, LANES)) == h, top + jnp.log(total), lse_s[at])
        for d in range(cols):
            a_send[d, h] = pack_head(o_s[h, d * local : (d + 1) * local])
        start_all(head_copies(h))
        return carry

    lax.fori_loop(0, 1, one_head, 0)
    cot_step(2)
    lax.fori_loop(1, heads, one_head, 0)
    a_land[c] = a_send[c]
    stored = moves(
        [
            (xw, xw_out),
            (wq, wq_out),
            (qkv_s, qkv_out),
            (o_s, o_out),
            (lse_s, lse_out),
            (cos_s, cos_out),
            (sin_s, sin_out),
            (meta_s, meta_out),
        ],
        local_sem.at[pl.ds(4, 8)],
    )
    start_all(stored)
    relay(1)
    wait_all(wo_hand)
    for h in range(heads):
        wait_all(head_copies(h))
    mixed = jnp.concatenate([unpack_head(a_land[i, h]) for i in range(cols) for h in range(heads)], axis=1)
    mixed_s[...] = mixed
    middle = x_ref[...].astype(F32) + mm(mixed, wo[...], NT)
    middle_s[...] = middle
    n2_s[...] = (middle * norm_rows(middle) * fgain).astype(BF)
    n_step, n_drain = gather_chain(n2_s, n2w_ref, n_send, n_recv, cols)
    n_step(0)
    wait_all(prev_copies)
    stored_late = moves(
        [(n2_s, n2w_ref.at[c]), (wo, wo_out), (mixed_s, mixed_out), (middle_s, middle_out), (prevw, prevw_out)],
        local_sem.at[pl.ds(12, 5)],
    )
    start_all(stored_late)
    relay(2)
    n_step(1)
    hand_over(0)
    n_step(2)
    hand_over(1)
    hand_over(2)
    n_step(3)
    cot_step(3)
    x_drain()
    n_drain()
    cot_drain()
    for copy in wq_push + wo_push:
        copy.wait_send()
    for t in range(3):
        for copy in to_near(t) + to_far(t):
            copy.wait_send()
        wait_all(to_other_core(t))
    wait_all(kept + cot_kept + stored + stored_late)


def first_step(cols, ranks, x, cot, router, const, vector, again, fgain, carry, wq, wo, prev, routes, lengths, gate, up, down):
    local = x.shape[0]
    rows = local * cols
    heads, width = 3, 3 * HEAD_DIM
    experts, depth, ff = gate.shape
    spots = np.arange(rows, dtype=np.float64)[:, None]
    pair = np.arange(LANES) % HEAD_DIM // 2
    freq = np.exp(-(2.0 * pair / HEAD_DIM) * math.log(BASE))[None, :]
    tables = [np.cos(spots * freq), np.sin(spots * freq), freq]
    tables = [jnp.asarray(value.astype(np.float32)) for value in tables]
    vm = pl.BlockSpec(memory_space=pltpu.VMEM)
    dma = pltpu.SemaphoreType.DMA
    return pl.pallas_call(
        functools.partial(first_kernel, cols, ranks),
        out_shape=(
            jax.ShapeDtypeStruct((3, experts, D, ff), BF),
            jax.ShapeDtypeStruct((3 * heads, rows, HEAD_DIM), BF),
            jax.ShapeDtypeStruct((heads, rows, HEAD_DIM), BF),
            jax.ShapeDtypeStruct((rows, LANES), F32),
            jax.ShapeDtypeStruct((cols, local, D), BF),
            jax.ShapeDtypeStruct((D, 3 * width), BF),
            jax.ShapeDtypeStruct((D, D), BF),
            jax.ShapeDtypeStruct((rows, LANES), F32),
            jax.ShapeDtypeStruct((rows, LANES), F32),
            jax.ShapeDtypeStruct((rows, LANES), F32),
            jax.ShapeDtypeStruct((experts, rows), jnp.int32),
            jax.ShapeDtypeStruct((local, D), BF),
            jax.ShapeDtypeStruct((local, D), F32),
            jax.ShapeDtypeStruct((cols, local, D), BF),
            jax.ShapeDtypeStruct((cols, 16, local), BF),
            jax.ShapeDtypeStruct((cols, local // EARLY, D), BF),
            jax.ShapeDtypeStruct((LANES, D), BF),
            jax.ShapeDtypeStruct((16, LANES), BF),
        ),
        in_specs=[vm] * 12 + [pl.BlockSpec(memory_space=pltpu.SMEM)] + [vm] * 3 + [ANY] * 3,
        out_specs=(ANY,) * 10 + (vm,) + (ANY,) * 5 + (vm, vm),
        scratch_shapes=[
            pltpu.VMEM((cols, local, D), BF),
            pltpu.VMEM((3, depth, width), BF),
            pltpu.VMEM((3, depth, width), BF),
            pltpu.VMEM((depth, width), BF),
            pltpu.VMEM((cols, depth, width), BF),
            pltpu.VMEM((D, 3 * width), BF),
            pltpu.VMEM((D, D), BF),
            pltpu.VMEM((cols, heads, local // 2, LANES), BF),
            pltpu.VMEM((cols, heads, local // 2, LANES), BF),
            pltpu.VMEM((16, local), BF),
            pltpu.VMEM((cols, 16, local), BF),
            pltpu.VMEM((3 * heads, rows, HEAD_DIM), BF),
            pltpu.VMEM((heads, rows, HEAD_DIM), BF),
            pltpu.VMEM((rows, LANES), F32),
            pltpu.VMEM((rows, LANES), F32),
            pltpu.VMEM((rows, LANES), F32),
            pltpu.VMEM((rows, LANES), F32),
            pltpu.VMEM((local, D), BF),
            pltpu.VMEM((local, D), F32),
            pltpu.VMEM((local, D), BF),
            pltpu.VMEM((3, experts, depth, ff), BF),
            dma((17,)),
            dma((2, cols - 1)),
            dma((2, cols - 1)),
            dma((2, cols - 1)),
            dma((2, cols - 1)),
            dma((2, cols - 1)),
            dma((2, cols - 1)),
            dma((2,)),
            dma((2,)),
            dma((2, cols - 1)),
            dma((2, cols - 1)),
            dma((2, 7)),
            dma((2, 7)),
            dma((3, 2)),
            dma((3, 2)),
            dma((3, 2)),
            dma((3, 2)),
            dma((3, 4)),
            dma((3, 4)),
            dma((heads, cols - 1)),
            dma((heads, cols - 1)),
        ],
        compiler_params=pltpu.CompilerParams(
            vmem_limit_bytes=60 * MIB, collective_id=5, has_side_effects=True
        ),
        cost_estimate=pl.CostEstimate(
            flops=8 * heads * rows * rows * HEAD_DIM, bytes_accessed=40 * MIB, transcendentals=heads * rows * rows
        ),
        name="first_step",
    )(x, cot, router, const, vector, again, fgain, carry, wq, wo, prev, routes, lengths, *tables, gate, up, down)


def experts_forward_kernel(
    cols,
    capacity,
    n2_ref,
    prev_ref,
    cot_ref,
    rw_ref,
    carry_ref,
    slots_ref,
    meta_ref,
    w_ref,
    x_ref,
    gu_ref,
    y_ref,
    gates_ref,
    cotb_ref,
    send,
    recv,
    local_sem,
):
    e = pl.program_id(0)
    experts = pl.num_programs(0)
    r, c = place()
    early = cot_ref.shape[0] // EARLY
    late = cot_ref.at[pl.ds(early, cot_ref.shape[0] - early)]
    step, drain = gather_chain(late, cotb_ref, send, recv, cols)
    own_copy = pltpu.make_async_copy(late, cotb_ref.at[c], local_sem.at[0])

    @pl.when(e == 0)
    def _():
        greet(col_peers(cols))
        own_copy.start()
        step(0)
        prev = jnp.concatenate([mm(prev_ref[i], carry_ref[...], TN) for i in range(cols)], axis=0)
        g = gate_lanes(mm(n2_ref[...], rw_ref[...], NT) + prev, meta_ref[...])
        high = g.astype(BF)
        gates_ref[:, :LANES] = high
        gates_ref[:, LANES:] = (g - high.astype(F32)).astype(BF)

    @pl.when(e == 3)
    def _():
        step(1)

    @pl.when(e == 6)
    def _():
        step(2)

    one = slot_rows(slots_ref, e, capacity)
    x = mm(one, n2_ref[...]).astype(BF)
    x_ref[0] = x
    sg = slot_gates(one, gates_ref, e)
    g = mm(x, w_ref[0, 0])
    u = mm(x, w_ref[1, 0])
    gu_ref[0, 0] = g.astype(BF)
    gu_ref[0, 1] = u.astype(BF)
    gh = (g * jax.nn.sigmoid(g) * u * sg).astype(BF)
    y_ref[0] = mm(gh, w_ref[2, 0], NT).astype(BF)

    @pl.when(e == experts - 1)
    def _():
        for k in range(3, cols):
            step(k)
        drain()
        own_copy.wait()


def experts_forward(cols, n2, prev, cot, rw, carry, meta, slots, w_all):
    rows = n2.shape[0]
    capacity = rows // 4
    three, experts, deep, ff = w_all.shape
    local = rows // cols
    rest = local - local // EARLY
    return pl.pallas_call(
        functools.partial(experts_forward_kernel, cols, capacity),
        grid=(experts,),
        out_shape=(
            jax.ShapeDtypeStruct((experts, capacity, D), BF),
            jax.ShapeDtypeStruct((experts, 2, capacity, ff), BF),
            jax.ShapeDtypeStruct((experts, capacity, D), BF),
            jax.ShapeDtypeStruct((rows, 2 * LANES), BF),
            jax.ShapeDtypeStruct((cols, rest, D), BF),
        ),
        in_specs=[
            whole((rows, D)),
            whole((cols, 16, local)),
            whole((local, D)),
            whole((LANES, D)),
            whole((16, LANES)),
            whole((experts, rows)),
            whole((rows, LANES)),
            pl.BlockSpec((three, 1, deep, ff), lambda e: (0, e, 0, 0)),
        ],
        out_specs=(
            pl.BlockSpec((1, capacity, D), lambda e: (e, 0, 0)),
            pl.BlockSpec((1, 2, capacity, ff), lambda e: (e, 0, 0, 0)),
            pl.BlockSpec((1, capacity, D), lambda e: (e, 0, 0)),
            whole((rows, 2 * LANES)),
            ANY,
        ),
        scratch_shapes=[
            pltpu.SemaphoreType.DMA((2, cols - 1)),
            pltpu.SemaphoreType.DMA((2, cols - 1)),
            pltpu.SemaphoreType.DMA((1,)),
        ],
        compiler_params=pltpu.CompilerParams(
            vmem_limit_bytes=60 * MIB, collective_id=1, has_side_effects=True
        ),
        cost_estimate=pl.CostEstimate(
            flops=experts * capacity * 2 * D * (3 * ff + rows),
            bytes_accessed=40 * MIB,
            transcendentals=experts * capacity * ff,
        ),
        name="experts_forward",
    )(n2, prev, cot, rw, carry, slots, meta, w_all)


def experts_backward_kernel(
    cols,
    capacity,
    cota_ref,
    cotb_ref,
    y_ref,
    gates_ref,
    slots_ref,
    meta_ref,
    w_ref,
    x_ref,
    gu_ref,
    dx_ref,
    dots_ref,
    mixsum_ref,
    gown_ref,
    sib_ref,
    hin_ref,
    glast_ref,
    cot_s,
    mix_s,
    gbuf,
    out,
    arrived,
    send,
    recv,
    own_sem,
    sib_send,
    sib_recv,
    cot_sem,
    lbuf,
    hbuf,
    l_sem,
    hsend,
    hrecv,
):
    e = pl.program_id(0)
    experts = pl.num_programs(0)
    r, c = place()
    core = r % 2
    local = mix_s.shape[1]
    early = cota_ref.shape[1]
    place_now = lax.rem(e, 2)
    slot, total, drain = reduce_chain(lambda d: mix_s[d], out, arrived, send, recv, cols)

    def own_copy(expert, at):
        return pltpu.make_async_copy(gbuf.at[at, :, :, core], gown_ref.at[expert], own_sem.at[at])

    def last_copy(at):
        return pltpu.make_async_copy(gbuf.at[at, :, :, 1 - core], glast_ref, sib_send.at[at])

    def sib_copy(expert, at):
        return send_to(
            gbuf.at[at, :, :, 1 - core],
            sib_ref.at[expert],
            sib_send.at[at],
            sib_recv.at[expert],
            (flip(r, 1), c),
        )

    cot_loads = moves(
        [(cota_ref.at[d], cot_s.at[pl.ds(d * local, early)]) for d in range(cols)]
        + [(cotb_ref.at[d], cot_s.at[pl.ds(d * local + early, local - early)]) for d in range(cols)],
        cot_sem,
    )
    before = jnp.maximum(e - 1, 0)
    sib_load = pltpu.make_async_copy(sib_ref.at[before], lbuf, l_sem.at[0])
    sends_now = (e >= 1) & (e <= SENT_SOON)

    def h_sends(i):
        return to_chips(lambda there: hbuf.at[i, :, there], hin_ref.at[i], hsend.at[i], hrecv.at[i])

    @pl.when(e == 0)
    def _():
        start_all(cot_loads)
        greet(col_peers(cols) + [(flip(r, m), c) for m in (1, 2, 4, 6)])
        for n, d in enumerate(chain_order(c)):
            mix_s[d] = combine(meta_ref, y_ref, d, local)
            if n == 0:
                slot(0)
        wait_all(cot_loads)

    @pl.when(e == 2)
    def _():
        slot(1)

    @pl.when(e == 5)
    def _():
        slot(2)

    one = slot_rows(slots_ref, e, capacity)
    ct = mm(one, cot_s[...]).astype(BF)
    sg = slot_gates(one, gates_ref, e)
    x = x_ref[0]

    @pl.when(sends_now)
    def _():
        sib_copy(before, 1 - place_now).wait_recv()
        sib_load.start()

    g, u = gu_ref[0, 0].astype(F32), gu_ref[0, 1].astype(F32)
    v = mm(ct, w_ref[2, 0])
    sig = jax.nn.sigmoid(g)
    act = g * sig
    h = act * u
    dot = jnp.sum(h * v, axis=1, keepdims=True)
    dots_ref[pl.ds(e, 1)] = jnp.sum(one.astype(F32) * dot, axis=0, keepdims=True)
    gh = (h * sg).astype(BF)
    gv = v * sg
    dg = (gv * u * (sig * (1.0 + g * (1.0 - sig)))).astype(BF)
    du = (gv * act).astype(BF)
    dx_ref[0] = (mm(dg, w_ref[0, 0], NT) + mm(du, w_ref[1, 0], NT)).astype(BF)

    @pl.when(e >= 2)
    def _():
        own_copy(e - 2, place_now).wait()
        sib_copy(e - 2, place_now).wait_send()

    shape = gbuf.shape[2:]
    gbuf[place_now, 0] = mm(x, dg, TN).astype(BF).reshape(shape)
    gbuf[place_now, 1] = mm(x, du, TN).astype(BF).reshape(shape)
    gbuf[place_now, 2] = mm(ct, gh, TN).astype(BF).reshape(shape)
    own_copy(e, place_now).start()

    @pl.when(e < experts - 1)
    def _():
        sib_copy(e, place_now).start()

    @pl.when(e == experts - 1)
    def _():
        last_copy(place_now).start()

    @pl.when(sends_now)
    def _():
        sib_load.wait()
        hbuf[before] = (gbuf[1 - place_now, :, :, core].astype(F32) + lbuf[...].astype(F32)).astype(BF)
        start_all(h_sends(before))

    @pl.when(e == experts - 1)
    def _():
        for s in range(3, cols):
            slot(s)
        total(mixsum_ref)
        drain()
        for back in (1, 0):
            own_copy(e - back, lax.rem(e - back, 2)).wait()
        sib_copy(e - 1, 1 - place_now).wait_send()
        last_copy(place_now).wait()
        for i in range(SENT_SOON, EXPERTS - 1):
            sib_copy(i, i % 2).wait_recv()
        for i in range(SENT_SOON):
            wait_all(h_sends(i))


def experts_backward(cols, ranks, cota, cotb, y, gates, meta, slots, w_all, x, gu):
    experts, capacity, _ = y.shape
    rows = slots.shape[1]
    three, _, deep, ff = w_all.shape
    local = rows // cols
    chips = ranks // 2
    depth = deep // ranks
    half = jax.ShapeDtypeStruct((experts, three, chips, depth, ff), BF)
    return pl.pallas_call(
        functools.partial(experts_backward_kernel, cols, capacity),
        grid=(experts,),
        out_shape=(
            jax.ShapeDtypeStruct((experts, capacity, D), BF),
            jax.ShapeDtypeStruct((experts, rows), F32),
            jax.ShapeDtypeStruct((local, D), F32),
            half,
            half,
            jax.ShapeDtypeStruct((SENT_SOON, 3, three, depth, ff), BF),
            jax.ShapeDtypeStruct((three, chips, depth, ff), BF),
        ),
        in_specs=[
            ANY,
            ANY,
            whole((experts, capacity, D)),
            whole((rows, 2 * LANES)),
            whole((experts, rows)),
            whole((rows, LANES)),
            pl.BlockSpec((three, 1, deep, ff), lambda e: (0, e, 0, 0)),
            pl.BlockSpec((1, capacity, D), lambda e: (e, 0, 0)),
            pl.BlockSpec((1, 2, capacity, ff), lambda e: (e, 0, 0, 0)),
        ],
        out_specs=(
            pl.BlockSpec((1, capacity, D), lambda e: (e, 0, 0)),
            whole((experts, rows)),
            whole((local, D)),
            ANY,
            ANY,
            ANY,
            ANY,
        ),
        scratch_shapes=[
            pltpu.VMEM((rows, D), BF),
            pltpu.VMEM((cols, local, D), BF),
            pltpu.VMEM((2, three, chips, 2, depth, ff), BF),
            *chain_scratch(cols, local),
            pltpu.SemaphoreType.DMA((2,)),
            pltpu.SemaphoreType.DMA((2,)),
            pltpu.SemaphoreType.DMA((experts,)),
            pltpu.SemaphoreType.DMA((2 * cols,)),
            pltpu.VMEM((three, chips, depth, ff), BF),
            pltpu.VMEM((SENT_SOON, three, chips, depth, ff), BF),
            pltpu.SemaphoreType.DMA((1,)),
            pltpu.SemaphoreType.DMA((SENT_SOON, 3)),
            pltpu.SemaphoreType.DMA((SENT_SOON, 3)),
        ],
        compiler_params=pltpu.CompilerParams(
            vmem_limit_bytes=60 * MIB, collective_id=2, has_side_effects=True
        ),
        cost_estimate=pl.CostEstimate(
            flops=experts * capacity * 4 * D * (3 * ff + rows),
            bytes_accessed=60 * MIB,
            transcendentals=experts * capacity * ff,
        ),
        name="experts_backward",
    )(cota, cotb, y, gates, slots, meta, w_all, x, gu)


def resid_kernel(
    cols,
    count,
    dx_ref,
    meta_ref,
    dots_ref,
    rw_ref,
    prev_ref,
    carry_ref,
    cot_ref,
    mixsum_in,
    n2w_in,
    middle_in,
    out_t_in,
    mixed_in,
    gown_ref,
    glast_ref,
    sib_in,
    layer_ref,
    resid_ref,
    gm_ref,
    og_ref,
    small_ref,
    pg_ref,
    hin_ref,
    hrest_ref,
    sib_ref,
    mixsum,
    n2_s,
    middle_s,
    out_t,
    mixed_s,
    resid_s,
    load_sem,
    gt_s,
    out,
    arrived,
    send,
    recv,
    dots_in,
    dsend,
    drecv,
    grad,
    gm_out,
    gsend,
    grecv,
    gm_sem,
    lbuf,
    hbuf,
    hload,
    hsend,
    hrecv,
    hkeep,
    last_sem,
    og_s,
    og_sib,
):
    r, c = place()
    chip = r // 2
    local = cot_ref.shape[0]
    held = hbuf.shape[0]
    loads = moves(
        [
            (n2w_in.at[c], n2_s),
            (middle_in, middle_s),
            (mixsum_in, mixsum),
            (out_t_in, out_t),
            (mixed_in, mixed_s),
        ],
        load_sem,
    )
    greet(col_peers(cols) + [(flip(r, m), c) for m in (1, 2, 4, 6)])
    last = gown_ref.shape[0] - 1
    across = send_to(glast_ref, sib_ref.at[last], last_sem.at[0], last_sem.at[1], (flip(r, 1), c))
    across.start()
    slot, total, drain = reduce_chain(lambda d: gt_s[d], out, arrived, send, recv, cols)

    def dots_of(d):
        return dots_ref.at[:, pl.ds(pl.multiple_of(d * local, LANES), local)]

    dot_copies = to_cols(dots_of, dots_in, dsend, drecv, cols)
    start_all(dot_copies)
    dots_in[c] = dots_of(c)[...]
    for n, d in enumerate(chain_order(c)):
        gt_s[d] = combine(meta_ref, dx_ref, d, local)
        if n == 0:
            slot(0)

    def h_loads(i):
        at = lax.rem(i, 2)
        return [
            pltpu.make_async_copy(ref.at[SENT_SOON + i], lbuf.at[at, j], hload.at[at, j])
            for j, ref in enumerate((gown_ref, sib_ref))
        ]

    def h_sends(i):
        return to_chips(lambda there: hbuf.at[i, :, there], hin_ref.at[i], hsend.at[i], hrecv.at[i])

    def h_keeps(i):
        return moves(
            [(hbuf.at[i, :, flip(chip, k)], hrest_ref.at[i - count, k - 1]) for k in range(1, 4)],
            hkeep.at[i - count],
        )

    start_all(h_loads(0))

    def add_cores(i, carry):
        @pl.when(i + 2 == held)
        def _():
            across.wait()

        @pl.when(i + 1 < held)
        def _():
            start_all(h_loads(i + 1))

        wait_all(h_loads(i))
        at = lax.rem(i, 2)
        hbuf[i] = (lbuf[at, 0].astype(F32) + lbuf[at, 1].astype(F32)).astype(BF)

        @pl.when(i < count)
        def _():
            start_all(h_sends(i))

        @pl.when(i >= count)
        def _():
            start_all(h_keeps(jnp.maximum(i, count)))

        return carry

    lax.fori_loop(0, held, add_cores, 0)
    start_all(loads)
    slot(1)
    wait_all(loads)

    meta = meta_ref[pl.ds(pl.multiple_of(c * local, LANES), local)]
    n2, cot = n2_s[...], cot_ref[...]
    n2f, cotf = n2.astype(F32), cot.astype(F32)
    middle = middle_s[...]
    rw = rw_ref[...]
    lin = mm(n2, rw, NT)
    prev = prev_ref[c]
    gates = gate_lanes(lin + mm(prev, carry_ref[...], TN), meta)
    lane = lane_iota((local, LANES))
    cot_lin = mm(cot, rw, NT)
    dot_keep = jnp.sum(cotf * n2f, axis=1, keepdims=True)
    wait_all(dot_copies)
    d = jnp.concatenate([all_sum(dots_in, cols), jnp.zeros((LANES - EXPERTS, local), F32)], axis=0).T
    g_gates = jnp.where(lane == EXPERTS + 1, dot_keep, d)
    keep = gates[:, EXPERTS + 1 : EXPERTS + 2]
    mixes, packs = [], jnp.zeros((local, LANES), F32)
    for j in range(2):
        l0 = lin[:, ROW_CONST + 2 * j : ROW_CONST + 2 * j + 1]
        l1 = lin[:, ROW_CONST + 2 * j + 1 : ROW_CONST + 2 * j + 2]
        top = jnp.maximum(l0, l1)
        e0, e1 = jnp.exp(l0 - top), jnp.exp(l1 - top)
        a0, a1 = e0 / (e0 + e1), e1 / (e0 + e1)
        share = gates[:, EXPERTS + 2 + j : EXPERTS + 3 + j]
        dot_vec = cot_lin[:, ROW_VEC + j : ROW_VEC + j + 1]
        keep = keep + share * a0
        mixes.append(share * a1)
        g_gates = jnp.where(lane == EXPERTS + 2 + j, a0 * dot_keep + a1 * dot_vec, g_gates)
        gk, gv = share * dot_keep, share * dot_vec
        mean = a0 * gk + a1 * gv
        packs = packs + jnp.where(lane == ROW_CONST + 2 * j, a0 * (gk - mean), 0.0)
        packs = packs + jnp.where(lane == ROW_CONST + 2 * j + 1, a1 * (gv - mean), 0.0)
        packs = packs + jnp.where(lane == ROW_VEC + j, share * a1, 0.0)
    packs = packs + gates * (g_gates - jnp.sum(gates * g_gates, axis=1, keepdims=True))
    vec = rw[ROW_VEC : ROW_VEC + 2].astype(F32)
    layer = middle + mixsum[...] + keep * n2f + mixes[0] * vec[0:1] + mixes[1] * vec[1:2]
    layer_ref[...] = layer.astype(BF)

    high = packs.astype(BF)
    low = (packs - high.astype(F32)).astype(BF)
    back = lane < ROW_VEC
    high_b = jnp.where(back, packs, 0.0).astype(BF)
    low_b = jnp.where(back, packs - high.astype(F32), 0.0).astype(BF)
    grad_local = keep * cotf + mm(high_b, rw) + mm(low_b, rw)
    by_n2 = mm(high, n2, TN) + mm(low, n2, TN)
    by_cot = mm(high, cot, TN) + mm(low, cot, TN)
    by_prev = mm(prev, high) + mm(prev, low)
    pg = mm(carry_ref[...], high_b, NT) + mm(carry_ref[...], low_b, NT)
    pg_ref[...] = pg[:ROUTES]
    sub = lax.broadcasted_iota(jnp.int32, (SMALL_ROWS, D), 0)
    small_ref[:, :D] = jnp.where(sub < ROW_VEC, by_n2[:SMALL_ROWS], by_cot[:SMALL_ROWS])
    small_ref[:16, D : D + LANES] = by_prev
    small_ref[16:, D : D + LANES] = jnp.zeros((SMALL_ROWS - 16, LANES), F32)
    small_ref[:, D + LANES :] = jnp.zeros((SMALL_ROWS, LANES), F32)
    fgain = rw[ROW_GAIN + 1 : ROW_GAIN + 2].astype(F32)
    scale = norm_rows(middle)

    for s in range(2, cols):
        slot(s)
    total(grad)
    grad_normed = grad[...] + grad_local
    gained = grad_normed * fgain
    mid_dot = jnp.sum(gained * middle, axis=1, keepdims=True)
    resid = cotf + scale * gained - middle * (scale * scale * scale * (mid_dot * (1.0 / D)))
    cut = resid.astype(BF)
    gm = (mm(cut, out_t[...]) * meta[:, META_VALID : META_VALID + 1]).astype(BF)
    width = D // cols
    for i in range(cols):
        for h in range(width // HEAD_DIM):
            at = i * width + h * HEAD_DIM
            gm_out[i, h] = pack_head(gm[:, at : at + HEAD_DIM])
    gm_copies = to_cols(lambda i: gm_out.at[i], gm_ref, gsend, grecv, cols)
    start_all(gm_copies)
    resid_s[...] = resid
    stored = moves([(gm_out.at[c], gm_ref.at[c]), (resid_s, resid_ref)], gm_sem)
    start_all(stored)
    small_ref[ROW_GAIN : ROW_GAIN + 1, :D] = jnp.sum(grad_normed * middle * scale, axis=0, keepdims=True)
    core = r % 2
    og_s[...] = mm(cut, mixed_s[...], TN).astype(BF).reshape(og_s.shape)
    og_across = send_to(og_s.at[:, 1 - core], og_sib, last_sem.at[2], last_sem.at[3], (flip(r, 1), c))
    og_across.start()
    og_across.wait()
    for k in range(og_s.shape[0]):
        og_ref[k] = (og_s[k, core].astype(F32) + og_sib[k].astype(F32)).astype(BF)
    wait_all(stored + gm_copies)
    drain()

    def end(i, carry):
        @pl.when(i < count)
        def _():
            wait_all(h_sends(i))

        @pl.when(i >= count)
        def _():
            wait_all(h_keeps(jnp.maximum(i, count)))

        return carry

    lax.fori_loop(0, held, end, 0)


def resid_step(cols, dx, meta, dots, rw, prev, carry, cot, mixsum, n2w, middle, out_t, mixed, gown, glast, sib):
    local = cot.shape[0]
    experts, three, chips, depth, ff = gown.shape
    count, held = SENT_NEXT, experts - SENT_SOON
    vm = pl.BlockSpec(memory_space=pltpu.VMEM)
    dma = pltpu.SemaphoreType.DMA
    return pl.pallas_call(
        functools.partial(resid_kernel, cols, count),
        out_shape=(
            jax.ShapeDtypeStruct((local, D), BF),
            jax.ShapeDtypeStruct((local, D), F32),
            jax.ShapeDtypeStruct((cols, 3, local // 2, LANES), BF),
            jax.ShapeDtypeStruct((chips, depth, D), BF),
            jax.ShapeDtypeStruct((SMALL_ROWS, D + 2 * LANES), F32),
            jax.ShapeDtypeStruct((ROUTES, local), F32),
            jax.ShapeDtypeStruct((count, 3, three, depth, ff), BF),
            jax.ShapeDtypeStruct((held - count, 3, three, depth, ff), BF),
            jax.ShapeDtypeStruct(sib.shape, BF),
        ),
        in_specs=[vm] * 7 + [ANY] * 8,
        out_specs=(vm, ANY, ANY, vm, vm, vm, ANY, ANY, ANY),
        input_output_aliases={14: 8},
        scratch_shapes=[
            pltpu.VMEM((local, D), F32),
            pltpu.VMEM((local, D), BF),
            pltpu.VMEM((local, D), F32),
            pltpu.VMEM((D, D), BF),
            pltpu.VMEM((local, D), BF),
            pltpu.VMEM((local, D), F32),
            dma((5,)),
            pltpu.VMEM((cols, local, D), BF),
            *chain_scratch(cols, local),
            pltpu.VMEM((cols, EXPERTS, local), F32),
            dma((cols - 1,)),
            dma((cols - 1,)),
            pltpu.VMEM((local, D), F32),
            pltpu.VMEM((cols, 3, local // 2, LANES), BF),
            dma((cols - 1,)),
            dma((cols - 1,)),
            dma((2,)),
            pltpu.VMEM((2, 2, three, chips, depth, ff), BF),
            pltpu.VMEM((held, three, chips, depth, ff), BF),
            dma((2, 2)),
            dma((count, 3)),
            dma((count, 3)),
            dma((held - count, 3)),
            dma((4,)),
            pltpu.VMEM((chips, 2, depth, D), BF),
            pltpu.VMEM((chips, depth, D), BF),
        ],
        compiler_params=pltpu.CompilerParams(
            vmem_limit_bytes=60 * MIB, collective_id=3, has_side_effects=True
        ),
        cost_estimate=pl.CostEstimate(flops=6 * local * D * D, bytes_accessed=40 * MIB, transcendentals=0),
        name="resid_step",
    )(dx, meta, dots, rw, prev, carry, cot, mixsum, n2w, middle, out_t, mixed, gown, glast, sib)


def finish_kernel(
    cols,
    ranks,
    gm_ref,
    meta_ref,
    lse_ref,
    small_ref,
    og_ref,
    xown_ref,
    rw_ref,
    qkv_in,
    o_in,
    x_in,
    w_in,
    cos_in,
    sin_in,
    resid_in,
    gown_ref,
    sib_ref,
    hsoon_ref,
    hin0_ref,
    hrest_ref,
    ig_ref,
    small_out,
    qg_out,
    og_out,
    gg_ref,
    ug_ref,
    dg_ref,
    hin_ref,
    qkv_s,
    o_s,
    x_s,
    w_s,
    cos_s,
    sin_s,
    resid_s,
    head_sem,
    load_sem,
    do_s,
    dq_s,
    dk_s,
    dv_s,
    gn_s,
    qg_acc,
    qg_cut,
    out,
    arrived,
    send,
    recv,
    small_s,
    small_rows,
    small_cols,
    small_all,
    og_chips,
    og_parts,
    og_cols,
    qg_sib,
    qg_half,
    qg_chips,
    q_parts,
    q_land,
    total_s,
    fbuf,
    fsem,
    row_send,
    row_recv,
    chip_send,
    chip_recv,
    sib_send,
    sib_recv,
    col_send,
    col_recv,
    hsend,
    hrecv,
):
    r, c = place()
    chip, core = r // 2, r % 2
    heads = 3
    rows = meta_ref.shape[0]
    local = rows // cols
    width = heads * HEAD_DIM
    rest = hrest_ref.shape[0]
    first = gown_ref.shape[0] - rest
    score_scale = 1.0 / math.sqrt(HEAD_DIM)

    def head_loads(h):
        pairs = [(qkv_in.at[i * heads + h], qkv_s.at[i * heads + h]) for i in range(3)]
        return moves(pairs + [(o_in.at[h], o_s.at[h])], head_sem.at[h])

    loads = moves(
        [(x_in, x_s), (w_in, w_s), (cos_in, cos_s), (sin_in, sin_s), (resid_in, resid_s)], load_sem
    )
    start_all(head_loads(0))
    greet(col_peers(cols) + [(flip(r, m), c) for m in range(1, ranks)])
    for h in range(1, heads):
        start_all(head_loads(h))
    start_all(loads)

    def to_sibling(src, dst, at):
        return send_to(src.at[:, 1 - core], dst, sib_send.at[at], sib_recv.at[at], (flip(r, 1), c))

    og_to_chips = to_chips(lambda there: og_ref.at[there], og_chips, chip_send.at[0], chip_recv.at[0])
    start_all(og_to_chips)

    for d in range(cols):
        at = slice(d * local, (d + 1) * local)
        for h in range(heads):
            do_s[h, at] = unpack_head(gm_ref[d, h])

    def halves(ref, sib, half):
        for k in range(ranks // 2):
            half[k] = (ref[k, core].astype(F32) + sib[k].astype(F32)).astype(BF)

    def h_sends(i):
        r_, c_ = place()
        return [
            send_to(
                hrest_ref.at[i, k - 1],
                hin_ref.at[i, k - 1],
                hsend.at[i, k - 1],
                hrecv.at[i, k - 1],
                (flip(r_, 2 * k), c_),
            )
            for k in range(1, 4)
        ]

    def start_sends(i, carry):
        start_all(h_sends(i))
        return carry

    lax.fori_loop(0, rest, start_sends, 0)

    blocks = rows // Q_ROWS

    def one_head(h, carry):
        wait_all(head_loads(h))
        for i in reversed(range(blocks)):
            at = slice(i * Q_ROWS, (i + 1) * Q_ROWS)
            length = (i + 1) * Q_ROWS
            q, do = qkv_s[h, at], do_s[h, at]
            k, v = qkv_s[heads + h, :length], qkv_s[2 * heads + h, :length]
            delta = jnp.sum(do.astype(F32) * o_s[h, at].astype(F32), axis=1, keepdims=True)
            lse = jnp.sum(jnp.where(lane_iota((Q_ROWS, LANES)) == h, lse_ref[at], 0.0), axis=1, keepdims=True)
            s = mm(q, k, NT)
            ok = seen(column(meta_ref, at, META_BEGIN).astype(jnp.int32), i * Q_ROWS, Q_ROWS, length)
            p = jnp.where(ok, jnp.exp(s - lse), 0.0)
            ds = (p * (mm(do, v, NT) - delta)).astype(BF)
            dq_s[h, at] = mm(ds, k) * score_scale
            dk, dv = mm(ds, q, TN), mm(p.astype(BF), do, TN)
            if i == blocks - 1:
                dk_s[h], dv_s[h] = dk, dv
            else:
                dk_s[h, :length] += dk
                dv_s[h, :length] += dv
        return carry

    lax.fori_loop(0, heads, one_head, 0)

    slot, total, drain = reduce_chain(lambda d: gn_s[d], out, arrived, send, recv, cols)
    wait_all(loads)
    gain_total = jnp.zeros((1, D), F32)
    weight = w_s[...]
    again = rw_ref[ROW_GAIN : ROW_GAIN + 1].astype(F32)
    for n, d in enumerate(chain_order(c)):
        at = pl.ds(pl.multiple_of(d * local, LANES), local)
        cosine, sines = cos_s[at], sin_s[at]
        turned = [dq_s[h, at] for h in range(heads)] + [dk_s[h, at] for h in range(heads)]
        parts = []
        for part in range(heads):
            v = jnp.concatenate(turned[2 * part : 2 * part + 2], axis=1)
            parts.append((v * cosine - swap_pairs(v) * sines).astype(BF))
        parts += [dv_s[h, at].astype(BF) for h in range(heads)]
        gp = jnp.concatenate(parts, axis=1)
        x = x_s[d].astype(F32)
        xs = x * norm_rows(x)
        gn = mm(gp, weight, NT)
        gn_s[d] = gn.astype(BF)
        if n == 0:
            slot(0)
        gain_total = gain_total + jnp.sum(gn * xs, axis=0, keepdims=True)
        grad = mm((xs * again).astype(BF), gp, TN)
        if n == 0:
            qg_acc[...] = grad
        else:
            qg_acc[...] += grad
    qg_cut[...] = qg_acc[...].astype(BF).reshape(qg_cut.shape)
    qg_across = to_sibling(qg_cut, qg_sib, 0)
    qg_across.start()

    sub = lax.broadcasted_iota(jnp.int32, (SMALL_ROWS, D), 0)
    for i in range(ranks):
        block = small_ref[:, i * LANES : (i + 1) * LANES]
        if i < D // LANES:
            own = sub[:, :LANES] == ROW_GAIN + 1
            block = jnp.where(own, gain_total[:, i * LANES : (i + 1) * LANES], block)
        small_s[i] = block
    small_to_rows = to_rows(lambda d: small_s.at[d], small_rows, row_send.at[0], row_recv.at[0], ranks)
    start_all(small_to_rows)
    small_rows[r] = small_s[r]

    def sum_grads(low, high, hin, base):
        def f_loads(i):
            at = lax.rem(i, 2)
            return moves(
                [
                    (gown_ref.at[i, :, chip], fbuf.at[at, 0]),
                    (sib_ref.at[i, :, chip], fbuf.at[at, 1]),
                    (hin.at[i - base], fbuf.at[at, pl.ds(2, 3)]),
                ],
                fsem.at[at],
            )

        start_all(f_loads(low))

        def body(i, carry):
            @pl.when(i + 1 < high)
            def _():
                start_all(f_loads(jnp.minimum(i + 1, high - 1)))

            wait_all(f_loads(i))
            at = lax.rem(i, 2)
            total_grad = fbuf[at, 0].astype(F32)
            for j in range(1, 5):
                total_grad = total_grad + fbuf[at, j].astype(F32)
            gg_ref[i] = total_grad[0].astype(BF)
            ug_ref[i] = total_grad[1].astype(BF)
            dg_ref[i] = total_grad[2].astype(BF)
            return carry

        lax.fori_loop(low, high, body, 0)

    sum_grads(0, SENT_SOON, hsoon_ref, 0)
    slot(1)
    qg_across.wait()
    halves(qg_cut, qg_sib, qg_half)
    qg_to_chips = to_chips(lambda there: qg_half.at[there], qg_chips, chip_send.at[1], chip_recv.at[1])
    start_all(qg_to_chips)
    wait_all(small_to_rows)
    small_cols[c] = all_sum(small_rows, ranks)
    small_to_cols = to_cols(lambda d: small_cols.at[c], small_cols, col_send.at[0], col_recv.at[0], cols)
    start_all(small_to_cols)
    slot(2)
    wait_all(og_to_chips)
    og_sum = og_ref[chip].astype(F32) + all_sum(og_chips, 3)
    for i in range(cols):
        og_parts[i] = og_sum[:, i * width : (i + 1) * width]
    og_to_cols = to_cols(lambda d: og_parts.at[d], og_cols, col_send.at[1], col_recv.at[1], cols)
    start_all(og_to_cols)
    og_cols[c] = og_parts[c]
    wait_all(qg_to_chips)
    q_sum = qg_cut[chip, core].astype(F32) + qg_sib[chip].astype(F32) + all_sum(qg_chips, 3)
    for i in range(3):
        q_parts[i] = q_sum[:, i * width : (i + 1) * width]
    odd, high = c % 2, c // 2
    q_copies = [
        send_to(
            q_parts.at[1 - odd + high],
            q_land.at[1],
            col_send.at[2, 0],
            col_recv.at[2, 0],
            (r, flip(c, 1)),
        ),
        send_to(
            q_parts.at[2 - 2 * high],
            q_land.at[2 - 2 * odd],
            col_send.at[2, 1],
            col_recv.at[2, 1],
            (r, flip(c, 2)),
        ),
    ]
    start_all(q_copies)
    q_land[2 * odd] = q_parts[(c + 1) // 2]
    wait_all(small_to_cols)
    small_all[r] = all_sum(small_cols, cols)
    small_back = to_rows(lambda d: small_all.at[r], small_all, row_send.at[1], row_recv.at[1], ranks)
    start_all(small_back)
    sum_grads(SENT_SOON, first, hin0_ref, SENT_SOON)

    def end_sends(i, carry):
        wait_all(h_sends(i))
        return carry

    lax.fori_loop(0, rest, end_sends, 0)
    sum_grads(first, first + rest, hin_ref, first)
    wait_all(og_to_cols + q_copies + small_back)
    og_out[...] = all_sum(og_cols, cols)
    for i in range(3):
        qg_out[:, i * width : (i + 1) * width] = q_land[i]
    for i in range(ranks):
        small_out[:, i * LANES : (i + 1) * LANES] = small_all[i]
    slot(3)
    total(total_s)
    gn = total_s[...]
    x = xown_ref[...].astype(F32)
    scale = norm_rows(x)
    gained = gn * again
    x_dot = jnp.sum(gained * x, axis=1, keepdims=True)
    ig_ref[...] = resid_s[...] + scale * gained - x * (scale * scale * scale * (x_dot * (1.0 / D)))
    drain()


def finish_step(cols, ranks, gm, meta, lse, small, og, xown, rw, qkv, o, x, w, cosine, sines, resid, gown, sib, hsoon, hin0, hrest):
    rows = meta.shape[0]
    local = rows // cols
    experts, three, chips, depth, ff = gown.shape
    rest = hrest.shape[0]
    heads, width = 3, 3 * HEAD_DIM
    vm = pl.BlockSpec(memory_space=pltpu.VMEM)
    dma = pltpu.SemaphoreType.DMA
    wide = D + 2 * LANES
    weight_grad = jax.ShapeDtypeStruct((experts, depth, ff), BF)
    return pl.pallas_call(
        functools.partial(finish_kernel, cols, ranks),
        out_shape=(
            jax.ShapeDtypeStruct((local, D), F32),
            jax.ShapeDtypeStruct((SMALL_ROWS, wide), F32),
            jax.ShapeDtypeStruct((depth, 3 * width), F32),
            jax.ShapeDtypeStruct((depth, width), F32),
            weight_grad,
            weight_grad,
            weight_grad,
            jax.ShapeDtypeStruct((rest, 3, three, depth, ff), BF),
        ),
        in_specs=[vm] * 7 + [ANY] * 12,
        out_specs=(vm,) * 7 + (ANY,),
        scratch_shapes=[
            pltpu.VMEM((3 * heads, rows, HEAD_DIM), BF),
            pltpu.VMEM((heads, rows, HEAD_DIM), BF),
            pltpu.VMEM((cols, local, D), BF),
            pltpu.VMEM((D, 3 * width), BF),
            pltpu.VMEM((rows, LANES), F32),
            pltpu.VMEM((rows, LANES), F32),
            pltpu.VMEM((local, D), F32),
            dma((heads, 4)),
            dma((5,)),
            pltpu.VMEM((heads, rows, HEAD_DIM), BF),
            pltpu.VMEM((heads, rows, HEAD_DIM), F32),
            pltpu.VMEM((heads, rows, HEAD_DIM), F32),
            pltpu.VMEM((heads, rows, HEAD_DIM), F32),
            pltpu.VMEM((cols, local, D), BF),
            pltpu.VMEM((D, 3 * width), F32),
            pltpu.VMEM((chips, 2, depth, 3 * width), BF),
            *chain_scratch(cols, local),
            pltpu.VMEM((ranks, SMALL_ROWS, LANES), F32),
            pltpu.VMEM((ranks, SMALL_ROWS, LANES), F32),
            pltpu.VMEM((cols, SMALL_ROWS, LANES), F32),
            pltpu.VMEM((ranks, SMALL_ROWS, LANES), F32),
            pltpu.VMEM((3, depth, D), BF),
            pltpu.VMEM((cols, depth, width), F32),
            pltpu.VMEM((cols, depth, width), F32),
            pltpu.VMEM((chips, depth, 3 * width), BF),
            pltpu.VMEM((chips, depth, 3 * width), BF),
            pltpu.VMEM((3, depth, 3 * width), BF),
            pltpu.VMEM((3, depth, width), F32),
            pltpu.VMEM((3, depth, width), F32),
            pltpu.VMEM((local, D), F32),
            pltpu.VMEM((2, 5, three, depth, ff), BF),
            dma((2, 3)),
            dma((2, ranks - 1)),
            dma((2, ranks - 1)),
            dma((2, 3)),
            dma((2, 3)),
            dma((1,)),
            dma((1,)),
            dma((3, cols - 1)),
            dma((3, cols - 1)),
            dma((rest, 3)),
            dma((rest, 3)),
        ],
        compiler_params=pltpu.CompilerParams(
            vmem_limit_bytes=62 * MIB, collective_id=4, has_side_effects=True
        ),
        cost_estimate=pl.CostEstimate(
            flops=20 * heads * rows * rows * HEAD_DIM, bytes_accessed=40 * MIB, transcendentals=heads * rows * rows
        ),
        name="finish_step",
    )(gm, meta, lse, small, og, xown, rw, qkv, o, x, w, cosine, sines, resid, gown, sib, hsoon, hin0, hrest)


def place_kernel(
    small_ref,
    qg_ref,
    og_ref,
    pg_ref,
    layer_in,
    ig_in,
    gg_in,
    ug_in,
    dg_in,
    layer_ref,
    ig_ref,
    gg_ref,
    ug_ref,
    dg_ref,
    again_ref,
    qkv_ref,
    out_ref,
    fgain_ref,
    router_ref,
    carry_ref,
    const_ref,
    vector_ref,
    prev_ref,
    g_low,
    g_full,
    ig_s,
    layer_s,
    load_sem,
    store_sem,
):
    loads = moves(
        [(gg_in, g_low.at[0]), (ug_in, g_low.at[1]), (dg_in, g_low.at[2]), (ig_in, ig_s), (layer_in, layer_s)], load_sem
    )
    stores = moves(
        [(g_full.at[0], gg_ref), (g_full.at[1], ug_ref), (g_full.at[2], dg_ref), (ig_s, ig_ref), (layer_s, layer_ref)],
        store_sem,
    )
    start_all(loads)
    for i in (3, 4):
        loads[i].wait()
        stores[i].start()
    for i in range(3):
        loads[i].wait()
        g_full[i] = g_low[i].astype(F32)
        stores[i].start()
    again_ref[...] = small_ref[ROW_GAIN + 1 : ROW_GAIN + 2, :D].reshape(D)
    fgain_ref[...] = small_ref[ROW_GAIN : ROW_GAIN + 1, :D].reshape(D)
    qkv_ref[...] = qg_ref[...]
    out_ref[...] = og_ref[...].T
    router_ref[...] = small_ref[:ROUTES, :D]
    carry_ref[...] = small_ref[:ROUTES, D : D + ROUTES]
    for j in range(2):
        const_ref[j] = small_ref[ROW_CONST + 2 * j : ROW_CONST + 2 * j + 2, :D]
    vector_ref[...] = small_ref[ROW_VEC : ROW_VEC + 2, :D]
    prev_ref[...] = pg_ref[...]
    wait_all(stores)


def place_outputs(small, qg, og, pg, layer, ig, gg, ug, dg):
    vm = pl.BlockSpec(memory_space=pltpu.VMEM)
    shapes = [layer.shape, ig.shape, gg.shape, ug.shape, dg.shape]
    shapes += [(D,), qg.shape, og.shape[::-1], (D,), (ROUTES, D), (ROUTES, ROUTES), (2, 2, D), (2, D), pg.shape]
    return pl.pallas_call(
        place_kernel,
        out_shape=[jax.ShapeDtypeStruct(shape, F32 if i else BF) for i, shape in enumerate(shapes)],
        in_specs=[vm] * 4 + [ANY] * 5,
        out_specs=[ANY] * 5 + [vm] * 9,
        scratch_shapes=[
            pltpu.VMEM((3, *gg.shape), BF),
            pltpu.VMEM((3, *gg.shape), F32),
            pltpu.VMEM(ig.shape, F32),
            pltpu.VMEM(layer.shape, BF),
            pltpu.SemaphoreType.DMA((5,)),
            pltpu.SemaphoreType.DMA((5,)),
        ],
        compiler_params=pltpu.CompilerParams(vmem_limit_bytes=60 * MIB),
        cost_estimate=pl.CostEstimate(flops=0, bytes_accessed=16 * MIB, transcendentals=0),
        name="place_outputs",
    )(small, qg, og, pg, layer, ig, gg, ug, dg)


def on_device_heads(
    sizes,
    inputs,
    attn_gain,
    qkv_weight,
    out_weight,
    ffn_gain,
    router_weight,
    carry_weight,
    const_weight,
    const_vector,
    gate_weight,
    up_weight,
    down_weight,
    prev_logits,
    seq_lengths,
    expert_routes,
    cotangent,
):
    ranks, cols = sizes
    row_total = expert_routes.shape[0]
    depth = qkv_weight.shape[0]

    (
        w_all,
        qkv,
        mixed_heads,
        lse,
        whole_in,
        qkv_own,
        out_t,
        cosine,
        sines,
        meta,
        slots,
        mixed,
        middle,
        n2_whole,
        prev_whole,
        cot_early,
        rw,
        carry,
    ) = first_step(
        cols,
        ranks,
        inputs,
        cotangent,
        router_weight.T,
        const_weight.transpose(0, 2, 1),
        const_vector,
        attn_gain,
        ffn_gain,
        carry_weight,
        qkv_weight,
        out_weight,
        prev_logits,
        expert_routes.T,
        seq_lengths,
        gate_weight,
        up_weight,
        down_weight.transpose(0, 2, 1),
    )
    x, gu, y, gates, cot_late = experts_forward(
        cols, n2_whole.reshape(row_total, D), prev_whole, cotangent, rw, carry, meta, slots, w_all
    )
    dx, dots, mixsum, gown, sib, hsoon, glast = experts_backward(
        cols, ranks, cot_early, cot_late, y, gates, meta, slots, w_all, x, gu
    )
    layer_out, resid, gm, og, small, prev_grad, hin0, hrest, sib = resid_step(
        cols, dx, meta, dots, rw, prev_whole, carry, cotangent, mixsum, n2_whole, middle, out_t, mixed, gown, glast, sib
    )
    input_grad, small_all, qkv_grad, og_own, gate_grad, up_grad, down_grad, _ = finish_step(
        cols,
        ranks,
        gm,
        meta,
        lse,
        small,
        og,
        inputs,
        rw,
        qkv,
        mixed_heads,
        whole_in,
        qkv_own,
        cosine,
        sines,
        resid,
        gown,
        sib,
        hsoon,
        hin0,
        hrest,
    )
    layer_out, input_grad, gate_grad, up_grad, down_grad, again, qkv_grad, out_grad, fgain, router, carry, const, vector, prev = (
        place_outputs(small_all, qkv_grad, og_own, prev_grad, layer_out, input_grad, gate_grad, up_grad, down_grad)
    )
    return (
        layer_out,
        input_grad,
        again,
        qkv_grad,
        out_grad,
        fgain,
        router.T,
        carry,
        const.transpose(0, 2, 1),
        vector,
        gate_grad,
        up_grad,
        down_grad.transpose(0, 2, 1),
        prev,
    )


def solution(mesh):
    sizes = (mesh.shape["row"], mesh.shape["col"])
    body = functools.partial(on_device_heads, sizes) if sizes == (8, 4) else on_device
    placed = (
        P(("row", "col"), None),
        P(),
        P("row", "col"),
        P("col", "row"),
        P(),
        P(),
        P(),
        P(),
        P(),
        P(None, "row", "col"),
        P(None, "row", "col"),
        P(None, "col", "row"),
        P(None, ("row", "col")),
        P("row", None),
        P("row", None),
        P(("row", "col"), None),
    )
    return jax.shard_map(
        body,
        mesh=mesh,
        in_specs=placed,
        out_specs=(
            P(("row", "col"), None),
            P(("row", "col"), None),
            P(),
            P("row", "col"),
            P("col", "row"),
            P(),
            P(),
            P(),
            P(),
            P(),
            P(None, "row", "col"),
            P(None, "row", "col"),
            P(None, "col", "row"),
            P(None, ("row", "col")),
        ),
        check_vma=False,
    )
```

```python
import functools
import math

import jax
import jax.numpy as jnp
import numpy as np
from jax import lax
from jax.experimental import pallas as pl
from jax.experimental.pallas import tpu as pltpu
from jax.sharding import PartitionSpec as P

D = 768
HEADS = 12
HEAD_DIM = 64
EXPERTS = 8
ROUTES = 12


EPS = 1e-06
BASE = 10000.0
NEG = -1e30
HIGH = lax.Precision.HIGHEST
CONTRACT_FIRST = (((0,), (0,)), ((), ()))
CONTRACT_LAST = (((1,), (1,)), ((), ()))


def rotate(block_value, positions, first_col, direction):
    row_count, col_count = block_value.shape
    column = first_col + jnp.arange(0, col_count, 2, dtype=jnp.int32)
    inner_col = column % D
    section = column // D
    head_pair = inner_col % HEAD_DIM // 2
    exponent = (2 * head_pair).astype(jnp.float32) / HEAD_DIM
    frequency = jnp.exp(-exponent * math.log(BASE))
    turned_on = (section < 2).astype(jnp.float32)
    angles = positions.astype(jnp.float32)[:, None] * (frequency * turned_on)[None, :]
    cosine = jnp.cos(angles)
    sines = direction * jnp.sin(angles)
    paired = block_value.reshape(row_count, col_count // 2, 2)
    first_part = paired[:, :, 0]
    second_part = paired[:, :, 1]
    rotated = jnp.stack(
        [first_part * cosine - second_part * sines, second_part * cosine + first_part * sines],
        axis=2,
    )
    return rotated.reshape(row_count, col_count)


def sequence_info(lengths_row, row_total):
    seq_count = lengths_row.shape[0]
    ends = jnp.cumsum(lengths_row)
    starts = ends - lengths_row
    token_place = jnp.arange(row_total, dtype=jnp.int32)
    seq_index = jnp.sum((token_place[:, None] >= ends[None, :]).astype(jnp.int32), axis=1)
    member = seq_index[:, None] == jnp.arange(seq_count, dtype=jnp.int32)[None, :]
    begin = jnp.sum(jnp.where(member, starts[None, :], 0), axis=1)
    return (seq_index, token_place - begin, seq_index < seq_count)


def partial_sums(term_value):
    return lax.psum_scatter(
        term_value.astype(jnp.bfloat16), "col", scatter_dimension=0, tiled=True
    ).astype(jnp.float32)


def whole_columns(part_value):
    return lax.all_gather(part_value, "col", axis=0, tiled=True)


def to_heads(block_value):
    return lax.all_to_all(block_value, "col", split_axis=0, concat_axis=1, tiled=True)


def to_features(block_value):
    return lax.all_to_all(block_value, "col", split_axis=1, concat_axis=0, tiled=True)


def key_scores(query_heads, key_block, query_seq, query_place, key_seq, key_place, score_scale):
    raw_scores = (
        jnp.einsum("qhd,khd->hqk", query_heads, key_block, preferred_element_type=jnp.float32)
        * score_scale
    )
    allowed = (query_seq[:, None] == key_seq[None, :]) & (
        key_place[None, :] <= query_place[:, None]
    )
    return (jnp.where(allowed[None], raw_scores, NEG), allowed)


def split_keys(key_values, seq_index, token_place, block_rows):
    count_blocks = key_values.shape[0] // block_rows
    blocks_kv = key_values.reshape(count_blocks, block_rows, 2, HEADS, HEAD_DIM)
    return (
        blocks_kv,
        seq_index.reshape(count_blocks, block_rows),
        token_place.reshape(count_blocks, block_rows),
    )


def attend_forward(
    queries, key_values, query_seq, query_place, seq_index, token_place, block_rows, score_scale
):
    local_rows = queries.shape[0]
    query_heads = queries.reshape(local_rows, HEADS, HEAD_DIM)
    key_items = split_keys(key_values, seq_index, token_place, block_rows)

    def max_step(running, block_items):
        running_max, running_sum = running
        kv_block, key_seq, key_place = block_items
        scores, allowed = key_scores(
            query_heads, kv_block[:, 0], query_seq, query_place, key_seq, key_place, score_scale
        )
        new_max = jnp.maximum(running_max, jnp.max(scores, axis=2))
        shifted = jnp.where(allowed[None], jnp.exp(scores - new_max[:, :, None]), 0.0)
        new_sum = running_sum * jnp.exp(running_max - new_max) + jnp.sum(shifted, axis=2)
        return ((new_max, new_sum), None)

    start_state = (
        jnp.full((HEADS, local_rows), NEG, jnp.float32),
        jnp.zeros((HEADS, local_rows), jnp.float32),
    )
    (final_max, final_sum), unused = lax.scan(max_step, start_state, key_items)
    log_total = final_max + jnp.log(final_sum)

    def out_step(running, block_items):
        kv_block, key_seq, key_place = block_items
        scores, allowed = key_scores(
            query_heads, kv_block[:, 0], query_seq, query_place, key_seq, key_place, score_scale
        )
        probs_low = jnp.exp(scores - log_total[:, :, None]).astype(jnp.bfloat16)
        return (
            running
            + jnp.einsum(
                "hqk,khd->qhd", probs_low, kv_block[:, 1], preferred_element_type=jnp.float32
            ),
            None,
        )

    attended, unused = lax.scan(
        out_step, jnp.zeros((local_rows, HEADS, HEAD_DIM), jnp.float32), key_items
    )
    return (attended.reshape(local_rows, D), log_total)


def attend_backward(
    queries,
    key_values,
    log_total,
    row_delta,
    grad_heads_in,
    query_seq,
    query_place,
    seq_index,
    token_place,
    block_rows,
    score_scale,
):
    local_rows = queries.shape[0]
    query_heads = queries.reshape(local_rows, HEADS, HEAD_DIM)
    grad_heads = grad_heads_in.reshape(local_rows, HEADS, HEAD_DIM)
    key_items = split_keys(key_values, seq_index, token_place, block_rows)

    def grad_step(running, block_items):
        kv_block, key_seq, key_place = block_items
        scores, allowed = key_scores(
            query_heads, kv_block[:, 0], query_seq, query_place, key_seq, key_place, score_scale
        )
        probs_full = jnp.exp(scores - log_total[:, :, None])
        probs_low = probs_full.astype(jnp.bfloat16)
        grad_probs = jnp.einsum(
            "qhd,khd->hqk", grad_heads, kv_block[:, 1], preferred_element_type=jnp.float32
        )
        grad_scores = (probs_full * (grad_probs - row_delta[:, :, None])).astype(jnp.bfloat16)
        new_running = (
            running
            + jnp.einsum(
                "hqk,khd->qhd", grad_scores, kv_block[:, 0], preferred_element_type=jnp.float32
            )
            * score_scale
        )
        grad_keys = (
            jnp.einsum("hqk,qhd->khd", grad_scores, query_heads, preferred_element_type=jnp.float32)
            * score_scale
        )
        grad_values = jnp.einsum(
            "hqk,qhd->khd", probs_low, grad_heads, preferred_element_type=jnp.float32
        )
        return (new_running, jnp.stack([grad_keys, grad_values], axis=1))

    grad_queries, grad_kv = lax.scan(
        grad_step, jnp.zeros((local_rows, HEADS, HEAD_DIM), jnp.float32), key_items
    )
    return (grad_queries.reshape(local_rows, D), grad_kv.reshape(key_values.shape[0], 2 * D))


def on_device(
    inputs,
    attn_gain,
    qkv_weight,
    out_weight,
    ffn_gain,
    router_weight,
    carry_weight,
    const_weight,
    const_vector,
    gate_weight,
    up_weight,
    down_weight,
    prev_logits,
    seq_lengths,
    expert_routes,
    cotangent,
):
    col_index = lax.axis_index("col")
    row_total = expert_routes.shape[0]
    local_rows = inputs.shape[0]
    capacity = row_total // 4
    block_rows = min(row_total, 512)
    score_scale = 1.0 / math.sqrt(HEAD_DIM)
    full_weights = (
        lax.all_gather(qkv_weight, "row", axis=0, tiled=True),
        lax.all_gather(out_weight, "row", axis=1, tiled=True),
        lax.all_gather(gate_weight, "row", axis=1, tiled=True),
        lax.all_gather(up_weight, "row", axis=1, tiled=True),
        lax.all_gather(down_weight, "row", axis=2, tiled=True),
    )
    qkv_full, out_full, gate_full, up_full, down_full = full_weights
    whole_in, whole_cot, whole_prev = (
        lax.all_gather(inputs, "col", axis=0, tiled=True),
        lax.all_gather(cotangent, "col", axis=0, tiled=True),
        lax.all_gather(prev_logits, "col", axis=1, tiled=True),
    )
    seq_index, positions, valid_all = sequence_info(seq_lengths[0], row_total)
    token_place = jnp.arange(row_total, dtype=jnp.int32)
    first_row = col_index * local_rows

    def own_rows(whole_value):
        return lax.dynamic_slice_in_dim(whole_value, first_row, local_rows, 0)

    query_seq = own_rows(seq_index)
    query_place = own_rows(token_place)
    query_pos = own_rows(positions)
    query_valid = own_rows(valid_all).astype(jnp.float32)[:, None]
    input_rows = whole_in.astype(jnp.float32)
    attn_gain_full = attn_gain.astype(jnp.float32)
    scale_attn = lax.rsqrt(jnp.mean(input_rows * input_rows, axis=1, keepdims=True) + EPS)
    normed1 = (input_rows * scale_attn * attn_gain_full).astype(jnp.bfloat16)
    projected = jnp.dot(normed1, qkv_full, preferred_element_type=jnp.float32)
    turned = rotate(projected, positions, col_index * projected.shape[1], 1.0).astype(jnp.bfloat16)
    token_qkv = to_heads(turned)
    queries = token_qkv[:, :D]
    key_values = lax.all_gather(token_qkv[:, D:], "col", axis=0, tiled=True)
    attended, log_total = attend_forward(
        queries, key_values, query_seq, query_place, seq_index, token_place, block_rows, score_scale
    )
    attn_tok = (attended * query_valid).astype(jnp.bfloat16)
    attn_feat = to_features(attn_tok)
    attn_out = partial_sums(jnp.dot(attn_feat, out_full, preferred_element_type=jnp.float32))
    input_local = inputs.astype(jnp.float32)
    middle = input_local + attn_out
    scale_ffn = lax.rsqrt(jnp.mean(middle * middle, axis=1, keepdims=True) + EPS)
    ffn_gain_full = ffn_gain.astype(jnp.float32)
    normed2_local = (middle * scale_ffn * ffn_gain_full).astype(jnp.bfloat16)
    normed2 = whole_columns(normed2_local)
    carry_full = carry_weight.astype(jnp.float32)
    prev_rows = whole_prev.astype(jnp.float32).T
    route_hot = (
        expert_routes[:, :, None] == jnp.arange(ROUTES, dtype=jnp.int32)[None, None, :]
    ).astype(jnp.float32)
    logits = jnp.dot(normed2, router_weight, preferred_element_type=jnp.float32) + jnp.dot(
        prev_rows, carry_full, precision=HIGH
    )
    picked = jnp.sum(route_hot * logits[:, None, :], axis=2)
    gate_values = jax.nn.softmax(picked, axis=1)
    flat_route = expert_routes.reshape(-1)
    route_hits = (flat_route[:, None] == jnp.arange(EXPERTS, dtype=jnp.int32)[None, :]).astype(
        jnp.int32
    )
    slot_index = jnp.sum((jnp.cumsum(route_hits, axis=0) - 1) * route_hits, axis=1)
    dump_slot = EXPERTS * capacity
    target = jnp.where(flat_route < EXPERTS, flat_route * capacity + slot_index, dump_slot)
    slot_owner = (
        jnp.full((dump_slot + 1,), row_total, jnp.int32)
        .at[target]
        .set(jnp.arange(2 * row_total, dtype=jnp.int32) // 2)[:dump_slot]
    )
    slot_gate = (
        jnp.zeros((dump_slot + 1,), jnp.float32)
        .at[target]
        .set(gate_values.reshape(-1))[:dump_slot]
        .reshape(EXPERTS, capacity, 1)
    )
    zero_row = jnp.zeros((1, D), jnp.bfloat16)
    expert_in = jnp.concatenate([normed2, zero_row], axis=0)[slot_owner].reshape(
        EXPERTS, capacity, D
    )
    gate_pre = jnp.einsum("ecd,edf->ecf", expert_in, gate_full, preferred_element_type=jnp.float32)
    up_pre = jnp.einsum("ecd,edf->ecf", expert_in, up_full, preferred_element_type=jnp.float32)
    sigmoid_gate = jax.nn.sigmoid(gate_pre)
    activated = gate_pre * sigmoid_gate
    hidden = (activated * up_pre).astype(jnp.bfloat16)
    expert_out = jnp.einsum("ecf,efd->ecd", hidden, down_full, preferred_element_type=jnp.float32)
    out_rows = jnp.concatenate(
        [expert_out.reshape(dump_slot, D), jnp.zeros((1, D), jnp.float32)], axis=0
    )
    chosen_out = out_rows[target].reshape(row_total, 2, D)
    cot_rows = whole_cot.astype(jnp.float32)
    ffn_mix = jnp.sum(gate_values[:, :, None] * chosen_out, axis=1)
    ffn_dots = jnp.sum(cot_rows[:, None, :] * chosen_out, axis=2)
    mix_local = partial_sums(ffn_mix)
    normed_local = normed2_local.astype(jnp.float32)
    vector_full = const_vector.astype(jnp.float32)
    routes_local = own_rows(expert_routes)
    gates_local = own_rows(gate_values)
    hot_local = own_rows(route_hot)
    copy_hit = (routes_local == EXPERTS + 1).astype(jnp.float32)
    const_hit = (
        routes_local[:, :, None] == (EXPERTS + 2 + jnp.arange(2, dtype=jnp.int32))[None, None, :]
    ).astype(jnp.float32)
    copy_share = jnp.sum(gates_local * copy_hit, axis=1)
    const_share = jnp.sum(gates_local[:, :, None] * const_hit, axis=1)
    const_alpha = jax.nn.softmax(
        jnp.einsum("td,jdk->tjk", normed2_local, const_weight, preferred_element_type=jnp.float32),
        axis=2,
    )
    keep_share = copy_share + jnp.sum(const_share * const_alpha[:, :, 0], axis=1)
    local_mix = keep_share[:, None] * normed_local + jnp.dot(
        const_share * const_alpha[:, :, 1], vector_full, precision=HIGH
    )
    layer_out = (middle + mix_local + local_mix).astype(jnp.bfloat16)
    qkv_full, out_full, gate_full, up_full, down_full = full_weights
    ffn_total = lax.psum(ffn_dots, "col")
    ffn_local = own_rows(ffn_total)
    cot_local = cotangent.astype(jnp.float32)
    dot_keep = jnp.sum(cot_local * normed_local, axis=1)
    dot_vector = jnp.dot(cot_local, vector_full.T, precision=HIGH)
    const_dots = const_alpha[:, :, 0] * dot_keep[:, None] + const_alpha[:, :, 1] * dot_vector
    grad_gates = (
        ffn_local
        + copy_hit * dot_keep[:, None]
        + jnp.sum(const_hit * const_dots[:, None, :], axis=2)
    )
    grad_picked = gates_local * (
        grad_gates - jnp.sum(gates_local * grad_gates, axis=1, keepdims=True)
    )
    grad_logits = jnp.sum(hot_local * grad_picked[:, :, None], axis=1)
    prev_local = prev_logits.astype(jnp.float32).T
    router_grad = lax.dot_general(normed_local, grad_logits, CONTRACT_FIRST, precision=HIGH)
    carry_grad = lax.dot_general(prev_local, grad_logits, CONTRACT_FIRST, precision=HIGH)
    prev_grad = lax.dot_general(carry_full, grad_logits, CONTRACT_LAST, precision=HIGH)
    grad_alpha_keep = const_share * dot_keep[:, None]
    grad_alpha_vector = const_share * dot_vector
    alpha_mean = const_alpha[:, :, 0] * grad_alpha_keep + const_alpha[:, :, 1] * grad_alpha_vector
    grad_alpha_logits = jnp.stack(
        [
            const_alpha[:, :, 0] * (grad_alpha_keep - alpha_mean),
            const_alpha[:, :, 1] * (grad_alpha_vector - alpha_mean),
        ],
        axis=2,
    )
    const_grad = jnp.einsum("td,tjk->jdk", normed_local, grad_alpha_logits, precision=HIGH)
    vector_grad = lax.dot_general(
        const_share * const_alpha[:, :, 1], cot_local, CONTRACT_FIRST, precision=HIGH
    )
    router_full = router_weight.astype(jnp.float32)
    const_full = const_weight.astype(jnp.float32)
    grad_normed_local = (
        keep_share[:, None] * cot_local
        + lax.dot_general(grad_logits, router_full, CONTRACT_LAST, precision=HIGH)
        + jnp.einsum("tjk,jdk->td", grad_alpha_logits, const_full, precision=HIGH)
    )
    cot_in = jnp.concatenate([whole_cot, zero_row], axis=0)[slot_owner].reshape(
        EXPERTS, capacity, D
    )
    grad_expert = (slot_gate * cot_in.astype(jnp.float32)).astype(jnp.bfloat16)
    down_grad = jnp.einsum("ecf,ecd->efd", hidden, grad_expert, preferred_element_type=jnp.float32)
    grad_hidden = jnp.einsum(
        "ecd,efd->ecf", grad_expert, down_full, preferred_element_type=jnp.float32
    )
    grad_gate_pre = (
        grad_hidden * up_pre * sigmoid_gate * (1.0 + gate_pre * (1.0 - sigmoid_gate))
    ).astype(jnp.bfloat16)
    grad_up_pre = (grad_hidden * activated).astype(jnp.bfloat16)
    gate_grad = jnp.einsum(
        "ecd,ecf->edf", expert_in, grad_gate_pre, preferred_element_type=jnp.float32
    )
    up_grad = jnp.einsum("ecd,ecf->edf", expert_in, grad_up_pre, preferred_element_type=jnp.float32)
    grad_expert_in = jnp.einsum(
        "ecf,edf->ecd", grad_gate_pre, gate_full, preferred_element_type=jnp.float32
    ) + jnp.einsum("ecf,edf->ecd", grad_up_pre, up_full, preferred_element_type=jnp.float32)
    grad_slots = jnp.concatenate(
        [grad_expert_in.reshape(dump_slot, D), jnp.zeros((1, D), jnp.float32)], axis=0
    )
    grad_tokens = jnp.sum(grad_slots[target].reshape(row_total, 2, D), axis=1)
    grad_normed = partial_sums(grad_tokens) + grad_normed_local
    gained_ffn = grad_normed * ffn_gain_full
    ffn_dots_rows = jnp.sum(gained_ffn * middle, axis=1, keepdims=True)
    grad_middle = scale_ffn * gained_ffn - middle * scale_ffn**3 * (ffn_dots_rows / D)
    ffn_gain_grad = jnp.sum(grad_normed * middle * scale_ffn, axis=0)
    grad_resid = cot_local + grad_middle
    branch_cot = whole_columns(grad_resid.astype(jnp.bfloat16))
    out_grad = lax.dot_general(
        attn_feat, branch_cot, CONTRACT_FIRST, preferred_element_type=jnp.float32
    )
    grad_mixed = lax.dot_general(
        branch_cot, out_full, CONTRACT_LAST, preferred_element_type=jnp.float32
    )
    grad_tok = to_heads(grad_mixed.astype(jnp.bfloat16))
    grad_heads_in = (grad_tok.astype(jnp.float32) * query_valid).astype(jnp.bfloat16)
    row_delta = jnp.sum(
        grad_heads_in.astype(jnp.float32).reshape(local_rows, HEADS, HEAD_DIM)
        * attended.reshape(local_rows, HEADS, HEAD_DIM),
        axis=2,
    ).T
    grad_queries, grad_kv = attend_backward(
        queries,
        key_values,
        log_total,
        row_delta,
        grad_heads_in,
        query_seq,
        query_place,
        seq_index,
        token_place,
        block_rows,
        score_scale,
    )
    grad_kv_local = lax.psum_scatter(
        grad_kv.astype(jnp.bfloat16), "col", scatter_dimension=0, tiled=True
    ).astype(jnp.float32)
    grad_turned = jnp.concatenate([grad_queries, grad_kv_local], axis=1)
    grad_proj_tok = rotate(grad_turned, query_pos, 0, -1.0).astype(jnp.bfloat16)
    grad_projected = to_features(grad_proj_tok)
    qkv_grad = lax.dot_general(
        normed1, grad_projected, CONTRACT_FIRST, preferred_element_type=jnp.float32
    )
    grad_normed1 = partial_sums(
        lax.dot_general(grad_projected, qkv_full, CONTRACT_LAST, preferred_element_type=jnp.float32)
    )
    scale_attn_local = own_rows(scale_attn)
    gained_attn = grad_normed1 * attn_gain_full
    attn_dots_rows = jnp.sum(gained_attn * input_local, axis=1, keepdims=True)
    input_grad = (
        grad_resid
        + scale_attn_local * gained_attn
        - input_local * scale_attn_local**3 * (attn_dots_rows / D)
    )
    attn_gain_grad = jnp.sum(grad_normed1 * input_local * scale_attn_local, axis=0)
    qkv_grad, out_grad, gate_grad, up_grad, down_grad = (
        lax.psum_scatter(
            qkv_grad.astype(jnp.bfloat16), "row", scatter_dimension=0, tiled=True
        ).astype(jnp.float32),
        lax.psum_scatter(
            out_grad.astype(jnp.bfloat16), "row", scatter_dimension=1, tiled=True
        ).astype(jnp.float32),
        lax.psum_scatter(
            gate_grad.astype(jnp.bfloat16), "row", scatter_dimension=1, tiled=True
        ).astype(jnp.float32),
        lax.psum_scatter(
            up_grad.astype(jnp.bfloat16), "row", scatter_dimension=1, tiled=True
        ).astype(jnp.float32),
        lax.psum_scatter(
            down_grad.astype(jnp.bfloat16), "row", scatter_dimension=2, tiled=True
        ).astype(jnp.float32),
    )
    attn_gain_grad, ffn_gain_grad, router_grad, carry_grad, const_grad, vector_grad = lax.psum(
        (attn_gain_grad, ffn_gain_grad, router_grad, carry_grad, const_grad, vector_grad),
        ("row", "col"),
    )
    return (
        layer_out,
        input_grad,
        attn_gain_grad,
        qkv_grad,
        out_grad,
        ffn_gain_grad,
        router_grad,
        carry_grad,
        const_grad,
        vector_grad,
        gate_grad,
        up_grad,
        down_grad,
        prev_grad,
    )


BF = jnp.bfloat16
F32 = jnp.float32
LANES = 128
NN = (((1,), (0,)), ((), ()))
NT = (((1,), (1,)), ((), ()))
TN = (((0,), (0,)), ((), ()))
ROW_CONST = 12
ROW_VEC = 16
ROW_GAIN = 18
SMALL_ROWS = 24
Q_ROWS = 256
MIB = 1 << 20


def mm(a, b, dims=NN):
    return lax.dot_general(a, b, dims, preferred_element_type=F32)


def lane_iota(shape):
    return lax.broadcasted_iota(jnp.int32, shape, len(shape) - 1)


def whole(shape):
    return pl.BlockSpec(tuple(shape), lambda *_: (0,) * len(shape), pipeline_mode=pl.Buffered(1))


def swap_pairs(v):
    even = lane_iota(v.shape) % 2 == 0
    return jnp.where(even, pltpu.roll(v, LANES - 1, 1), pltpu.roll(v, 1, 1))


def norm_rows(x):
    return lax.rsqrt(jnp.mean(x * x, axis=1, keepdims=True) + EPS)


def seen(begin, first, rows, length):
    u = lax.broadcasted_iota(jnp.int32, (rows, length), 1)
    t = lax.broadcasted_iota(jnp.int32, (rows, length), 0) + first
    return (u >= begin) & (u <= t)


def gate_lanes(logits, meta):
    lane = lane_iota(logits.shape)
    hit = (pltpu.roll(meta, LANES - META_HIT, 1) > 0.0) & (lane < ROUTES)
    held = jnp.where(hit, logits, NEG)
    e = jnp.where(hit, jnp.exp(held - jnp.max(held, axis=1, keepdims=True)), 0.0)
    return e / jnp.sum(e, axis=1, keepdims=True)


MESH = pl.DeviceIdType.MESH
ANY = pl.BlockSpec(memory_space=pl.ANY)


def place():
    return lax.axis_index("row"), lax.axis_index("col")


def flip(index, mask):
    for bit in (1, 2, 4):
        if mask & bit:
            index = index + bit - 2 * bit * (index // bit % 2)
    return index


def greet(devices):
    barrier = pltpu.get_barrier_semaphore()
    for device in devices:
        pl.semaphore_signal(barrier, inc=1, device_id=device, device_id_type=MESH)
    pl.semaphore_wait(barrier, len(devices))


def send_to(src, dst, send, recv, device):
    return pltpu.make_async_remote_copy(
        src_ref=src, dst_ref=dst, send_sem=send, recv_sem=recv, device_id=device, device_id_type=MESH
    )


def col_peers(n):
    r, c = place()
    return [(r, (c + k) % n) for k in range(1, n)]


def gather_chain(own, dst, send, recv, n):
    r, c = place()

    def right(k):
        i = jnp.maximum(c - k, 0)
        src = own if k == 0 else dst.at[i]
        return send_to(src, dst.at[i], send.at[0, k], recv.at[0, k], (r, jnp.minimum(c + 1, n - 1)))

    def left(k):
        i = jnp.minimum(c + k, n - 1)
        src = own if k == 0 else dst.at[i]
        return send_to(src, dst.at[i], send.at[1, k], recv.at[1, k], (r, jnp.maximum(c - 1, 0)))

    def step(k):
        if k > 0:

            @pl.when(c >= k)
            def _():
                right(k - 1).wait_recv()

            @pl.when(c + k < n)
            def _():
                left(k - 1).wait_recv()

        if k < n - 1:

            @pl.when((c >= k) & (c + 1 < n))
            def _():
                right(k).start()

            @pl.when((c + k < n) & (c >= 1))
            def _():
                left(k).start()

    def drain():
        for k in range(n - 1):

            @pl.when((c >= k) & (c + 1 < n))
            def _():
                right(k).wait_send()

            @pl.when((c + k < n) & (c >= 1))
            def _():
                left(k).wait_send()

    return step, drain


def reduce_chain(own, out, arrived, send, recv, n):
    r, c = place()

    def right(k):
        return send_to(out.at[0, k], arrived.at[0, k], send.at[0, k], recv.at[0, k], (r, jnp.minimum(c + 1, n - 1)))

    def left(k):
        return send_to(out.at[1, k], arrived.at[1, k], send.at[1, k], recv.at[1, k], (r, jnp.maximum(c - 1, 0)))

    def slot(s):
        if s == n - 1:

            @pl.when(c >= 1)
            def _():
                right(n - 1 - c).wait_recv()

            @pl.when(c <= n - 2)
            def _():
                left(c).wait_recv()

            return

        @pl.when(c <= s)
        def _():
            k = jnp.maximum(s - c, 0)

            @pl.when(c >= 1)
            def _():
                right(k).wait_recv()
                out[0, k] = (own(n - 1 - k).astype(F32) + arrived[0, k].astype(F32)).astype(BF)

            @pl.when(c == 0)
            def _():
                out[0, k] = own(n - 1 - k).astype(BF)

            right(k).start()

        @pl.when(n - 1 - c <= s)
        def _():
            k = jnp.maximum(s - (n - 1 - c), 0)

            @pl.when(c <= n - 2)
            def _():
                left(k).wait_recv()
                out[1, k] = (own(k).astype(F32) + arrived[1, k].astype(F32)).astype(BF)

            @pl.when(c == n - 1)
            def _():
                out[1, k] = own(k).astype(BF)

            left(k).start()

    def total(dst):
        dst[...] = own(c).astype(F32)

        @pl.when(c >= 1)
        def _():
            dst[...] += arrived[0, n - 1 - c].astype(F32)

        @pl.when(c <= n - 2)
        def _():
            dst[...] += arrived[1, c].astype(F32)

    def drain():
        for k in range(n - 1):

            @pl.when(c < n - 1 - k)
            def _():
                right(k).wait_send()

            @pl.when(c > k)
            def _():
                left(k).wait_send()

    return slot, total, drain


def chain_scratch(n, rows):
    return [
        pltpu.VMEM((2, n - 1, rows, D), BF),
        pltpu.VMEM((2, n - 1, rows, D), BF),
        pltpu.SemaphoreType.DMA((2, n - 1)),
        pltpu.SemaphoreType.DMA((2, n - 1)),
    ]


def slot_rows(slots_ref, e, capacity):
    rows = slots_ref.shape[1]
    spots = lax.broadcasted_iota(jnp.int32, (capacity, rows), 0)
    return jnp.where(spots == slots_ref[pl.ds(e, 1)], 1.0, 0.0).astype(BF)


def slot_gates(one, gates_ref, e):
    sg = mm(one, gates_ref[...])
    return jnp.sum(jnp.where(lane_iota(sg.shape) % LANES == e, sg, 0.0), axis=1, keepdims=True)


def chain_order(c):
    return [d + (3 - 2 * d) * (c // 2) for d in (3, 2, 0, 1)]


def combine(meta_ref, y_ref, d, local):
    experts, capacity, width = y_ref.shape
    at = pl.ds(pl.multiple_of(d * local, LANES), local)
    lane = lane_iota((local, capacity)).astype(F32)
    ones = [jnp.where(lane == column(meta_ref, at, e), 1.0, 0.0).astype(BF) for e in range(experts)]
    return mm(jnp.concatenate(ones, axis=1), y_ref[...].reshape(experts * capacity, width)).astype(BF)


META_HIT, META_BEGIN, META_VALID = 8, 20, 21
EARLY = 3
SENT_SOON, SENT_NEXT = 2, 3


def column(ref, at, lane):
    return ref[at, lane : lane + 1]


def start_all(copies):
    for copy in copies:
        copy.start()


def wait_all(copies):
    for copy in copies:
        copy.wait()


def moves(pairs, sem):
    return [pltpu.make_async_copy(src, dst, sem.at[i]) for i, (src, dst) in enumerate(pairs)]


def pack_head(value):
    half = value.shape[0] // 2
    return jnp.concatenate([value[:half], value[half:]], axis=1)


def unpack_head(packed):
    return jnp.concatenate([packed[:, :HEAD_DIM], packed[:, HEAD_DIM:]], axis=0)


def to_rows(src_of, dst, send, recv, ranks):
    r, c = place()
    copies = []
    for m in range(1, ranks):
        there = flip(r, m)
        copies.append(send_to(src_of(there), dst.at[r], send.at[m - 1], recv.at[m - 1], (there, c)))
    return copies


def to_cols(src_of, dst, send, recv, n):
    r, c = place()
    copies = []
    for k in range(1, n):
        there = (c + k) % n
        copies.append(send_to(src_of(there), dst.at[c], send.at[k - 1], recv.at[k - 1], (r, there)))
    return copies


def to_chips(src_of, dst, send, recv):
    r, c = place()
    return [
        send_to(src_of(flip(r // 2, k)), dst.at[k - 1], send.at[k - 1], recv.at[k - 1], (flip(r, 2 * k), c))
        for k in range(1, 4)
    ]


def all_sum(ref, count):
    total = ref[0].astype(F32)
    for i in range(1, count):
        total = total + ref[i].astype(F32)
    return total


def tokens_meta(routes_ref, lengths_ref, rows, experts):
    kinds = lax.broadcasted_iota(jnp.int32, (16, rows), 0)
    hits = jnp.where((kinds == routes_ref[0:1]) | (kinds == routes_ref[1:2]), 1.0, 0.0)
    step = 256
    earlier = lax.broadcasted_iota(jnp.int32, (step, step), 0) < lax.broadcasted_iota(
        jnp.int32, (step, step), 1
    )
    earlier = jnp.where(earlier, 1.0, 0.0).astype(BF)
    counts, running = [], jnp.zeros((16, 1), F32)
    for b in range(rows // step):
        block = hits[:, b * step : (b + 1) * step]
        counts.append(mm(block.astype(BF), earlier) + running)
        running = running + jnp.sum(block, axis=1, keepdims=True)
    slots = jnp.where(hits > 0.0, jnp.concatenate(counts, axis=1), -1.0)[:experts]
    spot = lax.broadcasted_iota(jnp.int32, (8, rows), 1)
    begin, end = jnp.zeros((8, rows), F32), 0
    for i in range(lengths_ref.shape[1]):
        end = end + lengths_ref[0, i]
        begin = jnp.where(spot >= end, end.astype(F32), begin)
    valid = jnp.where(spot < end, 1.0, 0.0)
    tail = jnp.where(lax.broadcasted_iota(jnp.int32, (8, rows), 0) == 0, begin, valid)
    spare = jnp.zeros((LANES - experts - 12 - 8, rows), F32)
    meta = jnp.concatenate([slots, hits[:12], tail, spare], axis=0).T
    return slots.astype(jnp.int32), meta


def first_kernel(
    cols,
    ranks,
    x_ref,
    cot_ref,
    router_ref,
    const_ref,
    vector_ref,
    again_ref,
    fgain_ref,
    carry_ref,
    wq_ref,
    wo_ref,
    prev_ref,
    routes_ref,
    lengths_ref,
    cos_ref,
    sin_ref,
    freq_ref,
    gate_ref,
    up_ref,
    down_ref,
    wall_ref,
    qkv_out,
    o_out,
    lse_out,
    xw_out,
    wq_out,
    wo_out,
    cos_out,
    sin_out,
    meta_out,
    slots_ref,
    mixed_out,
    middle_out,
    n2w_ref,
    prevw_out,
    cota_ref,
    rw_out,
    carry_out,
    xw,
    q_parts,
    q_land,
    o_parts,
    o_land,
    wq,
    wo,
    a_send,
    a_land,
    prev_s,
    prevw,
    qkv_s,
    o_s,
    lse_s,
    cos_s,
    sin_s,
    meta_s,
    mixed_s,
    middle_s,
    n2_s,
    w_s,
    local_sem,
    x_send,
    x_recv,
    n_send,
    n_recv,
    t_send,
    t_recv,
    q_send,
    q_recv,
    c_send,
    c_recv,
    r_send,
    r_recv,
    e_send,
    e_recv,
    d_send,
    d_recv,
    s_send,
    s_recv,
    h_send,
    h_recv,
):
    r, c = place()
    heads = 3
    local = x_ref.shape[0]
    rows = local * cols
    width = heads * HEAD_DIM
    depth = D // ranks
    odd, high = c % 2, c // 2
    again = again_ref[...].astype(F32).reshape(1, D)
    fgain = fgain_ref[...].astype(F32).reshape(1, D)
    greet(col_peers(cols) + [(flip(r, m), c) for m in (1, 2, 4, 6)])

    for s in range(3):
        q_parts[s] = wq_ref[:, s * width : (s + 1) * width]
    q_copies = [
        send_to(q_parts.at[1], q_land.at[(c + 1) // 2], q_send.at[0], q_recv.at[0], (r, flip(c, 1))),
        send_to(q_parts.at[2 - 2 * odd], q_land.at[2 * high], q_send.at[1], q_recv.at[1], (r, flip(c, 2))),
    ]
    start_all(q_copies)
    o_parts[...] = wo_ref[...].astype(F32).T.astype(BF)
    prev_s[...] = jnp.concatenate([prev_ref[...].astype(F32), jnp.zeros((16 - ROUTES, local), F32)], axis=0).astype(BF)
    o_copies = to_cols(lambda d: o_parts, o_land, c_send.at[0], c_recv.at[0], cols)
    prev_copies = to_cols(lambda d: prev_s, prevw, c_send.at[1], c_recv.at[1], cols)
    x_step, x_drain = gather_chain(x_ref, xw, x_send, x_recv, cols)
    x_step(0)
    start_all(o_copies + prev_copies)
    q_land[(c + 1) // 2] = q_parts[2 * odd]
    o_land[c] = o_parts[...]
    prevw[c] = prev_s[...]
    xw[c] = x_ref[...]

    def rows_at(d):
        return pl.ds(pl.multiple_of(d * depth, 16), depth)

    def push(ref, at):
        here = ref.at[rows_at(r)]
        return [
            send_to(here, here, r_send.at[at, k - 1], r_recv.at[at, k - 1], (flip(r, 2 * k), c))
            for k in range(1, 4)
        ]

    def hand(ref, at):
        copies = []
        for k in range(4):
            here = ref.at[rows_at(flip(r, 2 * k))]
            copies.append(send_to(here, here, r_send.at[at, 3 + k], r_recv.at[at, 3 + k], (flip(r, 1), c)))
        return copies

    wait_all(q_copies)
    wq[rows_at(r)] = jnp.concatenate([q_land[i] for i in range(3)], axis=1)
    wq_push, wq_hand = push(wq, 0), hand(wq, 0)
    start_all(wq_push)
    wait_all(o_copies)
    wo[rows_at(r)] = jnp.concatenate([o_land[i] for i in range(cols)], axis=1)
    wo_push, wo_hand = push(wo, 1), hand(wo, 1)
    start_all(wo_push)

    weights = (gate_ref, up_ref, down_ref)
    half = gate_ref.shape[0] // 2
    held = moves([(ref, w_s.at[t]) for t, ref in enumerate(weights)], local_sem)
    kept = moves([(w_s.at[t], wall_ref.at[t, :, rows_at(r)]) for t in range(3)], local_sem)

    def to_near(t):
        dst = wall_ref.at[t, :, rows_at(r)]
        return [
            send_to(weights[t], dst, e_send.at[t, k - 1], e_recv.at[t, k - 1], (flip(r, 2 * k), c))
            for k in (1, 2)
        ]

    def to_far(t):
        copies = []
        for k in (1, 2):
            here = wall_ref.at[t, pl.ds((k - 1) * half, half), rows_at(flip(r, 2 * k))]
            copies.append(send_to(here, here, d_send.at[t, k - 1], d_recv.at[t, k - 1], (flip(r, 6 - 2 * k), c)))
        return copies

    def to_other_core(t):
        copies = []
        for k in range(4):
            here = wall_ref.at[t, :, rows_at(flip(r, 2 * k))]
            src = weights[t] if k == 0 else here
            copies.append(send_to(src, here, s_send.at[t, k], s_recv.at[t, k], (flip(r, 1), c)))
        return copies

    def relay(t):
        for near, far, across in zip(to_near(t), to_far(t), to_other_core(t)[1:3]):
            near.wait_recv()
            far.start()
            across.start()

    def hand_over(t):
        for far in to_far(t):
            far.wait_recv()
        to_other_core(t)[3].start()

    for t in range(3):
        start_all(to_near(t))
        to_other_core(t)[0].start()
    start_all(held)

    small = [ref[...].astype(F32) for ref in (router_ref, const_ref.at[0], const_ref.at[1], vector_ref)]
    small += [again, fgain, jnp.zeros((LANES - ROW_GAIN - 2, D), F32)]
    rw_out[...] = jnp.concatenate(small, axis=0).astype(BF)
    carry = jnp.concatenate([carry_ref[...].astype(F32), jnp.zeros((ROUTES, LANES - ROUTES), F32)], axis=1)
    carry_out[...] = jnp.concatenate([carry, jnp.zeros((16 - ROUTES, LANES), F32)], axis=0).astype(BF)
    slots, meta = tokens_meta(routes_ref, lengths_ref, rows, EXPERTS)
    slots_ref[...] = slots
    meta_s[...] = meta
    sub = lax.broadcasted_iota(jnp.int32, (8, LANES), 0)
    firsts, end, ends = jnp.zeros((8, LANES), F32), 0, []
    for i in range(lengths_ref.shape[1]):
        firsts = jnp.where(sub == i, jnp.asarray(end, jnp.int32).astype(F32), firsts)
        end = end + lengths_ref[0, i]
        ends.append(end)
    angle = firsts * freq_ref[...]
    cos_first, sin_first = jnp.cos(angle), jnp.sin(angle)
    spot = lax.broadcasted_iota(jnp.int32, (rows, LANES), 0)
    cb, sb = jnp.ones((rows, LANES), F32), jnp.zeros((rows, LANES), F32)
    for i in range(1, len(ends)):
        cb = jnp.where(spot >= ends[i - 1], cos_first[i : i + 1], cb)
        sb = jnp.where(spot >= ends[i - 1], sin_first[i : i + 1], sb)
    cb, sb = jnp.where(spot >= end, 1.0, cb), jnp.where(spot >= end, 0.0, sb)
    sign = jnp.where(lane_iota((rows, LANES)) % 2 == 0, -1.0, 1.0)
    cos_s[...] = cos_ref[...] * cb + sin_ref[...] * sb
    sin_s[...] = (sin_ref[...] * cb - cos_ref[...] * sb) * sign
    lse_s[...] = jnp.zeros_like(lse_s)

    def project(d):
        at = pl.ds(pl.multiple_of(d * local, LANES), local)
        x = xw[d].astype(F32)
        normed = (x * norm_rows(x) * again).astype(BF)
        proj = mm(normed, wq[...])
        cosine, sines = cos_s[at], sin_s[at]
        for part in range(2 * width // LANES):
            v = proj[:, part * LANES : (part + 1) * LANES]
            t = v * cosine + swap_pairs(v) * sines
            for side in range(2):
                head = 2 * part + side
                piece = t[:, side * HEAD_DIM : (side + 1) * HEAD_DIM].astype(BF)
                if head < heads:
                    piece = piece * jnp.asarray(1.0 / math.sqrt(HEAD_DIM), BF)
                qkv_s[head, at] = piece
        for head in range(2 * heads, 3 * heads):
            qkv_s[head, at] = proj[:, head * HEAD_DIM : (head + 1) * HEAD_DIM].astype(BF)

    def project_at(k):
        def side(way, carry):
            d = c + k * (2 * way - 1)

            @pl.when((d >= 0) & (d < cols))
            def _():
                project(jnp.clip(d, 0, cols - 1))

            return carry

        lax.fori_loop(0, 2 if k else 1, side, 0)

    early = local // EARLY
    cot_step, cot_drain = gather_chain(cot_ref.at[pl.ds(0, early)], cota_ref, t_send, t_recv, cols)
    cot_kept = moves([(cot_ref.at[pl.ds(0, early)], cota_ref.at[c])], local_sem.at[pl.ds(3, 1)])

    wait_all(held)
    start_all(kept)
    x_step(1)
    for copy in wq_push:
        copy.wait_recv()
    start_all(wq_hand)
    x_step(2)
    for copy in wo_push:
        copy.wait_recv()
    start_all(wo_hand)
    wait_all(wq_hand)
    project_at(0)
    project_at(1)
    project_at(2)
    relay(0)
    x_step(3)
    cot_step(0)
    start_all(cot_kept)
    project_at(3)
    cot_step(1)

    blocks = rows // Q_ROWS

    def head_copies(h):
        copies = []
        for k in range(1, cols):
            there = (c + k) % cols
            copies.append(
                send_to(a_send.at[there, h], a_land.at[c, h], h_send.at[h, k - 1], h_recv.at[h, k - 1], (r, there))
            )
        return copies

    def one_head(h, carry):
        for i in range(blocks):
            at = slice(i * Q_ROWS, (i + 1) * Q_ROWS)
            length = (i + 1) * Q_ROWS
            s = mm(qkv_s[h, at], qkv_s[heads + h, :length], NT)
            begin = column(meta_s, at, META_BEGIN).astype(jnp.int32)
            s = jnp.where(seen(begin, i * Q_ROWS, Q_ROWS, length), s, NEG)
            top = jnp.max(s, axis=1, keepdims=True)
            p = jnp.exp(s - top)
            total = jnp.sum(p, axis=1, keepdims=True)
            o = mm(p.astype(BF), qkv_s[2 * heads + h, :length]) * (column(meta_s, at, META_VALID) / total)
            o_s[h, at] = o.astype(BF)
            lse_s[at] = jnp.where(lane_iota((Q_ROWS, LANES)) == h, top + jnp.log(total), lse_s[at])
        for d in range(cols):
            a_send[d, h] = pack_head(o_s[h, d * local : (d + 1) * local])
        start_all(head_copies(h))
        return carry

    lax.fori_loop(0, 1, one_head, 0)
    cot_step(2)
    lax.fori_loop(1, heads, one_head, 0)
    a_land[c] = a_send[c]
    stored = moves(
        [
            (xw, xw_out),
            (wq, wq_out),
            (qkv_s, qkv_out),
            (o_s, o_out),
            (lse_s, lse_out),
            (cos_s, cos_out),
            (sin_s, sin_out),
            (meta_s, meta_out),
        ],
        local_sem.at[pl.ds(4, 8)],
    )
    start_all(stored)
    relay(1)
    wait_all(wo_hand)
    for h in range(heads):
        wait_all(head_copies(h))
    mixed = jnp.concatenate([unpack_head(a_land[i, h]) for i in range(cols) for h in range(heads)], axis=1)
    mixed_s[...] = mixed
    middle = x_ref[...].astype(F32) + mm(mixed, wo[...], NT)
    middle_s[...] = middle
    n2_s[...] = (middle * norm_rows(middle) * fgain).astype(BF)
    n_step, n_drain = gather_chain(n2_s, n2w_ref, n_send, n_recv, cols)
    n_step(0)
    wait_all(prev_copies)
    stored_late = moves(
        [(n2_s, n2w_ref.at[c]), (wo, wo_out), (mixed_s, mixed_out), (middle_s, middle_out), (prevw, prevw_out)],
        local_sem.at[pl.ds(12, 5)],
    )
    start_all(stored_late)
    relay(2)
    n_step(1)
    hand_over(0)
    n_step(2)
    hand_over(1)
    hand_over(2)
    n_step(3)
    cot_step(3)
    x_drain()
    n_drain()
    cot_drain()
    for copy in wq_push + wo_push:
        copy.wait_send()
    for t in range(3):
        for copy in to_near(t) + to_far(t):
            copy.wait_send()
        wait_all(to_other_core(t))
    wait_all(kept + cot_kept + stored + stored_late)


def first_step(cols, ranks, x, cot, router, const, vector, again, fgain, carry, wq, wo, prev, routes, lengths, gate, up, down):
    local = x.shape[0]
    rows = local * cols
    heads, width = 3, 3 * HEAD_DIM
    experts, depth, ff = gate.shape
    spots = np.arange(rows, dtype=np.float64)[:, None]
    pair = np.arange(LANES) % HEAD_DIM // 2
    freq = np.exp(-(2.0 * pair / HEAD_DIM) * math.log(BASE))[None, :]
    tables = [np.cos(spots * freq), np.sin(spots * freq), freq]
    tables = [jnp.asarray(value.astype(np.float32)) for value in tables]
    vm = pl.BlockSpec(memory_space=pltpu.VMEM)
    dma = pltpu.SemaphoreType.DMA
    return pl.pallas_call(
        functools.partial(first_kernel, cols, ranks),
        out_shape=(
            jax.ShapeDtypeStruct((3, experts, D, ff), BF),
            jax.ShapeDtypeStruct((3 * heads, rows, HEAD_DIM), BF),
            jax.ShapeDtypeStruct((heads, rows, HEAD_DIM), BF),
            jax.ShapeDtypeStruct((rows, LANES), F32),
            jax.ShapeDtypeStruct((cols, local, D), BF),
            jax.ShapeDtypeStruct((D, 3 * width), BF),
            jax.ShapeDtypeStruct((D, D), BF),
            jax.ShapeDtypeStruct((rows, LANES), F32),
            jax.ShapeDtypeStruct((rows, LANES), F32),
            jax.ShapeDtypeStruct((rows, LANES), F32),
            jax.ShapeDtypeStruct((experts, rows), jnp.int32),
            jax.ShapeDtypeStruct((local, D), BF),
            jax.ShapeDtypeStruct((local, D), F32),
            jax.ShapeDtypeStruct((cols, local, D), BF),
            jax.ShapeDtypeStruct((cols, 16, local), BF),
            jax.ShapeDtypeStruct((cols, local // EARLY, D), BF),
            jax.ShapeDtypeStruct((LANES, D), BF),
            jax.ShapeDtypeStruct((16, LANES), BF),
        ),
        in_specs=[vm] * 12 + [pl.BlockSpec(memory_space=pltpu.SMEM)] + [vm] * 3 + [ANY] * 3,
        out_specs=(ANY,) * 10 + (vm,) + (ANY,) * 5 + (vm, vm),
        scratch_shapes=[
            pltpu.VMEM((cols, local, D), BF),
            pltpu.VMEM((3, depth, width), BF),
            pltpu.VMEM((3, depth, width), BF),
            pltpu.VMEM((depth, width), BF),
            pltpu.VMEM((cols, depth, width), BF),
            pltpu.VMEM((D, 3 * width), BF),
            pltpu.VMEM((D, D), BF),
            pltpu.VMEM((cols, heads, local // 2, LANES), BF),
            pltpu.VMEM((cols, heads, local // 2, LANES), BF),
            pltpu.VMEM((16, local), BF),
            pltpu.VMEM((cols, 16, local), BF),
            pltpu.VMEM((3 * heads, rows, HEAD_DIM), BF),
            pltpu.VMEM((heads, rows, HEAD_DIM), BF),
            pltpu.VMEM((rows, LANES), F32),
            pltpu.VMEM((rows, LANES), F32),
            pltpu.VMEM((rows, LANES), F32),
            pltpu.VMEM((rows, LANES), F32),
            pltpu.VMEM((local, D), BF),
            pltpu.VMEM((local, D), F32),
            pltpu.VMEM((local, D), BF),
            pltpu.VMEM((3, experts, depth, ff), BF),
            dma((17,)),
            dma((2, cols - 1)),
            dma((2, cols - 1)),
            dma((2, cols - 1)),
            dma((2, cols - 1)),
            dma((2, cols - 1)),
            dma((2, cols - 1)),
            dma((2,)),
            dma((2,)),
            dma((2, cols - 1)),
            dma((2, cols - 1)),
            dma((2, 7)),
            dma((2, 7)),
            dma((3, 2)),
            dma((3, 2)),
            dma((3, 2)),
            dma((3, 2)),
            dma((3, 4)),
            dma((3, 4)),
            dma((heads, cols - 1)),
            dma((heads, cols - 1)),
        ],
        compiler_params=pltpu.CompilerParams(
            vmem_limit_bytes=60 * MIB, collective_id=5, has_side_effects=True
        ),
        cost_estimate=pl.CostEstimate(
            flops=8 * heads * rows * rows * HEAD_DIM, bytes_accessed=40 * MIB, transcendentals=heads * rows * rows
        ),
        name="first_step",
    )(x, cot, router, const, vector, again, fgain, carry, wq, wo, prev, routes, lengths, *tables, gate, up, down)


def experts_forward_kernel(
    cols,
    capacity,
    n2_ref,
    prev_ref,
    cot_ref,
    rw_ref,
    carry_ref,
    slots_ref,
    meta_ref,
    w_ref,
    x_ref,
    gu_ref,
    y_ref,
    gates_ref,
    cotb_ref,
    send,
    recv,
    local_sem,
):
    e = pl.program_id(0)
    experts = pl.num_programs(0)
    r, c = place()
    early = cot_ref.shape[0] // EARLY
    late = cot_ref.at[pl.ds(early, cot_ref.shape[0] - early)]
    step, drain = gather_chain(late, cotb_ref, send, recv, cols)
    own_copy = pltpu.make_async_copy(late, cotb_ref.at[c], local_sem.at[0])

    @pl.when(e == 0)
    def _():
        greet(col_peers(cols))
        own_copy.start()
        step(0)
        prev = jnp.concatenate([mm(prev_ref[i], carry_ref[...], TN) for i in range(cols)], axis=0)
        g = gate_lanes(mm(n2_ref[...], rw_ref[...], NT) + prev, meta_ref[...])
        high = g.astype(BF)
        gates_ref[:, :LANES] = high
        gates_ref[:, LANES:] = (g - high.astype(F32)).astype(BF)

    @pl.when(e == 3)
    def _():
        step(1)

    @pl.when(e == 6)
    def _():
        step(2)

    one = slot_rows(slots_ref, e, capacity)
    x = mm(one, n2_ref[...]).astype(BF)
    x_ref[0] = x
    sg = slot_gates(one, gates_ref, e)
    g = mm(x, w_ref[0, 0])
    u = mm(x, w_ref[1, 0])
    gu_ref[0, 0] = g.astype(BF)
    gu_ref[0, 1] = u.astype(BF)
    gh = (g * jax.nn.sigmoid(g) * u * sg).astype(BF)
    y_ref[0] = mm(gh, w_ref[2, 0], NT).astype(BF)

    @pl.when(e == experts - 1)
    def _():
        for k in range(3, cols):
            step(k)
        drain()
        own_copy.wait()


def experts_forward(cols, n2, prev, cot, rw, carry, meta, slots, w_all):
    rows = n2.shape[0]
    capacity = rows // 4
    three, experts, deep, ff = w_all.shape
    local = rows // cols
    rest = local - local // EARLY
    return pl.pallas_call(
        functools.partial(experts_forward_kernel, cols, capacity),
        grid=(experts,),
        out_shape=(
            jax.ShapeDtypeStruct((experts, capacity, D), BF),
            jax.ShapeDtypeStruct((experts, 2, capacity, ff), BF),
            jax.ShapeDtypeStruct((experts, capacity, D), BF),
            jax.ShapeDtypeStruct((rows, 2 * LANES), BF),
            jax.ShapeDtypeStruct((cols, rest, D), BF),
        ),
        in_specs=[
            whole((rows, D)),
            whole((cols, 16, local)),
            whole((local, D)),
            whole((LANES, D)),
            whole((16, LANES)),
            whole((experts, rows)),
            whole((rows, LANES)),
            pl.BlockSpec((three, 1, deep, ff), lambda e: (0, e, 0, 0)),
        ],
        out_specs=(
            pl.BlockSpec((1, capacity, D), lambda e: (e, 0, 0)),
            pl.BlockSpec((1, 2, capacity, ff), lambda e: (e, 0, 0, 0)),
            pl.BlockSpec((1, capacity, D), lambda e: (e, 0, 0)),
            whole((rows, 2 * LANES)),
            ANY,
        ),
        scratch_shapes=[
            pltpu.SemaphoreType.DMA((2, cols - 1)),
            pltpu.SemaphoreType.DMA((2, cols - 1)),
            pltpu.SemaphoreType.DMA((1,)),
        ],
        compiler_params=pltpu.CompilerParams(
            vmem_limit_bytes=60 * MIB, collective_id=1, has_side_effects=True
        ),
        cost_estimate=pl.CostEstimate(
            flops=experts * capacity * 2 * D * (3 * ff + rows),
            bytes_accessed=40 * MIB,
            transcendentals=experts * capacity * ff,
        ),
        name="experts_forward",
    )(n2, prev, cot, rw, carry, slots, meta, w_all)


def experts_backward_kernel(
    cols,
    capacity,
    cota_ref,
    cotb_ref,
    y_ref,
    gates_ref,
    slots_ref,
    meta_ref,
    w_ref,
    x_ref,
    gu_ref,
    dx_ref,
    dots_ref,
    mixsum_ref,
    gown_ref,
    sib_ref,
    hin_ref,
    glast_ref,
    cot_s,
    mix_s,
    gbuf,
    out,
    arrived,
    send,
    recv,
    own_sem,
    sib_send,
    sib_recv,
    cot_sem,
    lbuf,
    hbuf,
    l_sem,
    hsend,
    hrecv,
):
    e = pl.program_id(0)
    experts = pl.num_programs(0)
    r, c = place()
    core = r % 2
    local = mix_s.shape[1]
    early = cota_ref.shape[1]
    place_now = lax.rem(e, 2)
    slot, total, drain = reduce_chain(lambda d: mix_s[d], out, arrived, send, recv, cols)

    def own_copy(expert, at):
        return pltpu.make_async_copy(gbuf.at[at, :, :, core], gown_ref.at[expert], own_sem.at[at])

    def last_copy(at):
        return pltpu.make_async_copy(gbuf.at[at, :, :, 1 - core], glast_ref, sib_send.at[at])

    def sib_copy(expert, at):
        return send_to(
            gbuf.at[at, :, :, 1 - core],
            sib_ref.at[expert],
            sib_send.at[at],
            sib_recv.at[expert],
            (flip(r, 1), c),
        )

    cot_loads = moves(
        [(cota_ref.at[d], cot_s.at[pl.ds(d * local, early)]) for d in range(cols)]
        + [(cotb_ref.at[d], cot_s.at[pl.ds(d * local + early, local - early)]) for d in range(cols)],
        cot_sem,
    )
    before = jnp.maximum(e - 1, 0)
    sib_load = pltpu.make_async_copy(sib_ref.at[before], lbuf, l_sem.at[0])
    sends_now = (e >= 1) & (e <= SENT_SOON)

    def h_sends(i):
        return to_chips(lambda there: hbuf.at[i, :, there], hin_ref.at[i], hsend.at[i], hrecv.at[i])

    @pl.when(e == 0)
    def _():
        start_all(cot_loads)
        greet(col_peers(cols) + [(flip(r, m), c) for m in (1, 2, 4, 6)])
        for n, d in enumerate(chain_order(c)):
            mix_s[d] = combine(meta_ref, y_ref, d, local)
            if n == 0:
                slot(0)
        wait_all(cot_loads)

    @pl.when(e == 2)
    def _():
        slot(1)

    @pl.when(e == 5)
    def _():
        slot(2)

    one = slot_rows(slots_ref, e, capacity)
    ct = mm(one, cot_s[...]).astype(BF)
    sg = slot_gates(one, gates_ref, e)
    x = x_ref[0]
    g, u = gu_ref[0, 0].astype(F32), gu_ref[0, 1].astype(F32)
    v = mm(ct, w_ref[2, 0])
    sig = jax.nn.sigmoid(g)
    act = g * sig
    h = act * u
    dot = jnp.sum(h * v, axis=1, keepdims=True)
    dots_ref[pl.ds(e, 1)] = jnp.sum(one.astype(F32) * dot, axis=0, keepdims=True)
    gh = (h * sg).astype(BF)
    gv = v * sg
    dg = (gv * u * (sig * (1.0 + g * (1.0 - sig)))).astype(BF)
    du = (gv * act).astype(BF)
    dx_ref[0] = (mm(dg, w_ref[0, 0], NT) + mm(du, w_ref[1, 0], NT)).astype(BF)

    @pl.when(e >= 2)
    def _():
        own_copy(e - 2, place_now).wait()
        sib_copy(e - 2, place_now).wait_send()

    @pl.when(sends_now)
    def _():
        sib_copy(before, 1 - place_now).wait_recv()
        sib_load.start()

    shape = gbuf.shape[2:]
    gbuf[place_now, 0] = mm(x, dg, TN).astype(BF).reshape(shape)
    gbuf[place_now, 1] = mm(x, du, TN).astype(BF).reshape(shape)
    gbuf[place_now, 2] = mm(ct, gh, TN).astype(BF).reshape(shape)
    own_copy(e, place_now).start()

    @pl.when(e < experts - 1)
    def _():
        sib_copy(e, place_now).start()

    @pl.when(e == experts - 1)
    def _():
        last_copy(place_now).start()

    @pl.when(sends_now)
    def _():
        sib_load.wait()
        hbuf[before] = (gbuf[1 - place_now, :, :, core].astype(F32) + lbuf[...].astype(F32)).astype(BF)
        start_all(h_sends(before))

    @pl.when(e == experts - 1)
    def _():
        for s in range(3, cols):
            slot(s)
        total(mixsum_ref)
        drain()
        for back in (1, 0):
            own_copy(e - back, lax.rem(e - back, 2)).wait()
        sib_copy(e - 1, 1 - place_now).wait_send()
        last_copy(place_now).wait()
        for i in range(SENT_SOON, EXPERTS - 1):
            sib_copy(i, i % 2).wait_recv()
        for i in range(SENT_SOON):
            wait_all(h_sends(i))


def experts_backward(cols, ranks, cota, cotb, y, gates, meta, slots, w_all, x, gu):
    experts, capacity, _ = y.shape
    rows = slots.shape[1]
    three, _, deep, ff = w_all.shape
    local = rows // cols
    chips = ranks // 2
    depth = deep // ranks
    half = jax.ShapeDtypeStruct((experts, three, chips, depth, ff), BF)
    return pl.pallas_call(
        functools.partial(experts_backward_kernel, cols, capacity),
        grid=(experts,),
        out_shape=(
            jax.ShapeDtypeStruct((experts, capacity, D), BF),
            jax.ShapeDtypeStruct((experts, rows), F32),
            jax.ShapeDtypeStruct((local, D), F32),
            half,
            half,
            jax.ShapeDtypeStruct((SENT_SOON, 3, three, depth, ff), BF),
            jax.ShapeDtypeStruct((three, chips, depth, ff), BF),
        ),
        in_specs=[
            ANY,
            ANY,
            whole((experts, capacity, D)),
            whole((rows, 2 * LANES)),
            whole((experts, rows)),
            whole((rows, LANES)),
            pl.BlockSpec((three, 1, deep, ff), lambda e: (0, e, 0, 0)),
            pl.BlockSpec((1, capacity, D), lambda e: (e, 0, 0)),
            pl.BlockSpec((1, 2, capacity, ff), lambda e: (e, 0, 0, 0)),
        ],
        out_specs=(
            pl.BlockSpec((1, capacity, D), lambda e: (e, 0, 0)),
            whole((experts, rows)),
            whole((local, D)),
            ANY,
            ANY,
            ANY,
            ANY,
        ),
        scratch_shapes=[
            pltpu.VMEM((rows, D), BF),
            pltpu.VMEM((cols, local, D), BF),
            pltpu.VMEM((2, three, chips, 2, depth, ff), BF),
            *chain_scratch(cols, local),
            pltpu.SemaphoreType.DMA((2,)),
            pltpu.SemaphoreType.DMA((2,)),
            pltpu.SemaphoreType.DMA((experts,)),
            pltpu.SemaphoreType.DMA((2 * cols,)),
            pltpu.VMEM((three, chips, depth, ff), BF),
            pltpu.VMEM((SENT_SOON, three, chips, depth, ff), BF),
            pltpu.SemaphoreType.DMA((1,)),
            pltpu.SemaphoreType.DMA((SENT_SOON, 3)),
            pltpu.SemaphoreType.DMA((SENT_SOON, 3)),
        ],
        compiler_params=pltpu.CompilerParams(
            vmem_limit_bytes=60 * MIB, collective_id=2, has_side_effects=True
        ),
        cost_estimate=pl.CostEstimate(
            flops=experts * capacity * 4 * D * (3 * ff + rows),
            bytes_accessed=60 * MIB,
            transcendentals=experts * capacity * ff,
        ),
        name="experts_backward",
    )(cota, cotb, y, gates, slots, meta, w_all, x, gu)


def resid_kernel(
    cols,
    count,
    dx_ref,
    meta_ref,
    dots_ref,
    rw_ref,
    prev_ref,
    carry_ref,
    cot_ref,
    mixsum_in,
    n2w_in,
    middle_in,
    out_t_in,
    mixed_in,
    gown_ref,
    glast_ref,
    sib_in,
    layer_ref,
    resid_ref,
    gm_ref,
    og_ref,
    small_ref,
    pg_ref,
    hin_ref,
    hrest_ref,
    sib_ref,
    mixsum,
    n2_s,
    middle_s,
    out_t,
    mixed_s,
    resid_s,
    load_sem,
    gt_s,
    out,
    arrived,
    send,
    recv,
    dots_in,
    dsend,
    drecv,
    grad,
    gm_out,
    gsend,
    grecv,
    gm_sem,
    lbuf,
    hbuf,
    hload,
    hsend,
    hrecv,
    hkeep,
    last_sem,
    og_s,
    og_sib,
):
    r, c = place()
    chip = r // 2
    local = cot_ref.shape[0]
    held = hbuf.shape[0]
    loads = moves(
        [
            (n2w_in.at[c], n2_s),
            (middle_in, middle_s),
            (mixsum_in, mixsum),
            (out_t_in, out_t),
            (mixed_in, mixed_s),
        ],
        load_sem,
    )
    greet(col_peers(cols) + [(flip(r, m), c) for m in (1, 2, 4, 6)])
    last = gown_ref.shape[0] - 1
    across = send_to(glast_ref, sib_ref.at[last], last_sem.at[0], last_sem.at[1], (flip(r, 1), c))
    across.start()
    slot, total, drain = reduce_chain(lambda d: gt_s[d], out, arrived, send, recv, cols)

    def dots_of(d):
        return dots_ref.at[:, pl.ds(pl.multiple_of(d * local, LANES), local)]

    dot_copies = to_cols(dots_of, dots_in, dsend, drecv, cols)
    start_all(dot_copies)
    dots_in[c] = dots_of(c)[...]
    for n, d in enumerate(chain_order(c)):
        gt_s[d] = combine(meta_ref, dx_ref, d, local)
        if n == 0:
            slot(0)

    def h_loads(i):
        at = lax.rem(i, 2)
        return [
            pltpu.make_async_copy(ref.at[SENT_SOON + i], lbuf.at[at, j], hload.at[at, j])
            for j, ref in enumerate((gown_ref, sib_ref))
        ]

    def h_sends(i):
        return to_chips(lambda there: hbuf.at[i, :, there], hin_ref.at[i], hsend.at[i], hrecv.at[i])

    def h_keeps(i):
        return moves(
            [(hbuf.at[i, :, flip(chip, k)], hrest_ref.at[i - count, k - 1]) for k in range(1, 4)],
            hkeep.at[i - count],
        )

    start_all(h_loads(0))

    def add_cores(i, carry):
        @pl.when(i + 2 == held)
        def _():
            across.wait()

        @pl.when(i + 1 < held)
        def _():
            start_all(h_loads(i + 1))

        wait_all(h_loads(i))
        at = lax.rem(i, 2)
        hbuf[i] = (lbuf[at, 0].astype(F32) + lbuf[at, 1].astype(F32)).astype(BF)

        @pl.when(i < count)
        def _():
            start_all(h_sends(i))

        @pl.when(i >= count)
        def _():
            start_all(h_keeps(jnp.maximum(i, count)))

        return carry

    lax.fori_loop(0, held, add_cores, 0)
    start_all(loads)
    slot(1)
    wait_all(loads)

    meta = meta_ref[pl.ds(pl.multiple_of(c * local, LANES), local)]
    n2, cot = n2_s[...], cot_ref[...]
    n2f, cotf = n2.astype(F32), cot.astype(F32)
    middle = middle_s[...]
    rw = rw_ref[...]
    lin = mm(n2, rw, NT)
    prev = prev_ref[c]
    gates = gate_lanes(lin + mm(prev, carry_ref[...], TN), meta)
    lane = lane_iota((local, LANES))
    cot_lin = mm(cot, rw, NT)
    dot_keep = jnp.sum(cotf * n2f, axis=1, keepdims=True)
    wait_all(dot_copies)
    d = jnp.concatenate([all_sum(dots_in, cols), jnp.zeros((LANES - EXPERTS, local), F32)], axis=0).T
    g_gates = jnp.where(lane == EXPERTS + 1, dot_keep, d)
    keep = gates[:, EXPERTS + 1 : EXPERTS + 2]
    mixes, packs = [], jnp.zeros((local, LANES), F32)
    for j in range(2):
        l0 = lin[:, ROW_CONST + 2 * j : ROW_CONST + 2 * j + 1]
        l1 = lin[:, ROW_CONST + 2 * j + 1 : ROW_CONST + 2 * j + 2]
        top = jnp.maximum(l0, l1)
        e0, e1 = jnp.exp(l0 - top), jnp.exp(l1 - top)
        a0, a1 = e0 / (e0 + e1), e1 / (e0 + e1)
        share = gates[:, EXPERTS + 2 + j : EXPERTS + 3 + j]
        dot_vec = cot_lin[:, ROW_VEC + j : ROW_VEC + j + 1]
        keep = keep + share * a0
        mixes.append(share * a1)
        g_gates = jnp.where(lane == EXPERTS + 2 + j, a0 * dot_keep + a1 * dot_vec, g_gates)
        gk, gv = share * dot_keep, share * dot_vec
        mean = a0 * gk + a1 * gv
        packs = packs + jnp.where(lane == ROW_CONST + 2 * j, a0 * (gk - mean), 0.0)
        packs = packs + jnp.where(lane == ROW_CONST + 2 * j + 1, a1 * (gv - mean), 0.0)
        packs = packs + jnp.where(lane == ROW_VEC + j, share * a1, 0.0)
    packs = packs + gates * (g_gates - jnp.sum(gates * g_gates, axis=1, keepdims=True))
    vec = rw[ROW_VEC : ROW_VEC + 2].astype(F32)
    layer = middle + mixsum[...] + keep * n2f + mixes[0] * vec[0:1] + mixes[1] * vec[1:2]
    layer_ref[...] = layer.astype(BF)

    high = packs.astype(BF)
    low = (packs - high.astype(F32)).astype(BF)
    back = lane < ROW_VEC
    high_b = jnp.where(back, packs, 0.0).astype(BF)
    low_b = jnp.where(back, packs - high.astype(F32), 0.0).astype(BF)
    grad_local = keep * cotf + mm(high_b, rw) + mm(low_b, rw)
    by_n2 = mm(high, n2, TN) + mm(low, n2, TN)
    by_cot = mm(high, cot, TN) + mm(low, cot, TN)
    by_prev = mm(prev, high) + mm(prev, low)
    pg = mm(carry_ref[...], high_b, NT) + mm(carry_ref[...], low_b, NT)
    pg_ref[...] = pg[:ROUTES]
    sub = lax.broadcasted_iota(jnp.int32, (SMALL_ROWS, D), 0)
    small_ref[:, :D] = jnp.where(sub < ROW_VEC, by_n2[:SMALL_ROWS], by_cot[:SMALL_ROWS])
    small_ref[:16, D : D + LANES] = by_prev
    small_ref[16:, D : D + LANES] = jnp.zeros((SMALL_ROWS - 16, LANES), F32)
    small_ref[:, D + LANES :] = jnp.zeros((SMALL_ROWS, LANES), F32)
    fgain = rw[ROW_GAIN + 1 : ROW_GAIN + 2].astype(F32)
    scale = norm_rows(middle)

    for s in range(2, cols):
        slot(s)
    total(grad)
    grad_normed = grad[...] + grad_local
    gained = grad_normed * fgain
    mid_dot = jnp.sum(gained * middle, axis=1, keepdims=True)
    resid = cotf + scale * gained - middle * (scale * scale * scale * (mid_dot * (1.0 / D)))
    cut = resid.astype(BF)
    gm = (mm(cut, out_t[...]) * meta[:, META_VALID : META_VALID + 1]).astype(BF)
    width = D // cols
    for i in range(cols):
        for h in range(width // HEAD_DIM):
            at = i * width + h * HEAD_DIM
            gm_out[i, h] = pack_head(gm[:, at : at + HEAD_DIM])
    gm_copies = to_cols(lambda i: gm_out.at[i], gm_ref, gsend, grecv, cols)
    start_all(gm_copies)
    resid_s[...] = resid
    stored = moves([(gm_out.at[c], gm_ref.at[c]), (resid_s, resid_ref)], gm_sem)
    start_all(stored)
    small_ref[ROW_GAIN : ROW_GAIN + 1, :D] = jnp.sum(grad_normed * middle * scale, axis=0, keepdims=True)
    core = r % 2
    og_s[...] = mm(cut, mixed_s[...], TN).astype(BF).reshape(og_s.shape)
    og_across = send_to(og_s.at[:, 1 - core], og_sib, last_sem.at[2], last_sem.at[3], (flip(r, 1), c))
    og_across.start()
    og_across.wait()
    for k in range(og_s.shape[0]):
        og_ref[k] = (og_s[k, core].astype(F32) + og_sib[k].astype(F32)).astype(BF)
    wait_all(stored + gm_copies)
    drain()

    def end(i, carry):
        @pl.when(i < count)
        def _():
            wait_all(h_sends(i))

        @pl.when(i >= count)
        def _():
            wait_all(h_keeps(jnp.maximum(i, count)))

        return carry

    lax.fori_loop(0, held, end, 0)


def resid_step(cols, dx, meta, dots, rw, prev, carry, cot, mixsum, n2w, middle, out_t, mixed, gown, glast, sib):
    local = cot.shape[0]
    experts, three, chips, depth, ff = gown.shape
    count, held = SENT_NEXT, experts - SENT_SOON
    vm = pl.BlockSpec(memory_space=pltpu.VMEM)
    dma = pltpu.SemaphoreType.DMA
    return pl.pallas_call(
        functools.partial(resid_kernel, cols, count),
        out_shape=(
            jax.ShapeDtypeStruct((local, D), BF),
            jax.ShapeDtypeStruct((local, D), F32),
            jax.ShapeDtypeStruct((cols, 3, local // 2, LANES), BF),
            jax.ShapeDtypeStruct((chips, depth, D), BF),
            jax.ShapeDtypeStruct((SMALL_ROWS, D + 2 * LANES), F32),
            jax.ShapeDtypeStruct((ROUTES, local), F32),
            jax.ShapeDtypeStruct((count, 3, three, depth, ff), BF),
            jax.ShapeDtypeStruct((held - count, 3, three, depth, ff), BF),
            jax.ShapeDtypeStruct(sib.shape, BF),
        ),
        in_specs=[vm] * 7 + [ANY] * 8,
        out_specs=(vm, ANY, ANY, vm, vm, vm, ANY, ANY, ANY),
        input_output_aliases={14: 8},
        scratch_shapes=[
            pltpu.VMEM((local, D), F32),
            pltpu.VMEM((local, D), BF),
            pltpu.VMEM((local, D), F32),
            pltpu.VMEM((D, D), BF),
            pltpu.VMEM((local, D), BF),
            pltpu.VMEM((local, D), F32),
            dma((5,)),
            pltpu.VMEM((cols, local, D), BF),
            *chain_scratch(cols, local),
            pltpu.VMEM((cols, EXPERTS, local), F32),
            dma((cols - 1,)),
            dma((cols - 1,)),
            pltpu.VMEM((local, D), F32),
            pltpu.VMEM((cols, 3, local // 2, LANES), BF),
            dma((cols - 1,)),
            dma((cols - 1,)),
            dma((2,)),
            pltpu.VMEM((2, 2, three, chips, depth, ff), BF),
            pltpu.VMEM((held, three, chips, depth, ff), BF),
            dma((2, 2)),
            dma((count, 3)),
            dma((count, 3)),
            dma((held - count, 3)),
            dma((4,)),
            pltpu.VMEM((chips, 2, depth, D), BF),
            pltpu.VMEM((chips, depth, D), BF),
        ],
        compiler_params=pltpu.CompilerParams(
            vmem_limit_bytes=60 * MIB, collective_id=3, has_side_effects=True
        ),
        cost_estimate=pl.CostEstimate(flops=6 * local * D * D, bytes_accessed=40 * MIB, transcendentals=0),
        name="resid_step",
    )(dx, meta, dots, rw, prev, carry, cot, mixsum, n2w, middle, out_t, mixed, gown, glast, sib)


def finish_kernel(
    cols,
    ranks,
    gm_ref,
    meta_ref,
    lse_ref,
    small_ref,
    og_ref,
    xown_ref,
    rw_ref,
    qkv_in,
    o_in,
    x_in,
    w_in,
    cos_in,
    sin_in,
    resid_in,
    gown_ref,
    sib_ref,
    hsoon_ref,
    hin0_ref,
    hrest_ref,
    ig_ref,
    small_out,
    qg_out,
    og_out,
    gg_ref,
    ug_ref,
    dg_ref,
    hin_ref,
    qkv_s,
    o_s,
    x_s,
    w_s,
    cos_s,
    sin_s,
    resid_s,
    head_sem,
    load_sem,
    do_s,
    dq_s,
    dk_s,
    dv_s,
    gn_s,
    qg_acc,
    qg_cut,
    out,
    arrived,
    send,
    recv,
    small_s,
    small_rows,
    small_cols,
    small_all,
    og_chips,
    og_parts,
    og_cols,
    qg_sib,
    qg_half,
    qg_chips,
    q_parts,
    q_land,
    total_s,
    fbuf,
    fsem,
    row_send,
    row_recv,
    chip_send,
    chip_recv,
    sib_send,
    sib_recv,
    col_send,
    col_recv,
    hsend,
    hrecv,
    g_s,
    store_sem,
):
    r, c = place()
    chip, core = r // 2, r % 2
    heads = 3
    rows = meta_ref.shape[0]
    local = rows // cols
    width = heads * HEAD_DIM
    rest = hrest_ref.shape[0]
    first = gown_ref.shape[0] - rest
    score_scale = 1.0 / math.sqrt(HEAD_DIM)

    def head_loads(h):
        pairs = [(qkv_in.at[i * heads + h], qkv_s.at[i * heads + h]) for i in range(3)]
        return moves(pairs + [(o_in.at[h], o_s.at[h])], head_sem.at[h])

    loads = moves(
        [(x_in, x_s), (w_in, w_s), (cos_in, cos_s), (sin_in, sin_s), (resid_in, resid_s)], load_sem
    )
    start_all(head_loads(0))
    greet(col_peers(cols) + [(flip(r, m), c) for m in range(1, ranks)])
    for h in range(1, heads):
        start_all(head_loads(h))
    start_all(loads)

    def to_sibling(src, dst, at):
        return send_to(src.at[:, 1 - core], dst, sib_send.at[at], sib_recv.at[at], (flip(r, 1), c))

    og_to_chips = to_chips(lambda there: og_ref.at[there], og_chips, chip_send.at[0], chip_recv.at[0])
    start_all(og_to_chips)

    for d in range(cols):
        at = slice(d * local, (d + 1) * local)
        for h in range(heads):
            do_s[h, at] = unpack_head(gm_ref[d, h])

    def halves(ref, sib, half):
        for k in range(ranks // 2):
            half[k] = (ref[k, core].astype(F32) + sib[k].astype(F32)).astype(BF)

    def h_sends(i):
        r_, c_ = place()
        return [
            send_to(
                hrest_ref.at[i, k - 1],
                hin_ref.at[i, k - 1],
                hsend.at[i, k - 1],
                hrecv.at[i, k - 1],
                (flip(r_, 2 * k), c_),
            )
            for k in range(1, 4)
        ]

    def start_sends(i, carry):
        start_all(h_sends(i))
        return carry

    lax.fori_loop(0, rest - 1, start_sends, 0)

    blocks = rows // Q_ROWS

    def one_head(h, carry):
        wait_all(head_loads(h))
        for i in reversed(range(blocks)):
            at = slice(i * Q_ROWS, (i + 1) * Q_ROWS)
            length = (i + 1) * Q_ROWS
            q, do = qkv_s[h, at], do_s[h, at]
            k, v = qkv_s[heads + h, :length], qkv_s[2 * heads + h, :length]
            delta = jnp.sum(do.astype(F32) * o_s[h, at].astype(F32), axis=1, keepdims=True)
            lse = jnp.sum(jnp.where(lane_iota((Q_ROWS, LANES)) == h, lse_ref[at], 0.0), axis=1, keepdims=True)
            s = mm(q, k, NT)
            ok = seen(column(meta_ref, at, META_BEGIN).astype(jnp.int32), i * Q_ROWS, Q_ROWS, length)
            p = jnp.where(ok, jnp.exp(s - lse), 0.0)
            ds = (p * (mm(do, v, NT) - delta)).astype(BF)
            dq_s[h, at] = mm(ds, k) * score_scale
            dk, dv = mm(ds, q, TN), mm(p.astype(BF), do, TN)
            if i == blocks - 1:
                dk_s[h], dv_s[h] = dk, dv
            else:
                dk_s[h, :length] += dk
                dv_s[h, :length] += dv
        return carry

    lax.fori_loop(0, heads, one_head, 0)

    slot, total, drain = reduce_chain(lambda d: gn_s[d], out, arrived, send, recv, cols)
    wait_all(loads)
    gain_total = jnp.zeros((1, D), F32)
    weight = w_s[...]
    again = rw_ref[ROW_GAIN : ROW_GAIN + 1].astype(F32)
    for n, d in enumerate(chain_order(c)):
        at = pl.ds(pl.multiple_of(d * local, LANES), local)
        cosine, sines = cos_s[at], sin_s[at]
        turned = [dq_s[h, at] for h in range(heads)] + [dk_s[h, at] for h in range(heads)]
        parts = []
        for part in range(heads):
            v = jnp.concatenate(turned[2 * part : 2 * part + 2], axis=1)
            parts.append((v * cosine - swap_pairs(v) * sines).astype(BF))
        parts += [dv_s[h, at].astype(BF) for h in range(heads)]
        gp = jnp.concatenate(parts, axis=1)
        x = x_s[d].astype(F32)
        xs = x * norm_rows(x)
        gn = mm(gp, weight, NT)
        gn_s[d] = gn.astype(BF)
        if n == 0:
            slot(0)
        gain_total = gain_total + jnp.sum(gn * xs, axis=0, keepdims=True)
        grad = mm((xs * again).astype(BF), gp, TN)
        if n == 0:
            qg_acc[...] = grad
        else:
            qg_acc[...] += grad
    qg_cut[...] = qg_acc[...].astype(BF).reshape(qg_cut.shape)
    qg_across = to_sibling(qg_cut, qg_sib, 0)
    qg_across.start()

    sub = lax.broadcasted_iota(jnp.int32, (SMALL_ROWS, D), 0)
    for i in range(ranks):
        block = small_ref[:, i * LANES : (i + 1) * LANES]
        if i < D // LANES:
            own = sub[:, :LANES] == ROW_GAIN + 1
            block = jnp.where(own, gain_total[:, i * LANES : (i + 1) * LANES], block)
        small_s[i] = block
    small_to_rows = to_rows(lambda d: small_s.at[d], small_rows, row_send.at[0], row_recv.at[0], ranks)
    start_all(small_to_rows)
    small_rows[r] = small_s[r]

    def sum_grads(low, high, hin, base):
        def f_loads(i):
            at = lax.rem(i, 2)
            return moves(
                [
                    (gown_ref.at[i, :, chip], fbuf.at[at, 0]),
                    (sib_ref.at[i, :, chip], fbuf.at[at, 1]),
                    (hin.at[i - base], fbuf.at[at, pl.ds(2, 3)]),
                ],
                fsem.at[at],
            )

        start_all(f_loads(low))

        def body(i, carry):
            @pl.when(i + 1 < high)
            def _():
                start_all(f_loads(jnp.minimum(i + 1, high - 1)))

            wait_all(f_loads(i))
            at = lax.rem(i, 2)
            total_grad = fbuf[at, 0].astype(F32)
            for j in range(1, 5):
                total_grad = total_grad + fbuf[at, j].astype(F32)
            for t in range(3):
                g_s[t, i] = total_grad[t].astype(BF)
            return carry

        lax.fori_loop(low, high, body, 0)

    qg_across.wait()
    halves(qg_cut, qg_sib, qg_half)
    qg_to_chips = to_chips(lambda there: qg_half.at[there], qg_chips, chip_send.at[1], chip_recv.at[1])
    start_all(qg_to_chips)
    start_sends(rest - 1, 0)
    slot(1)
    sum_grads(0, SENT_SOON, hsoon_ref, 0)
    wait_all(small_to_rows)
    small_cols[c] = all_sum(small_rows, ranks)
    small_to_cols = to_cols(lambda d: small_cols.at[c], small_cols, col_send.at[0], col_recv.at[0], cols)
    start_all(small_to_cols)
    sum_grads(SENT_SOON, first, hin0_ref, SENT_SOON)
    slot(2)
    wait_all(og_to_chips)
    og_sum = og_ref[chip].astype(F32) + all_sum(og_chips, 3)
    for i in range(cols):
        og_parts[i] = og_sum[:, i * width : (i + 1) * width]
    og_to_cols = to_cols(lambda d: og_parts.at[d], og_cols, col_send.at[1], col_recv.at[1], cols)
    start_all(og_to_cols)
    og_cols[c] = og_parts[c]
    wait_all(qg_to_chips)
    q_sum = qg_cut[chip, core].astype(F32) + qg_sib[chip].astype(F32) + all_sum(qg_chips, 3)
    for i in range(3):
        q_parts[i] = q_sum[:, i * width : (i + 1) * width]
    odd, high = c % 2, c // 2
    q_copies = [
        send_to(
            q_parts.at[1 - odd + high],
            q_land.at[1],
            col_send.at[2, 0],
            col_recv.at[2, 0],
            (r, flip(c, 1)),
        ),
        send_to(
            q_parts.at[2 - 2 * high],
            q_land.at[2 - 2 * odd],
            col_send.at[2, 1],
            col_recv.at[2, 1],
            (r, flip(c, 2)),
        ),
    ]
    start_all(q_copies)
    q_land[2 * odd] = q_parts[(c + 1) // 2]
    wait_all(small_to_cols)
    small_all[r] = all_sum(small_cols, cols)
    small_back = to_rows(lambda d: small_all.at[r], small_all, row_send.at[1], row_recv.at[1], ranks)
    start_all(small_back)

    def end_sends(i, carry):
        wait_all(h_sends(i))
        return carry

    lax.fori_loop(0, rest, end_sends, 0)
    sum_grads(first, first + rest, hin_ref, first)
    wait_all(og_to_cols + q_copies + small_back)
    og_out[...] = all_sum(og_cols, cols)
    for i in range(3):
        qg_out[:, i * width : (i + 1) * width] = q_land[i]
    stored = moves([(g_s.at[i], ref) for i, ref in enumerate((gg_ref, ug_ref, dg_ref))], store_sem)
    start_all(stored)
    for i in range(ranks):
        small_out[:, i * LANES : (i + 1) * LANES] = small_all[i]
    slot(3)
    total(total_s)
    gn = total_s[...]
    x = xown_ref[...].astype(F32)
    scale = norm_rows(x)
    gained = gn * again
    x_dot = jnp.sum(gained * x, axis=1, keepdims=True)
    ig_ref[...] = resid_s[...] + scale * gained - x * (scale * scale * scale * (x_dot * (1.0 / D)))
    wait_all(stored)
    drain()


def finish_step(cols, ranks, gm, meta, lse, small, og, xown, rw, qkv, o, x, w, cosine, sines, resid, gown, sib, hsoon, hin0, hrest):
    rows = meta.shape[0]
    local = rows // cols
    experts, three, chips, depth, ff = gown.shape
    rest = hrest.shape[0]
    heads, width = 3, 3 * HEAD_DIM
    vm = pl.BlockSpec(memory_space=pltpu.VMEM)
    dma = pltpu.SemaphoreType.DMA
    wide = D + 2 * LANES
    weight_grad = jax.ShapeDtypeStruct((experts, depth, ff), BF)
    return pl.pallas_call(
        functools.partial(finish_kernel, cols, ranks),
        out_shape=(
            jax.ShapeDtypeStruct((local, D), F32),
            jax.ShapeDtypeStruct((SMALL_ROWS, wide), F32),
            jax.ShapeDtypeStruct((depth, 3 * width), F32),
            jax.ShapeDtypeStruct((depth, width), F32),
            weight_grad,
            weight_grad,
            weight_grad,
            jax.ShapeDtypeStruct((rest, 3, three, depth, ff), BF),
        ),
        in_specs=[vm] * 7 + [ANY] * 12,
        out_specs=(vm,) * 4 + (ANY,) * 4,
        scratch_shapes=[
            pltpu.VMEM((3 * heads, rows, HEAD_DIM), BF),
            pltpu.VMEM((heads, rows, HEAD_DIM), BF),
            pltpu.VMEM((cols, local, D), BF),
            pltpu.VMEM((D, 3 * width), BF),
            pltpu.VMEM((rows, LANES), F32),
            pltpu.VMEM((rows, LANES), F32),
            pltpu.VMEM((local, D), F32),
            dma((heads, 4)),
            dma((5,)),
            pltpu.VMEM((heads, rows, HEAD_DIM), BF),
            pltpu.VMEM((heads, rows, HEAD_DIM), F32),
            pltpu.VMEM((heads, rows, HEAD_DIM), F32),
            pltpu.VMEM((heads, rows, HEAD_DIM), F32),
            pltpu.VMEM((cols, local, D), BF),
            pltpu.VMEM((D, 3 * width), F32),
            pltpu.VMEM((chips, 2, depth, 3 * width), BF),
            *chain_scratch(cols, local),
            pltpu.VMEM((ranks, SMALL_ROWS, LANES), F32),
            pltpu.VMEM((ranks, SMALL_ROWS, LANES), F32),
            pltpu.VMEM((cols, SMALL_ROWS, LANES), F32),
            pltpu.VMEM((ranks, SMALL_ROWS, LANES), F32),
            pltpu.VMEM((3, depth, D), BF),
            pltpu.VMEM((cols, depth, width), F32),
            pltpu.VMEM((cols, depth, width), F32),
            pltpu.VMEM((chips, depth, 3 * width), BF),
            pltpu.VMEM((chips, depth, 3 * width), BF),
            pltpu.VMEM((3, depth, 3 * width), BF),
            pltpu.VMEM((3, depth, width), F32),
            pltpu.VMEM((3, depth, width), F32),
            pltpu.VMEM((local, D), F32),
            pltpu.VMEM((2, 5, three, depth, ff), BF),
            dma((2, 3)),
            dma((2, ranks - 1)),
            dma((2, ranks - 1)),
            dma((2, 3)),
            dma((2, 3)),
            dma((1,)),
            dma((1,)),
            dma((3, cols - 1)),
            dma((3, cols - 1)),
            dma((rest, 3)),
            dma((rest, 3)),
            pltpu.VMEM((three, experts, depth, ff), BF),
            dma((3,)),
        ],
        compiler_params=pltpu.CompilerParams(
            vmem_limit_bytes=62 * MIB, collective_id=4, has_side_effects=True
        ),
        cost_estimate=pl.CostEstimate(
            flops=20 * heads * rows * rows * HEAD_DIM, bytes_accessed=40 * MIB, transcendentals=heads * rows * rows
        ),
        name="finish_step",
    )(gm, meta, lse, small, og, xown, rw, qkv, o, x, w, cosine, sines, resid, gown, sib, hsoon, hin0, hrest)


def place_kernel(*refs):
    ins, refs = refs[:9], refs[9:]
    outs, refs = refs[:14], refs[14:]
    held, refs = refs[:9], refs[9:]
    made, (load_sem, store_sem) = refs[:8], refs[8:]
    loads = moves(list(zip(ins, held)), load_sem)
    start_all(loads)
    small, qg, og, pg, layer, ig, *low = held
    full, again, out, fgain, router, carry, const, vector = made
    sources = [layer, ig, full.at[0], full.at[1], full.at[2], again, qg, out, fgain, router, carry, const, vector, pg]
    stores = moves(list(zip(sources, outs)), store_sem)
    for load, store in ((4, 0), (5, 1), (1, 6), (3, 13)):
        loads[load].wait()
        stores[store].start()
    for i in range(3):
        loads[6 + i].wait()
        full[i] = low[i][...].astype(F32)
        stores[2 + i].start()
    loads[2].wait()
    out[...] = og[...].T
    loads[0].wait()
    again[...] = small[ROW_GAIN + 1 : ROW_GAIN + 2, :D].reshape(D)
    fgain[...] = small[ROW_GAIN : ROW_GAIN + 1, :D].reshape(D)
    router[...] = small[:ROUTES, :D]
    carry[...] = small[:ROUTES, D : D + ROUTES]
    for j in range(2):
        const[j] = small[ROW_CONST + 2 * j : ROW_CONST + 2 * j + 2, :D]
    vector[...] = small[ROW_VEC : ROW_VEC + 2, :D]
    for i in (5, 7, 8, 9, 10, 11, 12):
        stores[i].start()
    wait_all(stores)


def place_outputs(*values):
    small, qg, og, pg, layer, ig, gg, ug, dg = values
    made = [(D,), og.shape[::-1], (D,), (ROUTES, D), (ROUTES, ROUTES), (2, 2, D), (2, D)]
    shapes = [layer.shape, ig.shape, gg.shape, ug.shape, dg.shape]
    shapes += [made[0], qg.shape, *made[1:], pg.shape]
    return pl.pallas_call(
        place_kernel,
        out_shape=[jax.ShapeDtypeStruct(shape, F32 if i else BF) for i, shape in enumerate(shapes)],
        in_specs=[ANY] * 9,
        out_specs=[ANY] * 14,
        scratch_shapes=[pltpu.VMEM(value.shape, value.dtype) for value in values]
        + [pltpu.VMEM((3, *gg.shape), F32)]
        + [pltpu.VMEM(shape, F32) for shape in made]
        + [pltpu.SemaphoreType.DMA((9,)), pltpu.SemaphoreType.DMA((14,))],
        compiler_params=pltpu.CompilerParams(vmem_limit_bytes=60 * MIB),
        cost_estimate=pl.CostEstimate(flops=0, bytes_accessed=16 * MIB, transcendentals=0),
        name="place_outputs",
    )(*values)


def on_device_heads(
    sizes,
    inputs,
    attn_gain,
    qkv_weight,
    out_weight,
    ffn_gain,
    router_weight,
    carry_weight,
    const_weight,
    const_vector,
    gate_weight,
    up_weight,
    down_weight,
    prev_logits,
    seq_lengths,
    expert_routes,
    cotangent,
):
    ranks, cols = sizes
    row_total = expert_routes.shape[0]
    depth = qkv_weight.shape[0]

    (
        w_all,
        qkv,
        mixed_heads,
        lse,
        whole_in,
        qkv_own,
        out_t,
        cosine,
        sines,
        meta,
        slots,
        mixed,
        middle,
        n2_whole,
        prev_whole,
        cot_early,
        rw,
        carry,
    ) = first_step(
        cols,
        ranks,
        inputs,
        cotangent,
        router_weight.T,
        const_weight.transpose(0, 2, 1),
        const_vector,
        attn_gain,
        ffn_gain,
        carry_weight,
        qkv_weight,
        out_weight,
        prev_logits,
        expert_routes.T,
        seq_lengths,
        gate_weight,
        up_weight,
        down_weight.transpose(0, 2, 1),
    )
    x, gu, y, gates, cot_late = experts_forward(
        cols, n2_whole.reshape(row_total, D), prev_whole, cotangent, rw, carry, meta, slots, w_all
    )
    dx, dots, mixsum, gown, sib, hsoon, glast = experts_backward(
        cols, ranks, cot_early, cot_late, y, gates, meta, slots, w_all, x, gu
    )
    layer_out, resid, gm, og, small, prev_grad, hin0, hrest, sib = resid_step(
        cols, dx, meta, dots, rw, prev_whole, carry, cotangent, mixsum, n2_whole, middle, out_t, mixed, gown, glast, sib
    )
    input_grad, small_all, qkv_grad, og_own, gate_grad, up_grad, down_grad, _ = finish_step(
        cols,
        ranks,
        gm,
        meta,
        lse,
        small,
        og,
        inputs,
        rw,
        qkv,
        mixed_heads,
        whole_in,
        qkv_own,
        cosine,
        sines,
        resid,
        gown,
        sib,
        hsoon,
        hin0,
        hrest,
    )
    layer_out, input_grad, gate_grad, up_grad, down_grad, again, qkv_grad, out_grad, fgain, router, carry, const, vector, prev = (
        place_outputs(small_all, qkv_grad, og_own, prev_grad, layer_out, input_grad, gate_grad, up_grad, down_grad)
    )
    return (
        layer_out,
        input_grad,
        again,
        qkv_grad,
        out_grad,
        fgain,
        router.T,
        carry,
        const.transpose(0, 2, 1),
        vector,
        gate_grad,
        up_grad,
        down_grad.transpose(0, 2, 1),
        prev,
    )


def solution(mesh):
    sizes = (mesh.shape["row"], mesh.shape["col"])
    body = functools.partial(on_device_heads, sizes) if sizes == (8, 4) else on_device
    placed = (
        P(("row", "col"), None),
        P(),
        P("row", "col"),
        P("col", "row"),
        P(),
        P(),
        P(),
        P(),
        P(),
        P(None, "row", "col"),
        P(None, "row", "col"),
        P(None, "col", "row"),
        P(None, ("row", "col")),
        P("row", None),
        P("row", None),
        P(("row", "col"), None),
    )
    return jax.shard_map(
        body,
        mesh=mesh,
        in_specs=placed,
        out_specs=(
            P(("row", "col"), None),
            P(("row", "col"), None),
            P(),
            P("row", "col"),
            P("col", "row"),
            P(),
            P(),
            P(),
            P(),
            P(),
            P(None, "row", "col"),
            P(None, "row", "col"),
            P(None, "col", "row"),
            P(None, ("row", "col")),
        ),
        check_vma=False,
    )
```

```python
import functools
import math

import jax
import jax.numpy as jnp
import numpy as np
from jax import lax
from jax.experimental import pallas as pl
from jax.experimental.pallas import tpu as pltpu
from jax.sharding import PartitionSpec as P

D = 768
HEADS = 12
HEAD_DIM = 64
EXPERTS = 8
ROUTES = 12


EPS = 1e-06
BASE = 10000.0
NEG = -1e30
HIGH = lax.Precision.HIGHEST
CONTRACT_FIRST = (((0,), (0,)), ((), ()))
CONTRACT_LAST = (((1,), (1,)), ((), ()))


def rotate(block_value, positions, first_col, direction):
    row_count, col_count = block_value.shape
    column = first_col + jnp.arange(0, col_count, 2, dtype=jnp.int32)
    inner_col = column % D
    section = column // D
    head_pair = inner_col % HEAD_DIM // 2
    exponent = (2 * head_pair).astype(jnp.float32) / HEAD_DIM
    frequency = jnp.exp(-exponent * math.log(BASE))
    turned_on = (section < 2).astype(jnp.float32)
    angles = positions.astype(jnp.float32)[:, None] * (frequency * turned_on)[None, :]
    cosine = jnp.cos(angles)
    sines = direction * jnp.sin(angles)
    paired = block_value.reshape(row_count, col_count // 2, 2)
    first_part = paired[:, :, 0]
    second_part = paired[:, :, 1]
    rotated = jnp.stack(
        [first_part * cosine - second_part * sines, second_part * cosine + first_part * sines],
        axis=2,
    )
    return rotated.reshape(row_count, col_count)


def sequence_info(lengths_row, row_total):
    seq_count = lengths_row.shape[0]
    ends = jnp.cumsum(lengths_row)
    starts = ends - lengths_row
    token_place = jnp.arange(row_total, dtype=jnp.int32)
    seq_index = jnp.sum((token_place[:, None] >= ends[None, :]).astype(jnp.int32), axis=1)
    member = seq_index[:, None] == jnp.arange(seq_count, dtype=jnp.int32)[None, :]
    begin = jnp.sum(jnp.where(member, starts[None, :], 0), axis=1)
    return (seq_index, token_place - begin, seq_index < seq_count)


def partial_sums(term_value):
    return lax.psum_scatter(
        term_value.astype(jnp.bfloat16), "col", scatter_dimension=0, tiled=True
    ).astype(jnp.float32)


def whole_columns(part_value):
    return lax.all_gather(part_value, "col", axis=0, tiled=True)


def to_heads(block_value):
    return lax.all_to_all(block_value, "col", split_axis=0, concat_axis=1, tiled=True)


def to_features(block_value):
    return lax.all_to_all(block_value, "col", split_axis=1, concat_axis=0, tiled=True)


def key_scores(query_heads, key_block, query_seq, query_place, key_seq, key_place, score_scale):
    raw_scores = (
        jnp.einsum("qhd,khd->hqk", query_heads, key_block, preferred_element_type=jnp.float32)
        * score_scale
    )
    allowed = (query_seq[:, None] == key_seq[None, :]) & (
        key_place[None, :] <= query_place[:, None]
    )
    return (jnp.where(allowed[None], raw_scores, NEG), allowed)


def split_keys(key_values, seq_index, token_place, block_rows):
    count_blocks = key_values.shape[0] // block_rows
    blocks_kv = key_values.reshape(count_blocks, block_rows, 2, HEADS, HEAD_DIM)
    return (
        blocks_kv,
        seq_index.reshape(count_blocks, block_rows),
        token_place.reshape(count_blocks, block_rows),
    )


def attend_forward(
    queries, key_values, query_seq, query_place, seq_index, token_place, block_rows, score_scale
):
    local_rows = queries.shape[0]
    query_heads = queries.reshape(local_rows, HEADS, HEAD_DIM)
    key_items = split_keys(key_values, seq_index, token_place, block_rows)

    def max_step(running, block_items):
        running_max, running_sum = running
        kv_block, key_seq, key_place = block_items
        scores, allowed = key_scores(
            query_heads, kv_block[:, 0], query_seq, query_place, key_seq, key_place, score_scale
        )
        new_max = jnp.maximum(running_max, jnp.max(scores, axis=2))
        shifted = jnp.where(allowed[None], jnp.exp(scores - new_max[:, :, None]), 0.0)
        new_sum = running_sum * jnp.exp(running_max - new_max) + jnp.sum(shifted, axis=2)
        return ((new_max, new_sum), None)

    start_state = (
        jnp.full((HEADS, local_rows), NEG, jnp.float32),
        jnp.zeros((HEADS, local_rows), jnp.float32),
    )
    (final_max, final_sum), unused = lax.scan(max_step, start_state, key_items)
    log_total = final_max + jnp.log(final_sum)

    def out_step(running, block_items):
        kv_block, key_seq, key_place = block_items
        scores, allowed = key_scores(
            query_heads, kv_block[:, 0], query_seq, query_place, key_seq, key_place, score_scale
        )
        probs_low = jnp.exp(scores - log_total[:, :, None]).astype(jnp.bfloat16)
        return (
            running
            + jnp.einsum(
                "hqk,khd->qhd", probs_low, kv_block[:, 1], preferred_element_type=jnp.float32
            ),
            None,
        )

    attended, unused = lax.scan(
        out_step, jnp.zeros((local_rows, HEADS, HEAD_DIM), jnp.float32), key_items
    )
    return (attended.reshape(local_rows, D), log_total)


def attend_backward(
    queries,
    key_values,
    log_total,
    row_delta,
    grad_heads_in,
    query_seq,
    query_place,
    seq_index,
    token_place,
    block_rows,
    score_scale,
):
    local_rows = queries.shape[0]
    query_heads = queries.reshape(local_rows, HEADS, HEAD_DIM)
    grad_heads = grad_heads_in.reshape(local_rows, HEADS, HEAD_DIM)
    key_items = split_keys(key_values, seq_index, token_place, block_rows)

    def grad_step(running, block_items):
        kv_block, key_seq, key_place = block_items
        scores, allowed = key_scores(
            query_heads, kv_block[:, 0], query_seq, query_place, key_seq, key_place, score_scale
        )
        probs_full = jnp.exp(scores - log_total[:, :, None])
        probs_low = probs_full.astype(jnp.bfloat16)
        grad_probs = jnp.einsum(
            "qhd,khd->hqk", grad_heads, kv_block[:, 1], preferred_element_type=jnp.float32
        )
        grad_scores = (probs_full * (grad_probs - row_delta[:, :, None])).astype(jnp.bfloat16)
        new_running = (
            running
            + jnp.einsum(
                "hqk,khd->qhd", grad_scores, kv_block[:, 0], preferred_element_type=jnp.float32
            )
            * score_scale
        )
        grad_keys = (
            jnp.einsum("hqk,qhd->khd", grad_scores, query_heads, preferred_element_type=jnp.float32)
            * score_scale
        )
        grad_values = jnp.einsum(
            "hqk,qhd->khd", probs_low, grad_heads, preferred_element_type=jnp.float32
        )
        return (new_running, jnp.stack([grad_keys, grad_values], axis=1))

    grad_queries, grad_kv = lax.scan(
        grad_step, jnp.zeros((local_rows, HEADS, HEAD_DIM), jnp.float32), key_items
    )
    return (grad_queries.reshape(local_rows, D), grad_kv.reshape(key_values.shape[0], 2 * D))


def on_device(
    inputs,
    attn_gain,
    qkv_weight,
    out_weight,
    ffn_gain,
    router_weight,
    carry_weight,
    const_weight,
    const_vector,
    gate_weight,
    up_weight,
    down_weight,
    prev_logits,
    seq_lengths,
    expert_routes,
    cotangent,
):
    col_index = lax.axis_index("col")
    row_total = expert_routes.shape[0]
    local_rows = inputs.shape[0]
    capacity = row_total // 4
    block_rows = min(row_total, 512)
    score_scale = 1.0 / math.sqrt(HEAD_DIM)
    full_weights = (
        lax.all_gather(qkv_weight, "row", axis=0, tiled=True),
        lax.all_gather(out_weight, "row", axis=1, tiled=True),
        lax.all_gather(gate_weight, "row", axis=1, tiled=True),
        lax.all_gather(up_weight, "row", axis=1, tiled=True),
        lax.all_gather(down_weight, "row", axis=2, tiled=True),
    )
    qkv_full, out_full, gate_full, up_full, down_full = full_weights
    whole_in, whole_cot, whole_prev = (
        lax.all_gather(inputs, "col", axis=0, tiled=True),
        lax.all_gather(cotangent, "col", axis=0, tiled=True),
        lax.all_gather(prev_logits, "col", axis=1, tiled=True),
    )
    seq_index, positions, valid_all = sequence_info(seq_lengths[0], row_total)
    token_place = jnp.arange(row_total, dtype=jnp.int32)
    first_row = col_index * local_rows

    def own_rows(whole_value):
        return lax.dynamic_slice_in_dim(whole_value, first_row, local_rows, 0)

    query_seq = own_rows(seq_index)
    query_place = own_rows(token_place)
    query_pos = own_rows(positions)
    query_valid = own_rows(valid_all).astype(jnp.float32)[:, None]
    input_rows = whole_in.astype(jnp.float32)
    attn_gain_full = attn_gain.astype(jnp.float32)
    scale_attn = lax.rsqrt(jnp.mean(input_rows * input_rows, axis=1, keepdims=True) + EPS)
    normed1 = (input_rows * scale_attn * attn_gain_full).astype(jnp.bfloat16)
    projected = jnp.dot(normed1, qkv_full, preferred_element_type=jnp.float32)
    turned = rotate(projected, positions, col_index * projected.shape[1], 1.0).astype(jnp.bfloat16)
    token_qkv = to_heads(turned)
    queries = token_qkv[:, :D]
    key_values = lax.all_gather(token_qkv[:, D:], "col", axis=0, tiled=True)
    attended, log_total = attend_forward(
        queries, key_values, query_seq, query_place, seq_index, token_place, block_rows, score_scale
    )
    attn_tok = (attended * query_valid).astype(jnp.bfloat16)
    attn_feat = to_features(attn_tok)
    attn_out = partial_sums(jnp.dot(attn_feat, out_full, preferred_element_type=jnp.float32))
    input_local = inputs.astype(jnp.float32)
    middle = input_local + attn_out
    scale_ffn = lax.rsqrt(jnp.mean(middle * middle, axis=1, keepdims=True) + EPS)
    ffn_gain_full = ffn_gain.astype(jnp.float32)
    normed2_local = (middle * scale_ffn * ffn_gain_full).astype(jnp.bfloat16)
    normed2 = whole_columns(normed2_local)
    carry_full = carry_weight.astype(jnp.float32)
    prev_rows = whole_prev.astype(jnp.float32).T
    route_hot = (
        expert_routes[:, :, None] == jnp.arange(ROUTES, dtype=jnp.int32)[None, None, :]
    ).astype(jnp.float32)
    logits = jnp.dot(normed2, router_weight, preferred_element_type=jnp.float32) + jnp.dot(
        prev_rows, carry_full, precision=HIGH
    )
    picked = jnp.sum(route_hot * logits[:, None, :], axis=2)
    gate_values = jax.nn.softmax(picked, axis=1)
    flat_route = expert_routes.reshape(-1)
    route_hits = (flat_route[:, None] == jnp.arange(EXPERTS, dtype=jnp.int32)[None, :]).astype(
        jnp.int32
    )
    slot_index = jnp.sum((jnp.cumsum(route_hits, axis=0) - 1) * route_hits, axis=1)
    dump_slot = EXPERTS * capacity
    target = jnp.where(flat_route < EXPERTS, flat_route * capacity + slot_index, dump_slot)
    slot_owner = (
        jnp.full((dump_slot + 1,), row_total, jnp.int32)
        .at[target]
        .set(jnp.arange(2 * row_total, dtype=jnp.int32) // 2)[:dump_slot]
    )
    slot_gate = (
        jnp.zeros((dump_slot + 1,), jnp.float32)
        .at[target]
        .set(gate_values.reshape(-1))[:dump_slot]
        .reshape(EXPERTS, capacity, 1)
    )
    zero_row = jnp.zeros((1, D), jnp.bfloat16)
    expert_in = jnp.concatenate([normed2, zero_row], axis=0)[slot_owner].reshape(
        EXPERTS, capacity, D
    )
    gate_pre = jnp.einsum("ecd,edf->ecf", expert_in, gate_full, preferred_element_type=jnp.float32)
    up_pre = jnp.einsum("ecd,edf->ecf", expert_in, up_full, preferred_element_type=jnp.float32)
    sigmoid_gate = jax.nn.sigmoid(gate_pre)
    activated = gate_pre * sigmoid_gate
    hidden = (activated * up_pre).astype(jnp.bfloat16)
    expert_out = jnp.einsum("ecf,efd->ecd", hidden, down_full, preferred_element_type=jnp.float32)
    out_rows = jnp.concatenate(
        [expert_out.reshape(dump_slot, D), jnp.zeros((1, D), jnp.float32)], axis=0
    )
    chosen_out = out_rows[target].reshape(row_total, 2, D)
    cot_rows = whole_cot.astype(jnp.float32)
    ffn_mix = jnp.sum(gate_values[:, :, None] * chosen_out, axis=1)
    ffn_dots = jnp.sum(cot_rows[:, None, :] * chosen_out, axis=2)
    mix_local = partial_sums(ffn_mix)
    normed_local = normed2_local.astype(jnp.float32)
    vector_full = const_vector.astype(jnp.float32)
    routes_local = own_rows(expert_routes)
    gates_local = own_rows(gate_values)
    hot_local = own_rows(route_hot)
    copy_hit = (routes_local == EXPERTS + 1).astype(jnp.float32)
    const_hit = (
        routes_local[:, :, None] == (EXPERTS + 2 + jnp.arange(2, dtype=jnp.int32))[None, None, :]
    ).astype(jnp.float32)
    copy_share = jnp.sum(gates_local * copy_hit, axis=1)
    const_share = jnp.sum(gates_local[:, :, None] * const_hit, axis=1)
    const_alpha = jax.nn.softmax(
        jnp.einsum("td,jdk->tjk", normed2_local, const_weight, preferred_element_type=jnp.float32),
        axis=2,
    )
    keep_share = copy_share + jnp.sum(const_share * const_alpha[:, :, 0], axis=1)
    local_mix = keep_share[:, None] * normed_local + jnp.dot(
        const_share * const_alpha[:, :, 1], vector_full, precision=HIGH
    )
    layer_out = (middle + mix_local + local_mix).astype(jnp.bfloat16)
    qkv_full, out_full, gate_full, up_full, down_full = full_weights
    ffn_total = lax.psum(ffn_dots, "col")
    ffn_local = own_rows(ffn_total)
    cot_local = cotangent.astype(jnp.float32)
    dot_keep = jnp.sum(cot_local * normed_local, axis=1)
    dot_vector = jnp.dot(cot_local, vector_full.T, precision=HIGH)
    const_dots = const_alpha[:, :, 0] * dot_keep[:, None] + const_alpha[:, :, 1] * dot_vector
    grad_gates = (
        ffn_local
        + copy_hit * dot_keep[:, None]
        + jnp.sum(const_hit * const_dots[:, None, :], axis=2)
    )
    grad_picked = gates_local * (
        grad_gates - jnp.sum(gates_local * grad_gates, axis=1, keepdims=True)
    )
    grad_logits = jnp.sum(hot_local * grad_picked[:, :, None], axis=1)
    prev_local = prev_logits.astype(jnp.float32).T
    router_grad = lax.dot_general(normed_local, grad_logits, CONTRACT_FIRST, precision=HIGH)
    carry_grad = lax.dot_general(prev_local, grad_logits, CONTRACT_FIRST, precision=HIGH)
    prev_grad = lax.dot_general(carry_full, grad_logits, CONTRACT_LAST, precision=HIGH)
    grad_alpha_keep = const_share * dot_keep[:, None]
    grad_alpha_vector = const_share * dot_vector
    alpha_mean = const_alpha[:, :, 0] * grad_alpha_keep + const_alpha[:, :, 1] * grad_alpha_vector
    grad_alpha_logits = jnp.stack(
        [
            const_alpha[:, :, 0] * (grad_alpha_keep - alpha_mean),
            const_alpha[:, :, 1] * (grad_alpha_vector - alpha_mean),
        ],
        axis=2,
    )
    const_grad = jnp.einsum("td,tjk->jdk", normed_local, grad_alpha_logits, precision=HIGH)
    vector_grad = lax.dot_general(
        const_share * const_alpha[:, :, 1], cot_local, CONTRACT_FIRST, precision=HIGH
    )
    router_full = router_weight.astype(jnp.float32)
    const_full = const_weight.astype(jnp.float32)
    grad_normed_local = (
        keep_share[:, None] * cot_local
        + lax.dot_general(grad_logits, router_full, CONTRACT_LAST, precision=HIGH)
        + jnp.einsum("tjk,jdk->td", grad_alpha_logits, const_full, precision=HIGH)
    )
    cot_in = jnp.concatenate([whole_cot, zero_row], axis=0)[slot_owner].reshape(
        EXPERTS, capacity, D
    )
    grad_expert = (slot_gate * cot_in.astype(jnp.float32)).astype(jnp.bfloat16)
    down_grad = jnp.einsum("ecf,ecd->efd", hidden, grad_expert, preferred_element_type=jnp.float32)
    grad_hidden = jnp.einsum(
        "ecd,efd->ecf", grad_expert, down_full, preferred_element_type=jnp.float32
    )
    grad_gate_pre = (
        grad_hidden * up_pre * sigmoid_gate * (1.0 + gate_pre * (1.0 - sigmoid_gate))
    ).astype(jnp.bfloat16)
    grad_up_pre = (grad_hidden * activated).astype(jnp.bfloat16)
    gate_grad = jnp.einsum(
        "ecd,ecf->edf", expert_in, grad_gate_pre, preferred_element_type=jnp.float32
    )
    up_grad = jnp.einsum("ecd,ecf->edf", expert_in, grad_up_pre, preferred_element_type=jnp.float32)
    grad_expert_in = jnp.einsum(
        "ecf,edf->ecd", grad_gate_pre, gate_full, preferred_element_type=jnp.float32
    ) + jnp.einsum("ecf,edf->ecd", grad_up_pre, up_full, preferred_element_type=jnp.float32)
    grad_slots = jnp.concatenate(
        [grad_expert_in.reshape(dump_slot, D), jnp.zeros((1, D), jnp.float32)], axis=0
    )
    grad_tokens = jnp.sum(grad_slots[target].reshape(row_total, 2, D), axis=1)
    grad_normed = partial_sums(grad_tokens) + grad_normed_local
    gained_ffn = grad_normed * ffn_gain_full
    ffn_dots_rows = jnp.sum(gained_ffn * middle, axis=1, keepdims=True)
    grad_middle = scale_ffn * gained_ffn - middle * scale_ffn**3 * (ffn_dots_rows / D)
    ffn_gain_grad = jnp.sum(grad_normed * middle * scale_ffn, axis=0)
    grad_resid = cot_local + grad_middle
    branch_cot = whole_columns(grad_resid.astype(jnp.bfloat16))
    out_grad = lax.dot_general(
        attn_feat, branch_cot, CONTRACT_FIRST, preferred_element_type=jnp.float32
    )
    grad_mixed = lax.dot_general(
        branch_cot, out_full, CONTRACT_LAST, preferred_element_type=jnp.float32
    )
    grad_tok = to_heads(grad_mixed.astype(jnp.bfloat16))
    grad_heads_in = (grad_tok.astype(jnp.float32) * query_valid).astype(jnp.bfloat16)
    row_delta = jnp.sum(
        grad_heads_in.astype(jnp.float32).reshape(local_rows, HEADS, HEAD_DIM)
        * attended.reshape(local_rows, HEADS, HEAD_DIM),
        axis=2,
    ).T
    grad_queries, grad_kv = attend_backward(
        queries,
        key_values,
        log_total,
        row_delta,
        grad_heads_in,
        query_seq,
        query_place,
        seq_index,
        token_place,
        block_rows,
        score_scale,
    )
    grad_kv_local = lax.psum_scatter(
        grad_kv.astype(jnp.bfloat16), "col", scatter_dimension=0, tiled=True
    ).astype(jnp.float32)
    grad_turned = jnp.concatenate([grad_queries, grad_kv_local], axis=1)
    grad_proj_tok = rotate(grad_turned, query_pos, 0, -1.0).astype(jnp.bfloat16)
    grad_projected = to_features(grad_proj_tok)
    qkv_grad = lax.dot_general(
        normed1, grad_projected, CONTRACT_FIRST, preferred_element_type=jnp.float32
    )
    grad_normed1 = partial_sums(
        lax.dot_general(grad_projected, qkv_full, CONTRACT_LAST, preferred_element_type=jnp.float32)
    )
    scale_attn_local = own_rows(scale_attn)
    gained_attn = grad_normed1 * attn_gain_full
    attn_dots_rows = jnp.sum(gained_attn * input_local, axis=1, keepdims=True)
    input_grad = (
        grad_resid
        + scale_attn_local * gained_attn
        - input_local * scale_attn_local**3 * (attn_dots_rows / D)
    )
    attn_gain_grad = jnp.sum(grad_normed1 * input_local * scale_attn_local, axis=0)
    qkv_grad, out_grad, gate_grad, up_grad, down_grad = (
        lax.psum_scatter(
            qkv_grad.astype(jnp.bfloat16), "row", scatter_dimension=0, tiled=True
        ).astype(jnp.float32),
        lax.psum_scatter(
            out_grad.astype(jnp.bfloat16), "row", scatter_dimension=1, tiled=True
        ).astype(jnp.float32),
        lax.psum_scatter(
            gate_grad.astype(jnp.bfloat16), "row", scatter_dimension=1, tiled=True
        ).astype(jnp.float32),
        lax.psum_scatter(
            up_grad.astype(jnp.bfloat16), "row", scatter_dimension=1, tiled=True
        ).astype(jnp.float32),
        lax.psum_scatter(
            down_grad.astype(jnp.bfloat16), "row", scatter_dimension=2, tiled=True
        ).astype(jnp.float32),
    )
    attn_gain_grad, ffn_gain_grad, router_grad, carry_grad, const_grad, vector_grad = lax.psum(
        (attn_gain_grad, ffn_gain_grad, router_grad, carry_grad, const_grad, vector_grad),
        ("row", "col"),
    )
    return (
        layer_out,
        input_grad,
        attn_gain_grad,
        qkv_grad,
        out_grad,
        ffn_gain_grad,
        router_grad,
        carry_grad,
        const_grad,
        vector_grad,
        gate_grad,
        up_grad,
        down_grad,
        prev_grad,
    )


BF = jnp.bfloat16
F32 = jnp.float32
LANES = 128
NN = (((1,), (0,)), ((), ()))
NT = (((1,), (1,)), ((), ()))
TN = (((0,), (0,)), ((), ()))
ROW_CONST = 12
ROW_VEC = 16
ROW_GAIN = 18
SMALL_ROWS = 24
Q_ROWS = 256
MIB = 1 << 20


def mm(a, b, dims=NN):
    return lax.dot_general(a, b, dims, preferred_element_type=F32)


def lane_iota(shape):
    return lax.broadcasted_iota(jnp.int32, shape, len(shape) - 1)


def whole(shape):
    return pl.BlockSpec(tuple(shape), lambda *_: (0,) * len(shape), pipeline_mode=pl.Buffered(1))


def swap_pairs(v):
    even = lane_iota(v.shape) % 2 == 0
    return jnp.where(even, pltpu.roll(v, LANES - 1, 1), pltpu.roll(v, 1, 1))


def norm_rows(x):
    return lax.rsqrt(jnp.mean(x * x, axis=1, keepdims=True) + EPS)


def seen(begin, first, rows, length):
    u = lax.broadcasted_iota(jnp.int32, (rows, length), 1)
    t = lax.broadcasted_iota(jnp.int32, (rows, length), 0) + first
    return (u >= begin) & (u <= t)


def gate_lanes(logits, meta):
    lane = lane_iota(logits.shape)
    hit = (pltpu.roll(meta, LANES - META_HIT, 1) > 0.0) & (lane < ROUTES)
    held = jnp.where(hit, logits, NEG)
    e = jnp.where(hit, jnp.exp(held - jnp.max(held, axis=1, keepdims=True)), 0.0)
    return e / jnp.sum(e, axis=1, keepdims=True)


MESH = pl.DeviceIdType.MESH
ANY = pl.BlockSpec(memory_space=pl.ANY)


def place():
    return lax.axis_index("row"), lax.axis_index("col")


def flip(index, mask):
    for bit in (1, 2, 4):
        if mask & bit:
            index = index + bit - 2 * bit * (index // bit % 2)
    return index


def greet(devices):
    barrier = pltpu.get_barrier_semaphore()
    for device in devices:
        pl.semaphore_signal(barrier, inc=1, device_id=device, device_id_type=MESH)
    pl.semaphore_wait(barrier, len(devices))


def send_to(src, dst, send, recv, device):
    return pltpu.make_async_remote_copy(
        src_ref=src, dst_ref=dst, send_sem=send, recv_sem=recv, device_id=device, device_id_type=MESH
    )


def col_peers(n):
    r, c = place()
    return [(r, (c + k) % n) for k in range(1, n)]


def gather_chain(own, dst, send, recv, n):
    r, c = place()

    def right(k):
        i = jnp.maximum(c - k, 0)
        src = own if k == 0 else dst.at[i]
        return send_to(src, dst.at[i], send.at[0, k], recv.at[0, k], (r, jnp.minimum(c + 1, n - 1)))

    def left(k):
        i = jnp.minimum(c + k, n - 1)
        src = own if k == 0 else dst.at[i]
        return send_to(src, dst.at[i], send.at[1, k], recv.at[1, k], (r, jnp.maximum(c - 1, 0)))

    def step(k):
        if k > 0:

            @pl.when(c >= k)
            def _():
                right(k - 1).wait_recv()

            @pl.when(c + k < n)
            def _():
                left(k - 1).wait_recv()

        if k < n - 1:

            @pl.when((c >= k) & (c + 1 < n))
            def _():
                right(k).start()

            @pl.when((c + k < n) & (c >= 1))
            def _():
                left(k).start()

    def drain():
        for k in range(n - 1):

            @pl.when((c >= k) & (c + 1 < n))
            def _():
                right(k).wait_send()

            @pl.when((c + k < n) & (c >= 1))
            def _():
                left(k).wait_send()

    return step, drain


def reduce_chain(own, out, arrived, send, recv, n):
    r, c = place()

    def right(k):
        return send_to(out.at[0, k], arrived.at[0, k], send.at[0, k], recv.at[0, k], (r, jnp.minimum(c + 1, n - 1)))

    def left(k):
        return send_to(out.at[1, k], arrived.at[1, k], send.at[1, k], recv.at[1, k], (r, jnp.maximum(c - 1, 0)))

    def slot(s):
        if s == n - 1:

            @pl.when(c >= 1)
            def _():
                right(n - 1 - c).wait_recv()

            @pl.when(c <= n - 2)
            def _():
                left(c).wait_recv()

            return

        @pl.when(c <= s)
        def _():
            k = jnp.maximum(s - c, 0)

            @pl.when(c >= 1)
            def _():
                right(k).wait_recv()
                out[0, k] = (own(n - 1 - k).astype(F32) + arrived[0, k].astype(F32)).astype(BF)

            @pl.when(c == 0)
            def _():
                out[0, k] = own(n - 1 - k).astype(BF)

            right(k).start()

        @pl.when(n - 1 - c <= s)
        def _():
            k = jnp.maximum(s - (n - 1 - c), 0)

            @pl.when(c <= n - 2)
            def _():
                left(k).wait_recv()
                out[1, k] = (own(k).astype(F32) + arrived[1, k].astype(F32)).astype(BF)

            @pl.when(c == n - 1)
            def _():
                out[1, k] = own(k).astype(BF)

            left(k).start()

    def total(dst):
        dst[...] = own(c).astype(F32)

        @pl.when(c >= 1)
        def _():
            dst[...] += arrived[0, n - 1 - c].astype(F32)

        @pl.when(c <= n - 2)
        def _():
            dst[...] += arrived[1, c].astype(F32)

    def drain():
        for k in range(n - 1):

            @pl.when(c < n - 1 - k)
            def _():
                right(k).wait_send()

            @pl.when(c > k)
            def _():
                left(k).wait_send()

    return slot, total, drain


def chain_scratch(n, rows):
    return [
        pltpu.VMEM((2, n - 1, rows, D), BF),
        pltpu.VMEM((2, n - 1, rows, D), BF),
        pltpu.SemaphoreType.DMA((2, n - 1)),
        pltpu.SemaphoreType.DMA((2, n - 1)),
    ]


def slot_rows(slots_ref, e, capacity):
    rows = slots_ref.shape[1]
    spots = lax.broadcasted_iota(jnp.int32, (capacity, rows), 0)
    return jnp.where(spots == slots_ref[pl.ds(e, 1)], 1.0, 0.0).astype(BF)


def slot_gates(one, gates_ref, e):
    sg = mm(one, gates_ref[...])
    return jnp.sum(jnp.where(lane_iota(sg.shape) % LANES == e, sg, 0.0), axis=1, keepdims=True)


def chain_order(c):
    return [d + (3 - 2 * d) * (c // 2) for d in (3, 2, 0, 1)]


def combine(meta_ref, y_ref, d, local):
    experts, capacity, width = y_ref.shape
    at = pl.ds(pl.multiple_of(d * local, LANES), local)
    lane = lane_iota((local, capacity)).astype(F32)
    ones = [jnp.where(lane == column(meta_ref, at, e), 1.0, 0.0).astype(BF) for e in range(experts)]
    return mm(jnp.concatenate(ones, axis=1), y_ref[...].reshape(experts * capacity, width)).astype(BF)


META_HIT, META_BEGIN, META_VALID = 8, 20, 21
EARLY = 6
SENT_SOON, SENT_NEXT = 2, 3


def column(ref, at, lane):
    return ref[at, lane : lane + 1]


def start_all(copies):
    for copy in copies:
        copy.start()


def wait_all(copies):
    for copy in copies:
        copy.wait()


def moves(pairs, sem):
    return [pltpu.make_async_copy(src, dst, sem.at[i]) for i, (src, dst) in enumerate(pairs)]


def pack_head(value):
    half = value.shape[0] // 2
    return jnp.concatenate([value[:half], value[half:]], axis=1)


def unpack_head(packed):
    return jnp.concatenate([packed[:, :HEAD_DIM], packed[:, HEAD_DIM:]], axis=0)


def to_rows(src_of, dst, send, recv, ranks):
    r, c = place()
    copies = []
    for m in range(1, ranks):
        there = flip(r, m)
        copies.append(send_to(src_of(there), dst.at[r], send.at[m - 1], recv.at[m - 1], (there, c)))
    return copies


def to_cols(src_of, dst, send, recv, n):
    r, c = place()
    copies = []
    for k in range(1, n):
        there = (c + k) % n
        copies.append(send_to(src_of(there), dst.at[c], send.at[k - 1], recv.at[k - 1], (r, there)))
    return copies


def to_chips(src_of, dst, send, recv):
    r, c = place()
    return [
        send_to(src_of(flip(r // 2, k)), dst.at[k - 1], send.at[k - 1], recv.at[k - 1], (flip(r, 2 * k), c))
        for k in range(1, 4)
    ]


def all_sum(ref, count):
    total = ref[0].astype(F32)
    for i in range(1, count):
        total = total + ref[i].astype(F32)
    return total


def tokens_meta(routes_ref, lengths_ref, rows, experts):
    kinds = lax.broadcasted_iota(jnp.int32, (16, rows), 0)
    hits = jnp.where((kinds == routes_ref[0:1]) | (kinds == routes_ref[1:2]), 1.0, 0.0)
    step = 256
    earlier = lax.broadcasted_iota(jnp.int32, (step, step), 0) < lax.broadcasted_iota(
        jnp.int32, (step, step), 1
    )
    earlier = jnp.where(earlier, 1.0, 0.0).astype(BF)
    counts, running = [], jnp.zeros((16, 1), F32)
    for b in range(rows // step):
        block = hits[:, b * step : (b + 1) * step]
        counts.append(mm(block.astype(BF), earlier) + running)
        running = running + jnp.sum(block, axis=1, keepdims=True)
    slots = jnp.where(hits > 0.0, jnp.concatenate(counts, axis=1), -1.0)[:experts]
    spot = lax.broadcasted_iota(jnp.int32, (8, rows), 1)
    begin, end = jnp.zeros((8, rows), F32), 0
    for i in range(lengths_ref.shape[1]):
        end = end + lengths_ref[0, i]
        begin = jnp.where(spot >= end, end.astype(F32), begin)
    valid = jnp.where(spot < end, 1.0, 0.0)
    tail = jnp.where(lax.broadcasted_iota(jnp.int32, (8, rows), 0) == 0, begin, valid)
    spare = jnp.zeros((LANES - experts - 12 - 8, rows), F32)
    meta = jnp.concatenate([slots, hits[:12], tail, spare], axis=0).T
    return slots.astype(jnp.int32), meta


def first_kernel(
    cols,
    ranks,
    x_ref,
    cot_ref,
    router_ref,
    const_ref,
    vector_ref,
    again_ref,
    fgain_ref,
    carry_ref,
    wq_ref,
    wo_ref,
    prev_ref,
    routes_ref,
    lengths_ref,
    cos_in,
    sin_in,
    freq_ref,
    gate_ref,
    up_ref,
    down_ref,
    wall_ref,
    qkv_out,
    o_out,
    lse_out,
    xw_out,
    wq_out,
    wo_out,
    cos_out,
    sin_out,
    meta_out,
    slots_ref,
    mixed_out,
    middle_out,
    n2w_ref,
    prevw_out,
    cota_ref,
    rw_out,
    carry_out,
    xw,
    q_parts,
    q_land,
    o_parts,
    o_land,
    wq,
    wo,
    a_send,
    a_land,
    prev_s,
    prevw,
    qkv_s,
    o_s,
    lse_s,
    cos_s,
    sin_s,
    meta_s,
    mixed_s,
    middle_s,
    n2_s,
    w_s,
    local_sem,
    x_send,
    x_recv,
    n_send,
    n_recv,
    t_send,
    t_recv,
    q_send,
    q_recv,
    c_send,
    c_recv,
    r_send,
    r_recv,
    e_send,
    e_recv,
    d_send,
    d_recv,
    s_send,
    s_recv,
    h_send,
    h_recv,
    cos_ref,
    sin_ref,
    soon_sem,
):
    r, c = place()
    heads = 3
    local = x_ref.shape[0]
    rows = local * cols
    width = heads * HEAD_DIM
    depth = D // ranks
    odd, high = c % 2, c // 2
    again = again_ref[...].astype(F32).reshape(1, D)
    fgain = fgain_ref[...].astype(F32).reshape(1, D)
    soon = moves([(cos_in, cos_ref), (sin_in, sin_ref)], soon_sem)
    start_all(soon)
    greet(col_peers(cols) + [(flip(r, m), c) for m in (1, 2, 4, 6)])

    for s in range(3):
        q_parts[s] = wq_ref[:, s * width : (s + 1) * width]
    q_copies = [
        send_to(q_parts.at[1], q_land.at[(c + 1) // 2], q_send.at[0], q_recv.at[0], (r, flip(c, 1))),
        send_to(q_parts.at[2 - 2 * odd], q_land.at[2 * high], q_send.at[1], q_recv.at[1], (r, flip(c, 2))),
    ]
    start_all(q_copies)
    x_step, x_drain = gather_chain(x_ref, xw, x_send, x_recv, cols)
    x_step(0)
    o_parts[...] = wo_ref[...].astype(F32).T.astype(BF)
    prev_s[...] = jnp.concatenate([prev_ref[...].astype(F32), jnp.zeros((16 - ROUTES, local), F32)], axis=0).astype(BF)
    o_copies = to_cols(lambda d: o_parts, o_land, c_send.at[0], c_recv.at[0], cols)
    prev_copies = to_cols(lambda d: prev_s, prevw, c_send.at[1], c_recv.at[1], cols)
    start_all(o_copies + prev_copies)
    q_land[(c + 1) // 2] = q_parts[2 * odd]
    o_land[c] = o_parts[...]
    prevw[c] = prev_s[...]
    xw[c] = x_ref[...]

    def rows_at(d):
        return pl.ds(pl.multiple_of(d * depth, 16), depth)

    def push(ref, at):
        here = ref.at[rows_at(r)]
        return [
            send_to(here, here, r_send.at[at, k - 1], r_recv.at[at, k - 1], (flip(r, 2 * k), c))
            for k in range(1, 4)
        ]

    def hand(ref, at):
        copies = []
        for k in range(4):
            here = ref.at[rows_at(flip(r, 2 * k))]
            copies.append(send_to(here, here, r_send.at[at, 3 + k], r_recv.at[at, 3 + k], (flip(r, 1), c)))
        return copies

    wait_all(q_copies)
    wq[rows_at(r)] = jnp.concatenate([q_land[i] for i in range(3)], axis=1)
    wq_push, wq_hand = push(wq, 0), hand(wq, 0)
    start_all(wq_push)
    wait_all(o_copies)
    wo[rows_at(r)] = jnp.concatenate([o_land[i] for i in range(cols)], axis=1)
    wo_push, wo_hand = push(wo, 1), hand(wo, 1)
    start_all(wo_push)

    weights = (gate_ref, up_ref, down_ref)
    half = gate_ref.shape[0] // 2
    held = moves([(ref, w_s.at[t]) for t, ref in enumerate(weights)], local_sem)
    kept = moves([(w_s.at[t], wall_ref.at[t, :, rows_at(r)]) for t in range(3)], local_sem)

    def to_near(t):
        dst = wall_ref.at[t, :, rows_at(r)]
        return [
            send_to(weights[t], dst, e_send.at[t, k - 1], e_recv.at[t, k - 1], (flip(r, 2 * k), c))
            for k in (1, 2)
        ]

    def to_far(t):
        copies = []
        for k in (1, 2):
            here = wall_ref.at[t, pl.ds((k - 1) * half, half), rows_at(flip(r, 2 * k))]
            copies.append(send_to(here, here, d_send.at[t, k - 1], d_recv.at[t, k - 1], (flip(r, 6 - 2 * k), c)))
        return copies

    def to_other_core(t):
        copies = []
        for k in range(4):
            here = wall_ref.at[t, :, rows_at(flip(r, 2 * k))]
            src = weights[t] if k == 0 else here
            copies.append(send_to(src, here, s_send.at[t, k], s_recv.at[t, k], (flip(r, 1), c)))
        return copies

    def relay(t):
        for near, far, across in zip(to_near(t), to_far(t), to_other_core(t)[1:3]):
            near.wait_recv()
            far.start()
            across.start()

    def hand_over(t):
        for far in to_far(t):
            far.wait_recv()
        to_other_core(t)[3].start()

    for t in range(3):
        start_all(to_near(t))
        to_other_core(t)[0].start()
    start_all(held)

    small = [ref[...].astype(F32) for ref in (router_ref, const_ref.at[0], const_ref.at[1], vector_ref)]
    small += [again, fgain, jnp.zeros((LANES - ROW_GAIN - 2, D), F32)]
    rw_out[...] = jnp.concatenate(small, axis=0).astype(BF)
    carry = jnp.concatenate([carry_ref[...].astype(F32), jnp.zeros((ROUTES, LANES - ROUTES), F32)], axis=1)
    carry_out[...] = jnp.concatenate([carry, jnp.zeros((16 - ROUTES, LANES), F32)], axis=0).astype(BF)
    slots, meta = tokens_meta(routes_ref, lengths_ref, rows, EXPERTS)
    slots_ref[...] = slots
    meta_s[...] = meta
    sub = lax.broadcasted_iota(jnp.int32, (8, LANES), 0)
    firsts, end, ends = jnp.zeros((8, LANES), F32), 0, []
    for i in range(lengths_ref.shape[1]):
        firsts = jnp.where(sub == i, jnp.asarray(end, jnp.int32).astype(F32), firsts)
        end = end + lengths_ref[0, i]
        ends.append(end)
    angle = firsts * freq_ref[...]
    cos_first, sin_first = jnp.cos(angle), jnp.sin(angle)
    spot = lax.broadcasted_iota(jnp.int32, (rows, LANES), 0)
    cb, sb = jnp.ones((rows, LANES), F32), jnp.zeros((rows, LANES), F32)
    for i in range(1, len(ends)):
        cb = jnp.where(spot >= ends[i - 1], cos_first[i : i + 1], cb)
        sb = jnp.where(spot >= ends[i - 1], sin_first[i : i + 1], sb)
    cb, sb = jnp.where(spot >= end, 1.0, cb), jnp.where(spot >= end, 0.0, sb)
    sign = jnp.where(lane_iota((rows, LANES)) % 2 == 0, -1.0, 1.0)
    wait_all(soon)
    cos_s[...] = cos_ref[...] * cb + sin_ref[...] * sb
    sin_s[...] = (sin_ref[...] * cb - cos_ref[...] * sb) * sign
    lse_s[...] = jnp.zeros_like(lse_s)

    def project(d):
        at = pl.ds(pl.multiple_of(d * local, LANES), local)
        x = xw[d].astype(F32)
        normed = (x * norm_rows(x) * again).astype(BF)
        proj = mm(normed, wq[...])
        cosine, sines = cos_s[at], sin_s[at]
        for part in range(2 * width // LANES):
            v = proj[:, part * LANES : (part + 1) * LANES]
            t = v * cosine + swap_pairs(v) * sines
            for side in range(2):
                head = 2 * part + side
                piece = t[:, side * HEAD_DIM : (side + 1) * HEAD_DIM].astype(BF)
                if head < heads:
                    piece = piece * jnp.asarray(1.0 / math.sqrt(HEAD_DIM), BF)
                qkv_s[head, at] = piece
        for head in range(2 * heads, 3 * heads):
            qkv_s[head, at] = proj[:, head * HEAD_DIM : (head + 1) * HEAD_DIM].astype(BF)

    def project_at(k):
        def side(way, carry):
            d = c + k * (2 * way - 1)

            @pl.when((d >= 0) & (d < cols))
            def _():
                project(jnp.clip(d, 0, cols - 1))

            return carry

        lax.fori_loop(0, 2 if k else 1, side, 0)

    early = local // EARLY
    cot_step, cot_drain = gather_chain(cot_ref.at[pl.ds(0, early)], cota_ref, t_send, t_recv, cols)
    cot_kept = moves([(cot_ref.at[pl.ds(0, early)], cota_ref.at[c])], local_sem.at[pl.ds(3, 1)])

    wait_all(held)
    start_all(kept)
    x_step(1)
    for copy in wq_push:
        copy.wait_recv()
    start_all(wq_hand)
    x_step(2)
    for copy in wo_push:
        copy.wait_recv()
    start_all(wo_hand)
    wait_all(wq_hand)
    project_at(0)
    project_at(1)
    project_at(2)
    relay(0)
    x_step(3)
    cot_step(0)
    start_all(cot_kept)
    project_at(3)
    cot_step(1)

    blocks = rows // Q_ROWS

    def head_copies(h):
        copies = []
        for k in range(1, cols):
            there = (c + k) % cols
            copies.append(
                send_to(a_send.at[there, h], a_land.at[c, h], h_send.at[h, k - 1], h_recv.at[h, k - 1], (r, there))
            )
        return copies

    def one_head(h, carry):
        for i in range(blocks):
            at = slice(i * Q_ROWS, (i + 1) * Q_ROWS)
            length = (i + 1) * Q_ROWS
            s = mm(qkv_s[h, at], qkv_s[heads + h, :length], NT)
            begin = column(meta_s, at, META_BEGIN).astype(jnp.int32)
            s = jnp.where(seen(begin, i * Q_ROWS, Q_ROWS, length), s, NEG)
            top = jnp.max(s, axis=1, keepdims=True)
            p = jnp.exp(s - top)
            total = jnp.sum(p, axis=1, keepdims=True)
            o = mm(p.astype(BF), qkv_s[2 * heads + h, :length]) * (column(meta_s, at, META_VALID) / total)
            o_s[h, at] = o.astype(BF)
            lse_s[at] = jnp.where(lane_iota((Q_ROWS, LANES)) == h, top + jnp.log(total), lse_s[at])
        for d in range(cols):
            a_send[d, h] = pack_head(o_s[h, d * local : (d + 1) * local])
        start_all(head_copies(h))
        return carry

    lax.fori_loop(0, 1, one_head, 0)
    cot_step(2)
    lax.fori_loop(1, heads, one_head, 0)
    a_land[c] = a_send[c]
    stored = moves(
        [
            (xw, xw_out),
            (wq, wq_out),
            (qkv_s, qkv_out),
            (o_s, o_out),
            (lse_s, lse_out),
            (cos_s, cos_out),
            (sin_s, sin_out),
            (meta_s, meta_out),
        ],
        local_sem.at[pl.ds(4, 8)],
    )
    start_all(stored)
    relay(1)
    wait_all(wo_hand)
    for h in range(heads):
        wait_all(head_copies(h))
    mixed = jnp.concatenate([unpack_head(a_land[i, h]) for i in range(cols) for h in range(heads)], axis=1)
    mixed_s[...] = mixed
    middle = x_ref[...].astype(F32) + mm(mixed, wo[...], NT)
    middle_s[...] = middle
    n2_s[...] = (middle * norm_rows(middle) * fgain).astype(BF)
    n_step, n_drain = gather_chain(n2_s, n2w_ref, n_send, n_recv, cols)
    n_step(0)
    wait_all(prev_copies)
    stored_late = moves(
        [(n2_s, n2w_ref.at[c]), (wo, wo_out), (mixed_s, mixed_out), (middle_s, middle_out), (prevw, prevw_out)],
        local_sem.at[pl.ds(12, 5)],
    )
    start_all(stored_late)
    relay(2)
    n_step(1)
    hand_over(0)
    n_step(2)
    hand_over(1)
    hand_over(2)
    n_step(3)
    cot_step(3)
    x_drain()
    n_drain()
    cot_drain()
    for copy in wq_push + wo_push:
        copy.wait_send()
    for t in range(3):
        for copy in to_near(t) + to_far(t):
            copy.wait_send()
        wait_all(to_other_core(t))
    wait_all(kept + cot_kept + stored + stored_late)


def first_step(cols, ranks, x, cot, router, const, vector, again, fgain, carry, wq, wo, prev, routes, lengths, gate, up, down):
    local = x.shape[0]
    rows = local * cols
    heads, width = 3, 3 * HEAD_DIM
    experts, depth, ff = gate.shape
    spots = np.arange(rows, dtype=np.float64)[:, None]
    pair = np.arange(LANES) % HEAD_DIM // 2
    freq = np.exp(-(2.0 * pair / HEAD_DIM) * math.log(BASE))[None, :]
    tables = [np.cos(spots * freq), np.sin(spots * freq), freq]
    tables = [jnp.asarray(value.astype(np.float32)) for value in tables]
    vm = pl.BlockSpec(memory_space=pltpu.VMEM)
    dma = pltpu.SemaphoreType.DMA
    return pl.pallas_call(
        functools.partial(first_kernel, cols, ranks),
        out_shape=(
            jax.ShapeDtypeStruct((3, experts, D, ff), BF),
            jax.ShapeDtypeStruct((3 * heads, rows, HEAD_DIM), BF),
            jax.ShapeDtypeStruct((heads, rows, HEAD_DIM), BF),
            jax.ShapeDtypeStruct((rows, LANES), F32),
            jax.ShapeDtypeStruct((cols, local, D), BF),
            jax.ShapeDtypeStruct((D, 3 * width), BF),
            jax.ShapeDtypeStruct((D, D), BF),
            jax.ShapeDtypeStruct((rows, LANES), F32),
            jax.ShapeDtypeStruct((rows, LANES), F32),
            jax.ShapeDtypeStruct((rows, LANES), F32),
            jax.ShapeDtypeStruct((experts, rows), jnp.int32),
            jax.ShapeDtypeStruct((local, D), BF),
            jax.ShapeDtypeStruct((local, D), F32),
            jax.ShapeDtypeStruct((cols, local, D), BF),
            jax.ShapeDtypeStruct((cols, 16, local), BF),
            jax.ShapeDtypeStruct((cols, local // EARLY, D), BF),
            jax.ShapeDtypeStruct((LANES, D), BF),
            jax.ShapeDtypeStruct((16, LANES), BF),
        ),
        in_specs=[vm] * 12 + [pl.BlockSpec(memory_space=pltpu.SMEM)] + [ANY, ANY, vm] + [ANY] * 3,
        out_specs=(ANY,) * 10 + (vm,) + (ANY,) * 5 + (vm, vm),
        scratch_shapes=[
            pltpu.VMEM((cols, local, D), BF),
            pltpu.VMEM((3, depth, width), BF),
            pltpu.VMEM((3, depth, width), BF),
            pltpu.VMEM((depth, width), BF),
            pltpu.VMEM((cols, depth, width), BF),
            pltpu.VMEM((D, 3 * width), BF),
            pltpu.VMEM((D, D), BF),
            pltpu.VMEM((cols, heads, local // 2, LANES), BF),
            pltpu.VMEM((cols, heads, local // 2, LANES), BF),
            pltpu.VMEM((16, local), BF),
            pltpu.VMEM((cols, 16, local), BF),
            pltpu.VMEM((3 * heads, rows, HEAD_DIM), BF),
            pltpu.VMEM((heads, rows, HEAD_DIM), BF),
            pltpu.VMEM((rows, LANES), F32),
            pltpu.VMEM((rows, LANES), F32),
            pltpu.VMEM((rows, LANES), F32),
            pltpu.VMEM((rows, LANES), F32),
            pltpu.VMEM((local, D), BF),
            pltpu.VMEM((local, D), F32),
            pltpu.VMEM((local, D), BF),
            pltpu.VMEM((3, experts, depth, ff), BF),
            dma((17,)),
            dma((2, cols - 1)),
            dma((2, cols - 1)),
            dma((2, cols - 1)),
            dma((2, cols - 1)),
            dma((2, cols - 1)),
            dma((2, cols - 1)),
            dma((2,)),
            dma((2,)),
            dma((2, cols - 1)),
            dma((2, cols - 1)),
            dma((2, 7)),
            dma((2, 7)),
            dma((3, 2)),
            dma((3, 2)),
            dma((3, 2)),
            dma((3, 2)),
            dma((3, 4)),
            dma((3, 4)),
            dma((heads, cols - 1)),
            dma((heads, cols - 1)),
            pltpu.VMEM((rows, LANES), F32),
            pltpu.VMEM((rows, LANES), F32),
            dma((2,)),
        ],
        compiler_params=pltpu.CompilerParams(
            vmem_limit_bytes=60 * MIB, collective_id=5, has_side_effects=True
        ),
        cost_estimate=pl.CostEstimate(
            flops=8 * heads * rows * rows * HEAD_DIM, bytes_accessed=40 * MIB, transcendentals=heads * rows * rows
        ),
        name="first_step",
    )(x, cot, router, const, vector, again, fgain, carry, wq, wo, prev, routes, lengths, *tables, gate, up, down)


def experts_forward_kernel(
    cols,
    capacity,
    n2_ref,
    prev_ref,
    cot_ref,
    rw_ref,
    carry_ref,
    slots_ref,
    meta_ref,
    w_ref,
    x_ref,
    gu_ref,
    y_ref,
    gates_ref,
    cotb_ref,
    send,
    recv,
    local_sem,
):
    e = pl.program_id(0)
    experts = pl.num_programs(0)
    r, c = place()
    early = cot_ref.shape[0] // EARLY
    late = cot_ref.at[pl.ds(early, cot_ref.shape[0] - early)]
    step, drain = gather_chain(late, cotb_ref, send, recv, cols)
    own_copy = pltpu.make_async_copy(late, cotb_ref.at[c], local_sem.at[0])

    @pl.when(e == 0)
    def _():
        greet(col_peers(cols))
        own_copy.start()
        step(0)
        prev = jnp.concatenate([mm(prev_ref[i], carry_ref[...], TN) for i in range(cols)], axis=0)
        g = gate_lanes(mm(n2_ref[...], rw_ref[...], NT) + prev, meta_ref[...])
        high = g.astype(BF)
        gates_ref[:, :LANES] = high
        gates_ref[:, LANES:] = (g - high.astype(F32)).astype(BF)

    @pl.when(e == 3)
    def _():
        step(1)

    @pl.when(e == 6)
    def _():
        step(2)

    one = slot_rows(slots_ref, e, capacity)
    x = mm(one, n2_ref[...]).astype(BF)
    x_ref[0] = x
    sg = slot_gates(one, gates_ref, e)
    g = mm(x, w_ref[0, 0])
    u = mm(x, w_ref[1, 0])
    gu_ref[0, 0] = g.astype(BF)
    gu_ref[0, 1] = u.astype(BF)
    gh = (g * jax.nn.sigmoid(g) * u * sg).astype(BF)
    y_ref[0] = mm(gh, w_ref[2, 0], NT).astype(BF)

    @pl.when(e == experts - 1)
    def _():
        for k in range(3, cols):
            step(k)
        drain()
        own_copy.wait()


def experts_forward(cols, n2, prev, cot, rw, carry, meta, slots, w_all):
    rows = n2.shape[0]
    capacity = rows // 4
    three, experts, deep, ff = w_all.shape
    local = rows // cols
    rest = local - local // EARLY
    return pl.pallas_call(
        functools.partial(experts_forward_kernel, cols, capacity),
        grid=(experts,),
        out_shape=(
            jax.ShapeDtypeStruct((experts, capacity, D), BF),
            jax.ShapeDtypeStruct((experts, 2, capacity, ff), BF),
            jax.ShapeDtypeStruct((experts, capacity, D), BF),
            jax.ShapeDtypeStruct((rows, 2 * LANES), BF),
            jax.ShapeDtypeStruct((cols, rest, D), BF),
        ),
        in_specs=[
            whole((rows, D)),
            whole((cols, 16, local)),
            whole((local, D)),
            whole((LANES, D)),
            whole((16, LANES)),
            whole((experts, rows)),
            whole((rows, LANES)),
            pl.BlockSpec((three, 1, deep, ff), lambda e: (0, e, 0, 0)),
        ],
        out_specs=(
            pl.BlockSpec((1, capacity, D), lambda e: (e, 0, 0)),
            pl.BlockSpec((1, 2, capacity, ff), lambda e: (e, 0, 0, 0)),
            pl.BlockSpec((1, capacity, D), lambda e: (e, 0, 0)),
            whole((rows, 2 * LANES)),
            ANY,
        ),
        scratch_shapes=[
            pltpu.SemaphoreType.DMA((2, cols - 1)),
            pltpu.SemaphoreType.DMA((2, cols - 1)),
            pltpu.SemaphoreType.DMA((1,)),
        ],
        compiler_params=pltpu.CompilerParams(
            vmem_limit_bytes=60 * MIB, collective_id=1, has_side_effects=True
        ),
        cost_estimate=pl.CostEstimate(
            flops=experts * capacity * 2 * D * (3 * ff + rows),
            bytes_accessed=40 * MIB,
            transcendentals=experts * capacity * ff,
        ),
        name="experts_forward",
    )(n2, prev, cot, rw, carry, slots, meta, w_all)


def experts_backward_kernel(
    cols,
    capacity,
    cota_ref,
    cotb_ref,
    y_ref,
    gates_ref,
    slots_ref,
    meta_ref,
    w_ref,
    x_ref,
    gu_ref,
    dx_ref,
    dots_ref,
    mixsum_ref,
    gown_ref,
    sib_ref,
    hin_ref,
    glast_ref,
    cot_s,
    mix_s,
    gbuf,
    out,
    arrived,
    send,
    recv,
    own_sem,
    sib_send,
    sib_recv,
    cot_sem,
    lbuf,
    hbuf,
    l_sem,
    hsend,
    hrecv,
):
    e = pl.program_id(0)
    experts = pl.num_programs(0)
    r, c = place()
    core = r % 2
    local = mix_s.shape[1]
    early = cota_ref.shape[1]
    place_now = lax.rem(e, 2)
    slot, total, drain = reduce_chain(lambda d: mix_s[d], out, arrived, send, recv, cols)

    def own_copy(expert, at):
        return pltpu.make_async_copy(gbuf.at[at, :, :, core], gown_ref.at[expert], own_sem.at[at])

    def last_copy(at):
        return pltpu.make_async_copy(gbuf.at[at, :, :, 1 - core], glast_ref, sib_send.at[at])

    def sib_copy(expert, at):
        return send_to(
            gbuf.at[at, :, :, 1 - core],
            sib_ref.at[expert],
            sib_send.at[at],
            sib_recv.at[expert],
            (flip(r, 1), c),
        )

    cot_loads = moves(
        [(cota_ref.at[d], cot_s.at[pl.ds(d * local, early)]) for d in range(cols)]
        + [(cotb_ref.at[d], cot_s.at[pl.ds(d * local + early, local - early)]) for d in range(cols)],
        cot_sem,
    )
    before = jnp.maximum(e - 1, 0)
    sib_load = pltpu.make_async_copy(sib_ref.at[before], lbuf, l_sem.at[0])
    sends_now = (e >= 1) & (e <= SENT_SOON)

    def h_sends(i):
        return to_chips(lambda there: hbuf.at[i, :, there], hin_ref.at[i], hsend.at[i], hrecv.at[i])

    @pl.when(e == 0)
    def _():
        start_all(cot_loads)
        greet(col_peers(cols) + [(flip(r, m), c) for m in (1, 2, 4, 6)])
        for n, d in enumerate(chain_order(c)):
            mix_s[d] = combine(meta_ref, y_ref, d, local)
            if n == 0:
                slot(0)
        wait_all(cot_loads)

    @pl.when(e == 2)
    def _():
        slot(1)

    @pl.when(e == 5)
    def _():
        slot(2)

    one = slot_rows(slots_ref, e, capacity)
    ct = mm(one, cot_s[...]).astype(BF)
    sg = slot_gates(one, gates_ref, e)
    x = x_ref[0]
    g, u = gu_ref[0, 0].astype(F32), gu_ref[0, 1].astype(F32)
    v = mm(ct, w_ref[2, 0])
    sig = jax.nn.sigmoid(g)
    act = g * sig
    h = act * u
    dot = jnp.sum(h * v, axis=1, keepdims=True)
    dots_ref[pl.ds(e, 1)] = jnp.sum(one.astype(F32) * dot, axis=0, keepdims=True)
    gh = (h * sg).astype(BF)
    gv = v * sg
    dg = (gv * u * (sig * (1.0 + g * (1.0 - sig)))).astype(BF)
    du = (gv * act).astype(BF)
    dx_ref[0] = (mm(dg, w_ref[0, 0], NT) + mm(du, w_ref[1, 0], NT)).astype(BF)

    @pl.when(e >= 2)
    def _():
        own_copy(e - 2, place_now).wait()
        sib_copy(e - 2, place_now).wait_send()

    @pl.when(sends_now)
    def _():
        sib_copy(before, 1 - place_now).wait_recv()
        sib_load.start()

    shape = gbuf.shape[2:]
    pair = mm(x, jnp.concatenate([dg, du], axis=1), TN).astype(BF)
    gbuf[place_now, 0] = pair[:, : dg.shape[1]].reshape(shape)
    gbuf[place_now, 1] = pair[:, dg.shape[1] :].reshape(shape)
    gbuf[place_now, 2] = mm(ct, gh, TN).astype(BF).reshape(shape)
    own_copy(e, place_now).start()

    @pl.when(e < experts - 1)
    def _():
        sib_copy(e, place_now).start()

    @pl.when(e == experts - 1)
    def _():
        last_copy(place_now).start()

    @pl.when(sends_now)
    def _():
        sib_load.wait()
        hbuf[before] = (gbuf[1 - place_now, :, :, core].astype(F32) + lbuf[...].astype(F32)).astype(BF)
        start_all(h_sends(before))

    @pl.when(e == experts - 1)
    def _():
        for s in range(3, cols):
            slot(s)
        total(mixsum_ref)
        drain()
        for back in (1, 0):
            own_copy(e - back, lax.rem(e - back, 2)).wait()
        sib_copy(e - 1, 1 - place_now).wait_send()
        last_copy(place_now).wait()
        for i in range(SENT_SOON, EXPERTS - 1):
            sib_copy(i, i % 2).wait_recv()
        for i in range(SENT_SOON):
            wait_all(h_sends(i))


def experts_backward(cols, ranks, cota, cotb, y, gates, meta, slots, w_all, x, gu):
    experts, capacity, _ = y.shape
    rows = slots.shape[1]
    three, _, deep, ff = w_all.shape
    local = rows // cols
    chips = ranks // 2
    depth = deep // ranks
    half = jax.ShapeDtypeStruct((experts, three, chips, depth, ff), BF)
    return pl.pallas_call(
        functools.partial(experts_backward_kernel, cols, capacity),
        grid=(experts,),
        out_shape=(
            jax.ShapeDtypeStruct((experts, capacity, D), BF),
            jax.ShapeDtypeStruct((experts, rows), F32),
            jax.ShapeDtypeStruct((local, D), F32),
            half,
            half,
            jax.ShapeDtypeStruct((SENT_SOON, 3, three, depth, ff), BF),
            jax.ShapeDtypeStruct((three, chips, depth, ff), BF),
        ),
        in_specs=[
            ANY,
            ANY,
            whole((experts, capacity, D)),
            whole((rows, 2 * LANES)),
            whole((experts, rows)),
            whole((rows, LANES)),
            pl.BlockSpec((three, 1, deep, ff), lambda e: (0, e, 0, 0)),
            pl.BlockSpec((1, capacity, D), lambda e: (e, 0, 0)),
            pl.BlockSpec((1, 2, capacity, ff), lambda e: (e, 0, 0, 0)),
        ],
        out_specs=(
            pl.BlockSpec((1, capacity, D), lambda e: (e, 0, 0)),
            whole((experts, rows)),
            whole((local, D)),
            ANY,
            ANY,
            ANY,
            ANY,
        ),
        scratch_shapes=[
            pltpu.VMEM((rows, D), BF),
            pltpu.VMEM((cols, local, D), BF),
            pltpu.VMEM((2, three, chips, 2, depth, ff), BF),
            *chain_scratch(cols, local),
            pltpu.SemaphoreType.DMA((2,)),
            pltpu.SemaphoreType.DMA((2,)),
            pltpu.SemaphoreType.DMA((experts,)),
            pltpu.SemaphoreType.DMA((2 * cols,)),
            pltpu.VMEM((three, chips, depth, ff), BF),
            pltpu.VMEM((SENT_SOON, three, chips, depth, ff), BF),
            pltpu.SemaphoreType.DMA((1,)),
            pltpu.SemaphoreType.DMA((SENT_SOON, 3)),
            pltpu.SemaphoreType.DMA((SENT_SOON, 3)),
        ],
        compiler_params=pltpu.CompilerParams(
            vmem_limit_bytes=60 * MIB, collective_id=2, has_side_effects=True
        ),
        cost_estimate=pl.CostEstimate(
            flops=experts * capacity * 4 * D * (3 * ff + rows),
            bytes_accessed=60 * MIB,
            transcendentals=experts * capacity * ff,
        ),
        name="experts_backward",
    )(cota, cotb, y, gates, slots, meta, w_all, x, gu)


def resid_kernel(
    cols,
    count,
    dx_in,
    meta_in,
    dots_ref,
    rw_ref,
    prev_ref,
    carry_ref,
    cot_ref,
    mixsum_in,
    n2w_in,
    middle_in,
    out_t_in,
    mixed_in,
    gown_ref,
    glast_ref,
    sib_in,
    layer_ref,
    resid_ref,
    gm_ref,
    og_ref,
    small_ref,
    pg_ref,
    hin_ref,
    hrest_ref,
    sib_ref,
    mixsum,
    n2_s,
    middle_s,
    out_t,
    mixed_s,
    resid_s,
    load_sem,
    gt_s,
    out,
    arrived,
    send,
    recv,
    dots_in,
    dsend,
    drecv,
    grad,
    gm_out,
    gsend,
    grecv,
    gm_sem,
    lbuf,
    hbuf,
    hload,
    hsend,
    hrecv,
    hkeep,
    last_sem,
    og_s,
    og_sib,
    dx_ref,
    meta_ref,
    soon_sem,
):
    r, c = place()
    chip = r // 2
    local = cot_ref.shape[0]
    held = hbuf.shape[0]
    loads = moves(
        [
            (n2w_in.at[c], n2_s),
            (middle_in, middle_s),
            (mixsum_in, mixsum),
            (out_t_in, out_t),
            (mixed_in, mixed_s),
        ],
        load_sem,
    )
    soon = moves([(meta_in, meta_ref), (dx_in, dx_ref)], soon_sem)
    start_all(soon)
    greet(col_peers(cols) + [(flip(r, m), c) for m in (1, 2, 4, 6)])
    last = gown_ref.shape[0] - 1
    across = send_to(glast_ref, sib_ref.at[last], last_sem.at[0], last_sem.at[1], (flip(r, 1), c))
    across.start()
    slot, total, drain = reduce_chain(lambda d: gt_s[d], out, arrived, send, recv, cols)

    def dots_of(d):
        return dots_ref.at[:, pl.ds(pl.multiple_of(d * local, LANES), local)]

    dot_copies = to_cols(dots_of, dots_in, dsend, drecv, cols)
    start_all(dot_copies)
    dots_in[c] = dots_of(c)[...]
    wait_all(soon)
    for n, d in enumerate(chain_order(c)):
        gt_s[d] = combine(meta_ref, dx_ref, d, local)
        if n == 0:
            slot(0)

    def h_loads(i):
        at = lax.rem(i, 2)
        return [
            pltpu.make_async_copy(ref.at[SENT_SOON + i], lbuf.at[at, j], hload.at[at, j])
            for j, ref in enumerate((gown_ref, sib_ref))
        ]

    def h_sends(i):
        return to_chips(lambda there: hbuf.at[i, :, there], hin_ref.at[i], hsend.at[i], hrecv.at[i])

    def h_keeps(i):
        return moves(
            [(hbuf.at[i, :, flip(chip, k)], hrest_ref.at[i - count, k - 1]) for k in range(1, 4)],
            hkeep.at[i - count],
        )

    start_all(h_loads(0))

    def add_cores(i, carry):
        @pl.when(i + 2 == held)
        def _():
            across.wait()

        @pl.when(i + 1 < held)
        def _():
            start_all(h_loads(i + 1))

        wait_all(h_loads(i))
        at = lax.rem(i, 2)
        hbuf[i] = (lbuf[at, 0].astype(F32) + lbuf[at, 1].astype(F32)).astype(BF)

        @pl.when(i < count)
        def _():
            start_all(h_sends(i))

        @pl.when(i >= count)
        def _():
            start_all(h_keeps(jnp.maximum(i, count)))

        return carry

    lax.fori_loop(0, held, add_cores, 0)
    start_all(loads)
    slot(1)
    wait_all(loads)

    meta = meta_ref[pl.ds(pl.multiple_of(c * local, LANES), local)]
    n2, cot = n2_s[...], cot_ref[...]
    n2f, cotf = n2.astype(F32), cot.astype(F32)
    middle = middle_s[...]
    rw = rw_ref[...]
    lin = mm(n2, rw, NT)
    prev = prev_ref[c]
    gates = gate_lanes(lin + mm(prev, carry_ref[...], TN), meta)
    lane = lane_iota((local, LANES))
    cot_lin = mm(cot, rw, NT)
    dot_keep = jnp.sum(cotf * n2f, axis=1, keepdims=True)
    wait_all(dot_copies)
    d = jnp.concatenate([all_sum(dots_in, cols), jnp.zeros((LANES - EXPERTS, local), F32)], axis=0).T
    g_gates = jnp.where(lane == EXPERTS + 1, dot_keep, d)
    keep = gates[:, EXPERTS + 1 : EXPERTS + 2]
    mixes, packs = [], jnp.zeros((local, LANES), F32)
    for j in range(2):
        l0 = lin[:, ROW_CONST + 2 * j : ROW_CONST + 2 * j + 1]
        l1 = lin[:, ROW_CONST + 2 * j + 1 : ROW_CONST + 2 * j + 2]
        top = jnp.maximum(l0, l1)
        e0, e1 = jnp.exp(l0 - top), jnp.exp(l1 - top)
        a0, a1 = e0 / (e0 + e1), e1 / (e0 + e1)
        share = gates[:, EXPERTS + 2 + j : EXPERTS + 3 + j]
        dot_vec = cot_lin[:, ROW_VEC + j : ROW_VEC + j + 1]
        keep = keep + share * a0
        mixes.append(share * a1)
        g_gates = jnp.where(lane == EXPERTS + 2 + j, a0 * dot_keep + a1 * dot_vec, g_gates)
        gk, gv = share * dot_keep, share * dot_vec
        mean = a0 * gk + a1 * gv
        packs = packs + jnp.where(lane == ROW_CONST + 2 * j, a0 * (gk - mean), 0.0)
        packs = packs + jnp.where(lane == ROW_CONST + 2 * j + 1, a1 * (gv - mean), 0.0)
        packs = packs + jnp.where(lane == ROW_VEC + j, share * a1, 0.0)
    packs = packs + gates * (g_gates - jnp.sum(gates * g_gates, axis=1, keepdims=True))
    vec = rw[ROW_VEC : ROW_VEC + 2].astype(F32)
    layer = middle + mixsum[...] + keep * n2f + mixes[0] * vec[0:1] + mixes[1] * vec[1:2]
    layer_ref[...] = layer.astype(BF)

    high = packs.astype(BF)
    low = (packs - high.astype(F32)).astype(BF)
    back = lane < ROW_VEC
    high_b = jnp.where(back, packs, 0.0).astype(BF)
    low_b = jnp.where(back, packs - high.astype(F32), 0.0).astype(BF)
    grad_local = keep * cotf + mm(high_b, rw) + mm(low_b, rw)
    by_n2 = mm(high, n2, TN) + mm(low, n2, TN)
    by_cot = mm(high, cot, TN) + mm(low, cot, TN)
    by_prev = mm(prev, high) + mm(prev, low)
    pg = mm(carry_ref[...], high_b, NT) + mm(carry_ref[...], low_b, NT)
    pg_ref[...] = pg[:ROUTES]
    sub = lax.broadcasted_iota(jnp.int32, (SMALL_ROWS, D), 0)
    small_ref[:, :D] = jnp.where(sub < ROW_VEC, by_n2[:SMALL_ROWS], by_cot[:SMALL_ROWS])
    small_ref[:16, D : D + LANES] = by_prev
    small_ref[16:, D : D + LANES] = jnp.zeros((SMALL_ROWS - 16, LANES), F32)
    small_ref[:, D + LANES :] = jnp.zeros((SMALL_ROWS, LANES), F32)
    fgain = rw[ROW_GAIN + 1 : ROW_GAIN + 2].astype(F32)
    scale = norm_rows(middle)

    for s in range(2, cols):
        slot(s)
    total(grad)
    grad_normed = grad[...] + grad_local
    gained = grad_normed * fgain
    mid_dot = jnp.sum(gained * middle, axis=1, keepdims=True)
    resid = cotf + scale * gained - middle * (scale * scale * scale * (mid_dot * (1.0 / D)))
    cut = resid.astype(BF)
    gm = (mm(cut, out_t[...]) * meta[:, META_VALID : META_VALID + 1]).astype(BF)
    width = D // cols
    for i in range(cols):
        for h in range(width // HEAD_DIM):
            at = i * width + h * HEAD_DIM
            gm_out[i, h] = pack_head(gm[:, at : at + HEAD_DIM])
    gm_copies = to_cols(lambda i: gm_out.at[i], gm_ref, gsend, grecv, cols)
    start_all(gm_copies)
    resid_s[...] = resid
    stored = moves([(gm_out.at[c], gm_ref.at[c]), (resid_s, resid_ref)], gm_sem)
    start_all(stored)
    small_ref[ROW_GAIN : ROW_GAIN + 1, :D] = jnp.sum(grad_normed * middle * scale, axis=0, keepdims=True)
    core = r % 2
    og_s[...] = mm(cut, mixed_s[...], TN).astype(BF).reshape(og_s.shape)
    og_across = send_to(og_s.at[:, 1 - core], og_sib, last_sem.at[2], last_sem.at[3], (flip(r, 1), c))
    og_across.start()
    og_across.wait()
    for k in range(og_s.shape[0]):
        og_ref[k] = (og_s[k, core].astype(F32) + og_sib[k].astype(F32)).astype(BF)
    wait_all(stored + gm_copies)
    drain()

    def end(i, carry):
        @pl.when(i < count)
        def _():
            wait_all(h_sends(i))

        @pl.when(i >= count)
        def _():
            wait_all(h_keeps(jnp.maximum(i, count)))

        return carry

    lax.fori_loop(0, held, end, 0)


def resid_step(cols, dx, meta, dots, rw, prev, carry, cot, mixsum, n2w, middle, out_t, mixed, gown, glast, sib):
    local = cot.shape[0]
    experts, three, chips, depth, ff = gown.shape
    count, held = SENT_NEXT, experts - SENT_SOON
    vm = pl.BlockSpec(memory_space=pltpu.VMEM)
    dma = pltpu.SemaphoreType.DMA
    return pl.pallas_call(
        functools.partial(resid_kernel, cols, count),
        out_shape=(
            jax.ShapeDtypeStruct((local, D), BF),
            jax.ShapeDtypeStruct((local, D), F32),
            jax.ShapeDtypeStruct((cols, 3, local // 2, LANES), BF),
            jax.ShapeDtypeStruct((chips, depth, D), BF),
            jax.ShapeDtypeStruct((SMALL_ROWS, D + 2 * LANES), F32),
            jax.ShapeDtypeStruct((ROUTES, local), F32),
            jax.ShapeDtypeStruct((count, 3, three, depth, ff), BF),
            jax.ShapeDtypeStruct((held - count, 3, three, depth, ff), BF),
            jax.ShapeDtypeStruct(sib.shape, BF),
        ),
        in_specs=[ANY] * 2 + [vm] * 5 + [ANY] * 8,
        out_specs=(vm, ANY, ANY, vm, vm, vm, ANY, ANY, ANY),
        input_output_aliases={14: 8},
        scratch_shapes=[
            pltpu.VMEM((local, D), F32),
            pltpu.VMEM((local, D), BF),
            pltpu.VMEM((local, D), F32),
            pltpu.VMEM((D, D), BF),
            pltpu.VMEM((local, D), BF),
            pltpu.VMEM((local, D), F32),
            dma((5,)),
            pltpu.VMEM((cols, local, D), BF),
            *chain_scratch(cols, local),
            pltpu.VMEM((cols, EXPERTS, local), F32),
            dma((cols - 1,)),
            dma((cols - 1,)),
            pltpu.VMEM((local, D), F32),
            pltpu.VMEM((cols, 3, local // 2, LANES), BF),
            dma((cols - 1,)),
            dma((cols - 1,)),
            dma((2,)),
            pltpu.VMEM((2, 2, three, chips, depth, ff), BF),
            pltpu.VMEM((held, three, chips, depth, ff), BF),
            dma((2, 2)),
            dma((count, 3)),
            dma((count, 3)),
            dma((held - count, 3)),
            dma((4,)),
            pltpu.VMEM((chips, 2, depth, D), BF),
            pltpu.VMEM((chips, depth, D), BF),
            pltpu.VMEM(dx.shape, BF),
            pltpu.VMEM(meta.shape, F32),
            dma((2,)),
        ],
        compiler_params=pltpu.CompilerParams(
            vmem_limit_bytes=60 * MIB, collective_id=3, has_side_effects=True
        ),
        cost_estimate=pl.CostEstimate(flops=6 * local * D * D, bytes_accessed=40 * MIB, transcendentals=0),
        name="resid_step",
    )(dx, meta, dots, rw, prev, carry, cot, mixsum, n2w, middle, out_t, mixed, gown, glast, sib)


def finish_kernel(
    cols,
    ranks,
    gm_in,
    meta_in,
    lse_in,
    small_ref,
    og_ref,
    xown_ref,
    rw_ref,
    qkv_in,
    o_in,
    x_in,
    w_in,
    cos_in,
    sin_in,
    resid_in,
    gown_ref,
    sib_ref,
    hsoon_ref,
    hin0_ref,
    hrest_ref,
    ig_ref,
    small_out,
    qg_out,
    og_out,
    gg_ref,
    ug_ref,
    dg_ref,
    hin_ref,
    qkv_s,
    o_s,
    x_s,
    w_s,
    cos_s,
    sin_s,
    resid_s,
    head_sem,
    load_sem,
    do_s,
    dq_s,
    dk_s,
    dv_s,
    gn_s,
    qg_acc,
    qg_cut,
    out,
    arrived,
    send,
    recv,
    small_s,
    small_rows,
    small_cols,
    small_all,
    og_chips,
    og_parts,
    og_cols,
    qg_sib,
    qg_half,
    qg_chips,
    q_parts,
    q_land,
    total_s,
    fbuf,
    fsem,
    row_send,
    row_recv,
    chip_send,
    chip_recv,
    sib_send,
    sib_recv,
    col_send,
    col_recv,
    hsend,
    hrecv,
    g_s,
    store_sem,
    gm_ref,
    meta_ref,
    lse_ref,
    soon_sem,
):
    r, c = place()
    chip, core = r // 2, r % 2
    heads = 3
    rows = meta_ref.shape[0]
    local = rows // cols
    width = heads * HEAD_DIM
    rest = hrest_ref.shape[0]
    first = gown_ref.shape[0] - rest
    score_scale = 1.0 / math.sqrt(HEAD_DIM)

    def head_loads(h):
        pairs = [(qkv_in.at[i * heads + h], qkv_s.at[i * heads + h]) for i in range(3)]
        return moves(pairs + [(o_in.at[h], o_s.at[h])], head_sem.at[h])

    loads = moves(
        [(x_in, x_s), (w_in, w_s), (cos_in, cos_s), (sin_in, sin_s), (resid_in, resid_s)], load_sem
    )
    soon = moves([(gm_in, gm_ref), (meta_in, meta_ref), (lse_in, lse_ref)], soon_sem)
    start_all(soon)
    start_all(head_loads(0))
    greet(col_peers(cols) + [(flip(r, m), c) for m in range(1, ranks)])
    for h in range(1, heads):
        start_all(head_loads(h))
    start_all(loads)

    def to_sibling(src, dst, at):
        return send_to(src.at[:, 1 - core], dst, sib_send.at[at], sib_recv.at[at], (flip(r, 1), c))

    og_to_chips = to_chips(lambda there: og_ref.at[there], og_chips, chip_send.at[0], chip_recv.at[0])
    start_all(og_to_chips)

    wait_all(soon)
    for d in range(cols):
        at = slice(d * local, (d + 1) * local)
        for h in range(heads):
            do_s[h, at] = unpack_head(gm_ref[d, h])

    def halves(ref, sib, half):
        for k in range(ranks // 2):
            half[k] = (ref[k, core].astype(F32) + sib[k].astype(F32)).astype(BF)

    def h_sends(i):
        r_, c_ = place()
        return [
            send_to(
                hrest_ref.at[i, k - 1],
                hin_ref.at[i, k - 1],
                hsend.at[i, k - 1],
                hrecv.at[i, k - 1],
                (flip(r_, 2 * k), c_),
            )
            for k in range(1, 4)
        ]

    def start_sends(i, carry):
        start_all(h_sends(i))
        return carry

    lax.fori_loop(0, rest - 1, start_sends, 0)

    blocks = rows // Q_ROWS

    def one_head(h, carry):
        wait_all(head_loads(h))
        for i in reversed(range(blocks)):
            at = slice(i * Q_ROWS, (i + 1) * Q_ROWS)
            length = (i + 1) * Q_ROWS
            q, do = qkv_s[h, at], do_s[h, at]
            k, v = qkv_s[heads + h, :length], qkv_s[2 * heads + h, :length]
            delta = jnp.sum(do.astype(F32) * o_s[h, at].astype(F32), axis=1, keepdims=True)
            lse = jnp.sum(jnp.where(lane_iota((Q_ROWS, LANES)) == h, lse_ref[at], 0.0), axis=1, keepdims=True)
            s = mm(q, k, NT)
            ok = seen(column(meta_ref, at, META_BEGIN).astype(jnp.int32), i * Q_ROWS, Q_ROWS, length)
            p = jnp.where(ok, jnp.exp(s - lse), 0.0)
            ds = (p * (mm(do, v, NT) - delta)).astype(BF)
            dq_s[h, at] = mm(ds, k) * score_scale
            dk, dv = mm(ds, q, TN), mm(p.astype(BF), do, TN)
            if i == blocks - 1:
                dk_s[h], dv_s[h] = dk, dv
            else:
                dk_s[h, :length] += dk
                dv_s[h, :length] += dv
        return carry

    lax.fori_loop(0, heads, one_head, 0)

    slot, total, drain = reduce_chain(lambda d: gn_s[d], out, arrived, send, recv, cols)
    wait_all(loads)
    gain_total = jnp.zeros((1, D), F32)
    weight = w_s[...]
    again = rw_ref[ROW_GAIN : ROW_GAIN + 1].astype(F32)
    for n, d in enumerate(chain_order(c)):
        at = pl.ds(pl.multiple_of(d * local, LANES), local)
        cosine, sines = cos_s[at], sin_s[at]
        turned = [dq_s[h, at] for h in range(heads)] + [dk_s[h, at] for h in range(heads)]
        parts = []
        for part in range(heads):
            v = jnp.concatenate(turned[2 * part : 2 * part + 2], axis=1)
            parts.append((v * cosine - swap_pairs(v) * sines).astype(BF))
        parts += [dv_s[h, at].astype(BF) for h in range(heads)]
        gp = jnp.concatenate(parts, axis=1)
        x = x_s[d].astype(F32)
        xs = x * norm_rows(x)
        gn = mm(gp, weight, NT)
        gn_s[d] = gn.astype(BF)
        if n == 0:
            slot(0)
        gain_total = gain_total + jnp.sum(gn * xs, axis=0, keepdims=True)
        grad = mm((xs * again).astype(BF), gp, TN)
        if n == 0:
            qg_acc[...] = grad
        else:
            qg_acc[...] += grad
    qg_cut[...] = qg_acc[...].astype(BF).reshape(qg_cut.shape)
    qg_across = to_sibling(qg_cut, qg_sib, 0)
    qg_across.start()

    sub = lax.broadcasted_iota(jnp.int32, (SMALL_ROWS, D), 0)
    for i in range(ranks):
        block = small_ref[:, i * LANES : (i + 1) * LANES]
        if i < D // LANES:
            own = sub[:, :LANES] == ROW_GAIN + 1
            block = jnp.where(own, gain_total[:, i * LANES : (i + 1) * LANES], block)
        small_s[i] = block
    small_to_rows = to_rows(lambda d: small_s.at[d], small_rows, row_send.at[0], row_recv.at[0], ranks)
    start_all(small_to_rows)
    small_rows[r] = small_s[r]

    def sum_grads(low, high, hin, base):
        def f_loads(i):
            at = lax.rem(i, 2)
            return moves(
                [
                    (gown_ref.at[i, :, chip], fbuf.at[at, 0]),
                    (sib_ref.at[i, :, chip], fbuf.at[at, 1]),
                    (hin.at[i - base], fbuf.at[at, pl.ds(2, 3)]),
                ],
                fsem.at[at],
            )

        start_all(f_loads(low))

        def body(i, carry):
            @pl.when(i + 1 < high)
            def _():
                start_all(f_loads(jnp.minimum(i + 1, high - 1)))

            wait_all(f_loads(i))
            at = lax.rem(i, 2)
            total_grad = fbuf[at, 0].astype(F32)
            for j in range(1, 5):
                total_grad = total_grad + fbuf[at, j].astype(F32)
            for t in range(3):
                g_s[t, i] = total_grad[t].astype(BF)
            return carry

        lax.fori_loop(low, high, body, 0)

    qg_across.wait()
    halves(qg_cut, qg_sib, qg_half)
    qg_to_chips = to_chips(lambda there: qg_half.at[there], qg_chips, chip_send.at[1], chip_recv.at[1])
    start_all(qg_to_chips)
    start_sends(rest - 1, 0)
    slot(1)
    sum_grads(0, SENT_SOON, hsoon_ref, 0)
    wait_all(small_to_rows)
    small_cols[c] = all_sum(small_rows, ranks)
    small_to_cols = to_cols(lambda d: small_cols.at[c], small_cols, col_send.at[0], col_recv.at[0], cols)
    start_all(small_to_cols)
    sum_grads(SENT_SOON, first, hin0_ref, SENT_SOON)
    slot(2)
    wait_all(og_to_chips)
    og_sum = og_ref[chip].astype(F32) + all_sum(og_chips, 3)
    for i in range(cols):
        og_parts[i] = og_sum[:, i * width : (i + 1) * width]
    og_to_cols = to_cols(lambda d: og_parts.at[d], og_cols, col_send.at[1], col_recv.at[1], cols)
    start_all(og_to_cols)
    og_cols[c] = og_parts[c]
    wait_all(qg_to_chips)
    q_sum = qg_cut[chip, core].astype(F32) + qg_sib[chip].astype(F32) + all_sum(qg_chips, 3)
    for i in range(3):
        q_parts[i] = q_sum[:, i * width : (i + 1) * width]
    odd, high = c % 2, c // 2
    q_copies = [
        send_to(
            q_parts.at[1 - odd + high],
            q_land.at[1],
            col_send.at[2, 0],
            col_recv.at[2, 0],
            (r, flip(c, 1)),
        ),
        send_to(
            q_parts.at[2 - 2 * high],
            q_land.at[2 - 2 * odd],
            col_send.at[2, 1],
            col_recv.at[2, 1],
            (r, flip(c, 2)),
        ),
    ]
    start_all(q_copies)
    q_land[2 * odd] = q_parts[(c + 1) // 2]
    wait_all(small_to_cols)
    small_all[r] = all_sum(small_cols, cols)
    small_back = to_rows(lambda d: small_all.at[r], small_all, row_send.at[1], row_recv.at[1], ranks)
    start_all(small_back)

    def end_sends(i, carry):
        wait_all(h_sends(i))
        return carry

    lax.fori_loop(0, rest, end_sends, 0)
    sum_grads(first, first + rest, hin_ref, first)
    wait_all(og_to_cols + q_copies + small_back)
    og_out[...] = all_sum(og_cols, cols)
    for i in range(3):
        qg_out[:, i * width : (i + 1) * width] = q_land[i]
    stored = moves([(g_s.at[i], ref) for i, ref in enumerate((gg_ref, ug_ref, dg_ref))], store_sem)
    start_all(stored)
    for i in range(ranks):
        small_out[:, i * LANES : (i + 1) * LANES] = small_all[i]
    slot(3)
    total(total_s)
    gn = total_s[...]
    x = xown_ref[...].astype(F32)
    scale = norm_rows(x)
    gained = gn * again
    x_dot = jnp.sum(gained * x, axis=1, keepdims=True)
    ig_ref[...] = resid_s[...] + scale * gained - x * (scale * scale * scale * (x_dot * (1.0 / D)))
    wait_all(stored)
    drain()


def finish_step(cols, ranks, gm, meta, lse, small, og, xown, rw, qkv, o, x, w, cosine, sines, resid, gown, sib, hsoon, hin0, hrest):
    rows = meta.shape[0]
    local = rows // cols
    experts, three, chips, depth, ff = gown.shape
    rest = hrest.shape[0]
    heads, width = 3, 3 * HEAD_DIM
    vm = pl.BlockSpec(memory_space=pltpu.VMEM)
    dma = pltpu.SemaphoreType.DMA
    wide = D + 2 * LANES
    weight_grad = jax.ShapeDtypeStruct((experts, depth, ff), BF)
    return pl.pallas_call(
        functools.partial(finish_kernel, cols, ranks),
        out_shape=(
            jax.ShapeDtypeStruct((local, D), F32),
            jax.ShapeDtypeStruct((SMALL_ROWS, wide), F32),
            jax.ShapeDtypeStruct((depth, 3 * width), F32),
            jax.ShapeDtypeStruct((depth, width), F32),
            weight_grad,
            weight_grad,
            weight_grad,
            jax.ShapeDtypeStruct((rest, 3, three, depth, ff), BF),
        ),
        in_specs=[ANY] * 3 + [vm] * 4 + [ANY] * 12,
        out_specs=(vm,) * 4 + (ANY,) * 4,
        scratch_shapes=[
            pltpu.VMEM((3 * heads, rows, HEAD_DIM), BF),
            pltpu.VMEM((heads, rows, HEAD_DIM), BF),
            pltpu.VMEM((cols, local, D), BF),
            pltpu.VMEM((D, 3 * width), BF),
            pltpu.VMEM((rows, LANES), F32),
            pltpu.VMEM((rows, LANES), F32),
            pltpu.VMEM((local, D), F32),
            dma((heads, 4)),
            dma((5,)),
            pltpu.VMEM((heads, rows, HEAD_DIM), BF),
            pltpu.VMEM((heads, rows, HEAD_DIM), F32),
            pltpu.VMEM((heads, rows, HEAD_DIM), F32),
            pltpu.VMEM((heads, rows, HEAD_DIM), F32),
            pltpu.VMEM((cols, local, D), BF),
            pltpu.VMEM((D, 3 * width), F32),
            pltpu.VMEM((chips, 2, depth, 3 * width), BF),
            *chain_scratch(cols, local),
            pltpu.VMEM((ranks, SMALL_ROWS, LANES), F32),
            pltpu.VMEM((ranks, SMALL_ROWS, LANES), F32),
            pltpu.VMEM((cols, SMALL_ROWS, LANES), F32),
            pltpu.VMEM((ranks, SMALL_ROWS, LANES), F32),
            pltpu.VMEM((3, depth, D), BF),
            pltpu.VMEM((cols, depth, width), F32),
            pltpu.VMEM((cols, depth, width), F32),
            pltpu.VMEM((chips, depth, 3 * width), BF),
            pltpu.VMEM((chips, depth, 3 * width), BF),
            pltpu.VMEM((3, depth, 3 * width), BF),
            pltpu.VMEM((3, depth, width), F32),
            pltpu.VMEM((3, depth, width), F32),
            pltpu.VMEM((local, D), F32),
            pltpu.VMEM((2, 5, three, depth, ff), BF),
            dma((2, 3)),
            dma((2, ranks - 1)),
            dma((2, ranks - 1)),
            dma((2, 3)),
            dma((2, 3)),
            dma((1,)),
            dma((1,)),
            dma((3, cols - 1)),
            dma((3, cols - 1)),
            dma((rest, 3)),
            dma((rest, 3)),
            pltpu.VMEM((three, experts, depth, ff), BF),
            dma((3,)),
            pltpu.VMEM(gm.shape, BF),
            pltpu.VMEM(meta.shape, F32),
            pltpu.VMEM(lse.shape, F32),
            dma((3,)),
        ],
        compiler_params=pltpu.CompilerParams(
            vmem_limit_bytes=62 * MIB, collective_id=4, has_side_effects=True
        ),
        cost_estimate=pl.CostEstimate(
            flops=20 * heads * rows * rows * HEAD_DIM, bytes_accessed=40 * MIB, transcendentals=heads * rows * rows
        ),
        name="finish_step",
    )(gm, meta, lse, small, og, xown, rw, qkv, o, x, w, cosine, sines, resid, gown, sib, hsoon, hin0, hrest)


def place_kernel(*refs):
    ins, refs = refs[:9], refs[9:]
    outs, refs = refs[:14], refs[14:]
    held, refs = refs[:9], refs[9:]
    made, (load_sem, store_sem) = refs[:8], refs[8:]
    loads = moves(list(zip(ins, held)), load_sem)
    start_all(loads)
    small, qg, og, pg, layer, ig, *low = held
    full, again, out, fgain, router, carry, const, vector = made
    sources = [layer, ig, full.at[0], full.at[1], full.at[2], again, qg, out, fgain, router, carry, const, vector, pg]
    stores = moves(list(zip(sources, outs)), store_sem)
    for load, store in ((4, 0), (5, 1), (1, 6), (3, 13)):
        loads[load].wait()
        stores[store].start()
    for i in range(3):
        loads[6 + i].wait()
        full[i] = low[i][...].astype(F32)
        stores[2 + i].start()
    loads[2].wait()
    out[...] = og[...].T
    loads[0].wait()
    again[...] = small[ROW_GAIN + 1 : ROW_GAIN + 2, :D].reshape(D)
    fgain[...] = small[ROW_GAIN : ROW_GAIN + 1, :D].reshape(D)
    router[...] = small[:ROUTES, :D]
    carry[...] = small[:ROUTES, D : D + ROUTES]
    for j in range(2):
        const[j] = small[ROW_CONST + 2 * j : ROW_CONST + 2 * j + 2, :D]
    vector[...] = small[ROW_VEC : ROW_VEC + 2, :D]
    for i in (5, 7, 8, 9, 10, 11, 12):
        stores[i].start()
    wait_all(stores)


def place_outputs(*values):
    small, qg, og, pg, layer, ig, gg, ug, dg = values
    made = [(D,), og.shape[::-1], (D,), (ROUTES, D), (ROUTES, ROUTES), (2, 2, D), (2, D)]
    shapes = [layer.shape, ig.shape, gg.shape, ug.shape, dg.shape]
    shapes += [made[0], qg.shape, *made[1:], pg.shape]
    return pl.pallas_call(
        place_kernel,
        out_shape=[jax.ShapeDtypeStruct(shape, F32 if i else BF) for i, shape in enumerate(shapes)],
        in_specs=[ANY] * 9,
        out_specs=[ANY] * 14,
        scratch_shapes=[pltpu.VMEM(value.shape, value.dtype) for value in values]
        + [pltpu.VMEM((3, *gg.shape), F32)]
        + [pltpu.VMEM(shape, F32) for shape in made]
        + [pltpu.SemaphoreType.DMA((9,)), pltpu.SemaphoreType.DMA((14,))],
        compiler_params=pltpu.CompilerParams(vmem_limit_bytes=60 * MIB),
        cost_estimate=pl.CostEstimate(flops=0, bytes_accessed=16 * MIB, transcendentals=0),
        name="place_outputs",
    )(*values)


def on_device_heads(
    sizes,
    inputs,
    attn_gain,
    qkv_weight,
    out_weight,
    ffn_gain,
    router_weight,
    carry_weight,
    const_weight,
    const_vector,
    gate_weight,
    up_weight,
    down_weight,
    prev_logits,
    seq_lengths,
    expert_routes,
    cotangent,
):
    ranks, cols = sizes
    row_total = expert_routes.shape[0]
    depth = qkv_weight.shape[0]

    (
        w_all,
        qkv,
        mixed_heads,
        lse,
        whole_in,
        qkv_own,
        out_t,
        cosine,
        sines,
        meta,
        slots,
        mixed,
        middle,
        n2_whole,
        prev_whole,
        cot_early,
        rw,
        carry,
    ) = first_step(
        cols,
        ranks,
        inputs,
        cotangent,
        router_weight.T,
        const_weight.transpose(0, 2, 1),
        const_vector,
        attn_gain,
        ffn_gain,
        carry_weight,
        qkv_weight,
        out_weight,
        prev_logits,
        expert_routes.T,
        seq_lengths,
        gate_weight,
        up_weight,
        down_weight.transpose(0, 2, 1),
    )
    x, gu, y, gates, cot_late = experts_forward(
        cols, n2_whole.reshape(row_total, D), prev_whole, cotangent, rw, carry, meta, slots, w_all
    )
    dx, dots, mixsum, gown, sib, hsoon, glast = experts_backward(
        cols, ranks, cot_early, cot_late, y, gates, meta, slots, w_all, x, gu
    )
    layer_out, resid, gm, og, small, prev_grad, hin0, hrest, sib = resid_step(
        cols, dx, meta, dots, rw, prev_whole, carry, cotangent, mixsum, n2_whole, middle, out_t, mixed, gown, glast, sib
    )
    input_grad, small_all, qkv_grad, og_own, gate_grad, up_grad, down_grad, _ = finish_step(
        cols,
        ranks,
        gm,
        meta,
        lse,
        small,
        og,
        inputs,
        rw,
        qkv,
        mixed_heads,
        whole_in,
        qkv_own,
        cosine,
        sines,
        resid,
        gown,
        sib,
        hsoon,
        hin0,
        hrest,
    )
    layer_out, input_grad, gate_grad, up_grad, down_grad, again, qkv_grad, out_grad, fgain, router, carry, const, vector, prev = (
        place_outputs(small_all, qkv_grad, og_own, prev_grad, layer_out, input_grad, gate_grad, up_grad, down_grad)
    )
    return (
        layer_out,
        input_grad,
        again,
        qkv_grad,
        out_grad,
        fgain,
        router.T,
        carry,
        const.transpose(0, 2, 1),
        vector,
        gate_grad,
        up_grad,
        down_grad.transpose(0, 2, 1),
        prev,
    )


def solution(mesh):
    sizes = (mesh.shape["row"], mesh.shape["col"])
    body = functools.partial(on_device_heads, sizes) if sizes == (8, 4) else on_device
    placed = (
        P(("row", "col"), None),
        P(),
        P("row", "col"),
        P("col", "row"),
        P(),
        P(),
        P(),
        P(),
        P(),
        P(None, "row", "col"),
        P(None, "row", "col"),
        P(None, "col", "row"),
        P(None, ("row", "col")),
        P("row", None),
        P("row", None),
        P(("row", "col"), None),
    )
    return jax.shard_map(
        body,
        mesh=mesh,
        in_specs=placed,
        out_specs=(
            P(("row", "col"), None),
            P(("row", "col"), None),
            P(),
            P("row", "col"),
            P("col", "row"),
            P(),
            P(),
            P(),
            P(),
            P(),
            P(None, "row", "col"),
            P(None, "row", "col"),
            P(None, "col", "row"),
            P(None, ("row", "col")),
        ),
        check_vma=False,
    )
```

```python
import functools
import math

import jax
import jax.numpy as jnp
import numpy as np
from jax import lax
from jax.experimental import pallas as pl
from jax.experimental.pallas import tpu as pltpu
from jax.sharding import PartitionSpec as P

D = 768
HEADS = 12
HEAD_DIM = 64
EXPERTS = 8
ROUTES = 12


EPS = 1e-06
BASE = 10000.0
NEG = -1e30
HIGH = lax.Precision.HIGHEST
CONTRACT_FIRST = (((0,), (0,)), ((), ()))
CONTRACT_LAST = (((1,), (1,)), ((), ()))


def rotate(block_value, positions, first_col, direction):
    row_count, col_count = block_value.shape
    column = first_col + jnp.arange(0, col_count, 2, dtype=jnp.int32)
    inner_col = column % D
    section = column // D
    head_pair = inner_col % HEAD_DIM // 2
    exponent = (2 * head_pair).astype(jnp.float32) / HEAD_DIM
    frequency = jnp.exp(-exponent * math.log(BASE))
    turned_on = (section < 2).astype(jnp.float32)
    angles = positions.astype(jnp.float32)[:, None] * (frequency * turned_on)[None, :]
    cosine = jnp.cos(angles)
    sines = direction * jnp.sin(angles)
    paired = block_value.reshape(row_count, col_count // 2, 2)
    first_part = paired[:, :, 0]
    second_part = paired[:, :, 1]
    rotated = jnp.stack(
        [first_part * cosine - second_part * sines, second_part * cosine + first_part * sines],
        axis=2,
    )
    return rotated.reshape(row_count, col_count)


def sequence_info(lengths_row, row_total):
    seq_count = lengths_row.shape[0]
    ends = jnp.cumsum(lengths_row)
    starts = ends - lengths_row
    token_place = jnp.arange(row_total, dtype=jnp.int32)
    seq_index = jnp.sum((token_place[:, None] >= ends[None, :]).astype(jnp.int32), axis=1)
    member = seq_index[:, None] == jnp.arange(seq_count, dtype=jnp.int32)[None, :]
    begin = jnp.sum(jnp.where(member, starts[None, :], 0), axis=1)
    return (seq_index, token_place - begin, seq_index < seq_count)


def partial_sums(term_value):
    return lax.psum_scatter(
        term_value.astype(jnp.bfloat16), "col", scatter_dimension=0, tiled=True
    ).astype(jnp.float32)


def whole_columns(part_value):
    return lax.all_gather(part_value, "col", axis=0, tiled=True)


def to_heads(block_value):
    return lax.all_to_all(block_value, "col", split_axis=0, concat_axis=1, tiled=True)


def to_features(block_value):
    return lax.all_to_all(block_value, "col", split_axis=1, concat_axis=0, tiled=True)


def key_scores(query_heads, key_block, query_seq, query_place, key_seq, key_place, score_scale):
    raw_scores = (
        jnp.einsum("qhd,khd->hqk", query_heads, key_block, preferred_element_type=jnp.float32)
        * score_scale
    )
    allowed = (query_seq[:, None] == key_seq[None, :]) & (
        key_place[None, :] <= query_place[:, None]
    )
    return (jnp.where(allowed[None], raw_scores, NEG), allowed)


def split_keys(key_values, seq_index, token_place, block_rows):
    count_blocks = key_values.shape[0] // block_rows
    blocks_kv = key_values.reshape(count_blocks, block_rows, 2, HEADS, HEAD_DIM)
    return (
        blocks_kv,
        seq_index.reshape(count_blocks, block_rows),
        token_place.reshape(count_blocks, block_rows),
    )


def attend_forward(
    queries, key_values, query_seq, query_place, seq_index, token_place, block_rows, score_scale
):
    local_rows = queries.shape[0]
    query_heads = queries.reshape(local_rows, HEADS, HEAD_DIM)
    key_items = split_keys(key_values, seq_index, token_place, block_rows)

    def max_step(running, block_items):
        running_max, running_sum = running
        kv_block, key_seq, key_place = block_items
        scores, allowed = key_scores(
            query_heads, kv_block[:, 0], query_seq, query_place, key_seq, key_place, score_scale
        )
        new_max = jnp.maximum(running_max, jnp.max(scores, axis=2))
        shifted = jnp.where(allowed[None], jnp.exp(scores - new_max[:, :, None]), 0.0)
        new_sum = running_sum * jnp.exp(running_max - new_max) + jnp.sum(shifted, axis=2)
        return ((new_max, new_sum), None)

    start_state = (
        jnp.full((HEADS, local_rows), NEG, jnp.float32),
        jnp.zeros((HEADS, local_rows), jnp.float32),
    )
    (final_max, final_sum), unused = lax.scan(max_step, start_state, key_items)
    log_total = final_max + jnp.log(final_sum)

    def out_step(running, block_items):
        kv_block, key_seq, key_place = block_items
        scores, allowed = key_scores(
            query_heads, kv_block[:, 0], query_seq, query_place, key_seq, key_place, score_scale
        )
        probs_low = jnp.exp(scores - log_total[:, :, None]).astype(jnp.bfloat16)
        return (
            running
            + jnp.einsum(
                "hqk,khd->qhd", probs_low, kv_block[:, 1], preferred_element_type=jnp.float32
            ),
            None,
        )

    attended, unused = lax.scan(
        out_step, jnp.zeros((local_rows, HEADS, HEAD_DIM), jnp.float32), key_items
    )
    return (attended.reshape(local_rows, D), log_total)


def attend_backward(
    queries,
    key_values,
    log_total,
    row_delta,
    grad_heads_in,
    query_seq,
    query_place,
    seq_index,
    token_place,
    block_rows,
    score_scale,
):
    local_rows = queries.shape[0]
    query_heads = queries.reshape(local_rows, HEADS, HEAD_DIM)
    grad_heads = grad_heads_in.reshape(local_rows, HEADS, HEAD_DIM)
    key_items = split_keys(key_values, seq_index, token_place, block_rows)

    def grad_step(running, block_items):
        kv_block, key_seq, key_place = block_items
        scores, allowed = key_scores(
            query_heads, kv_block[:, 0], query_seq, query_place, key_seq, key_place, score_scale
        )
        probs_full = jnp.exp(scores - log_total[:, :, None])
        probs_low = probs_full.astype(jnp.bfloat16)
        grad_probs = jnp.einsum(
            "qhd,khd->hqk", grad_heads, kv_block[:, 1], preferred_element_type=jnp.float32
        )
        grad_scores = (probs_full * (grad_probs - row_delta[:, :, None])).astype(jnp.bfloat16)
        new_running = (
            running
            + jnp.einsum(
                "hqk,khd->qhd", grad_scores, kv_block[:, 0], preferred_element_type=jnp.float32
            )
            * score_scale
        )
        grad_keys = (
            jnp.einsum("hqk,qhd->khd", grad_scores, query_heads, preferred_element_type=jnp.float32)
            * score_scale
        )
        grad_values = jnp.einsum(
            "hqk,qhd->khd", probs_low, grad_heads, preferred_element_type=jnp.float32
        )
        return (new_running, jnp.stack([grad_keys, grad_values], axis=1))

    grad_queries, grad_kv = lax.scan(
        grad_step, jnp.zeros((local_rows, HEADS, HEAD_DIM), jnp.float32), key_items
    )
    return (grad_queries.reshape(local_rows, D), grad_kv.reshape(key_values.shape[0], 2 * D))


def on_device(
    inputs,
    attn_gain,
    qkv_weight,
    out_weight,
    ffn_gain,
    router_weight,
    carry_weight,
    const_weight,
    const_vector,
    gate_weight,
    up_weight,
    down_weight,
    prev_logits,
    seq_lengths,
    expert_routes,
    cotangent,
):
    col_index = lax.axis_index("col")
    row_total = expert_routes.shape[0]
    local_rows = inputs.shape[0]
    capacity = row_total // 4
    block_rows = min(row_total, 512)
    score_scale = 1.0 / math.sqrt(HEAD_DIM)
    full_weights = (
        lax.all_gather(qkv_weight, "row", axis=0, tiled=True),
        lax.all_gather(out_weight, "row", axis=1, tiled=True),
        lax.all_gather(gate_weight, "row", axis=1, tiled=True),
        lax.all_gather(up_weight, "row", axis=1, tiled=True),
        lax.all_gather(down_weight, "row", axis=2, tiled=True),
    )
    qkv_full, out_full, gate_full, up_full, down_full = full_weights
    whole_in, whole_cot, whole_prev = (
        lax.all_gather(inputs, "col", axis=0, tiled=True),
        lax.all_gather(cotangent, "col", axis=0, tiled=True),
        lax.all_gather(prev_logits, "col", axis=1, tiled=True),
    )
    seq_index, positions, valid_all = sequence_info(seq_lengths[0], row_total)
    token_place = jnp.arange(row_total, dtype=jnp.int32)
    first_row = col_index * local_rows

    def own_rows(whole_value):
        return lax.dynamic_slice_in_dim(whole_value, first_row, local_rows, 0)

    query_seq = own_rows(seq_index)
    query_place = own_rows(token_place)
    query_pos = own_rows(positions)
    query_valid = own_rows(valid_all).astype(jnp.float32)[:, None]
    input_rows = whole_in.astype(jnp.float32)
    attn_gain_full = attn_gain.astype(jnp.float32)
    scale_attn = lax.rsqrt(jnp.mean(input_rows * input_rows, axis=1, keepdims=True) + EPS)
    normed1 = (input_rows * scale_attn * attn_gain_full).astype(jnp.bfloat16)
    projected = jnp.dot(normed1, qkv_full, preferred_element_type=jnp.float32)
    turned = rotate(projected, positions, col_index * projected.shape[1], 1.0).astype(jnp.bfloat16)
    token_qkv = to_heads(turned)
    queries = token_qkv[:, :D]
    key_values = lax.all_gather(token_qkv[:, D:], "col", axis=0, tiled=True)
    attended, log_total = attend_forward(
        queries, key_values, query_seq, query_place, seq_index, token_place, block_rows, score_scale
    )
    attn_tok = (attended * query_valid).astype(jnp.bfloat16)
    attn_feat = to_features(attn_tok)
    attn_out = partial_sums(jnp.dot(attn_feat, out_full, preferred_element_type=jnp.float32))
    input_local = inputs.astype(jnp.float32)
    middle = input_local + attn_out
    scale_ffn = lax.rsqrt(jnp.mean(middle * middle, axis=1, keepdims=True) + EPS)
    ffn_gain_full = ffn_gain.astype(jnp.float32)
    normed2_local = (middle * scale_ffn * ffn_gain_full).astype(jnp.bfloat16)
    normed2 = whole_columns(normed2_local)
    carry_full = carry_weight.astype(jnp.float32)
    prev_rows = whole_prev.astype(jnp.float32).T
    route_hot = (
        expert_routes[:, :, None] == jnp.arange(ROUTES, dtype=jnp.int32)[None, None, :]
    ).astype(jnp.float32)
    logits = jnp.dot(normed2, router_weight, preferred_element_type=jnp.float32) + jnp.dot(
        prev_rows, carry_full, precision=HIGH
    )
    picked = jnp.sum(route_hot * logits[:, None, :], axis=2)
    gate_values = jax.nn.softmax(picked, axis=1)
    flat_route = expert_routes.reshape(-1)
    route_hits = (flat_route[:, None] == jnp.arange(EXPERTS, dtype=jnp.int32)[None, :]).astype(
        jnp.int32
    )
    slot_index = jnp.sum((jnp.cumsum(route_hits, axis=0) - 1) * route_hits, axis=1)
    dump_slot = EXPERTS * capacity
    target = jnp.where(flat_route < EXPERTS, flat_route * capacity + slot_index, dump_slot)
    slot_owner = (
        jnp.full((dump_slot + 1,), row_total, jnp.int32)
        .at[target]
        .set(jnp.arange(2 * row_total, dtype=jnp.int32) // 2)[:dump_slot]
    )
    slot_gate = (
        jnp.zeros((dump_slot + 1,), jnp.float32)
        .at[target]
        .set(gate_values.reshape(-1))[:dump_slot]
        .reshape(EXPERTS, capacity, 1)
    )
    zero_row = jnp.zeros((1, D), jnp.bfloat16)
    expert_in = jnp.concatenate([normed2, zero_row], axis=0)[slot_owner].reshape(
        EXPERTS, capacity, D
    )
    gate_pre = jnp.einsum("ecd,edf->ecf", expert_in, gate_full, preferred_element_type=jnp.float32)
    up_pre = jnp.einsum("ecd,edf->ecf", expert_in, up_full, preferred_element_type=jnp.float32)
    sigmoid_gate = jax.nn.sigmoid(gate_pre)
    activated = gate_pre * sigmoid_gate
    hidden = (activated * up_pre).astype(jnp.bfloat16)
    expert_out = jnp.einsum("ecf,efd->ecd", hidden, down_full, preferred_element_type=jnp.float32)
    out_rows = jnp.concatenate(
        [expert_out.reshape(dump_slot, D), jnp.zeros((1, D), jnp.float32)], axis=0
    )
    chosen_out = out_rows[target].reshape(row_total, 2, D)
    cot_rows = whole_cot.astype(jnp.float32)
    ffn_mix = jnp.sum(gate_values[:, :, None] * chosen_out, axis=1)
    ffn_dots = jnp.sum(cot_rows[:, None, :] * chosen_out, axis=2)
    mix_local = partial_sums(ffn_mix)
    normed_local = normed2_local.astype(jnp.float32)
    vector_full = const_vector.astype(jnp.float32)
    routes_local = own_rows(expert_routes)
    gates_local = own_rows(gate_values)
    hot_local = own_rows(route_hot)
    copy_hit = (routes_local == EXPERTS + 1).astype(jnp.float32)
    const_hit = (
        routes_local[:, :, None] == (EXPERTS + 2 + jnp.arange(2, dtype=jnp.int32))[None, None, :]
    ).astype(jnp.float32)
    copy_share = jnp.sum(gates_local * copy_hit, axis=1)
    const_share = jnp.sum(gates_local[:, :, None] * const_hit, axis=1)
    const_alpha = jax.nn.softmax(
        jnp.einsum("td,jdk->tjk", normed2_local, const_weight, preferred_element_type=jnp.float32),
        axis=2,
    )
    keep_share = copy_share + jnp.sum(const_share * const_alpha[:, :, 0], axis=1)
    local_mix = keep_share[:, None] * normed_local + jnp.dot(
        const_share * const_alpha[:, :, 1], vector_full, precision=HIGH
    )
    layer_out = (middle + mix_local + local_mix).astype(jnp.bfloat16)
    qkv_full, out_full, gate_full, up_full, down_full = full_weights
    ffn_total = lax.psum(ffn_dots, "col")
    ffn_local = own_rows(ffn_total)
    cot_local = cotangent.astype(jnp.float32)
    dot_keep = jnp.sum(cot_local * normed_local, axis=1)
    dot_vector = jnp.dot(cot_local, vector_full.T, precision=HIGH)
    const_dots = const_alpha[:, :, 0] * dot_keep[:, None] + const_alpha[:, :, 1] * dot_vector
    grad_gates = (
        ffn_local
        + copy_hit * dot_keep[:, None]
        + jnp.sum(const_hit * const_dots[:, None, :], axis=2)
    )
    grad_picked = gates_local * (
        grad_gates - jnp.sum(gates_local * grad_gates, axis=1, keepdims=True)
    )
    grad_logits = jnp.sum(hot_local * grad_picked[:, :, None], axis=1)
    prev_local = prev_logits.astype(jnp.float32).T
    router_grad = lax.dot_general(normed_local, grad_logits, CONTRACT_FIRST, precision=HIGH)
    carry_grad = lax.dot_general(prev_local, grad_logits, CONTRACT_FIRST, precision=HIGH)
    prev_grad = lax.dot_general(carry_full, grad_logits, CONTRACT_LAST, precision=HIGH)
    grad_alpha_keep = const_share * dot_keep[:, None]
    grad_alpha_vector = const_share * dot_vector
    alpha_mean = const_alpha[:, :, 0] * grad_alpha_keep + const_alpha[:, :, 1] * grad_alpha_vector
    grad_alpha_logits = jnp.stack(
        [
            const_alpha[:, :, 0] * (grad_alpha_keep - alpha_mean),
            const_alpha[:, :, 1] * (grad_alpha_vector - alpha_mean),
        ],
        axis=2,
    )
    const_grad = jnp.einsum("td,tjk->jdk", normed_local, grad_alpha_logits, precision=HIGH)
    vector_grad = lax.dot_general(
        const_share * const_alpha[:, :, 1], cot_local, CONTRACT_FIRST, precision=HIGH
    )
    router_full = router_weight.astype(jnp.float32)
    const_full = const_weight.astype(jnp.float32)
    grad_normed_local = (
        keep_share[:, None] * cot_local
        + lax.dot_general(grad_logits, router_full, CONTRACT_LAST, precision=HIGH)
        + jnp.einsum("tjk,jdk->td", grad_alpha_logits, const_full, precision=HIGH)
    )
    cot_in = jnp.concatenate([whole_cot, zero_row], axis=0)[slot_owner].reshape(
        EXPERTS, capacity, D
    )
    grad_expert = (slot_gate * cot_in.astype(jnp.float32)).astype(jnp.bfloat16)
    down_grad = jnp.einsum("ecf,ecd->efd", hidden, grad_expert, preferred_element_type=jnp.float32)
    grad_hidden = jnp.einsum(
        "ecd,efd->ecf", grad_expert, down_full, preferred_element_type=jnp.float32
    )
    grad_gate_pre = (
        grad_hidden * up_pre * sigmoid_gate * (1.0 + gate_pre * (1.0 - sigmoid_gate))
    ).astype(jnp.bfloat16)
    grad_up_pre = (grad_hidden * activated).astype(jnp.bfloat16)
    gate_grad = jnp.einsum(
        "ecd,ecf->edf", expert_in, grad_gate_pre, preferred_element_type=jnp.float32
    )
    up_grad = jnp.einsum("ecd,ecf->edf", expert_in, grad_up_pre, preferred_element_type=jnp.float32)
    grad_expert_in = jnp.einsum(
        "ecf,edf->ecd", grad_gate_pre, gate_full, preferred_element_type=jnp.float32
    ) + jnp.einsum("ecf,edf->ecd", grad_up_pre, up_full, preferred_element_type=jnp.float32)
    grad_slots = jnp.concatenate(
        [grad_expert_in.reshape(dump_slot, D), jnp.zeros((1, D), jnp.float32)], axis=0
    )
    grad_tokens = jnp.sum(grad_slots[target].reshape(row_total, 2, D), axis=1)
    grad_normed = partial_sums(grad_tokens) + grad_normed_local
    gained_ffn = grad_normed * ffn_gain_full
    ffn_dots_rows = jnp.sum(gained_ffn * middle, axis=1, keepdims=True)
    grad_middle = scale_ffn * gained_ffn - middle * scale_ffn**3 * (ffn_dots_rows / D)
    ffn_gain_grad = jnp.sum(grad_normed * middle * scale_ffn, axis=0)
    grad_resid = cot_local + grad_middle
    branch_cot = whole_columns(grad_resid.astype(jnp.bfloat16))
    out_grad = lax.dot_general(
        attn_feat, branch_cot, CONTRACT_FIRST, preferred_element_type=jnp.float32
    )
    grad_mixed = lax.dot_general(
        branch_cot, out_full, CONTRACT_LAST, preferred_element_type=jnp.float32
    )
    grad_tok = to_heads(grad_mixed.astype(jnp.bfloat16))
    grad_heads_in = (grad_tok.astype(jnp.float32) * query_valid).astype(jnp.bfloat16)
    row_delta = jnp.sum(
        grad_heads_in.astype(jnp.float32).reshape(local_rows, HEADS, HEAD_DIM)
        * attended.reshape(local_rows, HEADS, HEAD_DIM),
        axis=2,
    ).T
    grad_queries, grad_kv = attend_backward(
        queries,
        key_values,
        log_total,
        row_delta,
        grad_heads_in,
        query_seq,
        query_place,
        seq_index,
        token_place,
        block_rows,
        score_scale,
    )
    grad_kv_local = lax.psum_scatter(
        grad_kv.astype(jnp.bfloat16), "col", scatter_dimension=0, tiled=True
    ).astype(jnp.float32)
    grad_turned = jnp.concatenate([grad_queries, grad_kv_local], axis=1)
    grad_proj_tok = rotate(grad_turned, query_pos, 0, -1.0).astype(jnp.bfloat16)
    grad_projected = to_features(grad_proj_tok)
    qkv_grad = lax.dot_general(
        normed1, grad_projected, CONTRACT_FIRST, preferred_element_type=jnp.float32
    )
    grad_normed1 = partial_sums(
        lax.dot_general(grad_projected, qkv_full, CONTRACT_LAST, preferred_element_type=jnp.float32)
    )
    scale_attn_local = own_rows(scale_attn)
    gained_attn = grad_normed1 * attn_gain_full
    attn_dots_rows = jnp.sum(gained_attn * input_local, axis=1, keepdims=True)
    input_grad = (
        grad_resid
        + scale_attn_local * gained_attn
        - input_local * scale_attn_local**3 * (attn_dots_rows / D)
    )
    attn_gain_grad = jnp.sum(grad_normed1 * input_local * scale_attn_local, axis=0)
    qkv_grad, out_grad, gate_grad, up_grad, down_grad = (
        lax.psum_scatter(
            qkv_grad.astype(jnp.bfloat16), "row", scatter_dimension=0, tiled=True
        ).astype(jnp.float32),
        lax.psum_scatter(
            out_grad.astype(jnp.bfloat16), "row", scatter_dimension=1, tiled=True
        ).astype(jnp.float32),
        lax.psum_scatter(
            gate_grad.astype(jnp.bfloat16), "row", scatter_dimension=1, tiled=True
        ).astype(jnp.float32),
        lax.psum_scatter(
            up_grad.astype(jnp.bfloat16), "row", scatter_dimension=1, tiled=True
        ).astype(jnp.float32),
        lax.psum_scatter(
            down_grad.astype(jnp.bfloat16), "row", scatter_dimension=2, tiled=True
        ).astype(jnp.float32),
    )
    attn_gain_grad, ffn_gain_grad, router_grad, carry_grad, const_grad, vector_grad = lax.psum(
        (attn_gain_grad, ffn_gain_grad, router_grad, carry_grad, const_grad, vector_grad),
        ("row", "col"),
    )
    return (
        layer_out,
        input_grad,
        attn_gain_grad,
        qkv_grad,
        out_grad,
        ffn_gain_grad,
        router_grad,
        carry_grad,
        const_grad,
        vector_grad,
        gate_grad,
        up_grad,
        down_grad,
        prev_grad,
    )


BF = jnp.bfloat16
F32 = jnp.float32
LANES = 128
NN = (((1,), (0,)), ((), ()))
NT = (((1,), (1,)), ((), ()))
TN = (((0,), (0,)), ((), ()))
ROW_CONST = 12
ROW_VEC = 16
ROW_GAIN = 18
SMALL_ROWS = 24
Q_ROWS = 256
MIB = 1 << 20


def mm(a, b, dims=NN):
    return lax.dot_general(a, b, dims, preferred_element_type=F32)


def lane_iota(shape):
    return lax.broadcasted_iota(jnp.int32, shape, len(shape) - 1)


def whole(shape):
    return pl.BlockSpec(tuple(shape), lambda *_: (0,) * len(shape), pipeline_mode=pl.Buffered(1))


def swap_pairs(v):
    even = lane_iota(v.shape) % 2 == 0
    return jnp.where(even, pltpu.roll(v, LANES - 1, 1), pltpu.roll(v, 1, 1))


def norm_rows(x):
    return lax.rsqrt(jnp.mean(x * x, axis=1, keepdims=True) + EPS)


def seen(begin, first, rows, length):
    u = lax.broadcasted_iota(jnp.int32, (rows, length), 1)
    t = lax.broadcasted_iota(jnp.int32, (rows, length), 0) + first
    return (u >= begin) & (u <= t)


def gate_lanes(logits, meta):
    lane = lane_iota(logits.shape)
    hit = (pltpu.roll(meta, LANES - META_HIT, 1) > 0.0) & (lane < ROUTES)
    held = jnp.where(hit, logits, NEG)
    e = jnp.where(hit, jnp.exp(held - jnp.max(held, axis=1, keepdims=True)), 0.0)
    return e / jnp.sum(e, axis=1, keepdims=True)


MESH = pl.DeviceIdType.MESH
ANY = pl.BlockSpec(memory_space=pl.ANY)


def place():
    return lax.axis_index("row"), lax.axis_index("col")


def flip(index, mask):
    for bit in (1, 2, 4):
        if mask & bit:
            index = index + bit - 2 * bit * (index // bit % 2)
    return index


def greet(devices):
    barrier = pltpu.get_barrier_semaphore()
    for device in devices:
        pl.semaphore_signal(barrier, inc=1, device_id=device, device_id_type=MESH)
    pl.semaphore_wait(barrier, len(devices))


def send_to(src, dst, send, recv, device):
    return pltpu.make_async_remote_copy(
        src_ref=src, dst_ref=dst, send_sem=send, recv_sem=recv, device_id=device, device_id_type=MESH
    )


def col_peers(n):
    r, c = place()
    return [(r, (c + k) % n) for k in range(1, n)]


def gather_chain(own, dst, send, recv, n):
    r, c = place()

    def right(k):
        i = jnp.maximum(c - k, 0)
        src = own if k == 0 else dst.at[i]
        return send_to(src, dst.at[i], send.at[0, k], recv.at[0, k], (r, jnp.minimum(c + 1, n - 1)))

    def left(k):
        i = jnp.minimum(c + k, n - 1)
        src = own if k == 0 else dst.at[i]
        return send_to(src, dst.at[i], send.at[1, k], recv.at[1, k], (r, jnp.maximum(c - 1, 0)))

    def step(k):
        if k > 0:

            @pl.when(c >= k)
            def _():
                right(k - 1).wait_recv()

            @pl.when(c + k < n)
            def _():
                left(k - 1).wait_recv()

        if k < n - 1:

            @pl.when((c >= k) & (c + 1 < n))
            def _():
                right(k).start()

            @pl.when((c + k < n) & (c >= 1))
            def _():
                left(k).start()

    def drain():
        for k in range(n - 1):

            @pl.when((c >= k) & (c + 1 < n))
            def _():
                right(k).wait_send()

            @pl.when((c + k < n) & (c >= 1))
            def _():
                left(k).wait_send()

    return step, drain


def reduce_chain(own, out, arrived, send, recv, n):
    r, c = place()

    def right(k):
        return send_to(out.at[0, k], arrived.at[0, k], send.at[0, k], recv.at[0, k], (r, jnp.minimum(c + 1, n - 1)))

    def left(k):
        return send_to(out.at[1, k], arrived.at[1, k], send.at[1, k], recv.at[1, k], (r, jnp.maximum(c - 1, 0)))

    def slot(s):
        if s == n - 1:

            @pl.when(c >= 1)
            def _():
                right(n - 1 - c).wait_recv()

            @pl.when(c <= n - 2)
            def _():
                left(c).wait_recv()

            return

        @pl.when(c <= s)
        def _():
            k = jnp.maximum(s - c, 0)

            @pl.when(c >= 1)
            def _():
                right(k).wait_recv()
                out[0, k] = (own(n - 1 - k).astype(F32) + arrived[0, k].astype(F32)).astype(BF)

            @pl.when(c == 0)
            def _():
                out[0, k] = own(n - 1 - k).astype(BF)

            right(k).start()

        @pl.when(n - 1 - c <= s)
        def _():
            k = jnp.maximum(s - (n - 1 - c), 0)

            @pl.when(c <= n - 2)
            def _():
                left(k).wait_recv()
                out[1, k] = (own(k).astype(F32) + arrived[1, k].astype(F32)).astype(BF)

            @pl.when(c == n - 1)
            def _():
                out[1, k] = own(k).astype(BF)

            left(k).start()

    def total(dst):
        dst[...] = own(c).astype(F32)

        @pl.when(c >= 1)
        def _():
            dst[...] += arrived[0, n - 1 - c].astype(F32)

        @pl.when(c <= n - 2)
        def _():
            dst[...] += arrived[1, c].astype(F32)

    def drain():
        for k in range(n - 1):

            @pl.when(c < n - 1 - k)
            def _():
                right(k).wait_send()

            @pl.when(c > k)
            def _():
                left(k).wait_send()

    return slot, total, drain


def chain_scratch(n, rows):
    return [
        pltpu.VMEM((2, n - 1, rows, D), BF),
        pltpu.VMEM((2, n - 1, rows, D), BF),
        pltpu.SemaphoreType.DMA((2, n - 1)),
        pltpu.SemaphoreType.DMA((2, n - 1)),
    ]


def slot_rows(slots_ref, e, capacity):
    rows = slots_ref.shape[1]
    spots = lax.broadcasted_iota(jnp.int32, (capacity, rows), 0)
    return jnp.where(spots == slots_ref[pl.ds(e, 1)], 1.0, 0.0).astype(BF)


def slot_gates(one, gates_ref, e):
    sg = mm(one, gates_ref[...])
    return jnp.sum(jnp.where(lane_iota(sg.shape) % LANES == e, sg, 0.0), axis=1, keepdims=True)


def chain_order(c):
    return [d + (3 - 2 * d) * (c // 2) for d in (3, 2, 0, 1)]


def combine(meta_ref, y_ref, d, local):
    experts, capacity, width = y_ref.shape
    at = pl.ds(pl.multiple_of(d * local, LANES), local)
    lane = lane_iota((local, capacity)).astype(F32)
    ones = [jnp.where(lane == column(meta_ref, at, e), 1.0, 0.0).astype(BF) for e in range(experts)]
    return mm(jnp.concatenate(ones, axis=1), y_ref[...].reshape(experts * capacity, width)).astype(BF)


META_HIT, META_BEGIN, META_VALID = 8, 20, 21
EARLY = 6
SENT_SOON, SENT_NEXT = 2, 3


def column(ref, at, lane):
    return ref[at, lane : lane + 1]


def start_all(copies):
    for copy in copies:
        copy.start()


def wait_all(copies):
    for copy in copies:
        copy.wait()


def moves(pairs, sem):
    return [pltpu.make_async_copy(src, dst, sem.at[i]) for i, (src, dst) in enumerate(pairs)]


def pack_head(value):
    half = value.shape[0] // 2
    return jnp.concatenate([value[:half], value[half:]], axis=1)


def unpack_head(packed):
    return jnp.concatenate([packed[:, :HEAD_DIM], packed[:, HEAD_DIM:]], axis=0)


def to_rows(src_of, dst, send, recv, ranks):
    r, c = place()
    copies = []
    for m in range(1, ranks):
        there = flip(r, m)
        copies.append(send_to(src_of(there), dst.at[r], send.at[m - 1], recv.at[m - 1], (there, c)))
    return copies


def to_cols(src_of, dst, send, recv, n):
    r, c = place()
    copies = []
    for k in range(1, n):
        there = (c + k) % n
        copies.append(send_to(src_of(there), dst.at[c], send.at[k - 1], recv.at[k - 1], (r, there)))
    return copies


def to_chips(src_of, dst, send, recv):
    r, c = place()
    return [
        send_to(src_of(flip(r // 2, k)), dst.at[k - 1], send.at[k - 1], recv.at[k - 1], (flip(r, 2 * k), c))
        for k in range(1, 4)
    ]


def all_sum(ref, count):
    total = ref[0].astype(F32)
    for i in range(1, count):
        total = total + ref[i].astype(F32)
    return total


def tokens_meta(routes_ref, lengths_ref, rows, experts):
    kinds = lax.broadcasted_iota(jnp.int32, (16, rows), 0)
    hits = jnp.where((kinds == routes_ref[0:1]) | (kinds == routes_ref[1:2]), 1.0, 0.0)
    step = 256
    earlier = lax.broadcasted_iota(jnp.int32, (step, step), 0) < lax.broadcasted_iota(
        jnp.int32, (step, step), 1
    )
    earlier = jnp.where(earlier, 1.0, 0.0).astype(BF)
    counts, running = [], jnp.zeros((16, 1), F32)
    for b in range(rows // step):
        block = hits[:, b * step : (b + 1) * step]
        counts.append(mm(block.astype(BF), earlier) + running)
        running = running + jnp.sum(block, axis=1, keepdims=True)
    slots = jnp.where(hits > 0.0, jnp.concatenate(counts, axis=1), -1.0)[:experts]
    spot = lax.broadcasted_iota(jnp.int32, (8, rows), 1)
    begin, end = jnp.zeros((8, rows), F32), 0
    for i in range(lengths_ref.shape[1]):
        end = end + lengths_ref[0, i]
        begin = jnp.where(spot >= end, end.astype(F32), begin)
    valid = jnp.where(spot < end, 1.0, 0.0)
    tail = jnp.where(lax.broadcasted_iota(jnp.int32, (8, rows), 0) == 0, begin, valid)
    spare = jnp.zeros((LANES - experts - 12 - 8, rows), F32)
    meta = jnp.concatenate([slots, hits[:12], tail, spare], axis=0).T
    return slots.astype(jnp.int32), meta


def first_kernel(
    cols,
    ranks,
    x_ref,
    cot_ref,
    router_ref,
    const_ref,
    vector_ref,
    again_ref,
    fgain_ref,
    carry_ref,
    wq_ref,
    wo_ref,
    prev_ref,
    routes_ref,
    lengths_ref,
    cos_in,
    sin_in,
    freq_ref,
    gate_ref,
    up_ref,
    down_ref,
    wall_ref,
    qkv_out,
    o_out,
    lse_out,
    xw_out,
    wq_out,
    wo_out,
    cos_out,
    sin_out,
    meta_out,
    slots_ref,
    mixed_out,
    middle_out,
    n2w_ref,
    prevw_out,
    cota_ref,
    rw_out,
    carry_out,
    xw,
    q_parts,
    q_land,
    o_parts,
    o_land,
    wq,
    wo,
    a_send,
    a_land,
    prev_s,
    prevw,
    qkv_s,
    o_s,
    lse_s,
    cos_s,
    sin_s,
    meta_s,
    mixed_s,
    middle_s,
    n2_s,
    w_s,
    local_sem,
    x_send,
    x_recv,
    n_send,
    n_recv,
    t_send,
    t_recv,
    q_send,
    q_recv,
    c_send,
    c_recv,
    r_send,
    r_recv,
    e_send,
    e_recv,
    d_send,
    d_recv,
    s_send,
    s_recv,
    h_send,
    h_recv,
    cos_ref,
    sin_ref,
    soon_sem,
):
    r, c = place()
    heads = 3
    local = x_ref.shape[0]
    rows = local * cols
    width = heads * HEAD_DIM
    depth = D // ranks
    odd, high = c % 2, c // 2
    again = again_ref[...].astype(F32).reshape(1, D)
    fgain = fgain_ref[...].astype(F32).reshape(1, D)
    soon = moves([(cos_in, cos_ref), (sin_in, sin_ref)], soon_sem)
    start_all(soon)
    greet(col_peers(cols) + [(flip(r, m), c) for m in (1, 2, 4, 6)])

    for s in range(3):
        q_parts[s] = wq_ref[:, s * width : (s + 1) * width]
    q_copies = [
        send_to(q_parts.at[1], q_land.at[(c + 1) // 2], q_send.at[0], q_recv.at[0], (r, flip(c, 1))),
        send_to(q_parts.at[2 - 2 * odd], q_land.at[2 * high], q_send.at[1], q_recv.at[1], (r, flip(c, 2))),
    ]
    start_all(q_copies)
    x_step, x_drain = gather_chain(x_ref, xw, x_send, x_recv, cols)
    x_step(0)
    o_parts[...] = wo_ref[...].astype(F32).T.astype(BF)
    prev_s[...] = jnp.concatenate([prev_ref[...].astype(F32), jnp.zeros((16 - ROUTES, local), F32)], axis=0).astype(BF)
    o_copies = to_cols(lambda d: o_parts, o_land, c_send.at[0], c_recv.at[0], cols)
    prev_copies = to_cols(lambda d: prev_s, prevw, c_send.at[1], c_recv.at[1], cols)
    start_all(o_copies + prev_copies)
    q_land[(c + 1) // 2] = q_parts[2 * odd]
    o_land[c] = o_parts[...]
    prevw[c] = prev_s[...]
    xw[c] = x_ref[...]

    def rows_at(d):
        return pl.ds(pl.multiple_of(d * depth, 16), depth)

    def push(ref, at):
        here = ref.at[rows_at(r)]
        return [
            send_to(here, here, r_send.at[at, k - 1], r_recv.at[at, k - 1], (flip(r, 2 * k), c))
            for k in range(1, 4)
        ]

    def hand(ref, at):
        copies = []
        for k in range(4):
            here = ref.at[rows_at(flip(r, 2 * k))]
            copies.append(send_to(here, here, r_send.at[at, 3 + k], r_recv.at[at, 3 + k], (flip(r, 1), c)))
        return copies

    wait_all(q_copies)
    wq[rows_at(r)] = jnp.concatenate([q_land[i] for i in range(3)], axis=1)
    wq_push, wq_hand = push(wq, 0), hand(wq, 0)
    start_all(wq_push)
    wait_all(o_copies)
    wo[rows_at(r)] = jnp.concatenate([o_land[i] for i in range(cols)], axis=1)
    wo_push, wo_hand = push(wo, 1), hand(wo, 1)
    start_all(wo_push)

    weights = (gate_ref, up_ref, down_ref)
    half = gate_ref.shape[0] // 2
    held = moves([(ref, w_s.at[t]) for t, ref in enumerate(weights)], local_sem)
    kept = moves([(w_s.at[t], wall_ref.at[t, :, rows_at(r)]) for t in range(3)], local_sem)

    def to_near(t):
        dst = wall_ref.at[t, :, rows_at(r)]
        return [
            send_to(weights[t], dst, e_send.at[t, k - 1], e_recv.at[t, k - 1], (flip(r, 2 * k), c))
            for k in (1, 2)
        ]

    def to_far(t):
        copies = []
        for k in (1, 2):
            here = wall_ref.at[t, pl.ds((k - 1) * half, half), rows_at(flip(r, 2 * k))]
            copies.append(send_to(here, here, d_send.at[t, k - 1], d_recv.at[t, k - 1], (flip(r, 6 - 2 * k), c)))
        return copies

    def to_other_core(t):
        copies = []
        for k in range(4):
            here = wall_ref.at[t, :, rows_at(flip(r, 2 * k))]
            src = weights[t] if k == 0 else here
            copies.append(send_to(src, here, s_send.at[t, k], s_recv.at[t, k], (flip(r, 1), c)))
        return copies

    def relay(t):
        for near, far, across in zip(to_near(t), to_far(t), to_other_core(t)[1:3]):
            near.wait_recv()
            far.start()
            across.start()

    def hand_over(t):
        for far in to_far(t):
            far.wait_recv()
        to_other_core(t)[3].start()

    for t in range(3):
        start_all(to_near(t))
        to_other_core(t)[0].start()
    start_all(held)

    small = [ref[...].astype(F32) for ref in (router_ref, const_ref.at[0], const_ref.at[1], vector_ref)]
    small += [again, fgain, jnp.zeros((LANES - ROW_GAIN - 2, D), F32)]
    rw_out[...] = jnp.concatenate(small, axis=0).astype(BF)
    carry = jnp.concatenate([carry_ref[...].astype(F32), jnp.zeros((ROUTES, LANES - ROUTES), F32)], axis=1)
    carry_out[...] = jnp.concatenate([carry, jnp.zeros((16 - ROUTES, LANES), F32)], axis=0).astype(BF)
    slots, meta = tokens_meta(routes_ref, lengths_ref, rows, EXPERTS)
    slots_ref[...] = slots
    meta_s[...] = meta
    sub = lax.broadcasted_iota(jnp.int32, (8, LANES), 0)
    firsts, end, ends = jnp.zeros((8, LANES), F32), 0, []
    for i in range(lengths_ref.shape[1]):
        firsts = jnp.where(sub == i, jnp.asarray(end, jnp.int32).astype(F32), firsts)
        end = end + lengths_ref[0, i]
        ends.append(end)
    angle = firsts * freq_ref[...]
    cos_first, sin_first = jnp.cos(angle), jnp.sin(angle)
    spot = lax.broadcasted_iota(jnp.int32, (rows, LANES), 0)
    cb, sb = jnp.ones((rows, LANES), F32), jnp.zeros((rows, LANES), F32)
    for i in range(1, len(ends)):
        cb = jnp.where(spot >= ends[i - 1], cos_first[i : i + 1], cb)
        sb = jnp.where(spot >= ends[i - 1], sin_first[i : i + 1], sb)
    cb, sb = jnp.where(spot >= end, 1.0, cb), jnp.where(spot >= end, 0.0, sb)
    sign = jnp.where(lane_iota((rows, LANES)) % 2 == 0, -1.0, 1.0)
    wait_all(soon)
    cos_s[...] = cos_ref[...] * cb + sin_ref[...] * sb
    sin_s[...] = (sin_ref[...] * cb - cos_ref[...] * sb) * sign
    lse_s[...] = jnp.zeros_like(lse_s)

    def project(d):
        at = pl.ds(pl.multiple_of(d * local, LANES), local)
        x = xw[d].astype(F32)
        normed = (x * norm_rows(x) * again).astype(BF)
        proj = mm(normed, wq[...])
        cosine, sines = cos_s[at], sin_s[at]
        for part in range(2 * width // LANES):
            v = proj[:, part * LANES : (part + 1) * LANES]
            t = v * cosine + swap_pairs(v) * sines
            for side in range(2):
                head = 2 * part + side
                piece = t[:, side * HEAD_DIM : (side + 1) * HEAD_DIM].astype(BF)
                if head < heads:
                    piece = piece * jnp.asarray(1.0 / math.sqrt(HEAD_DIM), BF)
                qkv_s[head, at] = piece
        for head in range(2 * heads, 3 * heads):
            qkv_s[head, at] = proj[:, head * HEAD_DIM : (head + 1) * HEAD_DIM].astype(BF)

    def project_at(k):
        def side(way, carry):
            d = c + k * (2 * way - 1)

            @pl.when((d >= 0) & (d < cols))
            def _():
                project(jnp.clip(d, 0, cols - 1))

            return carry

        lax.fori_loop(0, 2 if k else 1, side, 0)

    early = local // EARLY
    cot_step, cot_drain = gather_chain(cot_ref.at[pl.ds(0, early)], cota_ref, t_send, t_recv, cols)
    cot_kept = moves([(cot_ref.at[pl.ds(0, early)], cota_ref.at[c])], local_sem.at[pl.ds(3, 1)])

    wait_all(held)
    start_all(kept)
    x_step(1)
    for copy in wq_push:
        copy.wait_recv()
    start_all(wq_hand)
    x_step(2)
    for copy in wo_push:
        copy.wait_recv()
    start_all(wo_hand)
    wait_all(wq_hand)
    project_at(0)
    project_at(1)
    project_at(2)
    relay(0)
    x_step(3)
    cot_step(0)
    start_all(cot_kept)
    project_at(3)
    cot_step(1)

    blocks = rows // Q_ROWS

    def head_copies(h):
        copies = []
        for k in range(1, cols):
            there = (c + k) % cols
            copies.append(
                send_to(a_send.at[there, h], a_land.at[c, h], h_send.at[h, k - 1], h_recv.at[h, k - 1], (r, there))
            )
        return copies

    def one_head(h, carry):
        for i in range(blocks):
            at = slice(i * Q_ROWS, (i + 1) * Q_ROWS)
            length = (i + 1) * Q_ROWS
            s = mm(qkv_s[h, at], qkv_s[heads + h, :length], NT)
            begin = column(meta_s, at, META_BEGIN).astype(jnp.int32)
            s = jnp.where(seen(begin, i * Q_ROWS, Q_ROWS, length), s, NEG)
            top = jnp.max(s, axis=1, keepdims=True)
            p = jnp.exp(s - top)
            total = jnp.sum(p, axis=1, keepdims=True)
            o = mm(p.astype(BF), qkv_s[2 * heads + h, :length]) * (column(meta_s, at, META_VALID) / total)
            o_s[h, at] = o.astype(BF)
            lse_s[at] = jnp.where(lane_iota((Q_ROWS, LANES)) == h, top + jnp.log(total), lse_s[at])
        for d in range(cols):
            a_send[d, h] = pack_head(o_s[h, d * local : (d + 1) * local])
        start_all(head_copies(h))
        return carry

    lax.fori_loop(0, 1, one_head, 0)
    cot_step(2)
    lax.fori_loop(1, heads, one_head, 0)
    a_land[c] = a_send[c]
    stored = moves(
        [
            (xw, xw_out),
            (wq, wq_out),
            (qkv_s, qkv_out),
            (o_s, o_out),
            (lse_s, lse_out),
            (cos_s, cos_out),
            (sin_s, sin_out),
            (meta_s, meta_out),
        ],
        local_sem.at[pl.ds(4, 8)],
    )
    start_all(stored)
    relay(1)
    wait_all(wo_hand)
    for h in range(heads):
        wait_all(head_copies(h))
    mixed = jnp.concatenate([unpack_head(a_land[i, h]) for i in range(cols) for h in range(heads)], axis=1)
    mixed_s[...] = mixed
    middle = x_ref[...].astype(F32) + mm(mixed, wo[...], NT)
    middle_s[...] = middle
    n2_s[...] = (middle * norm_rows(middle) * fgain).astype(BF)
    n_step, n_drain = gather_chain(n2_s, n2w_ref, n_send, n_recv, cols)
    n_step(0)
    wait_all(prev_copies)
    stored_late = moves(
        [(n2_s, n2w_ref.at[c]), (wo, wo_out), (mixed_s, mixed_out), (middle_s, middle_out), (prevw, prevw_out)],
        local_sem.at[pl.ds(12, 5)],
    )
    start_all(stored_late)
    relay(2)
    n_step(1)
    hand_over(0)
    n_step(2)
    hand_over(1)
    hand_over(2)
    n_step(3)
    cot_step(3)
    x_drain()
    n_drain()
    cot_drain()
    for copy in wq_push + wo_push:
        copy.wait_send()
    for t in range(3):
        for copy in to_near(t) + to_far(t):
            copy.wait_send()
        wait_all(to_other_core(t))
    wait_all(kept + cot_kept + stored + stored_late)


def first_step(cols, ranks, x, cot, router, const, vector, again, fgain, carry, wq, wo, prev, routes, lengths, gate, up, down):
    local = x.shape[0]
    rows = local * cols
    heads, width = 3, 3 * HEAD_DIM
    experts, depth, ff = gate.shape
    spots = np.arange(rows, dtype=np.float64)[:, None]
    pair = np.arange(LANES) % HEAD_DIM // 2
    freq = np.exp(-(2.0 * pair / HEAD_DIM) * math.log(BASE))[None, :]
    tables = [np.cos(spots * freq), np.sin(spots * freq), freq]
    tables = [jnp.asarray(value.astype(np.float32)) for value in tables]
    vm = pl.BlockSpec(memory_space=pltpu.VMEM)
    dma = pltpu.SemaphoreType.DMA
    return pl.pallas_call(
        functools.partial(first_kernel, cols, ranks),
        out_shape=(
            jax.ShapeDtypeStruct((3, experts, D, ff), BF),
            jax.ShapeDtypeStruct((3 * heads, rows, HEAD_DIM), BF),
            jax.ShapeDtypeStruct((heads, rows, HEAD_DIM), BF),
            jax.ShapeDtypeStruct((rows, LANES), F32),
            jax.ShapeDtypeStruct((cols, local, D), BF),
            jax.ShapeDtypeStruct((D, 3 * width), BF),
            jax.ShapeDtypeStruct((D, D), BF),
            jax.ShapeDtypeStruct((rows, LANES), F32),
            jax.ShapeDtypeStruct((rows, LANES), F32),
            jax.ShapeDtypeStruct((rows, LANES), F32),
            jax.ShapeDtypeStruct((experts, rows), jnp.int32),
            jax.ShapeDtypeStruct((local, D), BF),
            jax.ShapeDtypeStruct((local, D), F32),
            jax.ShapeDtypeStruct((cols, local, D), BF),
            jax.ShapeDtypeStruct((cols, 16, local), BF),
            jax.ShapeDtypeStruct((cols, local // EARLY, D), BF),
            jax.ShapeDtypeStruct((LANES, D), BF),
            jax.ShapeDtypeStruct((16, LANES), BF),
        ),
        in_specs=[vm] * 12 + [pl.BlockSpec(memory_space=pltpu.SMEM)] + [ANY, ANY, vm] + [ANY] * 3,
        out_specs=(ANY,) * 10 + (vm,) + (ANY,) * 5 + (vm, vm),
        scratch_shapes=[
            pltpu.VMEM((cols, local, D), BF),
            pltpu.VMEM((3, depth, width), BF),
            pltpu.VMEM((3, depth, width), BF),
            pltpu.VMEM((depth, width), BF),
            pltpu.VMEM((cols, depth, width), BF),
            pltpu.VMEM((D, 3 * width), BF),
            pltpu.VMEM((D, D), BF),
            pltpu.VMEM((cols, heads, local // 2, LANES), BF),
            pltpu.VMEM((cols, heads, local // 2, LANES), BF),
            pltpu.VMEM((16, local), BF),
            pltpu.VMEM((cols, 16, local), BF),
            pltpu.VMEM((3 * heads, rows, HEAD_DIM), BF),
            pltpu.VMEM((heads, rows, HEAD_DIM), BF),
            pltpu.VMEM((rows, LANES), F32),
            pltpu.VMEM((rows, LANES), F32),
            pltpu.VMEM((rows, LANES), F32),
            pltpu.VMEM((rows, LANES), F32),
            pltpu.VMEM((local, D), BF),
            pltpu.VMEM((local, D), F32),
            pltpu.VMEM((local, D), BF),
            pltpu.VMEM((3, experts, depth, ff), BF),
            dma((17,)),
            dma((2, cols - 1)),
            dma((2, cols - 1)),
            dma((2, cols - 1)),
            dma((2, cols - 1)),
            dma((2, cols - 1)),
            dma((2, cols - 1)),
            dma((2,)),
            dma((2,)),
            dma((2, cols - 1)),
            dma((2, cols - 1)),
            dma((2, 7)),
            dma((2, 7)),
            dma((3, 2)),
            dma((3, 2)),
            dma((3, 2)),
            dma((3, 2)),
            dma((3, 4)),
            dma((3, 4)),
            dma((heads, cols - 1)),
            dma((heads, cols - 1)),
            pltpu.VMEM((rows, LANES), F32),
            pltpu.VMEM((rows, LANES), F32),
            dma((2,)),
        ],
        compiler_params=pltpu.CompilerParams(
            vmem_limit_bytes=60 * MIB, collective_id=5, has_side_effects=True
        ),
        cost_estimate=pl.CostEstimate(
            flops=8 * heads * rows * rows * HEAD_DIM, bytes_accessed=40 * MIB, transcendentals=heads * rows * rows
        ),
        name="first_step",
    )(x, cot, router, const, vector, again, fgain, carry, wq, wo, prev, routes, lengths, *tables, gate, up, down)


def experts_forward_kernel(
    cols,
    capacity,
    n2_ref,
    prev_ref,
    cot_ref,
    rw_ref,
    carry_ref,
    slots_ref,
    meta_ref,
    w_ref,
    x_ref,
    gu_ref,
    mix_ref,
    gates_ref,
    cotb_ref,
    y_s,
    send,
    recv,
    local_sem,
):
    e = pl.program_id(0)
    experts = pl.num_programs(0)
    r, c = place()
    early = cot_ref.shape[0] // EARLY
    late = cot_ref.at[pl.ds(early, cot_ref.shape[0] - early)]
    step, drain = gather_chain(late, cotb_ref, send, recv, cols)
    own_copy = pltpu.make_async_copy(late, cotb_ref.at[c], local_sem.at[0])

    @pl.when(e == 0)
    def _():
        greet(col_peers(cols))
        own_copy.start()
        step(0)
        prev = jnp.concatenate([mm(prev_ref[i], carry_ref[...], TN) for i in range(cols)], axis=0)
        g = gate_lanes(mm(n2_ref[...], rw_ref[...], NT) + prev, meta_ref[...])
        high = g.astype(BF)
        gates_ref[:, :LANES] = high
        gates_ref[:, LANES:] = (g - high.astype(F32)).astype(BF)

    @pl.when(e == 3)
    def _():
        step(1)

    @pl.when(e == 6)
    def _():
        step(2)

    one = slot_rows(slots_ref, e, capacity)
    x = mm(one, n2_ref[...]).astype(BF)
    x_ref[0] = x
    sg = slot_gates(one, gates_ref, e)
    g = mm(x, w_ref[0, 0])
    u = mm(x, w_ref[1, 0])
    gu_ref[0, 0] = g.astype(BF)
    gu_ref[0, 1] = u.astype(BF)
    gh = (g * jax.nn.sigmoid(g) * u * sg).astype(BF)
    y_s[e] = mm(gh, w_ref[2, 0], NT).astype(BF)

    @pl.when(e == experts - 1)
    def _():
        for d in range(cols):
            mix_ref[d] = combine(meta_ref, y_s, d, mix_ref.shape[1])
        for k in range(3, cols):
            step(k)
        drain()
        own_copy.wait()


def experts_forward(cols, n2, prev, cot, rw, carry, meta, slots, w_all):
    rows = n2.shape[0]
    capacity = rows // 4
    three, experts, deep, ff = w_all.shape
    local = rows // cols
    rest = local - local // EARLY
    return pl.pallas_call(
        functools.partial(experts_forward_kernel, cols, capacity),
        grid=(experts,),
        out_shape=(
            jax.ShapeDtypeStruct((experts, capacity, D), BF),
            jax.ShapeDtypeStruct((experts, 2, capacity, ff), BF),
            jax.ShapeDtypeStruct((cols, local, D), BF),
            jax.ShapeDtypeStruct((rows, 2 * LANES), BF),
            jax.ShapeDtypeStruct((cols, rest, D), BF),
        ),
        in_specs=[
            whole((rows, D)),
            whole((cols, 16, local)),
            whole((local, D)),
            whole((LANES, D)),
            whole((16, LANES)),
            whole((experts, rows)),
            whole((rows, LANES)),
            pl.BlockSpec((three, 1, deep, ff), lambda e: (0, e, 0, 0)),
        ],
        out_specs=(
            pl.BlockSpec((1, capacity, D), lambda e: (e, 0, 0)),
            pl.BlockSpec((1, 2, capacity, ff), lambda e: (e, 0, 0, 0)),
            whole((cols, local, D)),
            whole((rows, 2 * LANES)),
            ANY,
        ),
        scratch_shapes=[
            pltpu.VMEM((experts, capacity, D), BF),
            pltpu.SemaphoreType.DMA((2, cols - 1)),
            pltpu.SemaphoreType.DMA((2, cols - 1)),
            pltpu.SemaphoreType.DMA((1,)),
        ],
        compiler_params=pltpu.CompilerParams(
            vmem_limit_bytes=60 * MIB, collective_id=1, has_side_effects=True
        ),
        cost_estimate=pl.CostEstimate(
            flops=experts * capacity * 2 * D * (3 * ff + rows),
            bytes_accessed=40 * MIB,
            transcendentals=experts * capacity * ff,
        ),
        name="experts_forward",
    )(n2, prev, cot, rw, carry, slots, meta, w_all)


def experts_backward_kernel(
    cols,
    capacity,
    cota_ref,
    cotb_ref,
    mix_s,
    gates_ref,
    slots_ref,
    meta_ref,
    w_ref,
    x_ref,
    gu_ref,
    dx_ref,
    dots_ref,
    mixsum_ref,
    gown_ref,
    sib_ref,
    hin_ref,
    glast_ref,
    cot_s,
    gbuf,
    out,
    arrived,
    send,
    recv,
    own_sem,
    sib_send,
    sib_recv,
    cot_sem,
    lbuf,
    hbuf,
    l_sem,
    hsend,
    hrecv,
):
    e = pl.program_id(0)
    experts = pl.num_programs(0)
    r, c = place()
    core = r % 2
    local = mix_s.shape[1]
    early = cota_ref.shape[1]
    place_now = lax.rem(e, 2)
    slot, total, drain = reduce_chain(lambda d: mix_s[d], out, arrived, send, recv, cols)

    def own_copy(expert, at):
        return pltpu.make_async_copy(gbuf.at[at, :, :, core], gown_ref.at[expert], own_sem.at[at])

    def last_copy(at):
        return pltpu.make_async_copy(gbuf.at[at, :, :, 1 - core], glast_ref, sib_send.at[at])

    def sib_copy(expert, at):
        return send_to(
            gbuf.at[at, :, :, 1 - core],
            sib_ref.at[expert],
            sib_send.at[at],
            sib_recv.at[expert],
            (flip(r, 1), c),
        )

    cot_loads = moves(
        [(cota_ref.at[d], cot_s.at[pl.ds(d * local, early)]) for d in range(cols)]
        + [(cotb_ref.at[d], cot_s.at[pl.ds(d * local + early, local - early)]) for d in range(cols)],
        cot_sem,
    )
    before = jnp.maximum(e - 1, 0)
    sib_load = pltpu.make_async_copy(sib_ref.at[before], lbuf, l_sem.at[0])
    sends_now = (e >= 1) & (e <= SENT_SOON)

    def h_sends(i):
        return to_chips(lambda there: hbuf.at[i, :, there], hin_ref.at[i], hsend.at[i], hrecv.at[i])

    @pl.when(e == 0)
    def _():
        start_all(cot_loads)
        greet(col_peers(cols) + [(flip(r, m), c) for m in (1, 2, 4, 6)])
        slot(0)
        wait_all(cot_loads)

    @pl.when(e == 2)
    def _():
        slot(1)

    @pl.when(e == 5)
    def _():
        slot(2)

    one = slot_rows(slots_ref, e, capacity)
    ct = mm(one, cot_s[...]).astype(BF)
    sg = slot_gates(one, gates_ref, e)
    x = x_ref[0]
    g, u = gu_ref[0, 0].astype(F32), gu_ref[0, 1].astype(F32)
    v = mm(ct, w_ref[2, 0])
    sig = jax.nn.sigmoid(g)
    act = g * sig
    h = act * u
    dot = jnp.sum(h * v, axis=1, keepdims=True)
    dots_ref[pl.ds(e, 1)] = jnp.sum(one.astype(F32) * dot, axis=0, keepdims=True)
    gh = (h * sg).astype(BF)
    gv = v * sg
    dg = (gv * u * (sig * (1.0 + g * (1.0 - sig)))).astype(BF)
    du = (gv * act).astype(BF)
    dx_ref[0] = (mm(dg, w_ref[0, 0], NT) + mm(du, w_ref[1, 0], NT)).astype(BF)

    @pl.when(e >= 2)
    def _():
        own_copy(e - 2, place_now).wait()
        sib_copy(e - 2, place_now).wait_send()

    @pl.when(sends_now)
    def _():
        sib_copy(before, 1 - place_now).wait_recv()
        sib_load.start()

    shape = gbuf.shape[2:]
    pair = mm(x, jnp.concatenate([dg, du], axis=1), TN).astype(BF)
    gbuf[place_now, 0] = pair[:, : dg.shape[1]].reshape(shape)
    gbuf[place_now, 1] = pair[:, dg.shape[1] :].reshape(shape)
    gbuf[place_now, 2] = mm(ct, gh, TN).astype(BF).reshape(shape)
    own_copy(e, place_now).start()

    @pl.when(e < experts - 1)
    def _():
        sib_copy(e, place_now).start()

    @pl.when(e == experts - 1)
    def _():
        last_copy(place_now).start()

    @pl.when(sends_now)
    def _():
        sib_load.wait()
        hbuf[before] = (gbuf[1 - place_now, :, :, core].astype(F32) + lbuf[...].astype(F32)).astype(BF)
        start_all(h_sends(before))

    @pl.when(e == experts - 1)
    def _():
        for s in range(3, cols):
            slot(s)
        total(mixsum_ref)
        drain()
        for back in (1, 0):
            own_copy(e - back, lax.rem(e - back, 2)).wait()
        sib_copy(e - 1, 1 - place_now).wait_send()
        last_copy(place_now).wait()
        for i in range(SENT_SOON, EXPERTS - 1):
            sib_copy(i, i % 2).wait_recv()
        for i in range(SENT_SOON):
            wait_all(h_sends(i))


def experts_backward(cols, ranks, cota, cotb, mix, gates, meta, slots, w_all, x, gu):
    experts, capacity, _ = x.shape
    rows = slots.shape[1]
    three, _, deep, ff = w_all.shape
    local = rows // cols
    chips = ranks // 2
    depth = deep // ranks
    half = jax.ShapeDtypeStruct((experts, three, chips, depth, ff), BF)
    return pl.pallas_call(
        functools.partial(experts_backward_kernel, cols, capacity),
        grid=(experts,),
        out_shape=(
            jax.ShapeDtypeStruct((experts, capacity, D), BF),
            jax.ShapeDtypeStruct((experts, rows), F32),
            jax.ShapeDtypeStruct((local, D), F32),
            half,
            half,
            jax.ShapeDtypeStruct((SENT_SOON, 3, three, depth, ff), BF),
            jax.ShapeDtypeStruct((three, chips, depth, ff), BF),
        ),
        in_specs=[
            ANY,
            ANY,
            whole((cols, local, D)),
            whole((rows, 2 * LANES)),
            whole((experts, rows)),
            whole((rows, LANES)),
            pl.BlockSpec((three, 1, deep, ff), lambda e: (0, e, 0, 0)),
            pl.BlockSpec((1, capacity, D), lambda e: (e, 0, 0)),
            pl.BlockSpec((1, 2, capacity, ff), lambda e: (e, 0, 0, 0)),
        ],
        out_specs=(
            pl.BlockSpec((1, capacity, D), lambda e: (e, 0, 0)),
            whole((experts, rows)),
            whole((local, D)),
            ANY,
            ANY,
            ANY,
            ANY,
        ),
        scratch_shapes=[
            pltpu.VMEM((rows, D), BF),
            pltpu.VMEM((2, three, chips, 2, depth, ff), BF),
            *chain_scratch(cols, local),
            pltpu.SemaphoreType.DMA((2,)),
            pltpu.SemaphoreType.DMA((2,)),
            pltpu.SemaphoreType.DMA((experts,)),
            pltpu.SemaphoreType.DMA((2 * cols,)),
            pltpu.VMEM((three, chips, depth, ff), BF),
            pltpu.VMEM((SENT_SOON, three, chips, depth, ff), BF),
            pltpu.SemaphoreType.DMA((1,)),
            pltpu.SemaphoreType.DMA((SENT_SOON, 3)),
            pltpu.SemaphoreType.DMA((SENT_SOON, 3)),
        ],
        compiler_params=pltpu.CompilerParams(
            vmem_limit_bytes=60 * MIB, collective_id=2, has_side_effects=True
        ),
        cost_estimate=pl.CostEstimate(
            flops=experts * capacity * 4 * D * (3 * ff + rows),
            bytes_accessed=60 * MIB,
            transcendentals=experts * capacity * ff,
        ),
        name="experts_backward",
    )(cota, cotb, mix, gates, slots, meta, w_all, x, gu)


def resid_kernel(
    cols,
    count,
    dx_in,
    meta_in,
    dots_ref,
    rw_ref,
    prev_ref,
    carry_ref,
    cot_ref,
    mixsum_in,
    n2w_in,
    middle_in,
    out_t_in,
    mixed_in,
    gown_ref,
    glast_ref,
    sib_in,
    layer_ref,
    resid_ref,
    gm_ref,
    og_ref,
    small_ref,
    pg_ref,
    hin_ref,
    hrest_ref,
    sib_ref,
    mixsum,
    n2_s,
    middle_s,
    out_t,
    mixed_s,
    resid_s,
    load_sem,
    gt_s,
    out,
    arrived,
    send,
    recv,
    dots_in,
    dsend,
    drecv,
    grad,
    gm_out,
    gsend,
    grecv,
    gm_sem,
    lbuf,
    hbuf,
    hload,
    hsend,
    hrecv,
    hkeep,
    last_sem,
    og_s,
    og_sib,
    dx_ref,
    meta_ref,
    soon_sem,
):
    r, c = place()
    chip = r // 2
    local = cot_ref.shape[0]
    held = hbuf.shape[0]
    loads = moves(
        [
            (n2w_in.at[c], n2_s),
            (middle_in, middle_s),
            (mixsum_in, mixsum),
            (out_t_in, out_t),
            (mixed_in, mixed_s),
        ],
        load_sem,
    )
    soon = moves([(meta_in, meta_ref), (dx_in, dx_ref)], soon_sem)
    start_all(soon)
    greet(col_peers(cols) + [(flip(r, m), c) for m in (1, 2, 4, 6)])
    last = gown_ref.shape[0] - 1
    across = send_to(glast_ref, sib_ref.at[last], last_sem.at[0], last_sem.at[1], (flip(r, 1), c))
    across.start()
    slot, total, drain = reduce_chain(lambda d: gt_s[d], out, arrived, send, recv, cols)

    def dots_of(d):
        return dots_ref.at[:, pl.ds(pl.multiple_of(d * local, LANES), local)]

    dot_copies = to_cols(dots_of, dots_in, dsend, drecv, cols)
    start_all(dot_copies)
    dots_in[c] = dots_of(c)[...]
    wait_all(soon)
    for n, d in enumerate(chain_order(c)):
        gt_s[d] = combine(meta_ref, dx_ref, d, local)
        if n == 0:
            slot(0)

    def h_loads(i):
        at = lax.rem(i, 2)
        return [
            pltpu.make_async_copy(ref.at[SENT_SOON + i], lbuf.at[at, j], hload.at[at, j])
            for j, ref in enumerate((gown_ref, sib_ref))
        ]

    def h_sends(i):
        return to_chips(lambda there: hbuf.at[i, :, there], hin_ref.at[i], hsend.at[i], hrecv.at[i])

    def h_keeps(i):
        return moves(
            [(hbuf.at[i, :, flip(chip, k)], hrest_ref.at[i - count, k - 1]) for k in range(1, 4)],
            hkeep.at[i - count],
        )

    start_all(h_loads(0))

    def add_cores(i, carry):
        @pl.when(i + 2 == held)
        def _():
            across.wait()

        @pl.when(i + 1 < held)
        def _():
            start_all(h_loads(i + 1))

        wait_all(h_loads(i))
        at = lax.rem(i, 2)
        hbuf[i] = (lbuf[at, 0].astype(F32) + lbuf[at, 1].astype(F32)).astype(BF)

        @pl.when(i < count)
        def _():
            start_all(h_sends(i))

        @pl.when(i >= count)
        def _():
            start_all(h_keeps(jnp.maximum(i, count)))

        return carry

    lax.fori_loop(0, held, add_cores, 0)
    start_all(loads)
    slot(1)
    wait_all(loads)

    meta = meta_ref[pl.ds(pl.multiple_of(c * local, LANES), local)]
    n2, cot = n2_s[...], cot_ref[...]
    n2f, cotf = n2.astype(F32), cot.astype(F32)
    middle = middle_s[...]
    rw = rw_ref[...]
    lin = mm(n2, rw, NT)
    prev = prev_ref[c]
    gates = gate_lanes(lin + mm(prev, carry_ref[...], TN), meta)
    lane = lane_iota((local, LANES))
    cot_lin = mm(cot, rw, NT)
    dot_keep = jnp.sum(cotf * n2f, axis=1, keepdims=True)
    wait_all(dot_copies)
    d = jnp.concatenate([all_sum(dots_in, cols), jnp.zeros((LANES - EXPERTS, local), F32)], axis=0).T
    g_gates = jnp.where(lane == EXPERTS + 1, dot_keep, d)
    keep = gates[:, EXPERTS + 1 : EXPERTS + 2]
    mixes, packs = [], jnp.zeros((local, LANES), F32)
    for j in range(2):
        l0 = lin[:, ROW_CONST + 2 * j : ROW_CONST + 2 * j + 1]
        l1 = lin[:, ROW_CONST + 2 * j + 1 : ROW_CONST + 2 * j + 2]
        top = jnp.maximum(l0, l1)
        e0, e1 = jnp.exp(l0 - top), jnp.exp(l1 - top)
        a0, a1 = e0 / (e0 + e1), e1 / (e0 + e1)
        share = gates[:, EXPERTS + 2 + j : EXPERTS + 3 + j]
        dot_vec = cot_lin[:, ROW_VEC + j : ROW_VEC + j + 1]
        keep = keep + share * a0
        mixes.append(share * a1)
        g_gates = jnp.where(lane == EXPERTS + 2 + j, a0 * dot_keep + a1 * dot_vec, g_gates)
        gk, gv = share * dot_keep, share * dot_vec
        mean = a0 * gk + a1 * gv
        packs = packs + jnp.where(lane == ROW_CONST + 2 * j, a0 * (gk - mean), 0.0)
        packs = packs + jnp.where(lane == ROW_CONST + 2 * j + 1, a1 * (gv - mean), 0.0)
        packs = packs + jnp.where(lane == ROW_VEC + j, share * a1, 0.0)
    packs = packs + gates * (g_gates - jnp.sum(gates * g_gates, axis=1, keepdims=True))
    vec = rw[ROW_VEC : ROW_VEC + 2].astype(F32)
    layer = middle + mixsum[...] + keep * n2f + mixes[0] * vec[0:1] + mixes[1] * vec[1:2]
    layer_ref[...] = layer.astype(BF)

    high = packs.astype(BF)
    low = (packs - high.astype(F32)).astype(BF)
    back = lane < ROW_VEC
    high_b = jnp.where(back, packs, 0.0).astype(BF)
    low_b = jnp.where(back, packs - high.astype(F32), 0.0).astype(BF)
    grad_local = keep * cotf + mm(high_b, rw) + mm(low_b, rw)
    by_n2 = mm(high, n2, TN) + mm(low, n2, TN)
    by_cot = mm(high, cot, TN) + mm(low, cot, TN)
    by_prev = mm(prev, high) + mm(prev, low)
    pg = mm(carry_ref[...], high_b, NT) + mm(carry_ref[...], low_b, NT)
    pg_ref[...] = pg[:ROUTES]
    sub = lax.broadcasted_iota(jnp.int32, (SMALL_ROWS, D), 0)
    small_ref[:, :D] = jnp.where(sub < ROW_VEC, by_n2[:SMALL_ROWS], by_cot[:SMALL_ROWS])
    small_ref[:16, D : D + LANES] = by_prev
    small_ref[16:, D : D + LANES] = jnp.zeros((SMALL_ROWS - 16, LANES), F32)
    small_ref[:, D + LANES :] = jnp.zeros((SMALL_ROWS, LANES), F32)
    fgain = rw[ROW_GAIN + 1 : ROW_GAIN + 2].astype(F32)
    scale = norm_rows(middle)

    for s in range(2, cols):
        slot(s)
    total(grad)
    grad_normed = grad[...] + grad_local
    gained = grad_normed * fgain
    mid_dot = jnp.sum(gained * middle, axis=1, keepdims=True)
    resid = cotf + scale * gained - middle * (scale * scale * scale * (mid_dot * (1.0 / D)))
    cut = resid.astype(BF)
    gm = (mm(cut, out_t[...]) * meta[:, META_VALID : META_VALID + 1]).astype(BF)
    width = D // cols
    for i in range(cols):
        for h in range(width // HEAD_DIM):
            at = i * width + h * HEAD_DIM
            gm_out[i, h] = pack_head(gm[:, at : at + HEAD_DIM])
    gm_copies = to_cols(lambda i: gm_out.at[i], gm_ref, gsend, grecv, cols)
    start_all(gm_copies)
    resid_s[...] = resid
    stored = moves([(gm_out.at[c], gm_ref.at[c]), (resid_s, resid_ref)], gm_sem)
    start_all(stored)
    small_ref[ROW_GAIN : ROW_GAIN + 1, :D] = jnp.sum(grad_normed * middle * scale, axis=0, keepdims=True)
    core = r % 2
    og_s[...] = mm(cut, mixed_s[...], TN).astype(BF).reshape(og_s.shape)
    og_across = send_to(og_s.at[:, 1 - core], og_sib, last_sem.at[2], last_sem.at[3], (flip(r, 1), c))
    og_across.start()
    og_across.wait()
    for k in range(og_s.shape[0]):
        og_ref[k] = (og_s[k, core].astype(F32) + og_sib[k].astype(F32)).astype(BF)
    wait_all(stored + gm_copies)
    drain()

    def end(i, carry):
        @pl.when(i < count)
        def _():
            wait_all(h_sends(i))

        @pl.when(i >= count)
        def _():
            wait_all(h_keeps(jnp.maximum(i, count)))

        return carry

    lax.fori_loop(0, held, end, 0)


def resid_step(cols, dx, meta, dots, rw, prev, carry, cot, mixsum, n2w, middle, out_t, mixed, gown, glast, sib):
    local = cot.shape[0]
    experts, three, chips, depth, ff = gown.shape
    count, held = SENT_NEXT, experts - SENT_SOON
    vm = pl.BlockSpec(memory_space=pltpu.VMEM)
    dma = pltpu.SemaphoreType.DMA
    return pl.pallas_call(
        functools.partial(resid_kernel, cols, count),
        out_shape=(
            jax.ShapeDtypeStruct((local, D), BF),
            jax.ShapeDtypeStruct((local, D), F32),
            jax.ShapeDtypeStruct((cols, 3, local // 2, LANES), BF),
            jax.ShapeDtypeStruct((chips, depth, D), BF),
            jax.ShapeDtypeStruct((SMALL_ROWS, D + 2 * LANES), F32),
            jax.ShapeDtypeStruct((ROUTES, local), F32),
            jax.ShapeDtypeStruct((count, 3, three, depth, ff), BF),
            jax.ShapeDtypeStruct((held - count, 3, three, depth, ff), BF),
            jax.ShapeDtypeStruct(sib.shape, BF),
        ),
        in_specs=[ANY] * 2 + [vm] * 5 + [ANY] * 8,
        out_specs=(vm, ANY, ANY, vm, vm, vm, ANY, ANY, ANY),
        input_output_aliases={14: 8},
        scratch_shapes=[
            pltpu.VMEM((local, D), F32),
            pltpu.VMEM((local, D), BF),
            pltpu.VMEM((local, D), F32),
            pltpu.VMEM((D, D), BF),
            pltpu.VMEM((local, D), BF),
            pltpu.VMEM((local, D), F32),
            dma((5,)),
            pltpu.VMEM((cols, local, D), BF),
            *chain_scratch(cols, local),
            pltpu.VMEM((cols, EXPERTS, local), F32),
            dma((cols - 1,)),
            dma((cols - 1,)),
            pltpu.VMEM((local, D), F32),
            pltpu.VMEM((cols, 3, local // 2, LANES), BF),
            dma((cols - 1,)),
            dma((cols - 1,)),
            dma((2,)),
            pltpu.VMEM((2, 2, three, chips, depth, ff), BF),
            pltpu.VMEM((held, three, chips, depth, ff), BF),
            dma((2, 2)),
            dma((count, 3)),
            dma((count, 3)),
            dma((held - count, 3)),
            dma((4,)),
            pltpu.VMEM((chips, 2, depth, D), BF),
            pltpu.VMEM((chips, depth, D), BF),
            pltpu.VMEM(dx.shape, BF),
            pltpu.VMEM(meta.shape, F32),
            dma((2,)),
        ],
        compiler_params=pltpu.CompilerParams(
            vmem_limit_bytes=60 * MIB, collective_id=3, has_side_effects=True
        ),
        cost_estimate=pl.CostEstimate(flops=6 * local * D * D, bytes_accessed=40 * MIB, transcendentals=0),
        name="resid_step",
    )(dx, meta, dots, rw, prev, carry, cot, mixsum, n2w, middle, out_t, mixed, gown, glast, sib)


def finish_kernel(
    cols,
    ranks,
    gm_in,
    meta_in,
    lse_in,
    small_ref,
    og_ref,
    xown_ref,
    rw_ref,
    qkv_in,
    o_in,
    x_in,
    w_in,
    cos_in,
    sin_in,
    resid_in,
    gown_ref,
    sib_ref,
    hsoon_ref,
    hin0_ref,
    hrest_ref,
    ig_ref,
    small_out,
    qg_out,
    og_out,
    gg_ref,
    ug_ref,
    dg_ref,
    hin_ref,
    qkv_s,
    o_s,
    x_s,
    w_s,
    cos_s,
    sin_s,
    resid_s,
    head_sem,
    load_sem,
    do_s,
    dq_s,
    dk_s,
    dv_s,
    gn_s,
    qg_acc,
    qg_cut,
    out,
    arrived,
    send,
    recv,
    small_s,
    small_rows,
    small_cols,
    small_all,
    og_chips,
    og_parts,
    og_cols,
    qg_sib,
    qg_half,
    qg_chips,
    q_parts,
    q_land,
    total_s,
    fbuf,
    fsem,
    row_send,
    row_recv,
    chip_send,
    chip_recv,
    sib_send,
    sib_recv,
    col_send,
    col_recv,
    hsend,
    hrecv,
    g_s,
    store_sem,
    gm_ref,
    meta_ref,
    lse_ref,
    soon_sem,
):
    r, c = place()
    chip, core = r // 2, r % 2
    heads = 3
    rows = meta_ref.shape[0]
    local = rows // cols
    width = heads * HEAD_DIM
    rest = hrest_ref.shape[0]
    first = gown_ref.shape[0] - rest
    score_scale = 1.0 / math.sqrt(HEAD_DIM)

    def head_loads(h):
        pairs = [(qkv_in.at[i * heads + h], qkv_s.at[i * heads + h]) for i in range(3)]
        return moves(pairs + [(o_in.at[h], o_s.at[h])], head_sem.at[h])

    loads = moves(
        [(x_in, x_s), (w_in, w_s), (cos_in, cos_s), (sin_in, sin_s), (resid_in, resid_s)], load_sem
    )
    soon = moves([(gm_in, gm_ref), (meta_in, meta_ref), (lse_in, lse_ref)], soon_sem)
    start_all(soon)
    start_all(head_loads(0))
    greet(col_peers(cols) + [(flip(r, m), c) for m in range(1, ranks)])
    for h in range(1, heads):
        start_all(head_loads(h))
    start_all(loads)

    def to_sibling(src, dst, at):
        return send_to(src.at[:, 1 - core], dst, sib_send.at[at], sib_recv.at[at], (flip(r, 1), c))

    og_to_chips = to_chips(lambda there: og_ref.at[there], og_chips, chip_send.at[0], chip_recv.at[0])
    start_all(og_to_chips)

    wait_all(soon)
    for d in range(cols):
        at = slice(d * local, (d + 1) * local)
        for h in range(heads):
            do_s[h, at] = unpack_head(gm_ref[d, h])

    def halves(ref, sib, half):
        for k in range(ranks // 2):
            half[k] = (ref[k, core].astype(F32) + sib[k].astype(F32)).astype(BF)

    def h_sends(i):
        r_, c_ = place()
        return [
            send_to(
                hrest_ref.at[i, k - 1],
                hin_ref.at[i, k - 1],
                hsend.at[i, k - 1],
                hrecv.at[i, k - 1],
                (flip(r_, 2 * k), c_),
            )
            for k in range(1, 4)
        ]

    def start_sends(i, carry):
        start_all(h_sends(i))
        return carry

    lax.fori_loop(0, rest - 1, start_sends, 0)

    blocks = rows // Q_ROWS

    def one_head(h, carry):
        wait_all(head_loads(h))
        for i in reversed(range(blocks)):
            at = slice(i * Q_ROWS, (i + 1) * Q_ROWS)
            length = (i + 1) * Q_ROWS
            q, do = qkv_s[h, at], do_s[h, at]
            k, v = qkv_s[heads + h, :length], qkv_s[2 * heads + h, :length]
            delta = jnp.sum(do.astype(F32) * o_s[h, at].astype(F32), axis=1, keepdims=True)
            lse = jnp.sum(jnp.where(lane_iota((Q_ROWS, LANES)) == h, lse_ref[at], 0.0), axis=1, keepdims=True)
            s = mm(q, k, NT)
            ok = seen(column(meta_ref, at, META_BEGIN).astype(jnp.int32), i * Q_ROWS, Q_ROWS, length)
            p = jnp.where(ok, jnp.exp(s - lse), 0.0)
            ds = (p * (mm(do, v, NT) - delta)).astype(BF)
            dq_s[h, at] = mm(ds, k) * score_scale
            dk, dv = mm(ds, q, TN), mm(p.astype(BF), do, TN)
            if i == blocks - 1:
                dk_s[h], dv_s[h] = dk, dv
            else:
                dk_s[h, :length] += dk
                dv_s[h, :length] += dv
        return carry

    lax.fori_loop(0, heads, one_head, 0)

    slot, total, drain = reduce_chain(lambda d: gn_s[d], out, arrived, send, recv, cols)
    wait_all(loads)
    gain_total = jnp.zeros((1, D), F32)
    weight = w_s[...]
    again = rw_ref[ROW_GAIN : ROW_GAIN + 1].astype(F32)
    for n, d in enumerate(chain_order(c)):
        at = pl.ds(pl.multiple_of(d * local, LANES), local)
        cosine, sines = cos_s[at], sin_s[at]
        turned = [dq_s[h, at] for h in range(heads)] + [dk_s[h, at] for h in range(heads)]
        parts = []
        for part in range(heads):
            v = jnp.concatenate(turned[2 * part : 2 * part + 2], axis=1)
            parts.append((v * cosine - swap_pairs(v) * sines).astype(BF))
        parts += [dv_s[h, at].astype(BF) for h in range(heads)]
        gp = jnp.concatenate(parts, axis=1)
        x = x_s[d].astype(F32)
        xs = x * norm_rows(x)
        gn = mm(gp, weight, NT)
        gn_s[d] = gn.astype(BF)
        if n == 0:
            slot(0)
        gain_total = gain_total + jnp.sum(gn * xs, axis=0, keepdims=True)
        grad = mm((xs * again).astype(BF), gp, TN)
        if n == 0:
            qg_acc[...] = grad
        else:
            qg_acc[...] += grad
    qg_cut[...] = qg_acc[...].astype(BF).reshape(qg_cut.shape)
    qg_across = to_sibling(qg_cut, qg_sib, 0)
    qg_across.start()

    sub = lax.broadcasted_iota(jnp.int32, (SMALL_ROWS, D), 0)
    for i in range(ranks):
        block = small_ref[:, i * LANES : (i + 1) * LANES]
        if i < D // LANES:
            own = sub[:, :LANES] == ROW_GAIN + 1
            block = jnp.where(own, gain_total[:, i * LANES : (i + 1) * LANES], block)
        small_s[i] = block
    small_to_rows = to_rows(lambda d: small_s.at[d], small_rows, row_send.at[0], row_recv.at[0], ranks)
    start_all(small_to_rows)
    small_rows[r] = small_s[r]

    def sum_grads(low, high, hin, base):
        def f_loads(i):
            at = lax.rem(i, 2)
            return moves(
                [
                    (gown_ref.at[i, :, chip], fbuf.at[at, 0]),
                    (sib_ref.at[i, :, chip], fbuf.at[at, 1]),
                    (hin.at[i - base], fbuf.at[at, pl.ds(2, 3)]),
                ],
                fsem.at[at],
            )

        start_all(f_loads(low))

        def body(i, carry):
            @pl.when(i + 1 < high)
            def _():
                start_all(f_loads(jnp.minimum(i + 1, high - 1)))

            wait_all(f_loads(i))
            at = lax.rem(i, 2)
            total_grad = fbuf[at, 0].astype(F32)
            for j in range(1, 5):
                total_grad = total_grad + fbuf[at, j].astype(F32)
            for t in range(3):
                g_s[t, i] = total_grad[t].astype(BF)
            return carry

        lax.fori_loop(low, high, body, 0)

    qg_across.wait()
    halves(qg_cut, qg_sib, qg_half)
    qg_to_chips = to_chips(lambda there: qg_half.at[there], qg_chips, chip_send.at[1], chip_recv.at[1])
    start_all(qg_to_chips)
    start_sends(rest - 1, 0)
    slot(1)
    sum_grads(0, SENT_SOON, hsoon_ref, 0)
    wait_all(small_to_rows)
    small_cols[c] = all_sum(small_rows, ranks)
    small_to_cols = to_cols(lambda d: small_cols.at[c], small_cols, col_send.at[0], col_recv.at[0], cols)
    start_all(small_to_cols)
    sum_grads(SENT_SOON, first, hin0_ref, SENT_SOON)
    slot(2)
    wait_all(og_to_chips)
    og_sum = og_ref[chip].astype(F32) + all_sum(og_chips, 3)
    for i in range(cols):
        og_parts[i] = og_sum[:, i * width : (i + 1) * width]
    og_to_cols = to_cols(lambda d: og_parts.at[d], og_cols, col_send.at[1], col_recv.at[1], cols)
    start_all(og_to_cols)
    og_cols[c] = og_parts[c]
    wait_all(qg_to_chips)
    q_sum = qg_cut[chip, core].astype(F32) + qg_sib[chip].astype(F32) + all_sum(qg_chips, 3)
    for i in range(3):
        q_parts[i] = q_sum[:, i * width : (i + 1) * width]
    odd, high = c % 2, c // 2
    q_copies = [
        send_to(
            q_parts.at[1 - odd + high],
            q_land.at[1],
            col_send.at[2, 0],
            col_recv.at[2, 0],
            (r, flip(c, 1)),
        ),
        send_to(
            q_parts.at[2 - 2 * high],
            q_land.at[2 - 2 * odd],
            col_send.at[2, 1],
            col_recv.at[2, 1],
            (r, flip(c, 2)),
        ),
    ]
    start_all(q_copies)
    q_land[2 * odd] = q_parts[(c + 1) // 2]
    wait_all(small_to_cols)
    small_all[r] = all_sum(small_cols, cols)
    small_back = to_rows(lambda d: small_all.at[r], small_all, row_send.at[1], row_recv.at[1], ranks)
    start_all(small_back)

    def end_sends(i, carry):
        wait_all(h_sends(i))
        return carry

    lax.fori_loop(0, rest, end_sends, 0)
    sum_grads(first, first + rest, hin_ref, first)
    wait_all(og_to_cols + q_copies + small_back)
    og_out[...] = all_sum(og_cols, cols)
    for i in range(3):
        qg_out[:, i * width : (i + 1) * width] = q_land[i]
    stored = moves([(g_s.at[i], ref) for i, ref in enumerate((gg_ref, ug_ref, dg_ref))], store_sem)
    start_all(stored)
    for i in range(ranks):
        small_out[:, i * LANES : (i + 1) * LANES] = small_all[i]
    slot(3)
    total(total_s)
    gn = total_s[...]
    x = xown_ref[...].astype(F32)
    scale = norm_rows(x)
    gained = gn * again
    x_dot = jnp.sum(gained * x, axis=1, keepdims=True)
    ig_ref[...] = resid_s[...] + scale * gained - x * (scale * scale * scale * (x_dot * (1.0 / D)))
    wait_all(stored)
    drain()


def finish_step(cols, ranks, gm, meta, lse, small, og, xown, rw, qkv, o, x, w, cosine, sines, resid, gown, sib, hsoon, hin0, hrest):
    rows = meta.shape[0]
    local = rows // cols
    experts, three, chips, depth, ff = gown.shape
    rest = hrest.shape[0]
    heads, width = 3, 3 * HEAD_DIM
    vm = pl.BlockSpec(memory_space=pltpu.VMEM)
    dma = pltpu.SemaphoreType.DMA
    wide = D + 2 * LANES
    weight_grad = jax.ShapeDtypeStruct((experts, depth, ff), BF)
    return pl.pallas_call(
        functools.partial(finish_kernel, cols, ranks),
        out_shape=(
            jax.ShapeDtypeStruct((local, D), F32),
            jax.ShapeDtypeStruct((SMALL_ROWS, wide), F32),
            jax.ShapeDtypeStruct((depth, 3 * width), F32),
            jax.ShapeDtypeStruct((depth, width), F32),
            weight_grad,
            weight_grad,
            weight_grad,
            jax.ShapeDtypeStruct((rest, 3, three, depth, ff), BF),
        ),
        in_specs=[ANY] * 3 + [vm] * 4 + [ANY] * 12,
        out_specs=(vm,) * 4 + (ANY,) * 4,
        scratch_shapes=[
            pltpu.VMEM((3 * heads, rows, HEAD_DIM), BF),
            pltpu.VMEM((heads, rows, HEAD_DIM), BF),
            pltpu.VMEM((cols, local, D), BF),
            pltpu.VMEM((D, 3 * width), BF),
            pltpu.VMEM((rows, LANES), F32),
            pltpu.VMEM((rows, LANES), F32),
            pltpu.VMEM((local, D), F32),
            dma((heads, 4)),
            dma((5,)),
            pltpu.VMEM((heads, rows, HEAD_DIM), BF),
            pltpu.VMEM((heads, rows, HEAD_DIM), F32),
            pltpu.VMEM((heads, rows, HEAD_DIM), F32),
            pltpu.VMEM((heads, rows, HEAD_DIM), F32),
            pltpu.VMEM((cols, local, D), BF),
            pltpu.VMEM((D, 3 * width), F32),
            pltpu.VMEM((chips, 2, depth, 3 * width), BF),
            *chain_scratch(cols, local),
            pltpu.VMEM((ranks, SMALL_ROWS, LANES), F32),
            pltpu.VMEM((ranks, SMALL_ROWS, LANES), F32),
            pltpu.VMEM((cols, SMALL_ROWS, LANES), F32),
            pltpu.VMEM((ranks, SMALL_ROWS, LANES), F32),
            pltpu.VMEM((3, depth, D), BF),
            pltpu.VMEM((cols, depth, width), F32),
            pltpu.VMEM((cols, depth, width), F32),
            pltpu.VMEM((chips, depth, 3 * width), BF),
            pltpu.VMEM((chips, depth, 3 * width), BF),
            pltpu.VMEM((3, depth, 3 * width), BF),
            pltpu.VMEM((3, depth, width), F32),
            pltpu.VMEM((3, depth, width), F32),
            pltpu.VMEM((local, D), F32),
            pltpu.VMEM((2, 5, three, depth, ff), BF),
            dma((2, 3)),
            dma((2, ranks - 1)),
            dma((2, ranks - 1)),
            dma((2, 3)),
            dma((2, 3)),
            dma((1,)),
            dma((1,)),
            dma((3, cols - 1)),
            dma((3, cols - 1)),
            dma((rest, 3)),
            dma((rest, 3)),
            pltpu.VMEM((three, experts, depth, ff), BF),
            dma((3,)),
            pltpu.VMEM(gm.shape, BF),
            pltpu.VMEM(meta.shape, F32),
            pltpu.VMEM(lse.shape, F32),
            dma((3,)),
        ],
        compiler_params=pltpu.CompilerParams(
            vmem_limit_bytes=62 * MIB, collective_id=4, has_side_effects=True
        ),
        cost_estimate=pl.CostEstimate(
            flops=20 * heads * rows * rows * HEAD_DIM, bytes_accessed=40 * MIB, transcendentals=heads * rows * rows
        ),
        name="finish_step",
    )(gm, meta, lse, small, og, xown, rw, qkv, o, x, w, cosine, sines, resid, gown, sib, hsoon, hin0, hrest)


def place_kernel(*refs):
    ins, refs = refs[:9], refs[9:]
    outs, refs = refs[:14], refs[14:]
    held, refs = refs[:9], refs[9:]
    made, (load_sem, store_sem) = refs[:8], refs[8:]
    loads = moves(list(zip(ins, held)), load_sem)
    start_all(loads)
    small, qg, og, pg, layer, ig, *low = held
    full, again, out, fgain, router, carry, const, vector = made
    sources = [layer, ig, full.at[0], full.at[1], full.at[2], again, qg, out, fgain, router, carry, const, vector, pg]
    stores = moves(list(zip(sources, outs)), store_sem)
    for load, store in ((4, 0), (5, 1), (1, 6), (3, 13)):
        loads[load].wait()
        stores[store].start()
    for i in range(3):
        loads[6 + i].wait()
        full[i] = low[i][...].astype(F32)
        stores[2 + i].start()
    loads[2].wait()
    out[...] = og[...].T
    loads[0].wait()
    again[...] = small[ROW_GAIN + 1 : ROW_GAIN + 2, :D].reshape(D)
    fgain[...] = small[ROW_GAIN : ROW_GAIN + 1, :D].reshape(D)
    router[...] = small[:ROUTES, :D]
    carry[...] = small[:ROUTES, D : D + ROUTES]
    for j in range(2):
        const[j] = small[ROW_CONST + 2 * j : ROW_CONST + 2 * j + 2, :D]
    vector[...] = small[ROW_VEC : ROW_VEC + 2, :D]
    for i in (5, 7, 8, 9, 10, 11, 12):
        stores[i].start()
    wait_all(stores)


def place_outputs(*values):
    small, qg, og, pg, layer, ig, gg, ug, dg = values
    made = [(D,), og.shape[::-1], (D,), (ROUTES, D), (ROUTES, ROUTES), (2, 2, D), (2, D)]
    shapes = [layer.shape, ig.shape, gg.shape, ug.shape, dg.shape]
    shapes += [made[0], qg.shape, *made[1:], pg.shape]
    return pl.pallas_call(
        place_kernel,
        out_shape=[jax.ShapeDtypeStruct(shape, F32 if i else BF) for i, shape in enumerate(shapes)],
        in_specs=[ANY] * 9,
        out_specs=[ANY] * 14,
        scratch_shapes=[pltpu.VMEM(value.shape, value.dtype) for value in values]
        + [pltpu.VMEM((3, *gg.shape), F32)]
        + [pltpu.VMEM(shape, F32) for shape in made]
        + [pltpu.SemaphoreType.DMA((9,)), pltpu.SemaphoreType.DMA((14,))],
        compiler_params=pltpu.CompilerParams(vmem_limit_bytes=60 * MIB),
        cost_estimate=pl.CostEstimate(flops=0, bytes_accessed=16 * MIB, transcendentals=0),
        name="place_outputs",
    )(*values)


def on_device_heads(
    sizes,
    inputs,
    attn_gain,
    qkv_weight,
    out_weight,
    ffn_gain,
    router_weight,
    carry_weight,
    const_weight,
    const_vector,
    gate_weight,
    up_weight,
    down_weight,
    prev_logits,
    seq_lengths,
    expert_routes,
    cotangent,
):
    ranks, cols = sizes
    row_total = expert_routes.shape[0]
    depth = qkv_weight.shape[0]

    (
        w_all,
        qkv,
        mixed_heads,
        lse,
        whole_in,
        qkv_own,
        out_t,
        cosine,
        sines,
        meta,
        slots,
        mixed,
        middle,
        n2_whole,
        prev_whole,
        cot_early,
        rw,
        carry,
    ) = first_step(
        cols,
        ranks,
        inputs,
        cotangent,
        router_weight.T,
        const_weight.transpose(0, 2, 1),
        const_vector,
        attn_gain,
        ffn_gain,
        carry_weight,
        qkv_weight,
        out_weight,
        prev_logits,
        expert_routes.T,
        seq_lengths,
        gate_weight,
        up_weight,
        down_weight.transpose(0, 2, 1),
    )
    x, gu, mix, gates, cot_late = experts_forward(
        cols, n2_whole.reshape(row_total, D), prev_whole, cotangent, rw, carry, meta, slots, w_all
    )
    dx, dots, mixsum, gown, sib, hsoon, glast = experts_backward(
        cols, ranks, cot_early, cot_late, mix, gates, meta, slots, w_all, x, gu
    )
    layer_out, resid, gm, og, small, prev_grad, hin0, hrest, sib = resid_step(
        cols, dx, meta, dots, rw, prev_whole, carry, cotangent, mixsum, n2_whole, middle, out_t, mixed, gown, glast, sib
    )
    input_grad, small_all, qkv_grad, og_own, gate_grad, up_grad, down_grad, _ = finish_step(
        cols,
        ranks,
        gm,
        meta,
        lse,
        small,
        og,
        inputs,
        rw,
        qkv,
        mixed_heads,
        whole_in,
        qkv_own,
        cosine,
        sines,
        resid,
        gown,
        sib,
        hsoon,
        hin0,
        hrest,
    )
    layer_out, input_grad, gate_grad, up_grad, down_grad, again, qkv_grad, out_grad, fgain, router, carry, const, vector, prev = (
        place_outputs(small_all, qkv_grad, og_own, prev_grad, layer_out, input_grad, gate_grad, up_grad, down_grad)
    )
    return (
        layer_out,
        input_grad,
        again,
        qkv_grad,
        out_grad,
        fgain,
        router.T,
        carry,
        const.transpose(0, 2, 1),
        vector,
        gate_grad,
        up_grad,
        down_grad.transpose(0, 2, 1),
        prev,
    )


def solution(mesh):
    sizes = (mesh.shape["row"], mesh.shape["col"])
    body = functools.partial(on_device_heads, sizes) if sizes == (8, 4) else on_device
    placed = (
        P(("row", "col"), None),
        P(),
        P("row", "col"),
        P("col", "row"),
        P(),
        P(),
        P(),
        P(),
        P(),
        P(None, "row", "col"),
        P(None, "row", "col"),
        P(None, "col", "row"),
        P(None, ("row", "col")),
        P("row", None),
        P("row", None),
        P(("row", "col"), None),
    )
    return jax.shard_map(
        body,
        mesh=mesh,
        in_specs=placed,
        out_specs=(
            P(("row", "col"), None),
            P(("row", "col"), None),
            P(),
            P("row", "col"),
            P("col", "row"),
            P(),
            P(),
            P(),
            P(),
            P(),
            P(None, "row", "col"),
            P(None, "row", "col"),
            P(None, "col", "row"),
            P(None, ("row", "col")),
        ),
        check_vma=False,
    )
```
